32 devices in a mesh: expert: 8 (over y, x, core), hidden: 4 (over z).
Axes of the slice: x: 2, y: 2, z: 4, core: 2. Of those that a mesh axis runs over, the one named last changes fastest.
Arguments:
- tokens: bfloat16 [2, 32, 512, 768], P(None, ('expert', 'hidden')), may hold values from -6 to 6
- cotangent: bfloat16 [2, 32, 512, 768], P(None, ('expert', 'hidden')), may hold values from -6 to 6
- lengths: int32 [2, 32], P(None, ('expert', 'hidden')), may hold values from 256 to 512
- routes: int32 [2, 32, 512, 1], P(None, ('expert', 'hidden')), may hold values from 0 to 63
- gain_attn: float32 [768], replicated, may hold values from 0.1 to 1.9
- w_query: bfloat16 [768, 768], replicated, may hold values from -0.21875 to 0.21875
- w_key: bfloat16 [768, 768], replicated, may hold values from -0.21875 to 0.21875
- w_value: bfloat16 [768, 768], replicated, may hold values from -0.21875 to 0.21875
- w_output: bfloat16 [768, 768], replicated, may hold values from -1.75 to 1.75
- bucket_head_bias: float32 [32, 12], replicated, may hold values from -4 to 4
- gain_ffn: float32 [768], replicated, may hold values from 0.1 to 1.9
- w_router: bfloat16 [768, 64], replicated, may hold values from -0.107910156 to 0.107910156
- w_inner: bfloat16 [64, 768, 3072], P('expert', None, 'hidden'), may hold values from -0.21875 to 0.21875
- w_outer: bfloat16 [64, 3072, 768], P('expert', 'hidden'), may hold values from -10.375 to 10.375
Outputs:
- layer_out: bfloat16 [2, 32, 512, 768], P(None, ('expert', 'hidden'))
- tokens_grad: bfloat16 [2, 32, 512, 768], P(None, ('expert', 'hidden'))
- gain_attn_grad: float32 [768], replicated
- query_grad: float32 [768, 768], replicated
- key_grad: float32 [768, 768], replicated
- value_grad: float32 [768, 768], replicated
- output_grad: float32 [768, 768], replicated
- bias_grad: float32 [32, 12], replicated
- gain_ffn_grad: float32 [768], replicated
- router_grad: float32 [768, 64], replicated
- inner_grad: float32 [64, 768, 3072], P('expert', None, 'hidden')
- outer_grad: float32 [64, 3072, 768], P('expert', 'hidden')
The draws below stay inside these ranges and needn't reach their ends.
All inputs are finite; a program needn't handle non-finite values.
Results may differ from the reference program's by a relative error of at most 0.018.
Values may be sent and summed in bfloat16 or wider, within the bound.
No kernel may reach another device: no remote copies, remote signals or barrier semaphores. Data moves between devices by JAX's collectives and lax.ppermute only.
A program may use at most 320 MiB of HBM per device.

```python
import jax
import jax.numpy as jnp
import numpy as np
from jax import lax

D = 768
HEADS = 12
HEAD_DIM = 64
FF = 3072
BUCKETS = 32
MAXDIST = 128
LEN = 512
MB = 2
NSEQ = 32
EXPERTS = 64
CAP = 10


def set_ends(values, key, least, largest):
    spot = [jax.random.randint(jax.random.fold_in(key, axis), (), 0, length) for axis, length in enumerate(values.shape)]
    widest = values.shape.index(max(values.shape))
    beside = spot[:widest] + [(spot[widest] + 1) % values.shape[widest]] + spot[widest + 1:]
    return values.at[tuple(spot)].set(least).at[tuple(beside)].set(largest)


def block_levels(own_key, shape, cuts, least, top_value):
    level = 1.0
    for position, shards_of in cuts:
        draws = jax.random.uniform(jax.random.fold_in(jax.random.fold_in(own_key, 6), position), (shards_of,), jnp.float32, least / len(cuts), top_value / len(cuts))
        level = level * jnp.repeat(jnp.exp(draws), shape[position] // shards_of).reshape((-1,) + (1,) * (len(shape) - 1 - position))
    return level


def different_ones(key, rows, number_of, top, lift):
    ranking = jax.random.permutation(jax.random.fold_in(key, 1), number_of)
    favour = ranking
    for power in range(3):
        favour = favour * favour // number_of
    favour = favour * lift // number_of
    tickets = jax.random.randint(jax.random.fold_in(key, 2), (rows, number_of), 0, 4096) + favour
    holders = jax.random.permutation(jax.random.fold_in(key, 3), rows)[jnp.arange(number_of) % rows]
    tickets = jnp.where(jnp.arange(rows)[:, None] == holders[None, :], 1 << 14, tickets)
    priority = tickets * number_of + jnp.arange(number_of)
    return lax.top_k(priority.astype(jnp.int32), top)[1].astype(jnp.int32)


def noise(rng, extent, scale, limit, split=(), kind=jnp.bfloat16):
    factor_of = block_levels(rng, extent, split, -0.22, 0.18) if split else 1.0
    array = jax.random.normal(rng, extent, jnp.float32) * scale * factor_of
    return jnp.minimum(jnp.maximum(array, -limit), limit).astype(kind)


def setup_inputs(seed: int = 0) -> dict:
    splits = jax.random.split(jax.random.key(seed), 15)
    return {
        "tokens": noise(splits[0], (MB, NSEQ, LEN, D), 1.0, 6.0, ((1, 32),)),
        "cotangent": noise(splits[1], (MB, NSEQ, LEN, D), 1.0, 6.0, ((1, 32),)),
        "lengths": set_ends(jax.random.randint(splits[2], (MB, NSEQ), LEN // 2, LEN + 1), jax.random.fold_in(splits[2], 1), LEN // 2, LEN).astype(jnp.int32),
        "routes": different_ones(splits[3], MB * NSEQ * LEN, EXPERTS, 1, 128).reshape((MB, NSEQ, LEN, 1)),
        "gain_attn": jnp.clip(1.0 + 0.18 * jax.random.normal(splits[4], (D,), jnp.float32), 0.1, 1.9),
        "w_query": noise(splits[5], (D, D), D ** -0.5, 0.21875),
        "w_key": noise(splits[6], (D, D), D ** -0.5, 0.21875),
        "w_value": noise(splits[7], (D, D), D ** -0.5, 0.21875),
        "w_output": noise(splits[8], (D, D), (D // 64) ** -0.5, 1.75),
        "bucket_head_bias": noise(splits[9], (BUCKETS, HEADS), 1.0, 4.0, (), jnp.float32),
        "gain_ffn": jnp.clip(1.0 + 0.18 * jax.random.normal(splits[10], (D,), jnp.float32), 0.1, 1.9),
        "w_router": noise(splits[11], (D, EXPERTS), (0.5 * D ** -0.5), 0.107910156),
        "w_inner": noise(splits[12], (EXPERTS, D, FF), D ** -0.5, 0.21875, ((0, 8), (2, 4))),
        "w_outer": noise(splits[13], (EXPERTS, FF, D), (1.5 * EXPERTS * FF ** -0.5), 10.375, ((0, 8), (1, 4))),
    }


epsilon = 1e-06
highest = lax.Precision.HIGHEST

@jax.custom_vjp
def low(v):
    return lax.optimization_barrier(v.astype(jnp.bfloat16)).astype(jnp.float32)

@jax.custom_vjp
def low_back(v):
    return v

def low_keep(v):
    return (low(v), None)

def low_pass(kept, grad):
    return (grad,)

def back_keep(v):
    return (v, None)

def back_low(kept, grad):
    return (low(grad),)
low.defvjp(low_keep, low_pass)
low_back.defvjp(back_keep, back_low)

def bucket_table(length):
    offsets = np.arange(length)[None, :] - np.arange(length)[:, None]
    halfway = BUCKETS // 2
    exact_count = halfway // 2
    relative_distance = np.abs(offsets)
    scaled = np.log(np.maximum(relative_distance, 1) / exact_count) / np.log(MAXDIST / exact_count) * (halfway - exact_count)
    far_bucket = np.minimum(exact_count + np.floor(scaled).astype(np.int64), halfway - 1)
    near_bucket = np.where(relative_distance < exact_count, relative_distance, far_bucket)
    return (np.where(offsets > 0, halfway, 0) + near_bucket).astype(np.int32)

def rms_norm(values, gain_vector):
    return values * lax.rsqrt(lax.optimization_barrier(jnp.mean(values * values, axis=-1, keepdims=True)) + epsilon) * gain_vector

def attend_group(packed, w_query, w_key, w_value, w_output, position_bias_heads):
    normed, true_mask = packed
    group_size = normed.shape[0]

    def project(weight):
        return low(low_back(jnp.einsum('gtd,de->gte', normed, weight, precision=highest)))
    queries = project(w_query).reshape(group_size, LEN, HEADS, HEAD_DIM)
    key_heads = project(w_key).reshape(group_size, LEN, HEADS, HEAD_DIM)
    value_heads = project(w_value).reshape(group_size, LEN, HEADS, HEAD_DIM)
    scores = jnp.einsum('gqhc,gkhc->ghqk', queries, key_heads, precision=highest) * HEAD_DIM ** (-0.5) + position_bias_heads[None]
    scores = low_back(scores)
    scores = jnp.where(true_mask[:, None, None, :] > 0, scores, -1e+30)
    attn_probs = jax.nn.softmax(scores, axis=-1)
    mixed = jnp.einsum('ghqk,gkhc->gqhc', low(attn_probs), value_heads, precision=highest).reshape(group_size, LEN, D)
    mixed = low(low_back(mixed))
    return low_back(jnp.einsum('gtd,de->gte', mixed, w_output, precision=highest))

def expert_branch(slot_input, w_inner, w_outer):
    pre_act = low_back(jnp.einsum('secd,edf->secf', slot_input, w_inner, precision=highest))
    activation = low(jax.nn.gelu(pre_act))
    return low(low_back(jnp.einsum('secf,efd->secd', activation, w_outer, precision=highest)))

def layer_forward(tokens, gain_attn, w_query, w_key, w_value, w_output, bucket_head_bias, gain_ffn, w_router, w_inner, w_outer, lengths, routes):
    bucket_ids = jnp.asarray(bucket_table(LEN))
    position_bias_heads = jnp.transpose(bucket_head_bias[bucket_ids], (2, 0, 1))
    positions = jnp.arange(LEN, dtype=jnp.int32)
    group_size = min(NSEQ, max(1, 4096 // LEN))
    expert_ids = jnp.arange(EXPERTS, dtype=jnp.int32)
    slot_ids = jnp.arange(CAP, dtype=jnp.int32)
    layer_rows = []
    for batch_index in range(MB):
        hidden_in = tokens[batch_index]
        true_mask = (positions[None, :] < lengths[batch_index][:, None]).astype(jnp.float32)
        normed = low(rms_norm(hidden_in, gain_attn))
        attend_heads = jax.checkpoint(lambda packed: attend_group(packed, w_query, w_key, w_value, w_output, position_bias_heads))
        attended = lax.map(attend_heads, (normed.reshape(NSEQ // group_size, group_size, LEN, D), true_mask.reshape(NSEQ // group_size, group_size, LEN)))
        residual = hidden_in + attended.reshape(NSEQ, LEN, D)
        routed = low(rms_norm(residual, gain_ffn))
        router_logits = low_back(jnp.einsum('std,de->ste', routed, w_router, precision=highest))
        router_probs = jax.nn.softmax(router_logits, axis=-1)
        chosen = (routes[batch_index, :, :, 0][:, :, None] == expert_ids).astype(jnp.int32)
        gate_prob = lax.optimization_barrier(jnp.sum(router_probs * chosen.astype(jnp.float32), axis=-1))
        counted = chosen * (true_mask[:, :, None] > 0).astype(jnp.int32)
        queue_rank = jnp.cumsum(counted, axis=1) - counted
        placed = counted * (queue_rank < CAP).astype(jnp.int32)
        dispatch = (placed[..., None] * (queue_rank[..., None] == slot_ids).astype(jnp.int32)).astype(jnp.float32)
        slot_input = jnp.einsum('stec,std->secd', dispatch, low_back(routed), precision=highest)
        slot_output = jax.checkpoint(expert_branch)(slot_input, w_inner, w_outer)
        returned = jnp.einsum('stec,secd->std', dispatch, slot_output, precision=highest)
        layer_rows.append(true_mask[..., None] * (residual + gate_prob[..., None] * returned))
    return jnp.stack(layer_rows)

def reference(tokens, cotangent, lengths, routes, gain_attn, w_query, w_key, w_value, w_output, bucket_head_bias, gain_ffn, w_router, w_inner, w_outer):
    floats = (tokens.astype(jnp.float32), gain_attn, w_query.astype(jnp.float32), w_key.astype(jnp.float32), w_value.astype(jnp.float32), w_output.astype(jnp.float32), bucket_head_bias, gain_ffn, w_router.astype(jnp.float32), w_inner.astype(jnp.float32), w_outer.astype(jnp.float32))

    def forward(*params):
        return layer_forward(*params, lengths, routes)
    layer_out, pullback = jax.vjp(forward, *floats)
    grads = pullback(cotangent.astype(jnp.float32))
    return (layer_out.astype(jnp.bfloat16), grads[0].astype(jnp.bfloat16), grads[1], grads[2], grads[3], grads[4], grads[5], grads[6], grads[7], grads[8], grads[9], grads[10])
```

```python
import functools

import jax
import jax.numpy as jnp
import numpy as np
from jax import lax
from jax.experimental import pallas as pl
from jax.experimental.pallas import tpu as pltpu
from jax.sharding import PartitionSpec as P

HEADS = 12
HEAD_DIM = 64
BUCKETS = 32
MAXDIST = 128
PAIR = 2 * HEAD_DIM
PAIRS = HEADS // 2
ROWS = 128

epsilon = 1e-06
negative = -1e30
F32 = jnp.float32
BF16 = jnp.bfloat16
MIB = 1 << 20


def params(mib):
    return pltpu.CompilerParams(vmem_limit_bytes=mib * MIB)


def cost(flops, moved, special=0):
    return pl.CostEstimate(flops=int(flops), bytes_accessed=int(moved), transcendentals=int(special))


def offset_bucket(offsets):
    halfway = BUCKETS // 2
    exact_count = halfway // 2
    relative_distance = np.abs(offsets)
    scaled = (
        np.log(np.maximum(relative_distance, 1) / exact_count)
        / np.log(MAXDIST / exact_count)
        * (halfway - exact_count)
    )
    far_bucket = np.minimum(exact_count + np.floor(scaled).astype(np.int64), halfway - 1)
    near_bucket = np.where(relative_distance < exact_count, relative_distance, far_bucket)
    return (np.where(offsets > 0, halfway, 0) + near_bucket).astype(np.int32)


def dot(a, b):
    return lax.dot_general(a, b, (((1,), (0,)), ((), ())), preferred_element_type=F32)


def dot_t(a, b):
    return lax.dot_general(a, b, (((1,), (1,)), ((), ())), preferred_element_type=F32)


def t_dot(a, b):
    return lax.dot_general(a, b, (((0,), (0,)), ((), ())), preferred_element_type=F32)


def one_hot(condition):
    return jnp.where(condition, 1.0, 0.0).astype(BF16)


def iota(shape, axis):
    return lax.broadcasted_iota(jnp.int32, shape, axis)


def prep_kernel(experts, capacity, len_ref, row_ref, col_ref, cot_ref, srow_ref, scol_ref, slots_ref):
    length = row_ref.shape[-1]
    count = len_ref[pl.program_id(0)]
    row = row_ref[0]
    col = col_ref[0]
    valid_row = iota((1, length), 1) < count
    valid_col = iota((length, 1), 0) < count
    chosen_row = iota((experts, length), 0) == row
    chosen_col = iota((length, experts), 1) == col
    before = one_hot(iota((length, length), 0) < iota((length, length), 1))
    after = one_hot(iota((length, length), 1) < iota((length, length), 0))
    earlier_row = dot(one_hot(chosen_row & valid_row), before)
    rank_row = jnp.sum(jnp.where(chosen_row, earlier_row, 0.0), axis=0, keepdims=True).astype(jnp.int32)
    earlier_col = dot(after, one_hot(chosen_col & valid_col))
    rank_col = jnp.sum(jnp.where(chosen_col, earlier_col, 0.0), axis=1, keepdims=True).astype(jnp.int32)
    slot_row = jnp.where(valid_row & (rank_row < capacity), row * capacity + rank_row, -1)
    srow_ref[0] = slot_row
    scol_ref[0] = jnp.where(valid_col & (rank_col < capacity), col * capacity + rank_col, -1)
    dispatch = one_hot(iota((experts * capacity, length), 0) == slot_row)
    slots_ref[0] = dot(dispatch, cot_ref[0]).astype(BF16)


def prep(lengths, routes, cotangent, experts, capacity):
    batches, length, width = cotangent.shape
    slots = experts * capacity
    block = lambda *shape: pl.BlockSpec((1,) + shape, lambda b: (b, 0, 0))
    return pl.pallas_call(
        functools.partial(prep_kernel, experts, capacity),
        grid=(batches,),
        in_specs=[
            pl.BlockSpec(memory_space=pltpu.SMEM),
            block(1, length),
            block(length, 1),
            block(length, width),
        ],
        out_specs=[block(1, length), block(length, 1), block(slots, width)],
        out_shape=[
            jax.ShapeDtypeStruct((batches, 1, length), jnp.int32),
            jax.ShapeDtypeStruct((batches, length, 1), jnp.int32),
            jax.ShapeDtypeStruct((batches, slots, width), BF16),
        ],
        compiler_params=params(32),
        cost_estimate=cost(2 * batches * slots * length * width, 4 * batches * slots * width),
    )(lengths, routes.reshape(batches, 1, length), routes.reshape(batches, length, 1), cotangent)


def band_bias(vector_ref, head):
    wide = jnp.broadcast_to(vector_ref[head], (ROWS, vector_ref.shape[-1]))
    return pltpu.roll(wide, 0, 1, stride=1, stride_axis=0)


def band_slice(block, length):
    start = length - ROWS * (block + 1)
    return slice(start, start + length)


def attn_kernel(
    capacity,
    len_ref,
    tok_ref,
    gain_ref,
    wq_ref,
    wk_ref,
    wv_ref,
    wo_ref,
    vec_ref,
    gffn_ref,
    wr_ref,
    srow_ref,
    rcol_ref,
    qkv_ref,
    mixed_ref,
    lse_ref,
    res_ref,
    probs_ref,
    gate_ref,
    slots_ref,
    band_ref,
):
    length, width = tok_ref.shape
    count = len_ref[0]
    tokens = tok_ref[...].astype(F32)
    inverse = lax.rsqrt(jnp.mean(tokens * tokens, axis=-1, keepdims=True) + epsilon)
    normed = (tokens * inverse * gain_ref[...]).astype(BF16)
    for which, w_ref in enumerate((wq_ref, wk_ref, wv_ref)):
        for part in range(width // 256):
            rows = dot(normed, w_ref[:, 256 * part : 256 * part + 256]).astype(BF16)
            qkv_ref[which, 2 * part] = rows[:, :PAIR]
            qkv_ref[which, 2 * part + 1] = rows[:, PAIR:]
    mask = jnp.where(iota((1, length), 1) < count, 0.0, negative)
    lane = iota((ROWS, PAIR), 1)
    lse_ref[...] = jnp.zeros_like(lse_ref)

    def one_pair(pair, carry):
        keys = qkv_ref[1, pair]
        values = qkv_ref[2, pair]
        for side in range(2):
            head = 2 * pair + side
            band_ref[...] = band_bias(vec_ref, head)
            mine = (lane >= HEAD_DIM) if side else (lane < HEAD_DIM)
            for block in range(length // ROWS):
                here = slice(ROWS * block, ROWS * (block + 1))
                queries = qkv_ref[0, pair, here, :] * 0.125
                queries = jnp.where(mine, queries, jnp.zeros_like(queries))
                scores = dot_t(queries, keys) + band_ref[:, band_slice(block, length)] + mask
                highest = jnp.max(scores, axis=-1, keepdims=True)
                powers = jnp.exp(scores - highest)
                total = jnp.sum(powers, axis=-1, keepdims=True)
                mixed = (dot(powers.astype(BF16), values) / total).astype(BF16)
                column = iota((ROWS, lse_ref.shape[1]), 1)
                lse_ref[here, :] = jnp.where(column == head, highest + jnp.log(total), lse_ref[here, :])
                if side:
                    mixed = jnp.where(mine, mixed, mixed_ref[pair, here, :])
                mixed_ref[pair, here, :] = mixed
        return carry

    lax.fori_loop(0, PAIRS, one_pair, 0)
    mixed_all = jnp.concatenate([mixed_ref[p] for p in range(PAIRS)], axis=1)
    residual = tokens + dot(mixed_all, wo_ref[...])
    res_ref[...] = residual
    inverse = lax.rsqrt(jnp.mean(residual * residual, axis=-1, keepdims=True) + epsilon)
    routed = (residual * inverse * gffn_ref[...]).astype(BF16)
    logits = dot(routed, wr_ref[...])
    powers = jnp.exp(logits - jnp.max(logits, axis=-1, keepdims=True))
    probs = powers / jnp.sum(powers, axis=-1, keepdims=True)
    probs_ref[...] = probs
    gate = jnp.sum(jnp.where(iota(probs.shape, 1) == rcol_ref[...], probs, 0.0), axis=-1, keepdims=True)
    first = gate.astype(BF16).astype(F32)
    second = (gate - first).astype(BF16).astype(F32)
    third = gate - first - second
    column = iota((length, PAIR), 1)
    pieces = jnp.where(column == 0, first, jnp.where(column == 1, second, jnp.where(column == 2, third, 0.0)))
    dispatch = one_hot(iota((slots_ref.shape[0], length), 0) == srow_ref[...])
    gate_ref[...] = jnp.sum(dot(dispatch, pieces.astype(BF16)), axis=-1, keepdims=True)
    slots_ref[...] = dot(dispatch, routed).astype(BF16)


def attention_forward(count, tokens, gain, wq, wk, wv, wo, vector, gain_ffn, w_router, srow, rcol, capacity):
    length, width = tokens.shape
    experts = w_router.shape[1]
    slots = experts * capacity
    vmem = pl.BlockSpec(memory_space=pltpu.VMEM)
    return pl.pallas_call(
        functools.partial(attn_kernel, capacity),
        in_specs=[pl.BlockSpec(memory_space=pltpu.SMEM)] + [vmem] * 11,
        out_specs=[vmem] * 7,
        out_shape=[
            jax.ShapeDtypeStruct((3, PAIRS, length, PAIR), BF16),
            jax.ShapeDtypeStruct((PAIRS, length, PAIR), BF16),
            jax.ShapeDtypeStruct((length, 128), F32),
            jax.ShapeDtypeStruct((length, width), F32),
            jax.ShapeDtypeStruct((length, experts), F32),
            jax.ShapeDtypeStruct((slots, 1), F32),
            jax.ShapeDtypeStruct((slots, width), BF16),
        ],
        scratch_shapes=[pltpu.VMEM((ROWS, vector.shape[-1]), F32)],
        compiler_params=params(48),
        cost_estimate=cost(14e9, 14e6, HEADS * length * length),
    )(count, tokens, gain, wq, wk, wv, wo, vector, gain_ffn, w_router, srow, rcol)


GELU_SCALE = 0.7978845608028654
GELU_CUBIC = 0.044715


def expert_kernel(x_ref, c_ref, wi_ref, wo_ref, out_ref, in_ref, act_ref, pre_ref):
    planes, _, rows, width = x_ref.shape
    inputs = x_ref[...].reshape(planes * rows, width)
    grads = c_ref[...].reshape(planes * rows, width)
    pre = dot(inputs, wi_ref[0])
    square = pre * pre
    curve = jnp.tanh(GELU_SCALE * pre * (1.0 + GELU_CUBIC * square))
    half = 0.5 * (1.0 + curve)
    act = (pre * half).astype(BF16)
    slope = half + 0.5 * pre * (1.0 - curve * curve) * (GELU_SCALE * (1.0 + 3.0 * GELU_CUBIC * square))
    act_ref[0] = act
    out_ref[...] = dot(act, wo_ref[0]).astype(BF16).reshape(planes, 1, rows, width)
    pre_grad = (slope * dot_t(grads, wo_ref[0])).astype(BF16)
    pre_ref[0] = pre_grad
    in_ref[...] = dot_t(pre_grad, wi_ref[0]).astype(BF16).reshape(planes, 1, rows, width)


def experts_both(x, c, w_inner, w_outer):
    planes, local, rows, width = x.shape
    hidden = w_inner.shape[2]
    slab = pl.BlockSpec((planes, 1, rows, width), lambda e: (0, e, 0, 0))
    weight = lambda a, b: pl.BlockSpec((1, a, b), lambda e: (e, 0, 0))
    total = planes * rows
    return pl.pallas_call(
        expert_kernel,
        grid=(local,),
        in_specs=[slab, slab, weight(width, hidden), weight(hidden, width)],
        out_specs=[slab, slab, weight(total, hidden), weight(total, hidden)],
        out_shape=[
            jax.ShapeDtypeStruct(x.shape, BF16),
            jax.ShapeDtypeStruct(x.shape, BF16),
            jax.ShapeDtypeStruct((local, total, hidden), BF16),
            jax.ShapeDtypeStruct((local, total, hidden), BF16),
        ],
        compiler_params=params(40),
        cost_estimate=cost(
            8 * local * total * width * hidden, 4 * local * hidden * width + 12 * local * total * width, local * total * hidden
        ),
    )(x, c, w_inner, w_outer)


def expert_grad_kernel(batches, *refs):
    xs, cs, acts, pres = (refs[k * batches : (k + 1) * batches] for k in range(4))
    gate_ref, outer_ref, inner_ref = refs[4 * batches :]
    rows = acts[0].shape[1]
    width = xs[0].shape[-1]
    outer = inner = None
    for b in range(batches):
        gate = gate_ref[0, b * rows : (b + 1) * rows, :]
        grads = (cs[b][...].reshape(rows, width).astype(F32) * gate).astype(BF16)
        pre_grad = (pres[b][0].astype(F32) * gate).astype(BF16)
        outer_part = t_dot(acts[b][0], grads)
        inner_part = t_dot(xs[b][...].reshape(rows, width), pre_grad)
        outer = outer_part if outer is None else outer + outer_part
        inner = inner_part if inner is None else inner + inner_part
    outer_ref[0] = outer
    inner_ref[0] = inner


def expert_grads(xs, cs, acts, pres, gates):
    batches = len(xs)
    planes, local, rows, width = xs[0].shape
    hidden = acts[0].shape[2]
    slab = pl.BlockSpec((planes, 1, rows, width), lambda e: (0, e, 0, 0))
    mat = lambda a, b: pl.BlockSpec((1, a, b), lambda e: (e, 0, 0))
    total = planes * rows
    return pl.pallas_call(
        functools.partial(expert_grad_kernel, batches),
        grid=(local,),
        in_specs=[slab] * (2 * batches) + [mat(total, hidden)] * (2 * batches) + [mat(batches * total, 1)],
        out_specs=[mat(hidden, width), mat(width, hidden)],
        out_shape=[
            jax.ShapeDtypeStruct((local, hidden, width), F32),
            jax.ShapeDtypeStruct((local, width, hidden), F32),
        ],
        compiler_params=params(48),
        cost_estimate=cost(
            4 * batches * local * total * width * hidden, 8 * local * hidden * width + 8 * batches * local * total * width
        ),
    )(*xs, *cs, *acts, *pres, gates)


def combine_kernel(
    len_ref,
    out_ref,
    in_ref,
    scol_ref,
    rcol_ref,
    res_ref,
    probs_ref,
    cot_ref,
    gffn_ref,
    wr_ref,
    wo_ref,
    mixed_ref,
    layer_ref,
    resgrad_ref,
    mgrad_ref,
    ograd_ref,
    rgrad_ref,
    ggrad_ref,
):
    length, width = cot_ref.shape
    slots = out_ref.shape[0]
    valid = iota((length, 1), 0) < len_ref[0]
    collect = one_hot(iota((length, slots), 1) == scol_ref[...])
    returned = dot(collect, out_ref[...])
    residual = res_ref[...]
    probs = probs_ref[...]
    chosen = iota(probs.shape, 1) == rcol_ref[...]
    gate = jnp.sum(jnp.where(chosen, probs, 0.0), axis=-1, keepdims=True)
    layer_ref[...] = jnp.where(valid, residual + gate * returned, 0.0).astype(BF16)
    out_grad = jnp.where(valid, cot_ref[...].astype(F32), 0.0)
    gate_grad = jnp.sum(out_grad * returned, axis=-1, keepdims=True)
    prob_grad = jnp.where(chosen, gate_grad, 0.0)
    logit_grad = (probs * (prob_grad - jnp.sum(probs * prob_grad, axis=-1, keepdims=True))).astype(BF16)
    inverse = lax.rsqrt(jnp.mean(residual * residual, axis=-1, keepdims=True) + epsilon)
    gain = gffn_ref[...]
    scaled = residual * inverse
    routed = (scaled * gain).astype(BF16)
    rgrad_ref[...] = t_dot(logit_grad, routed)
    routed_grad = dot_t(logit_grad, wr_ref[...]) + gate * dot(collect, in_ref[...])
    ggrad_ref[...] = jnp.sum(routed_grad * scaled, axis=0, keepdims=True)
    upstream = routed_grad * gain
    middle = jnp.mean(upstream * scaled, axis=-1, keepdims=True)
    residual_grad = out_grad + inverse * (upstream - scaled * middle)
    resgrad_ref[...] = residual_grad
    attended = residual_grad.astype(BF16)
    mixed_all = jnp.concatenate([mixed_ref[p] for p in range(PAIRS)], axis=1)
    ograd_ref[...] = t_dot(mixed_all, attended)
    mixed_grad = dot_t(attended, wo_ref[...]).astype(BF16)
    for pair in range(PAIRS):
        mgrad_ref[pair] = mixed_grad[:, pair * PAIR : (pair + 1) * PAIR]


def combine(count, outs, ins, scol, rcol, residual, probs, cot, gain_ffn, w_router, w_output, mixed):
    length, width = cot.shape
    experts = w_router.shape[1]
    vmem = pl.BlockSpec(memory_space=pltpu.VMEM)
    return pl.pallas_call(
        combine_kernel,
        in_specs=[pl.BlockSpec(memory_space=pltpu.SMEM)] + [vmem] * 11,
        out_specs=[vmem] * 6,
        out_shape=[
            jax.ShapeDtypeStruct((length, width), BF16),
            jax.ShapeDtypeStruct((length, width), F32),
            jax.ShapeDtypeStruct((PAIRS, length, PAIR), BF16),
            jax.ShapeDtypeStruct((width, width), F32),
            jax.ShapeDtypeStruct((experts, width), F32),
            jax.ShapeDtypeStruct((1, width), F32),
        ],
        compiler_params=params(48),
        cost_estimate=cost(8e9, 12e6),
    )(count, outs, ins, scol, rcol, residual, probs, cot, gain_ffn, w_router, w_output, mixed)


def attn_back_kernel(
    len_ref,
    qkv_ref,
    lse_ref,
    vec_ref,
    mgrad_ref,
    tok_ref,
    gain_ref,
    wq_ref,
    wk_ref,
    wv_ref,
    resgrad_ref,
    wgrad_ref,
    diag_ref,
    tgrad_ref,
    ggrad_ref,
    band_ref,
    probs_ref,
    sgrad_ref,
    spread_ref,
    low_ref,
    kt_ref,
    vt_ref,
):
    length, width = tok_ref.shape
    mask = jnp.where(iota((1, length), 1) < len_ref[0], 0.0, negative)
    lane = iota((ROWS, PAIR), 1)

    def one_pair(pair, carry):
        keys = qkv_ref[1, pair]
        values = qkv_ref[2, pair]
        queries_t = qkv_ref[0, pair].T
        grads_t = mgrad_ref[pair].T
        for side in range(2):
            head = 2 * pair + side
            band_ref[...] = band_bias(vec_ref, head)
            spread_ref[...] = jnp.zeros_like(spread_ref)
            mine = (lane >= HEAD_DIM) if side else (lane < HEAD_DIM)
            for block in range(length // ROWS):
                here = slice(ROWS * block, ROWS * (block + 1))
                window = band_slice(block, length)
                queries = qkv_ref[0, pair, here, :] * 0.125
                queries = jnp.where(mine, queries, jnp.zeros_like(queries))
                grads = mgrad_ref[pair, here, :]
                grads = jnp.where(mine, grads, jnp.zeros_like(grads))
                column = iota((ROWS, lse_ref.shape[1]), 1)
                log_total = jnp.sum(jnp.where(column == head, lse_ref[here, :], 0.0), axis=-1, keepdims=True)
                scores = dot_t(queries, keys) + band_ref[:, window] + mask
                probs = jnp.exp(scores - log_total)
                probs_ref[here, :] = probs.astype(BF16)
                weighted = probs * dot_t(grads, values)
                score_grad = weighted - probs * jnp.sum(weighted, axis=-1, keepdims=True)
                spread_ref[:, window] += score_grad
                low = score_grad.astype(BF16)
                sgrad_ref[here, :] = low
                query_grad = (dot(low, keys) * 0.125).astype(BF16)
                if side:
                    query_grad = jnp.where(mine, query_grad, low_ref[0, pair, here, :])
                low_ref[0, pair, here, :] = query_grad
            rows = slice(HEAD_DIM * side, HEAD_DIM * (side + 1))
            kt_ref[rows, :] = dot(queries_t[rows, :], sgrad_ref[...]) * 0.125
            vt_ref[rows, :] = dot(grads_t[rows, :], probs_ref[...])
            size = spread_ref.shape[1]
            eight = spread_ref[0:8, :]
            for step in range(8, ROWS, 8):
                eight = eight + pltpu.roll(spread_ref[step : step + 8, :], size - step, 1)
            diagonal = eight[0:1, :]
            for step in range(1, 8):
                diagonal = diagonal + pltpu.roll(eight[step : step + 1, :], size - step, 1)
            diag_ref[head] = diagonal
        low_ref[1, pair] = kt_ref[...].T.astype(BF16)
        low_ref[2, pair] = vt_ref[...].T.astype(BF16)
        return carry

    lax.fori_loop(0, PAIRS, one_pair, 0)
    tokens = tok_ref[...].astype(F32)
    inverse = lax.rsqrt(jnp.mean(tokens * tokens, axis=-1, keepdims=True) + epsilon)
    gain = gain_ref[...]
    scaled = tokens * inverse
    normed_t = (scaled * gain).astype(BF16).T
    normed_grad = jnp.zeros((length, width), F32)
    for which, w_ref in enumerate((wq_ref, wk_ref, wv_ref)):
        low = jnp.concatenate([low_ref[which, p] for p in range(PAIRS)], axis=1)
        wgrad_ref[which] = dot(normed_t, low)
        normed_grad = normed_grad + dot_t(low, w_ref[...])
    ggrad_ref[...] = jnp.sum(normed_grad * scaled, axis=0, keepdims=True)
    upstream = normed_grad * gain
    middle = jnp.mean(upstream * scaled, axis=-1, keepdims=True)
    tgrad_ref[...] = (resgrad_ref[...] + inverse * (upstream - scaled * middle)).astype(BF16)


def attention_backward(count, qkv, lse, vector, mixed_grad, tokens, gain, wq, wk, wv, residual_grad):
    length, width = tokens.shape
    vmem = pl.BlockSpec(memory_space=pltpu.VMEM)
    size = vector.shape[-1]
    return pl.pallas_call(
        attn_back_kernel,
        in_specs=[pl.BlockSpec(memory_space=pltpu.SMEM)] + [vmem] * 10,
        out_specs=[vmem] * 4,
        out_shape=[
            jax.ShapeDtypeStruct((3, width, width), F32),
            jax.ShapeDtypeStruct((HEADS, 1, size), F32),
            jax.ShapeDtypeStruct((length, width), BF16),
            jax.ShapeDtypeStruct((1, width), F32),
        ],
        scratch_shapes=[
            pltpu.VMEM((ROWS, size), F32),
            pltpu.VMEM((length, length), BF16),
            pltpu.VMEM((length, length), BF16),
            pltpu.VMEM((ROWS, size), F32),
            pltpu.VMEM((3, PAIRS, length, PAIR), BF16),
            pltpu.VMEM((PAIR, length), F32),
            pltpu.VMEM((PAIR, length), F32),
        ],
        compiler_params=params(56),
        cost_estimate=cost(30e9, 20e6, HEADS * length * length),
    )(count, qkv, lse, vector, mixed_grad, tokens, gain, wq, wk, wv, residual_grad)


def offset_selector(length):
    place = np.arange(2 * length)
    offsets = np.where(place < 2 * length - ROWS, place, place - 2 * length) - (length - ROWS)
    offsets = np.clip(offsets, -(length - 1), length - 1)
    return (offset_bucket(offsets)[:, None] == np.arange(BUCKETS)[None, :]).astype(np.float32)


def shards(
    tokens,
    cotangent,
    lengths,
    routes,
    gain_attn,
    w_query,
    w_key,
    w_value,
    w_output,
    bucket_head_bias,
    gain_ffn,
    w_router,
    w_inner,
    w_outer,
):
    batches, _, length, width = tokens.shape
    experts = w_router.shape[1]
    local = w_inner.shape[0]
    groups = lax.axis_size("expert")
    planes = lax.axis_size("hidden")
    capacity = (5 * length + 4 * experts - 1) // (4 * experts)
    slots = experts * capacity
    rows = groups * capacity
    selector = jnp.asarray(offset_selector(length))
    vector = lax.dot_general(
        bucket_head_bias, selector, (((0,), (1,)), ((), ())), precision=lax.Precision.HIGHEST
    )[:, None, :]
    gain_a = gain_attn[None, :]
    gain_f = gain_ffn[None, :]
    counts = lengths[:, 0]

    def to_experts(values):
        sent = lax.all_to_all(
            values.reshape(groups, local, capacity, width), "expert", split_axis=0, concat_axis=0, tiled=True
        )
        mine = jnp.swapaxes(sent, 0, 1).reshape(local, rows, width)
        return lax.all_gather(mine, "hidden", axis=0)

    def to_tokens(values):
        summed = lax.psum_scatter(values, "hidden", scatter_dimension=0)
        sent = jnp.swapaxes(summed.reshape(local, groups, capacity, width), 0, 1)
        return lax.all_to_all(sent, "expert", split_axis=0, concat_axis=0, tiled=True).reshape(slots, width)

    srow, scol, cot_slots = prep(counts, routes.reshape(batches, length), cotangent[:, 0], experts, capacity)
    rcol = routes.reshape(batches, length, 1)
    each = range(batches)
    cs = [to_experts(cot_slots[b]) for b in each]
    forward = [
        attention_forward(
            counts[b : b + 1],
            tokens[b, 0],
            gain_a,
            w_query,
            w_key,
            w_value,
            w_output,
            vector,
            gain_f,
            w_router,
            srow[b],
            rcol[b],
            capacity,
        )
        for b in each
    ]
    xs = [to_experts(forward[b][6]) for b in each]
    worked = [experts_both(xs[b], cs[b], w_inner, w_outer) for b in each]
    gates = jnp.stack([forward[b][5][:, 0] for b in each])
    gates = lax.all_gather(gates, ("hidden", "expert"), axis=0)
    gates = gates.reshape(planes, groups, batches, groups, local, capacity)
    gates = lax.dynamic_index_in_dim(gates, lax.axis_index("expert"), 3, keepdims=False)
    gates = gates.transpose(3, 2, 0, 1, 4).reshape(local, batches * planes * rows, 1)
    outer_total, inner_total = expert_grads(
        xs, cs, [worked[b][2] for b in each], [worked[b][3] for b in each], gates
    )
    layer_rows, token_grads, terms = [], [], []
    for b in each:
        qkv, mixed, lse, residual, probs, _, _ = forward[b]
        outs = to_tokens(worked[b][0])
        ins = to_tokens(worked[b][1])
        layer, res_grad, mixed_grad, output_part, router_part, gain_f_part = combine(
            counts[b : b + 1],
            outs,
            ins,
            scol[b],
            rcol[b],
            residual,
            probs,
            cotangent[b, 0],
            gain_f,
            w_router,
            w_output,
            mixed,
        )
        qkv_part, diagonal, token_grad, gain_a_part = attention_backward(
            counts[b : b + 1],
            qkv,
            lse,
            vector,
            mixed_grad,
            tokens[b, 0],
            gain_a,
            w_query,
            w_key,
            w_value,
            res_grad,
        )
        layer_rows.append(layer)
        token_grads.append(token_grad)
        terms.append((gain_a_part, qkv_part, output_part, diagonal, gain_f_part, router_part))
    gain_a_part, qkv_part, output_part, diagonal, gain_f_part, router_part = (
        functools.reduce(jnp.add, parts) for parts in zip(*terms)
    )
    bias_part = lax.dot_general(
        selector, diagonal[:, 0], (((0,), (1,)), ((), ())), precision=lax.Precision.HIGHEST
    )
    big = lax.psum(
        jnp.concatenate([qkv_part.reshape(3 * width, width), output_part, router_part]).astype(BF16),
        ("expert", "hidden"),
    ).astype(F32)
    small = lax.psum(
        jnp.concatenate([gain_a_part[0], gain_f_part[0], bias_part.reshape(-1)]), ("expert", "hidden")
    )
    return (
        jnp.stack(layer_rows)[:, None],
        jnp.stack(token_grads)[:, None],
        small[:width],
        big[:width],
        big[width : 2 * width],
        big[2 * width : 3 * width],
        big[3 * width : 4 * width],
        small[2 * width :].reshape(BUCKETS, HEADS),
        small[width : 2 * width],
        big[4 * width :].T,
        inner_total,
        outer_total,
    )


def solution(mesh):
    token = P(None, ("expert", "hidden"), None, None)
    placed = (
        token,
        token,
        P(None, ("expert", "hidden")),
        token,
        *(P() for _ in range(8)),
        P("expert", None, "hidden"),
        P("expert", "hidden", None),
    )
    return jax.shard_map(
        shards,
        mesh=mesh,
        in_specs=placed,
        out_specs=(
            token,
            token,
            *(P() for _ in range(8)),
            P("expert", None, "hidden"),
            P("expert", "hidden", None),
        ),
        check_vma=False,
    )
```

```python
import functools

import jax
import jax.numpy as jnp
import numpy as np
from jax import lax
from jax.experimental import pallas as pl
from jax.experimental.pallas import tpu as pltpu
from jax.sharding import PartitionSpec as P

HEADS = 12
HEAD_DIM = 64
BUCKETS = 32
MAXDIST = 128
PAIR = 2 * HEAD_DIM
PAIRS = HEADS // 2
ROWS = 128

epsilon = 1e-06
negative = -1e30
F32 = jnp.float32
BF16 = jnp.bfloat16
MIB = 1 << 20


def params(mib):
    return pltpu.CompilerParams(vmem_limit_bytes=mib * MIB)


def cost(*_):
    return pl.CostEstimate(flops=1, bytes_accessed=1, transcendentals=0)


def offset_bucket(offsets):
    halfway = BUCKETS // 2
    exact_count = halfway // 2
    relative_distance = np.abs(offsets)
    scaled = (
        np.log(np.maximum(relative_distance, 1) / exact_count)
        / np.log(MAXDIST / exact_count)
        * (halfway - exact_count)
    )
    far_bucket = np.minimum(exact_count + np.floor(scaled).astype(np.int64), halfway - 1)
    near_bucket = np.where(relative_distance < exact_count, relative_distance, far_bucket)
    return (np.where(offsets > 0, halfway, 0) + near_bucket).astype(np.int32)


def dot(a, b):
    return lax.dot_general(a, b, (((1,), (0,)), ((), ())), preferred_element_type=F32)


def dot_t(a, b):
    return lax.dot_general(a, b, (((1,), (1,)), ((), ())), preferred_element_type=F32)


def t_dot(a, b):
    return lax.dot_general(a, b, (((0,), (0,)), ((), ())), preferred_element_type=F32)


def one_hot(condition):
    return jnp.where(condition, 1.0, 0.0).astype(BF16)


def batch_block(array, b):
    rest = array.shape[1:]
    return pl.BlockSpec((1,) + rest, lambda *_: (b,) + (0,) * len(rest))


ANYWHERE = pl.BlockSpec(memory_space=pl.ANY)
WHOLE = pl.BlockSpec(memory_space=pltpu.VMEM)
SCALARS = pl.BlockSpec(memory_space=pltpu.SMEM)


def iota(shape, axis):
    return lax.broadcasted_iota(jnp.int32, shape, axis)


def padded(rows):
    return -(-rows // 16) * 16


def spread_slots(slot, per, message):
    if message == per:
        return slot
    return jnp.where(slot < 0, -1, slot + lax.div(jnp.maximum(slot, 0), per) * (message - per))


def prep_kernel(per, capacity, len_ref, row_ref, col_ref, cot_ref, srow_ref, scol_ref, slots_ref):
    batches, _, length = row_ref.shape
    groups, message, width = slots_ref.shape
    experts = groups * per // capacity
    before = one_hot(iota((length, length), 0) < iota((length, length), 1))
    after = one_hot(iota((length, length), 1) < iota((length, length), 0))
    for b in range(batches):
        count = len_ref[b]
        row = row_ref[b]
        col = col_ref[b]
        valid_row = iota((1, length), 1) < count
        valid_col = iota((length, 1), 0) < count
        chosen_row = iota((experts, length), 0) == row
        chosen_col = iota((length, experts), 1) == col
        earlier_row = dot(one_hot(chosen_row & valid_row), before)
        rank_row = jnp.sum(jnp.where(chosen_row, earlier_row, 0.0), axis=0, keepdims=True).astype(jnp.int32)
        earlier_col = dot(after, one_hot(chosen_col & valid_col))
        rank_col = jnp.sum(jnp.where(chosen_col, earlier_col, 0.0), axis=1, keepdims=True).astype(jnp.int32)
        slot_row = jnp.where(valid_row & (rank_row < capacity), row * capacity + rank_row, -1)
        srow_ref[b] = slot_row
        scol_ref[b] = jnp.where(valid_col & (rank_col < capacity), col * capacity + rank_col, -1)
        if b == 0:
            dispatch = one_hot(iota((groups * message, length), 0) == spread_slots(slot_row, per, message))
            slots_ref[...] = dot(dispatch, cot_ref[0, 0]).astype(BF16).reshape(groups, message, width)


def prep(lengths, routes, cot, groups, per, capacity):
    batches, length = routes.shape
    width = cot.shape[-1]
    vmem = WHOLE
    message = padded(per)
    return pl.pallas_call(
        functools.partial(prep_kernel, per, capacity),
        grid=(1,),
        in_specs=[SCALARS, vmem, vmem, batch_block(cot, 0)],
        out_specs=[vmem] * 3,
        out_shape=[
            jax.ShapeDtypeStruct((batches, 1, length), jnp.int32),
            jax.ShapeDtypeStruct((batches, length, 1), jnp.int32),
            jax.ShapeDtypeStruct((groups, message, width), BF16),
        ],
        compiler_params=params(32),
        cost_estimate=cost(2 * groups * message * length * width, 4 * groups * message * width),
    )(lengths, routes.reshape(batches, 1, length), routes.reshape(batches, length, 1), cot)


def regroup_kernel(count, inputs, *refs):
    move_ref, out_ref = refs[0], refs[-1]
    total = refs[1][...].astype(F32)
    for ref in refs[2 : 1 + count]:
        total = total + ref[...].astype(F32)
    out_ref[...] = dot(move_ref[...], total.astype(BF16).reshape(inputs, -1)).astype(BF16).reshape(out_ref.shape)


def regroup(move, arrays, shape):
    inputs = move.shape[1]
    vmem = pl.BlockSpec(memory_space=pltpu.VMEM)
    return pl.pallas_call(
        functools.partial(regroup_kernel, len(arrays), inputs),
        in_specs=[vmem] * (1 + len(arrays)),
        out_specs=vmem,
        out_shape=jax.ShapeDtypeStruct(shape, BF16),
        compiler_params=params(32),
        cost_estimate=cost(2 * move.size * shape[-1], 4e6),
    )(move, *arrays)


def regroup_gated_kernel(capacity, move_ref, in_ref, out_ref):
    groups, message, width = in_ref.shape
    total = move_ref.shape[0]
    local = total // (groups * capacity)
    rows = groups * capacity
    flat = in_ref[...].reshape(groups * message, width)
    out_ref[:total, :] = dot(move_ref[...], flat).astype(BF16)
    place = iota((message, 128), 0)
    lane = iota((message, 128), 1)
    columns = []
    for g in range(groups):
        gates = in_ref[g, message - 16 : message, :].astype(F32)[0:1, :]
        parts = [
            jnp.sum(jnp.where(place == lane, gates[:, 128 * k : 128 * (k + 1)], 0.0), axis=1, keepdims=True)
            for k in range(3)
        ]
        wide = iota((message, 128), 1)
        columns.append(jnp.where(wide == 0, parts[0], jnp.where(wide == 1, parts[1], jnp.where(wide == 2, parts[2], 0.0))))
    column = jnp.concatenate(columns, axis=0).astype(BF16)
    moved = dot(move_ref[...], column)
    place = iota((rows, 128), 0)
    lane = iota((rows, 128), 1)
    lines = []
    for l in range(local):
        mine = moved[l * rows : (l + 1) * rows, :]
        parts = [
            jnp.sum(jnp.where(place == lane, mine[:, k : k + 1], 0.0), axis=0, keepdims=True) for k in range(3)
        ]
        lines.append(jnp.concatenate(parts + [jnp.zeros((1, width - 384), F32)], axis=1))
    lines.append(jnp.zeros((16 - local, width), F32))
    out_ref[total:, :] = jnp.concatenate(lines, axis=0).astype(BF16)


def regroup_gated(move, slots, capacity):
    width = slots.shape[-1]
    vmem = pl.BlockSpec(memory_space=pltpu.VMEM)
    return pl.pallas_call(
        functools.partial(regroup_gated_kernel, capacity),
        in_specs=[vmem] * 2,
        out_specs=vmem,
        out_shape=jax.ShapeDtypeStruct((move.shape[0] + 16, width), BF16),
        compiler_params=params(32),
        cost_estimate=cost(2 * move.size * width, 4e6),
    )(move, slots)


def band_bias(vector_ref, head):
    wide = jnp.broadcast_to(vector_ref[head], (ROWS, vector_ref.shape[-1]))
    return pltpu.roll(wide, 0, 1, stride=1, stride_axis=0)


def band_slice(block, length):
    start = length - ROWS * (block + 1)
    return slice(start, start + length)


def attn_kernel(
    per,
    gated,
    batch,
    waits,
    *refs,
):
    refs = refs[waits:]
    len_ref, tok_ref, cot_ref, gain_ref, wq_ref, wk_ref, wv_ref, wo_ref, vec_ref, gffn_ref, wr_ref, srow_ref, rcol_ref, *refs = refs
    qkv_ref, mixed_ref, lse_ref, res_ref, probs_ref, slots_ref, *rest = refs
    band_ref = rest[-1]
    length, width = tok_ref.shape[2:]
    count = len_ref[batch]
    tokens = tok_ref[0, 0].astype(F32)
    inverse = lax.rsqrt(jnp.mean(tokens * tokens, axis=-1, keepdims=True) + epsilon)
    normed = (tokens * inverse * gain_ref[...]).astype(BF16)
    for which, w_ref in enumerate((wq_ref, wk_ref, wv_ref)):
        for part in range(width // 256):
            rows = dot(normed, w_ref[:, 256 * part : 256 * part + 256]).astype(BF16)
            qkv_ref[which, 2 * part] = rows[:, :PAIR]
            qkv_ref[which, 2 * part + 1] = rows[:, PAIR:]
    mask = jnp.where(iota((1, length), 1) < count, 0.0, negative)
    lane = iota((ROWS, PAIR), 1)
    lse_ref[...] = jnp.zeros_like(lse_ref)

    def one_pair(pair, carry):
        keys = qkv_ref[1, pair]
        values = qkv_ref[2, pair]
        for side in range(2):
            head = 2 * pair + side
            band_ref[...] = band_bias(vec_ref, head)
            mine = (lane >= HEAD_DIM) if side else (lane < HEAD_DIM)
            for block in range(length // ROWS):
                here = slice(ROWS * block, ROWS * (block + 1))
                queries = qkv_ref[0, pair, here, :] * 0.125
                queries = jnp.where(mine, queries, jnp.zeros_like(queries))
                scores = dot_t(queries, keys) + band_ref[:, band_slice(block, length)] + mask
                highest = jnp.max(scores, axis=-1, keepdims=True)
                powers = jnp.exp(scores - highest)
                total = jnp.sum(powers, axis=-1, keepdims=True)
                mixed = (dot(powers.astype(BF16), values) / total).astype(BF16)
                column = iota((ROWS, lse_ref.shape[1]), 1)
                lse_ref[here, :] = jnp.where(column == head, highest + jnp.log(total), lse_ref[here, :])
                if side:
                    mixed = jnp.where(mine, mixed, mixed_ref[pair, here, :])
                mixed_ref[pair, here, :] = mixed
        return carry

    lax.fori_loop(0, PAIRS, one_pair, 0)
    mixed_all = jnp.concatenate([mixed_ref[p] for p in range(PAIRS)], axis=1)
    residual = tokens + dot(mixed_all, wo_ref[...])
    res_ref[...] = residual
    inverse = lax.rsqrt(jnp.mean(residual * residual, axis=-1, keepdims=True) + epsilon)
    routed = (residual * inverse * gffn_ref[...]).astype(BF16)
    logits = dot(routed, wr_ref[...])
    powers = jnp.exp(logits - jnp.max(logits, axis=-1, keepdims=True))
    probs = powers / jnp.sum(powers, axis=-1, keepdims=True)
    probs_ref[...] = probs
    gate = jnp.sum(jnp.where(iota(probs.shape, 1) == rcol_ref[0], probs, 0.0), axis=-1, keepdims=True)
    groups, message, _ = slots_ref.shape
    places = iota((groups * message, length), 0)
    dispatch = one_hot(places == spread_slots(srow_ref[0], per, message))
    slots_ref[...] = dot(dispatch, routed).astype(BF16).reshape(slots_ref.shape)
    if gated:
        grad_ref = rest[0]
        if grad_ref.shape[1] != message:
            dispatch = one_hot(
                iota((groups * grad_ref.shape[1], length), 0) == spread_slots(srow_ref[0], per, grad_ref.shape[1])
            )
        grads = (gate * cot_ref[0, 0].astype(F32)).astype(BF16)
        grad_ref[...] = dot(dispatch, grads).astype(BF16).reshape(grad_ref.shape)
        return
    first = gate.astype(BF16).astype(F32)
    second = (gate - first).astype(BF16).astype(F32)
    third = gate - first - second
    column = iota((length, PAIR), 1)
    pieces = jnp.where(column == 0, first, jnp.where(column == 1, second, jnp.where(column == 2, third, 0.0)))
    sorted_gates = dot(dispatch, pieces.astype(BF16))
    data = message - 16
    place = iota((data, 128), 0)
    lane = iota((data, 128), 1)
    for g in range(groups):
        mine = sorted_gates[g * message : g * message + data, :]
        parts = [
            jnp.sum(jnp.where(place == lane, mine[:, k : k + 1], 0.0), axis=0, keepdims=True) for k in range(3)
        ]
        line = jnp.concatenate(parts + [jnp.zeros((1, width - 384), F32)], axis=1)
        slots_ref[g, data:message, :] = jnp.broadcast_to(line, (16, width)).astype(BF16)


def attention_forward(
    batch, after, counts, tokens, cot, gain, wq, wk, wv, wo, vector, gain_ffn, w_router, srow, rcol, groups, per, gated
):
    length, width = tokens.shape[2:]
    experts = w_router.shape[1]
    message = padded(per) if gated else padded(per) + 16
    slabs = [jax.ShapeDtypeStruct((groups, message, width), BF16)]
    if gated:
        slabs = slabs + slabs
    return pl.pallas_call(
        functools.partial(attn_kernel, per, gated, batch, len(after)),
        grid=(1,),
        in_specs=[ANYWHERE] * len(after)
        + [SCALARS, batch_block(tokens, batch), batch_block(cot, batch)]
        + [WHOLE] * 8
        + [batch_block(srow, batch), batch_block(rcol, batch)],
        out_specs=[WHOLE] * (5 + len(slabs)),
        out_shape=[
            jax.ShapeDtypeStruct((3, PAIRS, length, PAIR), BF16),
            jax.ShapeDtypeStruct((PAIRS, length, PAIR), BF16),
            jax.ShapeDtypeStruct((length, 128), F32),
            jax.ShapeDtypeStruct((length, width), F32),
            jax.ShapeDtypeStruct((length, experts), F32),
            *slabs,
        ],
        scratch_shapes=[pltpu.VMEM((ROWS, vector.shape[-1]), F32)],
        compiler_params=params(48),
        cost_estimate=cost(20e9, 14e6, HEADS * length * length),
    )(*after, counts, tokens, cot, gain, wq, wk, wv, wo, vector, gain_ffn, w_router, srow, rcol)


GELU_SCALE = 0.7978845608028654
GELU_CUBIC = 0.044715


def expert_kernel(planes, gated, waits, *refs):
    pieces = 2 * planes - 1
    refs = refs[waits:]
    plane = refs[0][0]
    x_refs, refs = refs[1 : 1 + pieces], refs[1 + pieces :]
    c_refs, refs = refs[:pieces], refs[pieces:]
    gate_refs = ()
    if not gated:
        gate_refs, refs = refs[:pieces], refs[pieces:]
    wi_ref, wo_ref, *refs = refs
    out_refs, in_refs = refs[:planes], refs[planes : 2 * planes]
    act_ref, pre_ref, x_ref, c_ref = refs[2 * planes :]
    rows = x_refs[0].shape[0]

    def assemble(parts):
        found = [parts[0][...]]
        for k in range(1, planes):
            from_above = plane + k < planes
            found.append(jnp.where(from_above, parts[k][...], parts[2 * planes - 1 - k][...]))
        return found

    inputs = jnp.concatenate(assemble(x_refs), axis=0)
    grads = assemble(c_refs)
    if not gated:
        place = iota((rows, 128), 0)
        lane = iota((rows, 128), 1)
        expert = pl.program_id(0)
        for k, lines in enumerate(assemble(gate_refs)):
            lines = jnp.where(iota(lines.shape, 0) == expert, lines.astype(F32), 0.0)
            line = jnp.sum(lines, axis=0, keepdims=True)
            line = line[:, :128] + line[:, 128:256] + line[:, 256:384]
            gate = jnp.sum(jnp.where(place == lane, line, 0.0), axis=1, keepdims=True)
            grads[k] = (grads[k].astype(F32) * gate).astype(BF16)
    grads = jnp.concatenate(grads, axis=0)
    x_ref[0] = inputs
    c_ref[0] = grads
    pre = dot(inputs, wi_ref[0])
    square = pre * pre
    curve = jnp.tanh(GELU_SCALE * pre * (1.0 + GELU_CUBIC * square))
    half = 0.5 * (1.0 + curve)
    act = (pre * half).astype(BF16)
    slope = half + 0.5 * pre * (1.0 - curve * curve) * (GELU_SCALE * (1.0 + 3.0 * GELU_CUBIC * square))
    act_ref[0] = act
    outs = dot(act, wo_ref[0]).astype(BF16)
    pre_grad = (slope * dot_t(grads, wo_ref[0])).astype(BF16)
    pre_ref[0] = pre_grad
    ins = dot_t(pre_grad, wi_ref[0]).astype(BF16)
    for k in range(planes):
        out_refs[k][...] = outs[k * rows : (k + 1) * rows]
        in_refs[k][...] = ins[k * rows : (k + 1) * rows]


def experts_both(after, plane, xs, cs, w_inner, w_outer, gated):
    local, width, hidden = w_inner.shape
    pieces = len(xs)
    planes = (pieces + 1) // 2
    rows = cs[0].shape[0] // local
    slab = pl.BlockSpec((rows, width), lambda e: (e, 0))
    lines = pl.BlockSpec((16, width), lambda e: (local * rows // 16, 0))
    mat = lambda a, b: pl.BlockSpec((1, a, b), lambda e: (e, 0, 0))
    total = planes * rows
    part = jax.ShapeDtypeStruct((local * rows, width), BF16)
    kept = lambda n: jax.ShapeDtypeStruct((local, total, n), BF16)
    return pl.pallas_call(
        functools.partial(expert_kernel, planes, gated, len(after)),
        grid=(local,),
        in_specs=[ANYWHERE] * len(after)
        + [SCALARS]
        + [slab] * (2 * pieces)
        + ([] if gated else [lines] * pieces)
        + [mat(width, hidden), mat(hidden, width)],
        out_specs=[slab] * (2 * planes)
        + [mat(total, hidden), mat(total, hidden), mat(total, width), mat(total, width)],
        out_shape=[part] * (2 * planes) + [kept(hidden), kept(hidden), kept(width), kept(width)],
        compiler_params=params(48),
        cost_estimate=cost(
            8 * local * total * width * hidden, 4 * local * hidden * width + 24 * local * total * width, local * total * hidden
        ),
    )(*after, plane, *xs, *cs, *(() if gated else xs), w_inner, w_outer)


def expert_grad_kernel(batches, *refs):
    xs, cs, acts, pres = (refs[k * batches : (k + 1) * batches] for k in range(4))
    outer_ref, inner_ref = refs[4 * batches :]
    outer = inner = None
    for b in range(batches):
        outer_part = t_dot(acts[b][0], cs[b][0])
        inner_part = t_dot(xs[b][0], pres[b][0])
        outer = outer_part if outer is None else outer + outer_part
        inner = inner_part if inner is None else inner + inner_part
    outer_ref[0] = outer
    inner_ref[0] = inner


def expert_grads(xs, cs, acts, pres):
    batches = len(xs)
    local, total, width = xs[0].shape
    hidden = acts[0].shape[2]
    mat = lambda a, b: pl.BlockSpec((1, a, b), lambda e: (e, 0, 0))
    return pl.pallas_call(
        functools.partial(expert_grad_kernel, batches),
        grid=(local,),
        in_specs=[mat(total, width)] * (2 * batches) + [mat(total, hidden)] * (2 * batches),
        out_specs=[mat(hidden, width), mat(width, hidden)],
        out_shape=[
            jax.ShapeDtypeStruct((local, hidden, width), F32),
            jax.ShapeDtypeStruct((local, width, hidden), F32),
        ],
        compiler_params=params(48),
        cost_estimate=cost(
            4 * batches * local * total * width * hidden, 8 * local * hidden * width + 8 * batches * local * total * width
        ),
    )(*xs, *cs, *acts, *pres)


def combine_kernel(per, batch, waits, *refs):
    refs = refs[waits:]
    len_ref, out_ref, in_ref, scol_ref, rcol_ref, res_ref, probs_ref, cot_ref, gffn_ref, wr_ref, wo_ref, mixed_ref, *refs = refs
    past_ref = refs.pop(0) if batch else None
    layer_ref, resgrad_ref, mgrad_ref, shared_ref = refs
    length, width = cot_ref.shape[2:]
    experts = wr_ref.shape[1]
    groups, message, _ = out_ref.shape
    valid = iota((length, 1), 0) < len_ref[batch]
    collect = one_hot(iota((length, groups * message), 1) == spread_slots(scol_ref[0], per, message))
    returned = dot(collect, out_ref[...].reshape(groups * message, width))
    residual = res_ref[...]
    probs = probs_ref[...]
    chosen = iota(probs.shape, 1) == rcol_ref[0]
    gate = jnp.sum(jnp.where(chosen, probs, 0.0), axis=-1, keepdims=True)
    layer_ref[...] = jnp.where(valid, residual + gate * returned, 0.0).astype(BF16)
    out_grad = jnp.where(valid, cot_ref[0, 0].astype(F32), 0.0)
    gate_grad = jnp.sum(out_grad * returned, axis=-1, keepdims=True)
    prob_grad = jnp.where(chosen, gate_grad, 0.0)
    logit_grad = (probs * (prob_grad - jnp.sum(probs * prob_grad, axis=-1, keepdims=True))).astype(BF16)
    inverse = lax.rsqrt(jnp.mean(residual * residual, axis=-1, keepdims=True) + epsilon)
    gain = gffn_ref[...]
    scaled = residual * inverse
    routed = (scaled * gain).astype(BF16)

    def share(first, rows):
        if past_ref is not None:
            rows = rows + past_ref[first : first + rows.shape[0], :]
        shared_ref[first : first + rows.shape[0], :] = rows.astype(shared_ref.dtype)

    share(width, t_dot(logit_grad, routed))
    routed_grad = dot_t(logit_grad, wr_ref[...]) + dot(collect, in_ref[...].reshape(groups * message, width))
    gain_part = jnp.sum(routed_grad * scaled, axis=0, keepdims=True)
    left = shared_ref.shape[0] - width - experts
    share(width + experts, jnp.where(iota((left, width), 0) == 0, gain_part, 0.0))
    upstream = routed_grad * gain
    middle = jnp.mean(upstream * scaled, axis=-1, keepdims=True)
    residual_grad = out_grad + inverse * (upstream - scaled * middle)
    resgrad_ref[...] = residual_grad
    attended = residual_grad.astype(BF16)
    mixed_all = jnp.concatenate([mixed_ref[p] for p in range(PAIRS)], axis=1)
    share(0, t_dot(mixed_all, attended))
    mixed_grad = dot_t(attended, wo_ref[...]).astype(BF16)
    for pair in range(PAIRS):
        mgrad_ref[pair] = mixed_grad[:, pair * PAIR : (pair + 1) * PAIR]


def combine(
    batch, last, after, counts, outs, ins, scol, rcol, residual, probs, cot, gain_ffn, w_router, w_output, mixed, past, per, shared
):
    length, width = cot.shape[2:]
    return pl.pallas_call(
        functools.partial(combine_kernel, per, batch, len(after)),
        grid=(1,),
        in_specs=[ANYWHERE] * len(after)
        + [SCALARS, WHOLE, WHOLE, batch_block(scol, batch), batch_block(rcol, batch), WHOLE, WHOLE, batch_block(cot, batch)]
        + [WHOLE] * (5 if batch else 4),
        out_specs=[WHOLE] * 4,
        out_shape=[
            jax.ShapeDtypeStruct((length, width), BF16),
            jax.ShapeDtypeStruct((length, width), F32),
            jax.ShapeDtypeStruct((PAIRS, length, PAIR), BF16),
            jax.ShapeDtypeStruct((shared, width), BF16 if last else F32),
        ],
        compiler_params=params(48),
        cost_estimate=cost(8e9, 12e6),
    )(
        *after, counts, outs, ins, scol, rcol, residual, probs, cot, gain_ffn, w_router, w_output, mixed, *([past] if batch else [])
    )


def attn_back_kernel(batch, waits, *refs):
    refs = refs[waits:]
    len_ref, qkv_ref, lse_ref, vec_ref, sel_ref, mgrad_ref, tok_ref, gain_ref, wq_ref, wk_ref, wv_ref, resgrad_ref, *refs = refs
    past_ref = refs.pop(0) if batch else None
    shared_ref, tgrad_ref, band_ref, probs_ref, sgrad_ref, spread_ref, low_ref, kt_ref, vt_ref, diag_ref = refs
    length, width = tok_ref.shape[2:]
    mask = jnp.where(iota((1, length), 1) < len_ref[batch], 0.0, negative)
    lane = iota((ROWS, PAIR), 1)
    diag_ref[...] = jnp.zeros_like(diag_ref)

    def one_pair(pair, carry):
        keys = qkv_ref[1, pair]
        values = qkv_ref[2, pair]
        queries_t = qkv_ref[0, pair].T
        grads_t = mgrad_ref[pair].T
        for side in range(2):
            head = 2 * pair + side
            band_ref[...] = band_bias(vec_ref, head)
            spread_ref[...] = jnp.zeros_like(spread_ref)
            mine = (lane >= HEAD_DIM) if side else (lane < HEAD_DIM)
            for block in range(length // ROWS):
                here = slice(ROWS * block, ROWS * (block + 1))
                window = band_slice(block, length)
                queries = qkv_ref[0, pair, here, :] * 0.125
                queries = jnp.where(mine, queries, jnp.zeros_like(queries))
                grads = mgrad_ref[pair, here, :]
                grads = jnp.where(mine, grads, jnp.zeros_like(grads))
                column = iota((ROWS, lse_ref.shape[1]), 1)
                log_total = jnp.sum(jnp.where(column == head, lse_ref[here, :], 0.0), axis=-1, keepdims=True)
                scores = dot_t(queries, keys) + band_ref[:, window] + mask
                probs = jnp.exp(scores - log_total)
                probs_ref[here, :] = probs.astype(BF16)
                weighted = probs * dot_t(grads, values)
                score_grad = weighted - probs * jnp.sum(weighted, axis=-1, keepdims=True)
                spread_ref[:, window] += score_grad
                low = score_grad.astype(BF16)
                sgrad_ref[here, :] = low
                query_grad = (dot(low, keys) * 0.125).astype(BF16)
                if side:
                    query_grad = jnp.where(mine, query_grad, low_ref[0, pair, here, :])
                low_ref[0, pair, here, :] = query_grad
            rows = slice(HEAD_DIM * side, HEAD_DIM * (side + 1))
            kt_ref[rows, :] = dot(queries_t[rows, :], sgrad_ref[...]) * 0.125
            vt_ref[rows, :] = dot(grads_t[rows, :], probs_ref[...])
            size = spread_ref.shape[1]
            eight = spread_ref[0:8, :]
            for step in range(8, ROWS, 8):
                eight = eight + pltpu.roll(spread_ref[step : step + 8, :], size - step, 1)
            diagonal = eight[0:1, :]
            for step in range(1, 8):
                diagonal = diagonal + pltpu.roll(eight[step : step + 1, :], size - step, 1)
            diag_ref[...] = jnp.where(iota(diag_ref.shape, 0) == head, diagonal, diag_ref[...])
        low_ref[1, pair] = kt_ref[...].T.astype(BF16)
        low_ref[2, pair] = vt_ref[...].T.astype(BF16)
        return carry

    lax.fori_loop(0, PAIRS, one_pair, 0)

    def share(first, rows):
        if past_ref is not None:
            rows = rows + past_ref[first : first + rows.shape[0], :]
        shared_ref[first : first + rows.shape[0], :] = rows.astype(shared_ref.dtype)

    tokens = tok_ref[0, 0].astype(F32)
    inverse = lax.rsqrt(jnp.mean(tokens * tokens, axis=-1, keepdims=True) + epsilon)
    gain = gain_ref[...]
    scaled = tokens * inverse
    normed_t = (scaled * gain).astype(BF16).T
    normed_grad = jnp.zeros((length, width), F32)
    for which, w_ref in enumerate((wq_ref, wk_ref, wv_ref)):
        low = jnp.concatenate([low_ref[which, p] for p in range(PAIRS)], axis=1)
        share(which * width, dot(normed_t, low))
        normed_grad = normed_grad + dot_t(low, w_ref[...])
    gain_part = jnp.sum(normed_grad * scaled, axis=0, keepdims=True)
    bias_part = lax.dot_general(
        diag_ref[...], sel_ref[...], (((1,), (0,)), ((), ())), precision=lax.Precision.HIGHEST, preferred_element_type=F32
    )
    left = shared_ref.shape[0] - 3 * width - 24
    first = jnp.where(iota((8, width), 0) == 0, gain_part, 0.0)
    wide = jnp.concatenate([bias_part, jnp.zeros((16, width - bias_part.shape[1]), F32)], axis=1)
    share(3 * width, jnp.concatenate([first, wide, jnp.zeros((left, width), F32)], axis=0))
    upstream = normed_grad * gain
    middle = jnp.mean(upstream * scaled, axis=-1, keepdims=True)
    tgrad_ref[...] = (resgrad_ref[...] + inverse * (upstream - scaled * middle)).astype(BF16)


def attention_backward(
    batch, last, after, counts, qkv, lse, vector, selector, mixed_grad, tokens, gain, wq, wk, wv, residual_grad, past, shared
):
    length, width = tokens.shape[2:]
    size = vector.shape[-1]
    return pl.pallas_call(
        functools.partial(attn_back_kernel, batch, len(after)),
        grid=(1,),
        in_specs=[ANYWHERE] * len(after)
        + [SCALARS]
        + [WHOLE] * 5
        + [batch_block(tokens, batch)]
        + [WHOLE] * (6 if batch else 5),
        out_specs=[WHOLE] * 2,
        out_shape=[
            jax.ShapeDtypeStruct((shared, width), BF16 if last else F32),
            jax.ShapeDtypeStruct((length, width), BF16),
        ],
        scratch_shapes=[
            pltpu.VMEM((ROWS, size), F32),
            pltpu.VMEM((length, length), BF16),
            pltpu.VMEM((length, length), BF16),
            pltpu.VMEM((ROWS, size), F32),
            pltpu.VMEM((3, PAIRS, length, PAIR), BF16),
            pltpu.VMEM((PAIR, length), F32),
            pltpu.VMEM((PAIR, length), F32),
            pltpu.VMEM((16, size), F32),
        ],
        compiler_params=params(56),
        cost_estimate=cost(32e9, 20e6, HEADS * length * length),
    )(
        *after, counts, qkv, lse, vector, selector, mixed_grad, tokens, gain, wq, wk, wv, residual_grad, *([past] if batch else [])
    )


def upward(planes, first, last):
    return [(k, k + 1) for k in range(first, last)]


def downward(planes, first, last):
    return [(planes - 1 - k, planes - 2 - k) for k in range(first, last)]


def mix_kernel(both, planes, step, waits, here_ref, up_ref, down_ref, upsum_ref, downsum_ref, *refs):
    to_up, to_down = refs[waits:]
    for moving, sums, out, place in (
        (up_ref, upsum_ref, to_up, here_ref[0]),
        (down_ref, downsum_ref, to_down, planes - 1 - here_ref[0]),
    ):
        total = moving[...] + sums[...]
        out[...] = jnp.where(place <= step, total, moving[...]) if both else total


def mix(both, planes, step, here, up, down, upsum, downsum, after):
    rows, width = up.shape
    block = pl.BlockSpec((rows // 4, width), lambda i: (i, 0))
    return pl.pallas_call(
        functools.partial(mix_kernel, both, planes, step, len(after)),
        grid=(4,),
        in_specs=[SCALARS] + [block] * 4 + [ANYWHERE] * len(after),
        out_specs=[block] * 2,
        out_shape=[jax.ShapeDtypeStruct((rows, width), BF16)] * 2,
        compiler_params=params(32),
        cost_estimate=cost(),
    )(here, up, down, upsum, downsum, *after)


class Chain:
    def __init__(self, planes, own=None, sums=None):
        self.planes, self.own, self.sums = planes, own, sums
        self.here = lax.axis_index("hidden")[None]
        self.from_below, self.from_above = [], []
        if own is not None:
            self.up = self.down = own
        else:
            self.up, self.down = sums[planes - 1], sums[1]
        self.count = 0
        self.steps = planes if own is not None and sums is not None else planes - 1

    def send(self):
        planes, s = self.planes, self.count
        if self.own is not None and self.sums is not None:
            first, last = 0, planes - 1
        elif self.own is not None:
            first, last = s, planes - 1
        else:
            first, last = 0, s + 1
        self.up = lax.ppermute(self.up, "hidden", upward(planes, first, last))
        self.down = lax.ppermute(self.down, "hidden", downward(planes, first, last))
        self.count += 1
        if self.own is not None and s < planes - 1:
            self.from_below.append(self.up)
            self.from_above.append(self.down)

    def mix(self, *after):
        planes, s = self.planes, self.count - 1
        both = self.own is not None
        offset = 1 if both else 2
        self.up, self.down = mix(
            both, planes, s, self.here, self.up, self.down, self.sums[planes - offset - s], self.sums[s + offset], after
        )

    def run(self):
        while self.count < self.steps:
            self.send()
        return self

    def gathered(self):
        return (self.own, *self.from_above, *self.from_below)

    def scattered(self):
        return (self.sums[0], self.up, self.down)


def exchange_sum(values, axis_bits):
    me = lax.axis_index("expert")
    size = lax.axis_size("expert")
    for bit in axis_bits:
        halves = values.reshape(2, values.shape[0] // 2, values.shape[1])
        side = (me // bit) % 2
        mine = lax.dynamic_index_in_dim(halves, side, 0, keepdims=False)
        other = lax.dynamic_index_in_dim(halves, 1 - side, 0, keepdims=False)
        values = mine + lax.ppermute(other, "expert", [(k, k ^ bit) for k in range(size)])
    return values


def exchange_join(values, axis_bits):
    me = lax.axis_index("expert")
    size = lax.axis_size("expert")
    for bit in reversed(axis_bits):
        other = lax.ppermute(values, "expert", [(k, k ^ bit) for k in range(size)])
        second = (me // bit) % 2 == 1
        values = jnp.concatenate([jnp.where(second, other, values), jnp.where(second, values, other)])
    return values


def sum_everywhere(values):
    size = lax.axis_size("expert")
    planes = lax.axis_size("hidden")
    bits = [1 << k for k in range(size.bit_length() - 1)]
    count = values.shape[0]
    unit = 16 * size
    values = jnp.pad(values.astype(BF16), ((0, -count % unit), (0, 0)))
    near, far = bits[:1], bits[1:]
    values = exchange_sum(values, near)
    half = values.shape[0] // 2
    done = []
    for part, order in ((values[:half], far), (values[half:], far[::-1])):
        part = exchange_sum(part, order)
        total = part.astype(F32)
        for k in range(1, planes):
            total = total + lax.ppermute(part, "hidden", [(p, p ^ k) for p in range(planes)]).astype(F32)
        done.append(exchange_join(total.astype(BF16), order))
    return exchange_join(jnp.concatenate(done), near)[:count].astype(F32)


def offset_selector(length):
    place = np.arange(2 * length)
    offsets = np.where(place < 2 * length - ROWS, place, place - 2 * length) - (length - ROWS)
    offsets = np.clip(offsets, -(length - 1), length - 1)
    return (offset_bucket(offsets)[:, None] == np.arange(BUCKETS)[None, :]).astype(np.float32)


def moves(groups, local, capacity, message):
    expert, group, slot = np.meshgrid(np.arange(local), np.arange(groups), np.arange(capacity), indexing="ij")
    source = (group * message + expert * capacity + slot).reshape(-1)
    return (source[:, None] == np.arange(groups * message)[None, :]).astype(jnp.bfloat16)


def shards(
    tokens,
    cotangent,
    lengths,
    routes,
    gain_attn,
    w_query,
    w_key,
    w_value,
    w_output,
    bucket_head_bias,
    gain_ffn,
    w_router,
    w_inner,
    w_outer,
):
    batches, _, length, width = tokens.shape
    experts = w_router.shape[1]
    local = w_inner.shape[0]
    groups = lax.axis_size("expert")
    planes = lax.axis_size("hidden")
    capacity = (5 * length + 4 * experts - 1) // (4 * experts)
    per = local * capacity
    rows = groups * capacity
    message = padded(per)
    move = jnp.asarray(moves(groups, local, capacity, message))
    move_gated = jnp.asarray(moves(groups, local, capacity, message + 16))
    move_back = jnp.asarray(moves(groups, local, capacity, message).T)
    selector = jnp.asarray(offset_selector(length))
    vector = lax.dot_general(
        bucket_head_bias, selector, (((0,), (1,)), ((), ())), precision=lax.Precision.HIGHEST
    )[:, None, :]
    gain_a = gain_attn[None, :]
    gain_f = gain_ffn[None, :]
    counts = lengths[:, 0]
    plane = lax.axis_index("hidden")[None]

    def to_groups(values):
        return lax.all_to_all(values, "expert", split_axis=0, concat_axis=0, tiled=True)

    def leaving(values):
        sent = to_groups(values)
        if values.shape[1] != message:
            return regroup_gated(move_gated, sent, capacity)
        return regroup(move, [sent], (local * rows, width))

    def arriving(parts):
        return to_groups(regroup(move_back, parts, (groups, message, width)))

    def attend(b, *after):
        return attention_forward(
            b,
            after,
            counts,
            tokens,
            cotangent,
            gain_a,
            w_query,
            w_key,
            w_value,
            w_output,
            vector,
            gain_f,
            w_router,
            srow,
            rcol,
            groups,
            per,
            b > 0,
        )

    srow, scol, cot_slots = prep(counts, routes.reshape(batches, length), cotangent, groups, per, capacity)
    rcol = routes.reshape(batches, length, 1)
    each = range(batches)
    grads = leaving(cot_slots)
    forward = [attend(0, grads)]
    inputs = leaving(forward[0][5])
    grad_chain = Chain(planes, grads).run()
    input_chain = Chain(planes, inputs).run()
    early = width + experts + 16
    early = early + -early % (16 * groups)
    late = 3 * width + 24
    late = late + -late % (16 * groups)
    kept, layer_rows, token_grads = [], [], []
    early_part = late_part = None

    def finish(b, after, outs, ins):
        qkv, mixed, lse, residual, probs = forward[b][:5]
        last = b + 1 == batches
        layer, res_grad, mixed_grad, early_part_b = combine(
            b,
            last,
            after,
            counts,
            outs,
            ins,
            scol,
            rcol,
            residual,
            probs,
            cotangent,
            gain_f,
            w_router,
            w_output,
            mixed,
            early_part,
            per,
            early,
        )
        late_part_b, token_grad = attention_backward(
            b,
            last,
            (),
            counts,
            qkv,
            lse,
            vector,
            selector,
            mixed_grad,
            tokens,
            gain_a,
            w_query,
            w_key,
            w_value,
            res_grad,
            late_part,
            late,
        )
        layer_rows.append(layer)
        token_grads.append(token_grad)
        return early_part_b, late_part_b

    for b in each:
        xs, cs = input_chain.gathered(), grad_chain.gathered()
        last = b + 1 == batches
        if last:
            grads = inputs = None
            after = () if b == 0 else (grad_chain.up, input_chain.up)
        else:
            forward.append(attend(b + 1, inputs))
            grads, inputs = leaving(forward[b + 1][6]), leaving(forward[b + 1][5])
            after = (grads, inputs)
        worked = experts_both(after, plane, xs, cs, w_inner, w_outer, b > 0)
        kept.append(worked[2 * planes :])
        if b:
            grad_chain.send()
            input_chain.send()
            outs, ins = arriving(grad_chain.scattered()), arriving(input_chain.scattered())
        grad_chain = Chain(planes, grads, worked[:planes])
        input_chain = Chain(planes, inputs, worked[planes : 2 * planes])
        grad_chain.send()
        input_chain.send()
        if b:
            early_part, late_part = finish(b - 1, (), outs, ins)
        while grad_chain.count < grad_chain.steps - (0 if last else 1):
            held = (late_part,) if b and grad_chain.count == grad_chain.steps - 1 else ()
            grad_chain.mix(*held)
            grad_chain.send()
            input_chain.mix(*held)
            input_chain.send()
        if not last:
            grad_chain.mix()
            input_chain.mix()
    outer_total, inner_total = expert_grads(
        [k[2] for k in kept], [k[3] for k in kept], [k[0] for k in kept], [k[1] for k in kept]
    )
    outs, ins = arriving(grad_chain.scattered()), arriving(input_chain.scattered())
    early_part, late_part = finish(batches - 1, (inner_total,), outs, ins)
    early_sum = sum_everywhere(early_part)
    late_sum = sum_everywhere(late_part)
    bias = late_sum[3 * width + 8 : 3 * width + 8 + HEADS, :BUCKETS]
    return (
        jnp.stack(layer_rows)[:, None],
        jnp.stack(token_grads)[:, None],
        late_sum[3 * width],
        late_sum[:width],
        late_sum[width : 2 * width],
        late_sum[2 * width : 3 * width],
        early_sum[:width],
        bias.T,
        early_sum[width + experts],
        early_sum[width : width + experts].T,
        inner_total,
        outer_total,
    )


def solution(mesh):
    token = P(None, ("expert", "hidden"), None, None)
    placed = (
        token,
        token,
        P(None, ("expert", "hidden")),
        token,
        *(P() for _ in range(8)),
        P("expert", None, "hidden"),
        P("expert", "hidden", None),
    )
    return jax.shard_map(
        shards,
        mesh=mesh,
        in_specs=placed,
        out_specs=(
            token,
            token,
            *(P() for _ in range(8)),
            P("expert", None, "hidden"),
            P("expert", "hidden", None),
        ),
        check_vma=False,
    )
```

```python
import functools

import jax
import jax.numpy as jnp
import numpy as np
from jax import lax
from jax.experimental import pallas as pl
from jax.experimental.pallas import tpu as pltpu
from jax.sharding import PartitionSpec as P

HEADS = 12
HEAD_DIM = 64
BUCKETS = 32
MAXDIST = 128
PAIR = 2 * HEAD_DIM
PAIRS = HEADS // 2
ROWS = 128

epsilon = 1e-06
negative = -1e30
F32 = jnp.float32
BF16 = jnp.bfloat16
MIB = 1 << 20


def params(mib):
    return pltpu.CompilerParams(vmem_limit_bytes=mib * MIB)


def cost():
    return pl.CostEstimate(flops=1, bytes_accessed=1, transcendentals=0)


def offset_bucket(offsets):
    halfway = BUCKETS // 2
    exact_count = halfway // 2
    relative_distance = np.abs(offsets)
    scaled = (
        np.log(np.maximum(relative_distance, 1) / exact_count)
        / np.log(MAXDIST / exact_count)
        * (halfway - exact_count)
    )
    far_bucket = np.minimum(exact_count + np.floor(scaled).astype(np.int64), halfway - 1)
    near_bucket = np.where(relative_distance < exact_count, relative_distance, far_bucket)
    return (np.where(offsets > 0, halfway, 0) + near_bucket).astype(np.int32)


def dot(a, b):
    return lax.dot_general(a, b, (((1,), (0,)), ((), ())), preferred_element_type=F32)


def dot_t(a, b):
    return lax.dot_general(a, b, (((1,), (1,)), ((), ())), preferred_element_type=F32)


def t_dot(a, b):
    return lax.dot_general(a, b, (((0,), (0,)), ((), ())), preferred_element_type=F32)


def one_hot(condition):
    return jnp.where(condition, 1.0, 0.0).astype(BF16)


def batch_block(array, b):
    rest = array.shape[1:]
    return pl.BlockSpec((1,) + rest, lambda *_: (b,) + (0,) * len(rest))


ANYWHERE = pl.BlockSpec(memory_space=pl.ANY)
WHOLE = pl.BlockSpec(memory_space=pltpu.VMEM)
SCALARS = pl.BlockSpec(memory_space=pltpu.SMEM)


def iota(shape, axis):
    return lax.broadcasted_iota(jnp.int32, shape, axis)


def padded(rows):
    return -(-rows // 16) * 16


def spread_slots(slot, per, message, first=0, last=None):
    last = per if last is None else last
    group = lax.div(jnp.maximum(slot, 0), per)
    inside = slot - group * per
    held = (slot >= 0) & (inside >= first) & (inside < last)
    return jnp.where(held, group * message + inside - first, -1)


def prep_kernel(per, capacity, len_ref, row_ref, col_ref, cot_ref, srow_ref, scol_ref, slots_ref):
    batches, _, length = row_ref.shape
    groups, message, width = slots_ref.shape
    experts = groups * per // capacity
    before = one_hot(iota((length, length), 0) < iota((length, length), 1))
    after = one_hot(iota((length, length), 1) < iota((length, length), 0))
    for b in range(batches):
        count = len_ref[b]
        row = row_ref[b]
        col = col_ref[b]
        valid_row = iota((1, length), 1) < count
        valid_col = iota((length, 1), 0) < count
        chosen_row = iota((experts, length), 0) == row
        chosen_col = iota((length, experts), 1) == col
        earlier_row = dot(one_hot(chosen_row & valid_row), before)
        rank_row = jnp.sum(jnp.where(chosen_row, earlier_row, 0.0), axis=0, keepdims=True).astype(jnp.int32)
        earlier_col = dot(after, one_hot(chosen_col & valid_col))
        rank_col = jnp.sum(jnp.where(chosen_col, earlier_col, 0.0), axis=1, keepdims=True).astype(jnp.int32)
        slot_row = jnp.where(valid_row & (rank_row < capacity), row * capacity + rank_row, -1)
        srow_ref[b] = slot_row
        scol_ref[b] = jnp.where(valid_col & (rank_col < capacity), col * capacity + rank_col, -1)
        if b == 0:
            dispatch = one_hot(iota((groups * message, length), 0) == spread_slots(slot_row, per, message))
            slots_ref[...] = dot(dispatch, cot_ref[0, 0]).astype(BF16).reshape(groups, message, width)


def prep(lengths, routes, cot, groups, per, capacity):
    batches, length = routes.shape
    width = cot.shape[-1]
    vmem = WHOLE
    message = padded(per)
    return pl.pallas_call(
        functools.partial(prep_kernel, per, capacity),
        grid=(1,),
        in_specs=[SCALARS, vmem, vmem, batch_block(cot, 0)],
        out_specs=[vmem] * 3,
        out_shape=[
            jax.ShapeDtypeStruct((batches, 1, length), jnp.int32),
            jax.ShapeDtypeStruct((batches, length, 1), jnp.int32),
            jax.ShapeDtypeStruct((groups, message, width), BF16),
        ],
        compiler_params=params(32),
        cost_estimate=cost(),
    )(lengths, routes.reshape(batches, 1, length), routes.reshape(batches, length, 1), cot)


def regroup_kernel(count, inputs, waits, *refs):
    refs = refs[waits:]
    move_ref, out_ref = refs[0], refs[-1]
    total = refs[1][...].astype(F32)
    for ref in refs[2 : 1 + count]:
        total = total + ref[...].astype(F32)
    out_ref[...] = dot(move_ref[...], total.astype(BF16).reshape(inputs, -1)).astype(BF16).reshape(out_ref.shape)


def regroup(move, arrays, shape, after=()):
    inputs = move.shape[1]
    vmem = pl.BlockSpec(memory_space=pltpu.VMEM)
    return pl.pallas_call(
        functools.partial(regroup_kernel, len(arrays), inputs, len(after)),
        in_specs=[ANYWHERE] * len(after) + [vmem] * (1 + len(arrays)),
        out_specs=vmem,
        out_shape=jax.ShapeDtypeStruct(shape, BF16),
        compiler_params=params(32),
        cost_estimate=cost(),
    )(*after, move, *arrays)


def regroup_gated_kernel(capacity, *refs):
    move_ref, in_ref, out_ref = refs[-3:]
    groups, message, width = in_ref.shape
    total = move_ref.shape[0]
    local = total // (groups * capacity)
    rows = groups * capacity
    flat = in_ref[...].reshape(groups * message, width)
    out_ref[:total, :] = dot(move_ref[...], flat).astype(BF16)
    place = iota((message, 128), 0)
    lane = iota((message, 128), 1)
    columns = []
    for g in range(groups):
        gates = in_ref[g, message - 16 : message, :].astype(F32)[0:1, :]
        parts = [
            jnp.sum(jnp.where(place == lane, gates[:, 128 * k : 128 * (k + 1)], 0.0), axis=1, keepdims=True)
            for k in range(3)
        ]
        wide = iota((message, 128), 1)
        columns.append(jnp.where(wide == 0, parts[0], jnp.where(wide == 1, parts[1], jnp.where(wide == 2, parts[2], 0.0))))
    column = jnp.concatenate(columns, axis=0).astype(BF16)
    moved = dot(move_ref[...], column)
    place = iota((rows, 128), 0)
    lane = iota((rows, 128), 1)
    lines = []
    for l in range(local):
        mine = moved[l * rows : (l + 1) * rows, :]
        parts = [
            jnp.sum(jnp.where(place == lane, mine[:, k : k + 1], 0.0), axis=0, keepdims=True) for k in range(3)
        ]
        lines.append(jnp.concatenate(parts + [jnp.zeros((1, width - 384), F32)], axis=1))
    lines.append(jnp.zeros((16 - local, width), F32))
    out_ref[total:, :] = jnp.concatenate(lines, axis=0).astype(BF16)


def regroup_gated(move, slots, capacity, after=()):
    width = slots.shape[-1]
    vmem = pl.BlockSpec(memory_space=pltpu.VMEM)
    return pl.pallas_call(
        functools.partial(regroup_gated_kernel, capacity),
        in_specs=[ANYWHERE] * len(after) + [vmem] * 2,
        out_specs=vmem,
        out_shape=jax.ShapeDtypeStruct((move.shape[0] + 16, width), BF16),
        compiler_params=params(32),
        cost_estimate=cost(),
    )(*after, move, slots)


def band_bias(vector_ref, head):
    wide = jnp.broadcast_to(vector_ref[head], (ROWS, vector_ref.shape[-1]))
    return pltpu.roll(wide, 0, 1, stride=1, stride_axis=0)


def band_slice(block, length):
    start = length - ROWS * (block + 1)
    return slice(start, start + length)


def attn_kernel(batch, waits, *refs):
    refs = refs[waits:]
    len_ref, tok_ref, gain_ref, wq_ref, wk_ref, wv_ref, vec_ref, qkv_ref, mixed_ref, lse_ref, band_ref, probs_ref, mixed_t_ref = refs
    length, width = tok_ref.shape[2:]
    count = len_ref[batch]
    tokens = tok_ref[0, 0].astype(F32)
    inverse = lax.rsqrt(jnp.mean(tokens * tokens, axis=-1, keepdims=True) + epsilon)
    normed = (tokens * inverse * gain_ref[...]).astype(BF16)
    for which, w_ref in enumerate((wq_ref, wk_ref, wv_ref)):
        for part in range(width // 256):
            rows = dot(normed, w_ref[:, 256 * part : 256 * part + 256]).astype(BF16)
            qkv_ref[which, 2 * part] = rows[:, :PAIR]
            qkv_ref[which, 2 * part + 1] = rows[:, PAIR:]
    mask = jnp.where(iota((1, length), 1) < count, 0.0, negative)
    lane = iota((ROWS, PAIR), 1)
    lse_ref[...] = jnp.zeros_like(lse_ref)

    def one_pair(pair, carry):
        keys = qkv_ref[1, pair]
        values_t = qkv_ref[2, pair].T
        for side in range(2):
            head = 2 * pair + side
            band_ref[...] = band_bias(vec_ref, head)
            mine = (lane >= HEAD_DIM) if side else (lane < HEAD_DIM)
            for block in range(length // ROWS):
                here = slice(ROWS * block, ROWS * (block + 1))
                queries = qkv_ref[0, pair, here, :] * 0.125
                queries = jnp.where(mine, queries, jnp.zeros_like(queries))
                scores = dot_t(queries, keys) + band_ref[:, band_slice(block, length)] + mask
                highest = jnp.max(scores, axis=-1, keepdims=True)
                powers = jnp.exp(scores - highest)
                total = jnp.sum(powers, axis=-1, keepdims=True)
                probs_ref[here, :] = (powers * (1.0 / total)).astype(BF16)
                column = iota((ROWS, lse_ref.shape[1]), 1)
                lse_ref[here, :] = jnp.where(column == head, highest + jnp.log(total), lse_ref[here, :])
            rows = slice(HEAD_DIM * side, HEAD_DIM * (side + 1))
            mixed_t_ref[rows, :] = dot_t(values_t[rows, :], probs_ref[...])
        mixed_ref[pair] = mixed_t_ref[...].T.astype(BF16)
        return carry

    lax.fori_loop(0, PAIRS, one_pair, 0)


def attention_forward(batch, after, counts, tokens, gain, wq, wk, wv, vector):
    length = tokens.shape[2]
    return pl.pallas_call(
        functools.partial(attn_kernel, batch, len(after)),
        grid=(1,),
        in_specs=[ANYWHERE] * len(after) + [SCALARS, batch_block(tokens, batch)] + [WHOLE] * 5,
        out_specs=[WHOLE] * 3,
        out_shape=[
            jax.ShapeDtypeStruct((3, PAIRS, length, PAIR), BF16),
            jax.ShapeDtypeStruct((PAIRS, length, PAIR), BF16),
            jax.ShapeDtypeStruct((length, 128), F32),
        ],
        scratch_shapes=[
            pltpu.VMEM((ROWS, vector.shape[-1]), F32),
            pltpu.VMEM((length, length), BF16),
            pltpu.VMEM((PAIR, length), F32),
        ],
        compiler_params=params(48),
        cost_estimate=cost(),
    )(*after, counts, tokens, gain, wq, wk, wv, vector)


def route_kernel(per, gated, waits, *refs):
    refs = refs[waits:]
    tok_ref, cot_ref, mixed_ref, wo_ref, gffn_ref, wr_ref, srow_ref, rcol_ref, res_ref, probs_ref, *out_refs = refs
    length, width = tok_ref.shape[2:]
    mixed_all = jnp.concatenate([mixed_ref[p] for p in range(PAIRS)], axis=1)
    residual = tok_ref[0, 0].astype(F32) + dot(mixed_all, wo_ref[...])
    res_ref[...] = residual
    inverse = lax.rsqrt(jnp.mean(residual * residual, axis=-1, keepdims=True) + epsilon)
    routed = (residual * inverse * gffn_ref[...]).astype(BF16)
    logits = dot(routed, wr_ref[...])
    powers = jnp.exp(logits - jnp.max(logits, axis=-1, keepdims=True))
    probs = powers / jnp.sum(powers, axis=-1, keepdims=True)
    probs_ref[...] = probs
    gate = jnp.sum(jnp.where(iota(probs.shape, 1) == rcol_ref[0], probs, 0.0), axis=-1, keepdims=True)
    groups, message, _ = out_refs[0].shape
    places = iota((groups * message, length), 0)
    if gated:
        grads = (gate * cot_ref[0, 0].astype(F32)).astype(BF16)
        half = per // 2
        for which, out_ref in enumerate(out_refs):
            place = spread_slots(srow_ref[0], per, message, which * half, (which + 1) * half)
            rows = dot(one_hot(places == place), grads)
            rows = rows + dot(one_hot(places == jnp.where(place < 0, -1, place + half)), routed)
            out_ref[...] = rows.astype(BF16).reshape(out_ref.shape)
        return
    slots_ref = out_refs[0]
    dispatch = one_hot(places == spread_slots(srow_ref[0], per, message))
    slots_ref[...] = dot(dispatch, routed).astype(BF16).reshape(slots_ref.shape)
    first = gate.astype(BF16).astype(F32)
    second = (gate - first).astype(BF16).astype(F32)
    third = gate - first - second
    column = iota((length, PAIR), 1)
    pieces = jnp.where(column == 0, first, jnp.where(column == 1, second, jnp.where(column == 2, third, 0.0)))
    sorted_gates = dot(dispatch, pieces.astype(BF16))
    data = message - 16
    place = iota((data, 128), 0)
    lane = iota((data, 128), 1)
    for g in range(groups):
        mine = sorted_gates[g * message : g * message + data, :]
        parts = [
            jnp.sum(jnp.where(place == lane, mine[:, k : k + 1], 0.0), axis=0, keepdims=True) for k in range(3)
        ]
        line = jnp.concatenate(parts + [jnp.zeros((1, width - 384), F32)], axis=1)
        slots_ref[g, data:message, :] = jnp.broadcast_to(line, (16, width)).astype(BF16)


def route(batch, after, tokens, cot, mixed, wo, gain_ffn, w_router, srow, rcol, groups, per, gated):
    length, width = tokens.shape[2:]
    experts = w_router.shape[1]
    message = padded(per) if gated else padded(per) + 16
    return pl.pallas_call(
        functools.partial(route_kernel, per, gated, len(after)),
        grid=(1,),
        in_specs=[ANYWHERE] * len(after)
        + [batch_block(tokens, batch), batch_block(cot, batch)]
        + [WHOLE] * 4
        + [batch_block(srow, batch), batch_block(rcol, batch)],
        out_specs=[WHOLE] * (4 if gated else 3),
        out_shape=[
            jax.ShapeDtypeStruct((length, width), F32),
            jax.ShapeDtypeStruct((length, experts), F32),
        ]
        + [jax.ShapeDtypeStruct((groups, message, width), BF16)] * (2 if gated else 1),
        compiler_params=params(48),
        cost_estimate=cost(),
    )(*after, tokens, cot, mixed, wo, gain_ffn, w_router, srow, rcol)


GELU_SCALE = 0.7978845608028654
GELU_CUBIC = 0.044715


def expert_kernel(planes, gated, first_expert, waits, *refs):
    pieces = 2 * planes - 1
    refs = refs[waits:]
    plane = refs[0][0]
    x_refs, refs = refs[1 : 1 + pieces], refs[1 + pieces :]
    c_refs, refs = refs[:pieces], refs[pieces:]
    gate_refs = ()
    if not gated:
        gate_refs, refs = refs[:pieces], refs[pieces:]
    wi_ref, wo_ref, *refs = refs
    sum_refs = refs[:planes]
    act_ref, pre_ref, x_ref, c_ref = refs[planes:]
    rows = x_refs[0].shape[0]

    def assemble(parts):
        found = [parts[0][...]]
        for k in range(1, planes):
            from_above = plane + k < planes
            found.append(jnp.where(from_above, parts[k][...], parts[2 * planes - 1 - k][...]))
        return found

    inputs = jnp.concatenate(assemble(x_refs), axis=0)
    grads = assemble(c_refs)
    if not gated:
        place = iota((rows, 128), 0)
        lane = iota((rows, 128), 1)
        expert = first_expert + pl.program_id(0)
        for k, lines in enumerate(assemble(gate_refs)):
            lines = jnp.where(iota(lines.shape, 0) == expert, lines.astype(F32), 0.0)
            line = jnp.sum(lines, axis=0, keepdims=True)
            line = line[:, :128] + line[:, 128:256] + line[:, 256:384]
            gate = jnp.sum(jnp.where(place == lane, line, 0.0), axis=1, keepdims=True)
            grads[k] = (grads[k].astype(F32) * gate).astype(BF16)
    grads = jnp.concatenate(grads, axis=0)
    x_ref[0] = inputs
    c_ref[0] = grads
    pre = dot(inputs, wi_ref[0])
    square = pre * pre
    curve = jnp.tanh(GELU_SCALE * pre * (1.0 + GELU_CUBIC * square))
    half = 0.5 * (1.0 + curve)
    act = (pre * half).astype(BF16)
    slope = half + 0.5 * pre * (1.0 - curve * curve) * (GELU_SCALE * (1.0 + 3.0 * GELU_CUBIC * square))
    act_ref[0] = act
    outs = dot(act, wo_ref[0]).astype(BF16)
    pre_grad = (slope * dot_t(grads, wo_ref[0])).astype(BF16)
    pre_ref[0] = pre_grad
    ins = dot_t(pre_grad, wi_ref[0]).astype(BF16)
    for k in range(planes):
        sum_refs[k][0] = outs[k * rows : (k + 1) * rows]
        sum_refs[k][1] = ins[k * rows : (k + 1) * rows]


def experts_half(which, after, plane, messages, w_inner, w_outer, xs=None, cs=None):
    local, width, hidden = w_inner.shape
    mine = local // 2
    first = which * mine
    gated = messages is not None
    pieces = len(messages if gated else xs)
    planes = (pieces + 1) // 2
    if gated:
        rows = messages[0].shape[1] // mine
        x_block = pl.BlockSpec((None, rows, width), lambda e: (1, e, 0))
        c_block = pl.BlockSpec((None, rows, width), lambda e: (0, e, 0))
        arrays = (*messages, *messages)
        blocks = [x_block] * pieces + [c_block] * pieces
    else:
        rows = cs[0].shape[0] // local
        slab = pl.BlockSpec((rows, width), lambda e: (first + e, 0))
        lines = pl.BlockSpec((16, width), lambda e: (local * rows // 16, 0))
        arrays = (*xs, *cs, *xs)
        blocks = [slab] * (2 * pieces) + [lines] * pieces
    weight = lambda a, b: pl.BlockSpec((1, a, b), lambda e: (first + e, 0, 0))
    mat = lambda a, b: pl.BlockSpec((1, a, b), lambda e: (e, 0, 0))
    total = planes * rows
    kept = lambda n: jax.ShapeDtypeStruct((mine, total, n), BF16)
    return pl.pallas_call(
        functools.partial(expert_kernel, planes, gated, first, len(after)),
        grid=(mine,),
        in_specs=[ANYWHERE] * len(after) + [SCALARS] + blocks + [weight(width, hidden), weight(hidden, width)],
        out_specs=[pl.BlockSpec((2, rows, width), lambda e: (0, e, 0))] * planes
        + [mat(total, hidden), mat(total, hidden), mat(total, width), mat(total, width)],
        out_shape=[jax.ShapeDtypeStruct((2, mine * rows, width), BF16)] * planes
        + [kept(hidden), kept(hidden), kept(width), kept(width)],
        compiler_params=params(48),
        cost_estimate=cost(),
    )(*after, plane, *arrays, w_inner, w_outer)


def expert_grad_kernel(batches, waits, *refs):
    xs, cs, acts, pres = (refs[waits + k * batches : waits + (k + 1) * batches] for k in range(4))
    outer_ref, inner_ref = refs[-2:]
    whole = lambda refs: jnp.concatenate([ref[0] for ref in refs], axis=0)
    outer_ref[0] = t_dot(whole(acts), whole(cs))
    inner_ref[0] = t_dot(whole(xs), whole(pres))


def expert_grads(which, after, past, local, xs, cs, acts, pres):
    batches = len(xs)
    mine, total, width = xs[0].shape
    hidden = acts[0].shape[2]
    first = which * mine
    mat = lambda a, b: pl.BlockSpec((1, a, b), lambda e: (e, 0, 0))
    out = lambda a, b: pl.BlockSpec((1, a, b), lambda e: (first + e, 0, 0))
    behind = len(after) + 4 * batches
    return pl.pallas_call(
        functools.partial(expert_grad_kernel, batches, len(after)),
        grid=(mine,),
        in_specs=[ANYWHERE] * len(after)
        + [mat(total, width)] * (2 * batches)
        + [mat(total, hidden)] * (2 * batches)
        + [ANYWHERE] * len(past),
        out_specs=[out(hidden, width), out(width, hidden)],
        out_shape=[
            jax.ShapeDtypeStruct((local, hidden, width), F32),
            jax.ShapeDtypeStruct((local, width, hidden), F32),
        ],
        input_output_aliases={behind + k: k for k in range(len(past))},
        compiler_params=params(48),
        cost_estimate=cost(),
    )(*after, *xs, *cs, *acts, *pres, *past)


def combine_kernel(per, batch, waits, *refs):
    refs = refs[waits:]
    len_ref, low_ref, high_ref, scol_ref, rcol_ref, res_ref, probs_ref, cot_ref, gffn_ref, wr_ref, wo_ref, mixed_ref, *refs = refs
    past_ref = refs.pop(0) if batch else None
    layer_ref, resgrad_ref, mgrad_ref, shared_ref = refs
    length, width = cot_ref.shape[2:]
    experts = wr_ref.shape[1]
    groups, message, _ = low_ref.shape
    valid = iota((length, 1), 0) < len_ref[batch]
    places = iota((length, groups * message), 1)
    half = per // 2
    returned = input_grad = None
    for which, ref in enumerate((low_ref, high_ref)):
        place = spread_slots(scol_ref[0], per, message, which * half, (which + 1) * half)
        rows = ref[...].reshape(groups * message, width)
        out_part = dot(one_hot(places == place), rows)
        in_part = dot(one_hot(places == jnp.where(place < 0, -1, place + half)), rows)
        returned = out_part if returned is None else returned + out_part
        input_grad = in_part if input_grad is None else input_grad + in_part
    residual = res_ref[...]
    probs = probs_ref[...]
    chosen = iota(probs.shape, 1) == rcol_ref[0]
    gate = jnp.sum(jnp.where(chosen, probs, 0.0), axis=-1, keepdims=True)
    layer_ref[...] = jnp.where(valid, residual + gate * returned, 0.0).astype(BF16)
    out_grad = jnp.where(valid, cot_ref[0, 0].astype(F32), 0.0)
    gate_grad = jnp.sum(out_grad * returned, axis=-1, keepdims=True)
    prob_grad = jnp.where(chosen, gate_grad, 0.0)
    logit_grad = (probs * (prob_grad - jnp.sum(probs * prob_grad, axis=-1, keepdims=True))).astype(BF16)
    inverse = lax.rsqrt(jnp.mean(residual * residual, axis=-1, keepdims=True) + epsilon)
    gain = gffn_ref[...]
    scaled = residual * inverse
    routed = (scaled * gain).astype(BF16)

    def share(first, whole_rows):
        for side in range(2):
            rows = whole_rows[:, side * width // 2 : (side + 1) * width // 2]
            here = slice(side * shared_ref.shape[0] // 2 + first, side * shared_ref.shape[0] // 2 + first + rows.shape[0])
            if past_ref is not None:
                rows = rows + past_ref[here, :]
            shared_ref[here, :] = rows.astype(shared_ref.dtype)

    share(width, t_dot(logit_grad, routed))
    routed_grad = dot_t(logit_grad, wr_ref[...]) + input_grad
    gain_part = jnp.sum(routed_grad * scaled, axis=0, keepdims=True)
    left = shared_ref.shape[0] // 2 - width - experts
    share(width + experts, jnp.where(iota((left, width), 0) == 0, gain_part, 0.0))
    upstream = routed_grad * gain
    middle = jnp.mean(upstream * scaled, axis=-1, keepdims=True)
    residual_grad = out_grad + inverse * (upstream - scaled * middle)
    resgrad_ref[...] = residual_grad
    attended = residual_grad.astype(BF16)
    mixed_all = jnp.concatenate([mixed_ref[p] for p in range(PAIRS)], axis=1)
    share(0, t_dot(mixed_all, attended))
    mixed_grad = dot_t(attended, wo_ref[...]).astype(BF16)
    for pair in range(PAIRS):
        mgrad_ref[pair] = mixed_grad[:, pair * PAIR : (pair + 1) * PAIR]


def combine(
    batch, last, after, counts, low, high, scol, rcol, residual, probs, cot, gain_ffn, w_router, w_output, mixed, past, per, shared
):
    length, width = cot.shape[2:]
    return pl.pallas_call(
        functools.partial(combine_kernel, per, batch, len(after)),
        grid=(1,),
        in_specs=[ANYWHERE] * len(after)
        + [SCALARS, WHOLE, WHOLE, batch_block(scol, batch), batch_block(rcol, batch), WHOLE, WHOLE, batch_block(cot, batch)]
        + [WHOLE] * (4 + len(past)),
        out_specs=[WHOLE] * 4,
        out_shape=[
            jax.ShapeDtypeStruct((length, width), BF16),
            jax.ShapeDtypeStruct((length, width), F32),
            jax.ShapeDtypeStruct((PAIRS, length, PAIR), BF16),
            jax.ShapeDtypeStruct((shared, width // 2), BF16 if last else F32),
        ],
        compiler_params=params(48),
        cost_estimate=cost(),
    )(
        *after, counts, low, high, scol, rcol, residual, probs, cot, gain_ffn, w_router, w_output, mixed, *past
    )


def attn_back_kernel(batch, which, waits, *refs):
    refs = refs[waits:]
    len_ref, qkv_ref, lse_ref, vec_ref, sel_ref, mgrad_ref, tok_ref, gain_ref, wq_ref, wk_ref, wv_ref, *refs = refs
    past_ref = refs.pop(0) if batch else None
    if which:
        seen_ref, part_ref, resgrad_ref, *refs = refs
        shared_ref, tgrad_ref, *refs = refs
    else:
        early_ref = refs.pop(0) if batch else None
        shared_ref, diag_out_ref, part_out_ref, *refs = refs
    band_ref, probs_ref, sgrad_ref, spread_ref, low_ref, qt_ref, kt_ref, vt_ref, diag_ref, *buffers, sems = refs
    fetched = [tok_ref.at[batch, 0], wq_ref, wk_ref, wv_ref]
    if past_ref is not None:
        fetched.append(past_ref)
    if which:
        fetched += [part_ref, resgrad_ref]
    elif batch:
        fetched.append(early_ref)
    copies = [pltpu.make_async_copy(ref, buffer, sems.at[k]) for k, (ref, buffer) in enumerate(zip(fetched, buffers))]
    for copy in copies:
        copy.start()
    tok_ref, wq_ref, wk_ref, wv_ref, *buffers = buffers
    if past_ref is not None:
        past_ref = buffers.pop(0)
    if which:
        part_ref, resgrad_ref = buffers
    elif batch:
        early_ref = buffers[0]
    length, width = tok_ref.shape
    first_pair = which * (PAIRS // 2)
    mask = jnp.where(iota((1, length), 1) < len_ref[batch], 0.0, negative)
    lane = iota((ROWS, PAIR), 1)
    diag_ref[...] = seen_ref[...] if which else jnp.zeros_like(diag_ref)

    def one_pair(step, carry):
        pair = first_pair + step
        keys = qkv_ref[1, pair]
        values = qkv_ref[2, pair]
        queries_t = qkv_ref[0, pair].T
        keys_t = qkv_ref[1, pair].T
        grads_t = mgrad_ref[pair].T
        for side in range(2):
            head = 2 * pair + side
            band_ref[...] = band_bias(vec_ref, head)
            spread_ref[...] = jnp.zeros_like(spread_ref)
            mine = (lane >= HEAD_DIM) if side else (lane < HEAD_DIM)
            for block in range(length // ROWS):
                here = slice(ROWS * block, ROWS * (block + 1))
                window = band_slice(block, length)
                queries = qkv_ref[0, pair, here, :] * 0.125
                queries = jnp.where(mine, queries, jnp.zeros_like(queries))
                grads = mgrad_ref[pair, here, :]
                grads = jnp.where(mine, grads, jnp.zeros_like(grads))
                column = iota((ROWS, lse_ref.shape[1]), 1)
                log_total = jnp.sum(jnp.where(column == head, lse_ref[here, :], 0.0), axis=-1, keepdims=True)
                scores = dot_t(queries, keys) + band_ref[:, window] + mask
                probs = jnp.exp(scores - log_total)
                probs_ref[here, :] = probs.astype(BF16)
                weighted = probs * dot_t(grads, values)
                score_grad = weighted - probs * jnp.sum(weighted, axis=-1, keepdims=True)
                spread_ref[:, window] += score_grad
                sgrad_ref[here, :] = score_grad.astype(BF16)
            rows = slice(HEAD_DIM * side, HEAD_DIM * (side + 1))
            qt_ref[rows, :] = dot_t(keys_t[rows, :], sgrad_ref[...]) * 0.125
            kt_ref[rows, :] = dot(queries_t[rows, :], sgrad_ref[...]) * 0.125
            vt_ref[rows, :] = dot(grads_t[rows, :], probs_ref[...])
            size = spread_ref.shape[1]
            eight = spread_ref[0:8, :]
            for move in range(8, ROWS, 8):
                eight = eight + pltpu.roll(spread_ref[move : move + 8, :], size - move, 1)
            diagonal = eight[0:1, :]
            for move in range(1, 8):
                diagonal = diagonal + pltpu.roll(eight[move : move + 1, :], size - move, 1)
            diag_ref[...] = jnp.where(iota(diag_ref.shape, 0) == head, diagonal, diag_ref[...])
        low_ref[0, step] = qt_ref[...].T.astype(BF16)
        low_ref[1, step] = kt_ref[...].T.astype(BF16)
        low_ref[2, step] = vt_ref[...].T.astype(BF16)
        return carry

    lax.fori_loop(0, PAIRS // 2, one_pair, 0)
    for copy in copies:
        copy.wait()
    offset = 0 if which or shared_ref.dtype == F32 else early_ref.shape[0]

    def share(first, rows):
        if past_ref is not None:
            rows = rows + past_ref[first : first + rows.shape[0], :]
        shared_ref[offset + first : offset + first + rows.shape[0], :] = rows.astype(shared_ref.dtype)

    tokens = tok_ref[...].astype(F32)
    inverse = lax.rsqrt(jnp.mean(tokens * tokens, axis=-1, keepdims=True) + epsilon)
    gain = gain_ref[...]
    scaled = tokens * inverse
    normed_t = (scaled * gain).astype(BF16).T
    normed_grad = part_ref[...] if which else jnp.zeros((length, width), F32)
    half = width // 2
    for matrix, w_ref in enumerate((wq_ref, wk_ref, wv_ref)):
        low = jnp.concatenate([low_ref[matrix, p] for p in range(PAIRS // 2)], axis=1)
        share(matrix * width, dot(normed_t, low))
        normed_grad = normed_grad + dot_t(low, w_ref[:, which * half : (which + 1) * half])
    if not which:
        if offset:
            shared_ref[:offset, :] = early_ref[...]
            done = offset + 3 * width
            if done < shared_ref.shape[0]:
                shared_ref[done:, :] = jnp.zeros((shared_ref.shape[0] - done, half), shared_ref.dtype)
        diag_out_ref[...] = diag_ref[...]
        part_out_ref[...] = normed_grad
        return
    gain_part = jnp.sum(normed_grad * scaled, axis=0, keepdims=True)
    bias_part = lax.dot_general(
        diag_ref[...], sel_ref[...], (((1,), (0,)), ((), ())), precision=lax.Precision.HIGHEST, preferred_element_type=F32
    )
    row = iota((8, half), 0)
    gains = jnp.where(row == 0, gain_part[:, :half], jnp.where(row == 1, gain_part[:, half:], 0.0))
    wide = jnp.concatenate([bias_part, jnp.zeros((16, half - bias_part.shape[1]), F32)], axis=1)
    left = shared_ref.shape[0] - 3 * width - 24
    last = [gains, wide] + ([jnp.zeros((left, half), F32)] if left else [])
    share(3 * width, jnp.concatenate(last, axis=0))
    upstream = normed_grad * gain
    middle = jnp.mean(upstream * scaled, axis=-1, keepdims=True)
    tgrad_ref[...] = (resgrad_ref[...] + inverse * (upstream - scaled * middle)).astype(BF16)


def attention_backward(batch, which, last, after, counts, qkv, lse, vector, selector, mixed_grad, tokens, gain, wq, wk, wv, past, more, rows):
    length, width = tokens.shape[2:]
    half = width // 2
    size = vector.shape[-1]
    late = (wq, wk, wv, *past, *(more[1:] if which else more))
    buffers = [((length, width), BF16)] + [(array.shape, array.dtype) for array in late]
    shared = jax.ShapeDtypeStruct((rows, half), BF16 if last else F32)
    if which:
        outs = [shared, jax.ShapeDtypeStruct((length, width), BF16)]
    else:
        outs = [shared, jax.ShapeDtypeStruct((16, size), F32), jax.ShapeDtypeStruct((length, width), F32)]
    return pl.pallas_call(
        functools.partial(attn_back_kernel, batch, which, len(after)),
        grid=(1,),
        in_specs=[ANYWHERE] * len(after)
        + [SCALARS]
        + [WHOLE] * 5
        + [ANYWHERE, WHOLE]
        + [ANYWHERE] * (3 + len(past))
        + [WHOLE if which and k == 0 else ANYWHERE for k in range(len(more))],
        out_specs=[WHOLE] * len(outs),
        out_shape=outs,
        scratch_shapes=[
            pltpu.VMEM((ROWS, size), F32),
            pltpu.VMEM((length, length), BF16),
            pltpu.VMEM((length, length), BF16),
            pltpu.VMEM((ROWS, size), F32),
            pltpu.VMEM((3, PAIRS // 2, length, PAIR), BF16),
            pltpu.VMEM((PAIR, length), F32),
            pltpu.VMEM((PAIR, length), F32),
            pltpu.VMEM((PAIR, length), F32),
            pltpu.VMEM((16, size), F32),
            *(pltpu.VMEM(shape, kind) for shape, kind in buffers),
            pltpu.SemaphoreType.DMA((len(buffers),)),
        ],
        compiler_params=params(56),
        cost_estimate=cost(),
    )(*after, counts, qkv, lse, vector, selector, mixed_grad, tokens, gain, wq, wk, wv, *past, *more)


def unpack_kernel(early, experts, side_ref, mine_ref, other_ref, *refs):
    mine, other = mine_ref[...], other_ref[...]
    second = side_ref[0] == 1
    rows = jnp.concatenate([jnp.where(second, other, mine), jnp.where(second, mine, other)], axis=0).astype(F32)
    half = rows.shape[1]
    width = 2 * half
    if not early:
        q_ref, k_ref, v_ref, gain_ref, bias_ref = refs[3:]
        offset = 0
        gain_ref[...] = jnp.concatenate([rows[3 * width : 3 * width + 1], rows[3 * width + 1 : 3 * width + 2]], axis=1)
        bias_ref[...] = rows[3 * width + 8 : 3 * width + 8 + HEADS, :BUCKETS].T
    else:
        q_ref, k_ref, v_ref, output_ref, router_ref, gain_ref = refs
        offset = 2 * early
        output_ref[...] = jnp.concatenate([rows[:width], rows[early : early + width]], axis=1)
        last = early - 16
        router_ref[...] = jnp.concatenate([rows[width:last], rows[early + width : early + last]], axis=1).T
        gain_ref[...] = jnp.concatenate([rows[last : last + 1], rows[early + last : early + last + 1]], axis=1)
    for k, ref in enumerate((q_ref, k_ref, v_ref)):
        ref[...] = rows[offset + k * width : offset + (k + 1) * width]


def unpack(early, experts, side, mine, other, past):
    half = mine.shape[1]
    width = 2 * half
    matrix = jax.ShapeDtypeStruct((width, width), F32)
    line = jax.ShapeDtypeStruct((1, width), F32)
    columns = pl.BlockSpec((width, half), lambda _: (0, 0 if early else 1))
    if early:
        more = [matrix, jax.ShapeDtypeStruct((width, experts), F32), line]
    else:
        more = [line, jax.ShapeDtypeStruct((BUCKETS, HEADS), F32)]
    return pl.pallas_call(
        functools.partial(unpack_kernel, early, experts),
        grid=(1,),
        in_specs=[SCALARS, WHOLE, WHOLE] + [ANYWHERE] * len(past),
        out_specs=[columns] * 3 + [WHOLE] * len(more),
        out_shape=[matrix] * 3 + more,
        input_output_aliases={3 + k: k for k in range(len(past))},
        compiler_params=params(56),
        cost_estimate=cost(),
    )(side, mine, other, *past)


def upward(planes, first, last):
    return [(k, k + 1) for k in range(first, last)]


def downward(planes, first, last):
    return [(planes - 1 - k, planes - 2 - k) for k in range(first, last)]


def mix_kernel(both, planes, step, waits, here_ref, up_ref, down_ref, upsum_ref, downsum_ref, *refs):
    to_up, to_down = refs[waits:]
    for moving, sums, out, place in (
        (up_ref, upsum_ref, to_up, here_ref[0]),
        (down_ref, downsum_ref, to_down, planes - 1 - here_ref[0]),
    ):
        total = moving[...] + sums[...]
        out[...] = jnp.where(place <= step, total, moving[...]) if both else total


def mix(both, planes, step, here, up, down, upsum, downsum, after):
    kinds, rows, width = up.shape
    block = pl.BlockSpec((1, rows // 2, width), lambda i, j: (i, j, 0))
    return pl.pallas_call(
        functools.partial(mix_kernel, both, planes, step, len(after)),
        grid=(kinds, 2),
        in_specs=[SCALARS] + [block] * 4 + [ANYWHERE] * len(after),
        out_specs=[block] * 2,
        out_shape=[jax.ShapeDtypeStruct(up.shape, BF16)] * 2,
        compiler_params=params(32),
        cost_estimate=cost(),
    )(here, up, down, upsum, downsum, *after)


def gate_kernel(*refs):
    pass


def gate(arrays, after):
    count = len(arrays)
    return pl.pallas_call(
        gate_kernel,
        in_specs=[ANYWHERE] * (count + len(after)),
        out_specs=[ANYWHERE] * count,
        out_shape=[jax.ShapeDtypeStruct(array.shape, array.dtype) for array in arrays],
        input_output_aliases={k: k for k in range(count)},
        cost_estimate=cost(),
    )(*arrays, *after)


class Chain:
    def __init__(self, planes, own=None, sums=None):
        self.planes, self.own, self.sums = planes, own, sums
        self.here = lax.axis_index("hidden")[None]
        self.from_below, self.from_above = [], []
        if own is not None:
            self.up = self.down = own
        else:
            self.up, self.down = sums[planes - 1], sums[1]
        self.count = 0
        self.steps = planes if own is not None and sums is not None else planes - 1

    def send(self):
        planes, s = self.planes, self.count
        if self.own is not None and self.sums is not None:
            first, last = 0, planes - 1
        elif self.own is not None:
            first, last = s, planes - 1
        else:
            first, last = 0, s + 1
        self.up = lax.ppermute(self.up, "hidden", upward(planes, first, last))
        self.down = lax.ppermute(self.down, "hidden", downward(planes, first, last))
        self.count += 1
        if self.own is not None and s < planes - 1:
            self.from_below.append(self.up)
            self.from_above.append(self.down)

    def mix(self, *after):
        planes, s = self.planes, self.count - 1
        both = self.own is not None
        offset = 1 if both else 2
        self.up, self.down = mix(
            both, planes, s, self.here, self.up, self.down, self.sums[planes - offset - s], self.sums[s + offset], after
        )
        self.mixed = self.up

    def gate(self, *after):
        self.up, self.down = gate((self.up, self.down), after)
        self.from_below[-1], self.from_above[-1] = self.up, self.down

    def run(self):
        while self.count < self.steps:
            self.send()
        return self

    def gathered(self):
        return (self.own, *self.from_above, *self.from_below)

    def scattered(self):
        return (self.sums[0], self.up, self.down)


def swap(values, axis, distance):
    return lax.ppermute(values, axis, [(k, k ^ distance) for k in range(lax.axis_size(axis))])


def share_sums(values, axis, near, count):
    me = lax.axis_index(axis) // near
    parts = values.reshape(count, values.shape[0] // count, values.shape[1])
    total = lax.dynamic_index_in_dim(parts, me, 0, keepdims=False).astype(F32)
    for k in range(1, count):
        part = lax.dynamic_index_in_dim(parts, me ^ k, 0, keepdims=False)
        total = total + swap(part, axis, k * near).astype(F32)
    return total.astype(BF16)


def join_sums(values, axis, near, count):
    me = lax.axis_index(axis) // near
    found = [values] + [swap(values, axis, k * near) for k in range(1, count)]
    joined = []
    for j in range(count):
        piece = found[count - 1]
        for k in range(count - 2, -1, -1):
            piece = jnp.where(me ^ k == j, found[k], piece)
        joined.append(piece)
    return jnp.concatenate(joined)


def sum_everywhere(values):
    size = lax.axis_size("expert")
    planes = lax.axis_size("hidden")
    values = share_sums(values, "expert", 2, size // 2)
    values = share_sums(values, "hidden", 1, planes)
    values = join_sums(values, "hidden", 1, planes)
    values = join_sums(values, "expert", 2, size // 2)
    return values, swap(values, "expert", 1)


def share_half(values):
    side = lax.axis_index("expert") % 2
    parts = values.reshape(2, values.shape[0] // 2, values.shape[1])
    mine = lax.dynamic_index_in_dim(parts, side, 0, keepdims=False)
    other = lax.dynamic_index_in_dim(parts, 1 - side, 0, keepdims=False)
    return mine + swap(other, "expert", 1)


def offset_selector(length):
    place = np.arange(2 * length)
    offsets = np.where(place < 2 * length - ROWS, place, place - 2 * length) - (length - ROWS)
    offsets = np.clip(offsets, -(length - 1), length - 1)
    return (offset_bucket(offsets)[:, None] == np.arange(BUCKETS)[None, :]).astype(np.float32)


def moves(groups, local, capacity, message, kinds=1):
    kind, expert, group, slot = np.meshgrid(
        np.arange(kinds), np.arange(local), np.arange(groups), np.arange(capacity), indexing="ij"
    )
    source = (group * message + (kind * local + expert) * capacity + slot).reshape(-1)
    return (source[:, None] == np.arange(groups * message)[None, :]).astype(jnp.bfloat16)


def shards(
    tokens,
    cotangent,
    lengths,
    routes,
    gain_attn,
    w_query,
    w_key,
    w_value,
    w_output,
    bucket_head_bias,
    gain_ffn,
    w_router,
    w_inner,
    w_outer,
):
    batches, _, length, width = tokens.shape
    experts = w_router.shape[1]
    local = w_inner.shape[0]
    groups = lax.axis_size("expert")
    planes = lax.axis_size("hidden")
    capacity = (5 * length + 4 * experts - 1) // (4 * experts)
    per = local * capacity
    rows = groups * capacity
    message = padded(per)
    move = jnp.asarray(moves(groups, local, capacity, message))
    move_gated = jnp.asarray(moves(groups, local, capacity, message + 16))
    move_pair = jnp.asarray(moves(groups, local // 2, capacity, message, 2))
    move_back = jnp.asarray(moves(groups, local // 2, capacity, message, 2).T)
    selector = jnp.asarray(offset_selector(length))
    vector = lax.dot_general(
        bucket_head_bias, selector, (((0,), (1,)), ((), ())), precision=lax.Precision.HIGHEST
    )[:, None, :]
    gain_a = gain_attn[None, :]
    gain_f = gain_ffn[None, :]
    counts = lengths[:, 0]
    plane = lax.axis_index("hidden")[None]

    def to_groups(values):
        return lax.all_to_all(values, "expert", split_axis=0, concat_axis=0, tiled=True)

    def leaving(values, *after):
        return regroup(move_pair, [to_groups(values)], (2, local // 2 * rows, width), after)

    def arriving(chain, *after):
        return to_groups(regroup(move_back, chain.scattered(), (groups, message, width), after))

    def attend(b, *after):
        return attention_forward(b, after, counts, tokens, gain_a, w_query, w_key, w_value, vector)

    def routing(b, *after):
        return route(
            b, after, tokens, cotangent, forward[b][1], w_output, gain_f, w_router, srow, rcol, groups, per, b > 0
        )

    srow, scol, cot_slots = prep(counts, routes.reshape(batches, length), cotangent, groups, per, capacity)
    rcol = routes.reshape(batches, length, 1)
    early_rows = width + experts + 16
    unit = 16 * groups * planes
    first_rows = 2 * early_rows + 3 * width
    first_rows = first_rows + -first_rows % unit
    second_rows = 3 * width + 24
    second_rows = second_rows + -second_rows % unit
    kept, layer_rows, token_grads = [], [], []
    early_part, first_part, second_part = (), (), ()

    def back_tokens(b, after, low, high):
        return combine(
            b,
            b + 1 == batches,
            after,
            counts,
            low,
            high,
            scol,
            rcol,
            *routed[b][:2],
            cotangent,
            gain_f,
            w_router,
            w_output,
            forward[b][1],
            early_part,
            per,
            2 * early_rows,
        )

    def back_half(b, which, after, mixed_grad, more):
        qkv, _, lse = forward[b]
        last = b + 1 == batches
        return attention_backward(
            b,
            which,
            last,
            after,
            counts,
            qkv,
            lse,
            vector,
            selector,
            mixed_grad,
            tokens,
            gain_a,
            w_query,
            w_key,
            w_value,
            second_part if which else first_part,
            more,
            second_rows if which else first_rows if last else 3 * width,
        )

    def grads_half(h, after, past):
        return expert_grads(h, after, past, local, *([k[h][part] for k in kept] for part in (2, 3, 0, 1)))

    grads = regroup(move, [to_groups(cot_slots)], (local * rows, width))
    grad_chain = Chain(planes, grads)
    grad_chain.send()
    forward = [attend(0, grads)]
    routed = [routing(0, grad_chain.up, grad_chain.down)]
    grad_chain.send()
    inputs = regroup_gated(move_gated, to_groups(routed[0][2]), capacity)
    grad_chain.gate(inputs)
    grad_chain.run()
    input_chain = Chain(planes, inputs)
    input_chain.send()
    forward.append(attend(1, inputs))
    routed.append(routing(1))
    input_chain.gate(forward[1][1])
    input_chain.send()
    held = (input_chain.up, input_chain.down, grad_chain.up, grad_chain.down)
    input_chain.run()
    halves = range(2)
    chains = [None, None]
    for b in range(batches):
        last = b + 1 == batches
        before = chains
        messages = [None, None]
        ready = ()
        if not last:
            if b:
                forward.append(attend(b + 1))
                routed.append(routing(b + 1))
            messages = [leaving(m, *held) for m in routed[b + 1][2:]]
            held = ()
            ready = tuple(messages)
        chains, worked = [], []
        for h in halves:
            if b == 0:
                done = experts_half(
                    h, ready, plane, None, w_inner, w_outer, input_chain.gathered(), grad_chain.gathered()
                )
            else:
                before[h].mix(*(w[0] for w in worked))
                tied = (before[h].up, before[h].down)
                if h:
                    tied += (before[0].up, before[0].down)
                done = experts_half(h, ready + tied, plane, before[h].gathered(), w_inner, w_outer)
                before[h].send()
            worked.append(done)
            chains.append(Chain(planes, messages[h], done[:planes]))
            chains[h].send()
        kept.append([w[planes:] for w in worked])
        low_chain, high_chain = chains
        if not last:
            for step in range(1, planes):
                for chain in chains:
                    if step > 1:
                        chain.send()
                    if step < planes - 1:
                        chain.mix()
            if b == 0:
                continue
            low, high = (arriving(chain) for chain in before)
            layer, res_grad, mixed_grad, early_part = back_tokens(b - 1, (), low, high)
            first_part, *more = back_half(b - 1, 0, (), mixed_grad, (early_part,) if b > 1 else ())
            second_part, token_grad = back_half(b - 1, 1, (), mixed_grad, (*more, res_grad))
        else:
            low = arriving(before[0], before[1].up, before[1].down)
            high = arriving(before[1])
            low_chain.mix()
            low_chain.send()
            totals = grads_half(0, (low_chain.mixed,), ())
            high_chain.mix(totals[0])
            high_chain.send()
            low_chain.mix(high)
            low_chain.send()
            layer, res_grad, mixed_grad, early_part = back_tokens(b - 1, (low_chain.mixed,), low, high)
            high_chain.mix(mixed_grad)
            high_chain.send()
            first_part, *more = back_half(
                b - 1, 0, (high_chain.mixed,), mixed_grad, (early_part,) if b > 1 else ()
            )
            low = regroup(move_back, low_chain.scattered(), (groups, message, width), (first_part,))
            second_part, token_grad = back_half(b - 1, 1, (low,), mixed_grad, (*more, res_grad))
            low = to_groups(low)
            high = regroup(move_back, high_chain.scattered(), (groups, message, width), (second_part, low))
            totals = grads_half(1, (high,), totals)
            high = to_groups(high)
        layer_rows.append(layer)
        token_grads.append(token_grad)
        early_part, first_part, second_part = (early_part,), (first_part,), (second_part,)
    layer, res_grad, mixed_grad, early_part = back_tokens(batches - 1, (totals[0],), low, high)
    first_part, *more = back_half(batches - 1, 0, (), mixed_grad, (early_part,))
    side = (lax.axis_index("expert") % 2)[None]
    first_half = share_half(first_part)
    second_part, token_grad = back_half(batches - 1, 1, (first_half,), mixed_grad, (*more, res_grad))
    first_sums = sum_everywhere(first_half)
    second_sums = sum_everywhere(share_half(second_part))
    layer_rows.append(layer)
    token_grads.append(token_grad)
    *attended, output_grad, router_grad, gain_f_grad = unpack(early_rows, experts, side, *first_sums, ())
    query_grad, key_grad, value_grad, gain_a_grad, bias_grad = unpack(0, experts, side, *second_sums, attended)
    return (
        jnp.stack(layer_rows)[:, None],
        jnp.stack(token_grads)[:, None],
        gain_a_grad[0],
        query_grad,
        key_grad,
        value_grad,
        output_grad,
        bias_grad,
        gain_f_grad[0],
        router_grad,
        totals[1],
        totals[0],
    )


def solution(mesh):
    token = P(None, ("expert", "hidden"), None, None)
    placed = (
        token,
        token,
        P(None, ("expert", "hidden")),
        token,
        *(P() for _ in range(8)),
        P("expert", None, "hidden"),
        P("expert", "hidden", None),
    )
    return jax.shard_map(
        shards,
        mesh=mesh,
        in_specs=placed,
        out_specs=(
            token,
            token,
            *(P() for _ in range(8)),
            P("expert", None, "hidden"),
            P("expert", "hidden", None),
        ),
        check_vma=False,
    )
```

```python
import functools

import jax
import jax.numpy as jnp
import numpy as np
from jax import lax
from jax.experimental import pallas as pl
from jax.experimental.pallas import tpu as pltpu
from jax.sharding import PartitionSpec as P

HEADS = 12
HEAD_DIM = 64
BUCKETS = 32
MAXDIST = 128
PAIR = 2 * HEAD_DIM
PAIRS = HEADS // 2
ROWS = 128

epsilon = 1e-06
negative = -1e30
F32 = jnp.float32
BF16 = jnp.bfloat16
MIB = 1 << 20


def params(mib):
    return pltpu.CompilerParams(vmem_limit_bytes=mib * MIB)


def cost():
    return pl.CostEstimate(flops=1, bytes_accessed=1, transcendentals=0)


def offset_bucket(offsets):
    halfway = BUCKETS // 2
    exact_count = halfway // 2
    relative_distance = np.abs(offsets)
    scaled = (
        np.log(np.maximum(relative_distance, 1) / exact_count)
        / np.log(MAXDIST / exact_count)
        * (halfway - exact_count)
    )
    far_bucket = np.minimum(exact_count + np.floor(scaled).astype(np.int64), halfway - 1)
    near_bucket = np.where(relative_distance < exact_count, relative_distance, far_bucket)
    return (np.where(offsets > 0, halfway, 0) + near_bucket).astype(np.int32)


def dot(a, b):
    return lax.dot_general(a, b, (((1,), (0,)), ((), ())), preferred_element_type=F32)


def dot_t(a, b):
    return lax.dot_general(a, b, (((1,), (1,)), ((), ())), preferred_element_type=F32)


def t_dot(a, b):
    return lax.dot_general(a, b, (((0,), (0,)), ((), ())), preferred_element_type=F32)


def one_hot(condition):
    return jnp.where(condition, 1.0, 0.0).astype(BF16)


def batch_block(array, b):
    rest = array.shape[1:]
    return pl.BlockSpec((1,) + rest, lambda *_: (b,) + (0,) * len(rest))


ANYWHERE = pl.BlockSpec(memory_space=pl.ANY)
WHOLE = pl.BlockSpec(memory_space=pltpu.VMEM)
SCALARS = pl.BlockSpec(memory_space=pltpu.SMEM)


def iota(shape, axis):
    return lax.broadcasted_iota(jnp.int32, shape, axis)


def padded(rows):
    return -(-rows // 16) * 16


def spread_slots(slot, per, message, first=0, last=None):
    last = per if last is None else last
    group = lax.div(jnp.maximum(slot, 0), per)
    inside = slot - group * per
    held = (slot >= 0) & (inside >= first) & (inside < last)
    return jnp.where(held, group * message + inside - first, -1)


def prep_kernel(per, capacity, len_ref, row_ref, col_ref, cot_ref, srow_ref, scol_ref, slots_ref):
    batches, _, length = row_ref.shape
    groups, message, width = slots_ref.shape
    experts = groups * per // capacity
    before = one_hot(iota((length, length), 0) < iota((length, length), 1))
    after = one_hot(iota((length, length), 1) < iota((length, length), 0))
    for b in range(batches):
        count = len_ref[b]
        row = row_ref[b]
        col = col_ref[b]
        valid_row = iota((1, length), 1) < count
        valid_col = iota((length, 1), 0) < count
        chosen_row = iota((experts, length), 0) == row
        chosen_col = iota((length, experts), 1) == col
        earlier_row = dot(one_hot(chosen_row & valid_row), before)
        rank_row = jnp.sum(jnp.where(chosen_row, earlier_row, 0.0), axis=0, keepdims=True).astype(jnp.int32)
        earlier_col = dot(after, one_hot(chosen_col & valid_col))
        rank_col = jnp.sum(jnp.where(chosen_col, earlier_col, 0.0), axis=1, keepdims=True).astype(jnp.int32)
        slot_row = jnp.where(valid_row & (rank_row < capacity), row * capacity + rank_row, -1)
        srow_ref[b] = slot_row
        scol_ref[b] = jnp.where(valid_col & (rank_col < capacity), col * capacity + rank_col, -1)
        if b == 0:
            dispatch = one_hot(iota((groups * message, length), 0) == spread_slots(slot_row, per, message))
            slots_ref[...] = dot(dispatch, cot_ref[0, 0]).astype(BF16).reshape(groups, message, width)


def prep(lengths, routes, cot, groups, per, capacity):
    batches, length = routes.shape
    width = cot.shape[-1]
    vmem = WHOLE
    message = padded(per)
    return pl.pallas_call(
        functools.partial(prep_kernel, per, capacity),
        grid=(1,),
        in_specs=[SCALARS, vmem, vmem, batch_block(cot, 0)],
        out_specs=[vmem] * 3,
        out_shape=[
            jax.ShapeDtypeStruct((batches, 1, length), jnp.int32),
            jax.ShapeDtypeStruct((batches, length, 1), jnp.int32),
            jax.ShapeDtypeStruct((groups, message, width), BF16),
        ],
        compiler_params=params(32),
        cost_estimate=cost(),
    )(lengths, routes.reshape(batches, 1, length), routes.reshape(batches, length, 1), cot)


def regroup_kernel(count, inputs, waits, *refs):
    refs = refs[waits:]
    move_ref, out_ref = refs[0], refs[-1]
    total = refs[1][...].astype(F32)
    for ref in refs[2 : 1 + count]:
        total = total + ref[...].astype(F32)
    out_ref[...] = dot(move_ref[...], total.astype(BF16).reshape(inputs, -1)).astype(BF16).reshape(out_ref.shape)


def regroup(move, arrays, shape, after=()):
    inputs = move.shape[1]
    vmem = pl.BlockSpec(memory_space=pltpu.VMEM)
    return pl.pallas_call(
        functools.partial(regroup_kernel, len(arrays), inputs, len(after)),
        in_specs=[ANYWHERE] * len(after) + [vmem] * (1 + len(arrays)),
        out_specs=vmem,
        out_shape=jax.ShapeDtypeStruct(shape, BF16),
        compiler_params=params(32),
        cost_estimate=cost(),
    )(*after, move, *arrays)


def regroup_gated_kernel(capacity, *refs):
    move_ref, in_ref, out_ref = refs[-3:]
    groups, message, width = in_ref.shape
    total = move_ref.shape[0]
    local = total // (groups * capacity)
    rows = groups * capacity
    flat = in_ref[...].reshape(groups * message, width)
    out_ref[:total, :] = dot(move_ref[...], flat).astype(BF16)
    place = iota((message, 128), 0)
    lane = iota((message, 128), 1)
    columns = []
    for g in range(groups):
        gates = in_ref[g, message - 16 : message, :].astype(F32)[0:1, :]
        parts = [
            jnp.sum(jnp.where(place == lane, gates[:, 128 * k : 128 * (k + 1)], 0.0), axis=1, keepdims=True)
            for k in range(3)
        ]
        wide = iota((message, 128), 1)
        columns.append(jnp.where(wide == 0, parts[0], jnp.where(wide == 1, parts[1], jnp.where(wide == 2, parts[2], 0.0))))
    column = jnp.concatenate(columns, axis=0).astype(BF16)
    moved = dot(move_ref[...], column)
    place = iota((rows, 128), 0)
    lane = iota((rows, 128), 1)
    lines = []
    for l in range(local):
        mine = moved[l * rows : (l + 1) * rows, :]
        parts = [
            jnp.sum(jnp.where(place == lane, mine[:, k : k + 1], 0.0), axis=0, keepdims=True) for k in range(3)
        ]
        lines.append(jnp.concatenate(parts + [jnp.zeros((1, width - 384), F32)], axis=1))
    lines.append(jnp.zeros((16 - local, width), F32))
    out_ref[total:, :] = jnp.concatenate(lines, axis=0).astype(BF16)


def regroup_gated(move, slots, capacity, after=()):
    width = slots.shape[-1]
    vmem = pl.BlockSpec(memory_space=pltpu.VMEM)
    return pl.pallas_call(
        functools.partial(regroup_gated_kernel, capacity),
        in_specs=[ANYWHERE] * len(after) + [vmem] * 2,
        out_specs=vmem,
        out_shape=jax.ShapeDtypeStruct((move.shape[0] + 16, width), BF16),
        compiler_params=params(32),
        cost_estimate=cost(),
    )(*after, move, slots)


def band_bias(vector_ref, head):
    wide = jnp.broadcast_to(vector_ref[head], (ROWS, vector_ref.shape[-1]))
    return pltpu.roll(wide, 0, 1, stride=1, stride_axis=0)


def band_slice(block, length):
    start = length - ROWS * (block + 1)
    return slice(start, start + length)


def attn_kernel(batch, waits, *refs):
    refs = refs[waits:]
    len_ref, tok_ref, gain_ref, wq_ref, wk_ref, wv_ref, vec_ref, qkv_ref, mixed_ref, lse_ref, bands_ref, probs_ref, mixed_t_ref = refs
    length, width = tok_ref.shape[2:]
    count = len_ref[batch]
    tokens = tok_ref[0, 0].astype(F32)
    inverse = lax.rsqrt(jnp.mean(tokens * tokens, axis=-1, keepdims=True) + epsilon)
    normed = (tokens * inverse * gain_ref[...]).astype(BF16)
    for which, w_ref in enumerate((wq_ref, wk_ref, wv_ref)):
        for part in range(width // 256):
            rows = dot(normed, w_ref[:, 256 * part : 256 * part + 256]).astype(BF16)
            qkv_ref[which, 2 * part] = rows[:, :PAIR]
            qkv_ref[which, 2 * part + 1] = rows[:, PAIR:]
    mask = jnp.where(iota((1, length), 1) < count, 0.0, negative)
    lane = iota((ROWS, PAIR), 1)
    lse_ref[...] = jnp.zeros_like(lse_ref)

    def one_pair(pair, carry):
        keys = qkv_ref[1, pair]
        values_t = qkv_ref[2, pair].T
        for side in range(2):
            head = 2 * pair + side
            bands_ref[side] = band_bias(vec_ref, head)
            mine = (lane >= HEAD_DIM) if side else (lane < HEAD_DIM)
            for block in range(length // ROWS):
                here = slice(ROWS * block, ROWS * (block + 1))
                queries = qkv_ref[0, pair, here, :] * 0.125
                queries = jnp.where(mine, queries, jnp.zeros_like(queries))
                scores = dot_t(queries, keys) + bands_ref[side, :, band_slice(block, length)] + mask
                highest = jnp.max(scores, axis=-1, keepdims=True)
                powers = jnp.exp(scores - highest)
                total = jnp.sum(powers, axis=-1, keepdims=True)
                probs_ref[side, here, :] = (powers * (1.0 / total)).astype(BF16)
                column = iota((ROWS, lse_ref.shape[1]), 1)
                lse_ref[here, :] = jnp.where(column == head, highest + jnp.log(total), lse_ref[here, :])
            rows = slice(HEAD_DIM * side, HEAD_DIM * (side + 1))
            mixed_t_ref[rows, :] = dot_t(values_t[rows, :], probs_ref[side])
        mixed_ref[pair] = mixed_t_ref[...].T.astype(BF16)
        return carry

    lax.fori_loop(0, PAIRS, one_pair, 0)


def attention_forward(batch, after, counts, tokens, gain, wq, wk, wv, vector):
    length = tokens.shape[2]
    return pl.pallas_call(
        functools.partial(attn_kernel, batch, len(after)),
        grid=(1,),
        in_specs=[ANYWHERE] * len(after) + [SCALARS, batch_block(tokens, batch)] + [WHOLE] * 5,
        out_specs=[WHOLE] * 3,
        out_shape=[
            jax.ShapeDtypeStruct((3, PAIRS, length, PAIR), BF16),
            jax.ShapeDtypeStruct((PAIRS, length, PAIR), BF16),
            jax.ShapeDtypeStruct((length, 128), F32),
        ],
        scratch_shapes=[
            pltpu.VMEM((2, ROWS, vector.shape[-1]), F32),
            pltpu.VMEM((2, length, length), BF16),
            pltpu.VMEM((PAIR, length), F32),
        ],
        compiler_params=params(48),
        cost_estimate=cost(),
    )(*after, counts, tokens, gain, wq, wk, wv, vector)


def route_kernel(per, gated, waits, *refs):
    refs = refs[waits:]
    tok_ref, cot_ref, mixed_ref, wo_ref, gffn_ref, wr_ref, srow_ref, rcol_ref, res_ref, probs_ref, *out_refs = refs
    length, width = tok_ref.shape[2:]
    mixed_all = jnp.concatenate([mixed_ref[p] for p in range(PAIRS)], axis=1)
    residual = tok_ref[0, 0].astype(F32) + dot(mixed_all, wo_ref[...])
    res_ref[...] = residual
    inverse = lax.rsqrt(jnp.mean(residual * residual, axis=-1, keepdims=True) + epsilon)
    routed = (residual * inverse * gffn_ref[...]).astype(BF16)
    logits = dot_t(routed, wr_ref[...])
    powers = jnp.exp(logits - jnp.max(logits, axis=-1, keepdims=True))
    probs = powers / jnp.sum(powers, axis=-1, keepdims=True)
    probs_ref[...] = probs
    gate = jnp.sum(jnp.where(iota(probs.shape, 1) == rcol_ref[0], probs, 0.0), axis=-1, keepdims=True)
    groups, message, _ = out_refs[0].shape
    places = iota((groups * message, length), 0)
    if gated:
        grads = (gate * cot_ref[0, 0].astype(F32)).astype(BF16)
        half = per // 2
        for which, out_ref in enumerate(out_refs):
            place = spread_slots(srow_ref[0], per, message, which * half, (which + 1) * half)
            rows = dot(one_hot(places == place), grads)
            rows = rows + dot(one_hot(places == jnp.where(place < 0, -1, place + half)), routed)
            out_ref[...] = rows.astype(BF16).reshape(out_ref.shape)
        return
    slots_ref = out_refs[0]
    dispatch = one_hot(places == spread_slots(srow_ref[0], per, message))
    slots_ref[...] = dot(dispatch, routed).astype(BF16).reshape(slots_ref.shape)
    first = gate.astype(BF16).astype(F32)
    second = (gate - first).astype(BF16).astype(F32)
    third = gate - first - second
    column = iota((length, PAIR), 1)
    pieces = jnp.where(column == 0, first, jnp.where(column == 1, second, jnp.where(column == 2, third, 0.0)))
    sorted_gates = dot(dispatch, pieces.astype(BF16))
    data = message - 16
    place = iota((data, 128), 0)
    lane = iota((data, 128), 1)
    for g in range(groups):
        mine = sorted_gates[g * message : g * message + data, :]
        parts = [
            jnp.sum(jnp.where(place == lane, mine[:, k : k + 1], 0.0), axis=0, keepdims=True) for k in range(3)
        ]
        line = jnp.concatenate(parts + [jnp.zeros((1, width - 384), F32)], axis=1)
        slots_ref[g, data:message, :] = jnp.broadcast_to(line, (16, width)).astype(BF16)


def route(batch, after, tokens, cot, mixed, wo, gain_ffn, w_router, srow, rcol, groups, per, gated):
    length, width = tokens.shape[2:]
    experts = w_router.shape[0]
    message = padded(per) if gated else padded(per) + 16
    return pl.pallas_call(
        functools.partial(route_kernel, per, gated, len(after)),
        grid=(1,),
        in_specs=[ANYWHERE] * len(after)
        + [batch_block(tokens, batch), batch_block(cot, batch)]
        + [WHOLE] * 4
        + [batch_block(srow, batch), batch_block(rcol, batch)],
        out_specs=[WHOLE] * (4 if gated else 3),
        out_shape=[
            jax.ShapeDtypeStruct((length, width), F32),
            jax.ShapeDtypeStruct((length, experts), F32),
        ]
        + [jax.ShapeDtypeStruct((groups, message, width), BF16)] * (2 if gated else 1),
        compiler_params=params(48),
        cost_estimate=cost(),
    )(*after, tokens, cot, mixed, wo, gain_ffn, w_router, srow, rcol)


GELU_SCALE = 0.7978845608028654
GELU_CUBIC = 0.044715


def expert_kernel(planes, gated, first_expert, waits, *refs):
    pieces = 2 * planes - 1
    refs = refs[waits:]
    plane = refs[0][0]
    x_refs, refs = refs[1 : 1 + pieces], refs[1 + pieces :]
    c_refs, refs = refs[:pieces], refs[pieces:]
    gate_refs = ()
    if not gated:
        gate_refs, refs = refs[:pieces], refs[pieces:]
    wi_ref, wo_ref, *refs = refs
    sum_refs = refs[:planes]
    act_ref, pre_ref, x_ref, c_ref = refs[planes:]
    rows = x_refs[0].shape[0]

    def assemble(parts):
        found = [parts[0][...]]
        for k in range(1, planes):
            from_above = plane + k < planes
            found.append(jnp.where(from_above, parts[k][...], parts[2 * planes - 1 - k][...]))
        return found

    inputs = jnp.concatenate(assemble(x_refs), axis=0)
    grads = assemble(c_refs)
    if not gated:
        place = iota((rows, 128), 0)
        lane = iota((rows, 128), 1)
        expert = first_expert + pl.program_id(0)
        for k, lines in enumerate(assemble(gate_refs)):
            lines = jnp.where(iota(lines.shape, 0) == expert, lines.astype(F32), 0.0)
            line = jnp.sum(lines, axis=0, keepdims=True)
            line = line[:, :128] + line[:, 128:256] + line[:, 256:384]
            gate = jnp.sum(jnp.where(place == lane, line, 0.0), axis=1, keepdims=True)
            grads[k] = (grads[k].astype(F32) * gate).astype(BF16)
    grads = jnp.concatenate(grads, axis=0)
    x_ref[0] = inputs
    c_ref[0] = grads
    pre = dot(inputs, wi_ref[0])
    square = pre * pre
    curve = jnp.tanh(GELU_SCALE * pre * (1.0 + GELU_CUBIC * square))
    half = 0.5 * (1.0 + curve)
    act = (pre * half).astype(BF16)
    slope = half + 0.5 * pre * (1.0 - curve * curve) * (GELU_SCALE * (1.0 + 3.0 * GELU_CUBIC * square))
    act_ref[0] = act
    outs = dot(act, wo_ref[0]).astype(BF16)
    pre_grad = (slope * dot_t(grads, wo_ref[0])).astype(BF16)
    pre_ref[0] = pre_grad
    ins = dot_t(pre_grad, wi_ref[0]).astype(BF16)
    for k in range(planes):
        sum_refs[k][0] = outs[k * rows : (k + 1) * rows]
        sum_refs[k][1] = ins[k * rows : (k + 1) * rows]


def experts_half(which, after, plane, messages, w_inner, w_outer, xs=None, cs=None):
    local, width, hidden = w_inner.shape
    mine = local // 2
    first = which * mine
    gated = messages is not None
    pieces = len(messages if gated else xs)
    planes = (pieces + 1) // 2
    if gated:
        rows = messages[0].shape[1] // mine
        x_block = pl.BlockSpec((None, rows, width), lambda e: (1, e, 0))
        c_block = pl.BlockSpec((None, rows, width), lambda e: (0, e, 0))
        arrays = (*messages, *messages)
        blocks = [x_block] * pieces + [c_block] * pieces
    else:
        rows = cs[0].shape[0] // local
        slab = pl.BlockSpec((rows, width), lambda e: (first + e, 0))
        lines = pl.BlockSpec((16, width), lambda e: (local * rows // 16, 0))
        arrays = (*xs, *cs, *xs)
        blocks = [slab] * (2 * pieces) + [lines] * pieces
    weight = lambda a, b: pl.BlockSpec((1, a, b), lambda e: (first + e, 0, 0))
    mat = lambda a, b: pl.BlockSpec((1, a, b), lambda e: (e, 0, 0))
    total = planes * rows
    kept = lambda n: jax.ShapeDtypeStruct((mine, total, n), BF16)
    return pl.pallas_call(
        functools.partial(expert_kernel, planes, gated, first, len(after)),
        grid=(mine,),
        in_specs=[ANYWHERE] * len(after) + [SCALARS] + blocks + [weight(width, hidden), weight(hidden, width)],
        out_specs=[pl.BlockSpec((2, rows, width), lambda e: (0, e, 0))] * planes
        + [mat(total, hidden), mat(total, hidden), mat(total, width), mat(total, width)],
        out_shape=[jax.ShapeDtypeStruct((2, mine * rows, width), BF16)] * planes
        + [kept(hidden), kept(hidden), kept(width), kept(width)],
        compiler_params=params(48),
        cost_estimate=cost(),
    )(*after, plane, *arrays, w_inner, w_outer)


def expert_grad_kernel(batches, waits, *refs):
    xs, cs, acts, pres = (refs[waits + k * batches : waits + (k + 1) * batches] for k in range(4))
    outer_ref, inner_ref = refs[-2:]
    whole = lambda refs: jnp.concatenate([ref[0] for ref in refs], axis=0)
    outer_ref[0] = t_dot(whole(acts), whole(cs))
    inner_ref[0] = t_dot(whole(xs), whole(pres))


def expert_grads(which, after, past, local, xs, cs, acts, pres):
    batches = len(xs)
    mine, total, width = xs[0].shape
    hidden = acts[0].shape[2]
    first = which * mine
    mat = lambda a, b: pl.BlockSpec((1, a, b), lambda e: (e, 0, 0))
    out = lambda a, b: pl.BlockSpec((1, a, b), lambda e: (first + e, 0, 0))
    behind = len(after) + 4 * batches
    return pl.pallas_call(
        functools.partial(expert_grad_kernel, batches, len(after)),
        grid=(mine,),
        in_specs=[ANYWHERE] * len(after)
        + [mat(total, width)] * (2 * batches)
        + [mat(total, hidden)] * (2 * batches)
        + [ANYWHERE] * len(past),
        out_specs=[out(hidden, width), out(width, hidden)],
        out_shape=[
            jax.ShapeDtypeStruct((local, hidden, width), F32),
            jax.ShapeDtypeStruct((local, width, hidden), F32),
        ],
        input_output_aliases={behind + k: k for k in range(len(past))},
        compiler_params=params(48),
        cost_estimate=cost(),
    )(*after, *xs, *cs, *acts, *pres, *past)


def combine_kernel(per, batch, waits, *refs):
    refs = refs[waits:]
    len_ref, low_ref, high_ref, scol_ref, rcol_ref, res_ref, probs_ref, cot_ref, gffn_ref, wr_ref, wo_ref, mixed_ref, *refs = refs
    past_ref = refs.pop(0) if batch else None
    layer_ref, resgrad_ref, mgrad_ref, shared_ref = refs
    length, width = cot_ref.shape[2:]
    experts = wr_ref.shape[0]
    groups, message, _ = low_ref.shape
    valid = iota((length, 1), 0) < len_ref[batch]
    places = iota((length, groups * message), 1)
    half = per // 2
    returned = input_grad = None
    for which, ref in enumerate((low_ref, high_ref)):
        place = spread_slots(scol_ref[0], per, message, which * half, (which + 1) * half)
        rows = ref[...].reshape(groups * message, width)
        out_part = dot(one_hot(places == place), rows)
        in_part = dot(one_hot(places == jnp.where(place < 0, -1, place + half)), rows)
        returned = out_part if returned is None else returned + out_part
        input_grad = in_part if input_grad is None else input_grad + in_part
    residual = res_ref[...]
    probs = probs_ref[...]
    chosen = iota(probs.shape, 1) == rcol_ref[0]
    gate = jnp.sum(jnp.where(chosen, probs, 0.0), axis=-1, keepdims=True)
    layer_ref[...] = jnp.where(valid, residual + gate * returned, 0.0).astype(BF16)
    out_grad = jnp.where(valid, cot_ref[0, 0].astype(F32), 0.0)
    gate_grad = jnp.sum(out_grad * returned, axis=-1, keepdims=True)
    prob_grad = jnp.where(chosen, gate_grad, 0.0)
    logit_grad = (probs * (prob_grad - jnp.sum(probs * prob_grad, axis=-1, keepdims=True))).astype(BF16)
    inverse = lax.rsqrt(jnp.mean(residual * residual, axis=-1, keepdims=True) + epsilon)
    gain = gffn_ref[...]
    scaled = residual * inverse
    routed = (scaled * gain).astype(BF16)

    def share(first, whole_rows):
        for side in range(2):
            rows = whole_rows[:, side * width // 2 : (side + 1) * width // 2]
            here = slice(side * shared_ref.shape[0] // 2 + first, side * shared_ref.shape[0] // 2 + first + rows.shape[0])
            if past_ref is not None:
                rows = rows + past_ref[here, :]
            shared_ref[here, :] = rows.astype(shared_ref.dtype)

    share(width, t_dot(logit_grad, routed))
    routed_grad = dot(logit_grad, wr_ref[...]) + input_grad
    gain_part = jnp.sum(routed_grad * scaled, axis=0, keepdims=True)
    left = shared_ref.shape[0] // 2 - width - experts
    share(width + experts, jnp.where(iota((left, width), 0) == 0, gain_part, 0.0))
    upstream = routed_grad * gain
    middle = jnp.mean(upstream * scaled, axis=-1, keepdims=True)
    residual_grad = out_grad + inverse * (upstream - scaled * middle)
    resgrad_ref[...] = residual_grad
    attended = residual_grad.astype(BF16)
    mixed_all = jnp.concatenate([mixed_ref[p] for p in range(PAIRS)], axis=1)
    share(0, t_dot(mixed_all, attended))
    mixed_grad = dot_t(attended, wo_ref[...]).astype(BF16)
    for pair in range(PAIRS):
        mgrad_ref[pair] = mixed_grad[:, pair * PAIR : (pair + 1) * PAIR]


def combine(
    batch, last, after, counts, low, high, scol, rcol, residual, probs, cot, gain_ffn, w_router, w_output, mixed, past, per, shared
):
    length, width = cot.shape[2:]
    return pl.pallas_call(
        functools.partial(combine_kernel, per, batch, len(after)),
        grid=(1,),
        in_specs=[ANYWHERE] * len(after)
        + [SCALARS, WHOLE, WHOLE, batch_block(scol, batch), batch_block(rcol, batch), WHOLE, WHOLE, batch_block(cot, batch)]
        + [WHOLE] * (4 + len(past)),
        out_specs=[WHOLE] * 4,
        out_shape=[
            jax.ShapeDtypeStruct((length, width), BF16),
            jax.ShapeDtypeStruct((length, width), F32),
            jax.ShapeDtypeStruct((PAIRS, length, PAIR), BF16),
            jax.ShapeDtypeStruct((shared, width // 2), BF16 if last else F32),
        ],
        compiler_params=params(48),
        cost_estimate=cost(),
    )(
        *after, counts, low, high, scol, rcol, residual, probs, cot, gain_ffn, w_router, w_output, mixed, *past
    )


def attn_back_kernel(batch, which, waits, *refs):
    refs = refs[waits:]
    len_ref, qkv_ref, lse_ref, vec_ref, sel_ref, mgrad_ref, tok_ref, gain_ref, wq_ref, wk_ref, wv_ref, *refs = refs
    past_ref = refs.pop(0) if batch else None
    if which:
        seen_ref, part_ref, resgrad_ref, *refs = refs
        shared_ref, tgrad_ref, *refs = refs
    else:
        early_ref = refs.pop(0) if batch else None
        shared_ref, diag_out_ref, part_out_ref, *refs = refs
    bands_ref, probs_ref, sgrad_ref, spread_ref, low_ref, qt_ref, kt_ref, vt_ref, diag_ref, stage_ref, rest_ref, *buffers = refs
    *buffers, sems, out_sems = buffers
    half = wq_ref.shape[0] // 2
    columns = pl.ds(which * half, half)
    fetched = [tok_ref.at[batch, 0]] + [ref.at[:, columns] for ref in (wq_ref, wk_ref, wv_ref)]
    if past_ref is not None:
        fetched.append(past_ref)
    if which:
        fetched += [part_ref, resgrad_ref]
    elif batch:
        fetched.append(early_ref)
    copies = [pltpu.make_async_copy(ref, buffer, sems.at[k]) for k, (ref, buffer) in enumerate(zip(fetched, buffers))]
    for copy in copies:
        copy.start()
    going = []
    offset = 0 if which or shared_ref.dtype == F32 else early_ref.shape[0]
    tok_ref, wq_ref, wk_ref, wv_ref, *buffers = buffers
    if past_ref is not None:
        past_ref = buffers.pop(0)
    if which:
        part_ref, resgrad_ref = buffers
    elif batch:
        early_ref = buffers[0]
    length, width = tok_ref.shape
    first_pair = which * (PAIRS // 2)
    mask = jnp.where(iota((1, length), 1) < len_ref[batch], 0.0, negative)
    lane = iota((ROWS, PAIR), 1)
    diag_ref[...] = seen_ref[...] if which else jnp.zeros_like(diag_ref)

    def one_pair(step, carry):
        pair = first_pair + step
        keys = qkv_ref[1, step]
        values = qkv_ref[2, step]
        queries_t = qkv_ref[0, step].T
        keys_t = qkv_ref[1, step].T
        grads_t = mgrad_ref[step].T
        for side in range(2):
            head = 2 * pair + side
            bands_ref[side] = band_bias(vec_ref, head)
            spread_ref[side] = jnp.zeros(spread_ref.shape[1:], F32)
            mine = (lane >= HEAD_DIM) if side else (lane < HEAD_DIM)
            for block in range(length // ROWS):
                here = slice(ROWS * block, ROWS * (block + 1))
                window = band_slice(block, length)
                queries = qkv_ref[0, step, here, :] * 0.125
                queries = jnp.where(mine, queries, jnp.zeros_like(queries))
                grads = mgrad_ref[step, here, :]
                grads = jnp.where(mine, grads, jnp.zeros_like(grads))
                column = iota((ROWS, lse_ref.shape[1]), 1)
                log_total = jnp.sum(jnp.where(column == head, lse_ref[here, :], 0.0), axis=-1, keepdims=True)
                scores = dot_t(queries, keys) + bands_ref[side, :, window] + mask
                probs = jnp.exp(scores - log_total)
                probs_ref[side, here, :] = probs.astype(BF16)
                weighted = probs * dot_t(grads, values)
                score_grad = weighted - probs * jnp.sum(weighted, axis=-1, keepdims=True)
                spread_ref[side, :, window] += score_grad
                sgrad_ref[side, here, :] = score_grad.astype(BF16)
            rows = slice(HEAD_DIM * side, HEAD_DIM * (side + 1))
            qt_ref[rows, :] = dot_t(keys_t[rows, :], sgrad_ref[side]) * 0.125
            kt_ref[rows, :] = dot(queries_t[rows, :], sgrad_ref[side]) * 0.125
            vt_ref[rows, :] = dot(grads_t[rows, :], probs_ref[side])
            size = spread_ref.shape[2]
            eight = spread_ref[side, 0:8, :]
            for move in range(8, ROWS, 8):
                eight = eight + pltpu.roll(spread_ref[side, move : move + 8, :], size - move, 1)
            diagonal = eight[0:1, :]
            for move in range(1, 8):
                diagonal = diagonal + pltpu.roll(eight[move : move + 1, :], size - move, 1)
            diag_ref[...] = jnp.where(iota(diag_ref.shape, 0) == head, diagonal, diag_ref[...])
        low_ref[0, step] = qt_ref[...].T.astype(BF16)
        low_ref[1, step] = kt_ref[...].T.astype(BF16)
        low_ref[2, step] = vt_ref[...].T.astype(BF16)
        return carry

    lax.fori_loop(0, PAIRS // 2, one_pair, 0)
    for copy in copies:
        copy.wait()

    def send(source, first, place):
        target = shared_ref.at[pl.ds(offset + first, source.shape[0])]
        going.append(pltpu.make_async_copy(source, target, out_sems.at[place]))
        going[-1].start()

    if offset:
        going.append(pltpu.make_async_copy(early_ref, shared_ref.at[pl.ds(0, offset)], out_sems.at[0]))
        going[0].start()

    def past(first, count):
        return 0.0 if past_ref is None else past_ref[first : first + count, :]

    tokens = tok_ref[...].astype(F32)
    inverse = lax.rsqrt(jnp.mean(tokens * tokens, axis=-1, keepdims=True) + epsilon)
    gain = gain_ref[...]
    scaled = tokens * inverse
    normed_t = (scaled * gain).astype(BF16).T
    normed_grad = part_ref[...] if which else jnp.zeros((length, width), F32)
    for matrix, w_ref in enumerate((wq_ref, wk_ref, wv_ref)):
        low = jnp.concatenate([low_ref[matrix, p] for p in range(PAIRS // 2)], axis=1)
        stage_ref[matrix] = (dot(normed_t, low) + past(matrix * width, width)).astype(stage_ref.dtype)
        send(stage_ref.at[matrix], matrix * width, 1 + matrix)
        normed_grad = normed_grad + dot_t(low, w_ref[...])
    left = rest_ref.shape[0]
    if which:
        gain_part = jnp.sum(normed_grad * scaled, axis=0, keepdims=True)
        bias_part = lax.dot_general(
            diag_ref[...],
            sel_ref[...],
            (((1,), (0,)), ((), ())),
            precision=lax.Precision.HIGHEST,
            preferred_element_type=F32,
        )
        row = iota((8, half), 0)
        gains = jnp.where(row == 0, gain_part[:, :half], jnp.where(row == 1, gain_part[:, half:], 0.0))
        wide = jnp.concatenate([bias_part, jnp.zeros((16, half - bias_part.shape[1]), F32)], axis=1)
        last = [gains, wide] + ([jnp.zeros((left - 24, half), F32)] if left > 24 else [])
        rest_ref[...] = (jnp.concatenate(last, axis=0) + past(3 * width, left)).astype(rest_ref.dtype)
        send(rest_ref, 3 * width, 4)
        upstream = normed_grad * gain
        middle = jnp.mean(upstream * scaled, axis=-1, keepdims=True)
        tgrad_ref[...] = (resgrad_ref[...] + inverse * (upstream - scaled * middle)).astype(BF16)
    else:
        if offset and offset + 3 * width < shared_ref.shape[0]:
            rest_ref[...] = jnp.zeros_like(rest_ref)
            send(rest_ref, 3 * width, 4)
        diag_out_ref[...] = diag_ref[...]
        part_out_ref[...] = normed_grad
    for copy in going:
        copy.wait()


def attention_backward(batch, which, last, after, counts, qkv, lse, vector, selector, mixed_grad, tokens, gain, wq, wk, wv, past, more, rows):
    length, width = tokens.shape[2:]
    half = width // 2
    size = vector.shape[-1]
    late = (*past, *(more[1:] if which else more))
    buffers = [((length, width), BF16)] + [((width, half), BF16)] * 3 + [(array.shape, array.dtype) for array in late]
    sent = 0 if which or not last else more[0].shape[0]
    rest = max(rows - sent - 3 * width, 16)
    shared = jax.ShapeDtypeStruct((rows, half), BF16 if last else F32)
    if which:
        outs = [shared, jax.ShapeDtypeStruct((length, width), BF16)]
    else:
        outs = [shared, jax.ShapeDtypeStruct((16, size), F32), jax.ShapeDtypeStruct((length, width), F32)]
    return pl.pallas_call(
        functools.partial(attn_back_kernel, batch, which, len(after)),
        grid=(1,),
        in_specs=[ANYWHERE] * len(after)
        + [SCALARS, pl.BlockSpec((3, PAIRS // 2, length, PAIR), lambda _: (0, which, 0, 0))]
        + [WHOLE] * 3
        + [pl.BlockSpec((PAIRS // 2, length, PAIR), lambda _: (which, 0, 0))]
        + [ANYWHERE, WHOLE]
        + [ANYWHERE] * (3 + len(past))
        + [WHOLE if which and k == 0 else ANYWHERE for k in range(len(more))],
        out_specs=[ANYWHERE] + [WHOLE] * (len(outs) - 1),
        out_shape=outs,
        scratch_shapes=[
            pltpu.VMEM((2, ROWS, size), F32),
            pltpu.VMEM((2, length, length), BF16),
            pltpu.VMEM((2, length, length), BF16),
            pltpu.VMEM((2, ROWS, size), F32),
            pltpu.VMEM((3, PAIRS // 2, length, PAIR), BF16),
            pltpu.VMEM((PAIR, length), F32),
            pltpu.VMEM((PAIR, length), F32),
            pltpu.VMEM((PAIR, length), F32),
            pltpu.VMEM((16, size), F32),
            pltpu.VMEM((3, width, half), shared.dtype),
            pltpu.VMEM((rest, half), shared.dtype),
            *(pltpu.VMEM(shape, kind) for shape, kind in buffers),
            pltpu.SemaphoreType.DMA((len(buffers),)),
            pltpu.SemaphoreType.DMA((5,)),
        ],
        compiler_params=params(56),
        cost_estimate=cost(),
    )(*after, counts, qkv, lse, vector, selector, mixed_grad, tokens, gain, wq, wk, wv, *past, *more)


def unpack_kernel(early, experts, side_ref, mine_ref, other_ref, *refs):
    mine, other = mine_ref[...], other_ref[...]
    second = side_ref[0] == 1
    rows = jnp.concatenate([jnp.where(second, other, mine), jnp.where(second, mine, other)], axis=0).astype(F32)
    half = rows.shape[1]
    width = 2 * half
    if not early:
        q_ref, k_ref, v_ref, gain_ref, bias_ref = refs[3:]
        offset = 0
        gain_ref[...] = jnp.concatenate([rows[3 * width : 3 * width + 1], rows[3 * width + 1 : 3 * width + 2]], axis=1)
        bias_ref[...] = rows[3 * width + 8 : 3 * width + 8 + HEADS, :BUCKETS]
    else:
        q_ref, k_ref, v_ref, output_ref, router_ref, gain_ref = refs
        offset = 2 * early
        output_ref[...] = jnp.concatenate([rows[:width], rows[early : early + width]], axis=1)
        last = early - 16
        router_ref[...] = jnp.concatenate([rows[width:last], rows[early + width : early + last]], axis=1)
        gain_ref[...] = jnp.concatenate([rows[last : last + 1], rows[early + last : early + last + 1]], axis=1)
    for k, ref in enumerate((q_ref, k_ref, v_ref)):
        ref[...] = rows[offset + k * width : offset + (k + 1) * width]


def unpack(early, experts, side, mine, other, past):
    half = mine.shape[1]
    width = 2 * half
    matrix = jax.ShapeDtypeStruct((width, width), F32)
    line = jax.ShapeDtypeStruct((1, width), F32)
    columns = pl.BlockSpec((width, half), lambda _: (0, 0 if early else 1))
    if early:
        more = [matrix, jax.ShapeDtypeStruct((experts, width), F32), line]
    else:
        more = [line, jax.ShapeDtypeStruct((HEADS, BUCKETS), F32)]
    return pl.pallas_call(
        functools.partial(unpack_kernel, early, experts),
        grid=(1,),
        in_specs=[SCALARS, WHOLE, WHOLE] + [ANYWHERE] * len(past),
        out_specs=[columns] * 3 + [WHOLE] * len(more),
        out_shape=[matrix] * 3 + more,
        input_output_aliases={3 + k: k for k in range(len(past))},
        compiler_params=params(56),
        cost_estimate=cost(),
    )(side, mine, other, *past)


def upward(planes, first, last):
    return [(k, k + 1) for k in range(first, last)]


def downward(planes, first, last):
    return [(planes - 1 - k, planes - 2 - k) for k in range(first, last)]


def mix_kernel(both, planes, step, waits, here_ref, up_ref, down_ref, upsum_ref, downsum_ref, *refs):
    to_up, to_down = refs[waits:]
    for moving, sums, out, place in (
        (up_ref, upsum_ref, to_up, here_ref[0]),
        (down_ref, downsum_ref, to_down, planes - 1 - here_ref[0]),
    ):
        total = moving[...] + sums[...]
        out[...] = jnp.where(place <= step, total, moving[...]) if both else total


def mix(both, planes, step, here, up, down, upsum, downsum, after):
    kinds, rows, width = up.shape
    block = pl.BlockSpec((1, rows // 2, width), lambda i, j: (i, j, 0))
    return pl.pallas_call(
        functools.partial(mix_kernel, both, planes, step, len(after)),
        grid=(kinds, 2),
        in_specs=[SCALARS] + [block] * 4 + [ANYWHERE] * len(after),
        out_specs=[block] * 2,
        out_shape=[jax.ShapeDtypeStruct(up.shape, BF16)] * 2,
        compiler_params=params(32),
        cost_estimate=cost(),
    )(here, up, down, upsum, downsum, *after)


def gate_kernel(*refs):
    pass


def gate(arrays, after):
    count = len(arrays)
    return pl.pallas_call(
        gate_kernel,
        in_specs=[ANYWHERE] * (count + len(after)),
        out_specs=[ANYWHERE] * count,
        out_shape=[jax.ShapeDtypeStruct(array.shape, array.dtype) for array in arrays],
        input_output_aliases={k: k for k in range(count)},
        cost_estimate=cost(),
    )(*arrays, *after)


class Chain:
    def __init__(self, planes, own=None, sums=None):
        self.planes, self.own, self.sums = planes, own, sums
        self.here = lax.axis_index("hidden")[None]
        self.from_below, self.from_above = [], []
        if own is not None:
            self.up = self.down = own
        else:
            self.up, self.down = sums[planes - 1], sums[1]
        self.count = 0
        self.steps = planes if own is not None and sums is not None else planes - 1

    def send(self):
        planes, s = self.planes, self.count
        if self.own is not None and self.sums is not None:
            first, last = 0, planes - 1
        elif self.own is not None:
            first, last = s, planes - 1
        else:
            first, last = 0, s + 1
        self.up = lax.ppermute(self.up, "hidden", upward(planes, first, last))
        self.down = lax.ppermute(self.down, "hidden", downward(planes, first, last))
        self.count += 1
        if self.own is not None and s < planes - 1:
            self.from_below.append(self.up)
            self.from_above.append(self.down)

    def mix(self, *after):
        planes, s = self.planes, self.count - 1
        both = self.own is not None
        offset = 1 if both else 2
        self.up, self.down = mix(
            both, planes, s, self.here, self.up, self.down, self.sums[planes - offset - s], self.sums[s + offset], after
        )
        self.mixed = self.up

    def gate(self, *after):
        self.up, self.down = gate((self.up, self.down), after)
        self.from_below[-1], self.from_above[-1] = self.up, self.down

    def run(self):
        while self.count < self.steps:
            self.send()
        return self

    def gathered(self):
        return (self.own, *self.from_above, *self.from_below)

    def scattered(self):
        return (self.sums[0], self.up, self.down)


def swap(values, axis, distance):
    return lax.ppermute(values, axis, [(k, k ^ distance) for k in range(lax.axis_size(axis))])


def share_sums(values, axis, near, count):
    me = lax.axis_index(axis) // near
    parts = values.reshape(count, values.shape[0] // count, values.shape[1])
    total = lax.dynamic_index_in_dim(parts, me, 0, keepdims=False).astype(F32)
    for k in range(1, count):
        part = lax.dynamic_index_in_dim(parts, me ^ k, 0, keepdims=False)
        total = total + swap(part, axis, k * near).astype(F32)
    return total.astype(BF16)


def join_sums(values, axis, near, count):
    me = lax.axis_index(axis) // near
    found = [values] + [swap(values, axis, k * near) for k in range(1, count)]
    joined = []
    for j in range(count):
        piece = found[count - 1]
        for k in range(count - 2, -1, -1):
            piece = jnp.where(me ^ k == j, found[k], piece)
        joined.append(piece)
    return jnp.concatenate(joined)


def sum_everywhere(values):
    size = lax.axis_size("expert")
    planes = lax.axis_size("hidden")
    values = share_sums(values, "expert", 2, size // 2)
    values = share_sums(values, "hidden", 1, planes)
    values = join_sums(values, "hidden", 1, planes)
    values = join_sums(values, "expert", 2, size // 2)
    return values, swap(values, "expert", 1)


def share_half(values):
    side = lax.axis_index("expert") % 2
    parts = values.reshape(2, values.shape[0] // 2, values.shape[1])
    mine = lax.dynamic_index_in_dim(parts, side, 0, keepdims=False)
    other = lax.dynamic_index_in_dim(parts, 1 - side, 0, keepdims=False)
    return mine + swap(other, "expert", 1)


def offset_selector(length):
    place = np.arange(2 * length)
    offsets = np.where(place < 2 * length - ROWS, place, place - 2 * length) - (length - ROWS)
    offsets = np.clip(offsets, -(length - 1), length - 1)
    return (offset_bucket(offsets)[:, None] == np.arange(BUCKETS)[None, :]).astype(np.float32)


def moves(groups, local, capacity, message, kinds=1):
    kind, expert, group, slot = np.meshgrid(
        np.arange(kinds), np.arange(local), np.arange(groups), np.arange(capacity), indexing="ij"
    )
    source = (group * message + (kind * local + expert) * capacity + slot).reshape(-1)
    return (source[:, None] == np.arange(groups * message)[None, :]).astype(jnp.bfloat16)


def shards(
    tokens,
    cotangent,
    lengths,
    routes,
    gain_attn,
    w_query,
    w_key,
    w_value,
    w_output,
    bucket_head_bias,
    gain_ffn,
    w_router,
    w_inner,
    w_outer,
):
    batches, _, length, width = tokens.shape
    experts = w_router.shape[1]
    local = w_inner.shape[0]
    groups = lax.axis_size("expert")
    planes = lax.axis_size("hidden")
    capacity = (5 * length + 4 * experts - 1) // (4 * experts)
    per = local * capacity
    rows = groups * capacity
    message = padded(per)
    move = jnp.asarray(moves(groups, local, capacity, message))
    move_gated = jnp.asarray(moves(groups, local, capacity, message + 16))
    move_pair = jnp.asarray(moves(groups, local // 2, capacity, message, 2))
    move_back = jnp.asarray(moves(groups, local // 2, capacity, message, 2).T)
    selector = jnp.asarray(offset_selector(length))
    vector = lax.dot_general(
        bucket_head_bias, selector, (((0,), (1,)), ((), ())), precision=lax.Precision.HIGHEST
    )[:, None, :]
    gain_a = gain_attn[None, :]
    gain_f = gain_ffn[None, :]
    router_rows = w_router.T
    counts = lengths[:, 0]
    plane = lax.axis_index("hidden")[None]

    def to_groups(values):
        return lax.all_to_all(values, "expert", split_axis=0, concat_axis=0, tiled=True)

    def leaving(values, *after):
        return regroup(move_pair, [to_groups(values)], (2, local // 2 * rows, width), after)

    def arriving(chain, *after):
        return to_groups(regroup(move_back, chain.scattered(), (groups, message, width), after))

    def attend(b, *after):
        return attention_forward(b, after, counts, tokens, gain_a, w_query, w_key, w_value, vector)

    def routing(b, *after):
        return route(
            b, after, tokens, cotangent, forward[b][1], w_output, gain_f, router_rows, srow, rcol, groups, per, b > 0
        )

    srow, scol, cot_slots = prep(counts, routes.reshape(batches, length), cotangent, groups, per, capacity)
    rcol = routes.reshape(batches, length, 1)
    early_rows = width + experts + 16
    unit = 16 * groups * planes
    first_rows = 2 * early_rows + 3 * width
    first_rows = first_rows + -first_rows % unit
    second_rows = 3 * width + 24
    second_rows = second_rows + -second_rows % unit
    kept, layer_rows, token_grads = [], [], []
    early_part, first_part, second_part = (), (), ()

    def back_tokens(b, after, low, high):
        return combine(
            b,
            b + 1 == batches,
            after,
            counts,
            low,
            high,
            scol,
            rcol,
            *routed[b][:2],
            cotangent,
            gain_f,
            router_rows,
            w_output,
            forward[b][1],
            early_part,
            per,
            2 * early_rows,
        )

    def back_half(b, which, after, mixed_grad, more):
        qkv, _, lse = forward[b]
        last = b + 1 == batches
        return attention_backward(
            b,
            which,
            last,
            after,
            counts,
            qkv,
            lse,
            vector,
            selector,
            mixed_grad,
            tokens,
            gain_a,
            w_query,
            w_key,
            w_value,
            second_part if which else first_part,
            more,
            second_rows if which else first_rows if last else 3 * width,
        )

    def grads_half(h, after, past):
        return expert_grads(h, after, past, local, *([k[h][part] for k in kept] for part in (2, 3, 0, 1)))

    forward = [attend(0, cot_slots)]
    routed = [routing(0)]
    grads = regroup(move, [to_groups(cot_slots)], (local * rows, width), (routed[0][2],))
    grad_chain = Chain(planes, grads)
    grad_chain.send()
    inputs = regroup_gated(move_gated, to_groups(routed[0][2]), capacity, (grads,))
    input_chain = Chain(planes, inputs)
    input_chain.send()
    forward.append(attend(1, inputs, grad_chain.up, grad_chain.down))
    grad_chain.send()
    routed.append(routing(1, grad_chain.up, grad_chain.down))
    grad_chain.run()
    input_chain.gate(forward[1][1])
    input_chain.send()
    held = (input_chain.up, input_chain.down, grad_chain.up, grad_chain.down)
    input_chain.run()
    halves = range(2)
    chains = [None, None]
    for b in range(batches):
        last = b + 1 == batches
        before = chains
        messages = [None, None]
        ready = ()
        if not last:
            if b:
                forward.append(attend(b + 1))
                routed.append(routing(b + 1))
            messages = [leaving(m, *held) for m in routed[b + 1][2:]]
            held = ()
            ready = tuple(messages)
        chains, worked = [], []
        for h in halves:
            if b == 0:
                done = experts_half(
                    h, ready, plane, None, w_inner, w_outer, input_chain.gathered(), grad_chain.gathered()
                )
            else:
                before[h].mix(*(w[0] for w in worked))
                tied = (before[h].up, before[h].down)
                if h:
                    tied += (before[0].up, before[0].down)
                done = experts_half(h, ready + tied, plane, before[h].gathered(), w_inner, w_outer)
                before[h].send()
            worked.append(done)
            chains.append(Chain(planes, messages[h], done[:planes]))
            chains[h].send()
        kept.append([w[planes:] for w in worked])
        low_chain, high_chain = chains
        if not last:
            for step in range(1, planes):
                for chain in chains:
                    if step > 1:
                        chain.send()
                    if step < planes - 1:
                        chain.mix()
            if b == 0:
                continue
            low, high = (arriving(chain) for chain in before)
            layer, res_grad, mixed_grad, early_part = back_tokens(b - 1, (), low, high)
            first_part, *more = back_half(b - 1, 0, (), mixed_grad, (early_part,) if b > 1 else ())
            second_part, token_grad = back_half(b - 1, 1, (), mixed_grad, (*more, res_grad))
        else:
            low = arriving(before[0], before[1].up, before[1].down)
            high = arriving(before[1])
            low_chain.mix()
            low_chain.send()
            totals = grads_half(0, (low_chain.mixed,), ())
            high_chain.mix(totals[0])
            high_chain.send()
            low_chain.mix(high)
            low_chain.send()
            layer, res_grad, mixed_grad, early_part = back_tokens(b - 1, (low_chain.mixed,), low, high)
            high_chain.mix(mixed_grad)
            high_chain.send()
            first_part, *more = back_half(
                b - 1, 0, (high_chain.mixed,), mixed_grad, (early_part,) if b > 1 else ()
            )
            low = regroup(move_back, low_chain.scattered(), (groups, message, width), (first_part,))
            second_part, token_grad = back_half(b - 1, 1, (low,), mixed_grad, (*more, res_grad))
            low = to_groups(low)
            high = regroup(move_back, high_chain.scattered(), (groups, message, width), (second_part, low))
            totals = grads_half(1, (high,), totals)
            high = to_groups(high)
        layer_rows.append(layer)
        token_grads.append(token_grad)
        early_part, first_part, second_part = (early_part,), (first_part,), (second_part,)
    layer, res_grad, mixed_grad, early_part = back_tokens(batches - 1, (totals[0],), low, high)
    first_part, *more = back_half(batches - 1, 0, (), mixed_grad, (early_part,))
    side = (lax.axis_index("expert") % 2)[None]
    first_half = share_half(first_part)
    second_part, token_grad = back_half(batches - 1, 1, (first_half,), mixed_grad, (*more, res_grad))
    mine, other = sum_everywhere(first_half)
    mine_second, other_second = sum_everywhere(share_half(second_part))
    early_done = unpack(early_rows, experts, side, mine, other, ())
    layer_rows.append(layer)
    token_grads.append(token_grad)
    *attended, output_grad, router_grad, gain_f_grad = early_done
    query_grad, key_grad, value_grad, gain_a_grad, bias_grad = unpack(
        0, experts, side, mine_second, other_second, attended
    )
    return (
        jnp.stack(layer_rows)[:, None],
        jnp.stack(token_grads)[:, None],
        gain_a_grad[0],
        query_grad,
        key_grad,
        value_grad,
        output_grad,
        bias_grad.T,
        gain_f_grad[0],
        router_grad.T,
        totals[1],
        totals[0],
    )


def solution(mesh):
    token = P(None, ("expert", "hidden"), None, None)
    placed = (
        token,
        token,
        P(None, ("expert", "hidden")),
        token,
        *(P() for _ in range(8)),
        P("expert", None, "hidden"),
        P("expert", "hidden", None),
    )
    return jax.shard_map(
        shards,
        mesh=mesh,
        in_specs=placed,
        out_specs=(
            token,
            token,
            *(P() for _ in range(8)),
            P("expert", None, "hidden"),
            P("expert", "hidden", None),
        ),
        check_vma=False,
    )
```

```python
import functools

import jax
import jax.numpy as jnp
import numpy as np
from jax import lax
from jax.experimental import pallas as pl
from jax.experimental.pallas import tpu as pltpu
from jax.sharding import PartitionSpec as P

HEADS = 12
HEAD_DIM = 64
BUCKETS = 32
MAXDIST = 128
PAIR = 2 * HEAD_DIM
PAIRS = HEADS // 2
ROWS = 128

epsilon = 1e-06
negative = -1e30
F32 = jnp.float32
BF16 = jnp.bfloat16
MIB = 1 << 20


def params(mib):
    return pltpu.CompilerParams(vmem_limit_bytes=mib * MIB)


def cost():
    return pl.CostEstimate(flops=1, bytes_accessed=1, transcendentals=0)


def offset_bucket(offsets):
    halfway = BUCKETS // 2
    exact_count = halfway // 2
    relative_distance = np.abs(offsets)
    scaled = (
        np.log(np.maximum(relative_distance, 1) / exact_count)
        / np.log(MAXDIST / exact_count)
        * (halfway - exact_count)
    )
    far_bucket = np.minimum(exact_count + np.floor(scaled).astype(np.int64), halfway - 1)
    near_bucket = np.where(relative_distance < exact_count, relative_distance, far_bucket)
    return (np.where(offsets > 0, halfway, 0) + near_bucket).astype(np.int32)


def dot(a, b):
    return lax.dot_general(a, b, (((1,), (0,)), ((), ())), preferred_element_type=F32)


def dot_t(a, b):
    return lax.dot_general(a, b, (((1,), (1,)), ((), ())), preferred_element_type=F32)


def t_dot(a, b):
    return lax.dot_general(a, b, (((0,), (0,)), ((), ())), preferred_element_type=F32)


def one_hot(condition):
    return jnp.where(condition, 1.0, 0.0).astype(BF16)


def batch_block(array, b):
    rest = array.shape[1:]
    return pl.BlockSpec((1,) + rest, lambda *_: (b,) + (0,) * len(rest))


ANYWHERE = pl.BlockSpec(memory_space=pl.ANY)
WHOLE = pl.BlockSpec(memory_space=pltpu.VMEM)
SCALARS = pl.BlockSpec(memory_space=pltpu.SMEM)


def iota(shape, axis):
    return lax.broadcasted_iota(jnp.int32, shape, axis)


def padded(rows):
    return -(-rows // 16) * 16


def spread_slots(slot, per, message, first=0, last=None):
    last = per if last is None else last
    group = lax.div(jnp.maximum(slot, 0), per)
    inside = slot - group * per
    held = (slot >= 0) & (inside >= first) & (inside < last)
    return jnp.where(held, group * message + inside - first, -1)


def prep_kernel(per, capacity, len_ref, row_ref, col_ref, cot_ref, srow_ref, scol_ref, slots_ref):
    batches, _, length = row_ref.shape
    groups, message, width = slots_ref.shape
    experts = groups * per // capacity
    before = one_hot(iota((length, length), 0) < iota((length, length), 1))
    after = one_hot(iota((length, length), 1) < iota((length, length), 0))
    for b in range(batches):
        count = len_ref[b]
        row = row_ref[b]
        col = col_ref[b]
        valid_row = iota((1, length), 1) < count
        valid_col = iota((length, 1), 0) < count
        chosen_row = iota((experts, length), 0) == row
        chosen_col = iota((length, experts), 1) == col
        earlier_row = dot(one_hot(chosen_row & valid_row), before)
        rank_row = jnp.sum(jnp.where(chosen_row, earlier_row, 0.0), axis=0, keepdims=True).astype(jnp.int32)
        earlier_col = dot(after, one_hot(chosen_col & valid_col))
        rank_col = jnp.sum(jnp.where(chosen_col, earlier_col, 0.0), axis=1, keepdims=True).astype(jnp.int32)
        slot_row = jnp.where(valid_row & (rank_row < capacity), row * capacity + rank_row, -1)
        srow_ref[b] = slot_row
        scol_ref[b] = jnp.where(valid_col & (rank_col < capacity), col * capacity + rank_col, -1)
        if b == 0:
            dispatch = one_hot(iota((groups * message, length), 0) == spread_slots(slot_row, per, message))
            slots_ref[...] = dot(dispatch, cot_ref[0, 0]).astype(BF16).reshape(groups, message, width)


def prep(lengths, routes, cot, groups, per, capacity):
    batches, length = routes.shape
    width = cot.shape[-1]
    vmem = WHOLE
    message = padded(per)
    return pl.pallas_call(
        functools.partial(prep_kernel, per, capacity),
        grid=(1,),
        in_specs=[SCALARS, vmem, vmem, batch_block(cot, 0)],
        out_specs=[vmem] * 3,
        out_shape=[
            jax.ShapeDtypeStruct((batches, 1, length), jnp.int32),
            jax.ShapeDtypeStruct((batches, length, 1), jnp.int32),
            jax.ShapeDtypeStruct((groups, message, width), BF16),
        ],
        compiler_params=params(60),
        cost_estimate=cost(),
    )(lengths, routes.reshape(batches, 1, length), routes.reshape(batches, length, 1), cot)


def slot_places(kinds, local, groups, capacity, message):
    row = iota((1, kinds * local * groups * capacity), 1)
    slot = lax.rem(row, capacity)
    row = lax.div(row, capacity)
    group = lax.rem(row, groups)
    return group * message + lax.div(row, groups) * capacity + slot


def regroup_kernel(back, kinds, local, groups, capacity, message, waits, *refs):
    refs = refs[waits:]
    out_ref = refs[-1]
    total = refs[0][...].astype(F32)
    for ref in refs[1:-1]:
        total = total + ref[...].astype(F32)
    places = slot_places(kinds, local, groups, capacity, message)
    move = one_hot(iota((groups * message, places.shape[1]), 0) == places)
    if back:
        rows = dot(move, total.astype(BF16).reshape(places.shape[1], -1))
    else:
        rows = t_dot(move, total.astype(BF16).reshape(groups * message, -1))
    out_ref[...] = rows.astype(BF16).reshape(out_ref.shape)


def regroup(back, arrays, shape, kinds, local, groups, capacity, message, after=()):
    return pl.pallas_call(
        functools.partial(regroup_kernel, back, kinds, local, groups, capacity, message, len(after)),
        in_specs=[ANYWHERE] * len(after) + [WHOLE] * len(arrays),
        out_specs=WHOLE,
        out_shape=jax.ShapeDtypeStruct(shape, BF16),
        compiler_params=params(60),
        cost_estimate=cost(),
    )(*after, *arrays)


def regroup_gated_kernel(capacity, *refs):
    in_ref, out_ref = refs[-2:]
    groups, message, width = in_ref.shape
    total = out_ref.shape[0] - 16
    local = total // (groups * capacity)
    rows = groups * capacity
    flat = in_ref[...].reshape(groups * message, width)
    places = slot_places(1, local, groups, capacity, message)
    move = one_hot(iota((groups * message, total), 0) == places)
    out_ref[:total, :] = t_dot(move, flat).astype(BF16)
    place = iota((message, 128), 0)
    lane = iota((message, 128), 1)
    columns = []
    for g in range(groups):
        gates = in_ref[g, message - 16 : message, :].astype(F32)[0:1, :]
        parts = [
            jnp.sum(jnp.where(place == lane, gates[:, 128 * k : 128 * (k + 1)], 0.0), axis=1, keepdims=True)
            for k in range(3)
        ]
        wide = iota((message, 128), 1)
        columns.append(jnp.where(wide == 0, parts[0], jnp.where(wide == 1, parts[1], jnp.where(wide == 2, parts[2], 0.0))))
    column = jnp.concatenate(columns, axis=0).astype(BF16)
    moved = t_dot(move, column)
    place = iota((rows, 128), 0)
    lane = iota((rows, 128), 1)
    lines = []
    for l in range(local):
        mine = moved[l * rows : (l + 1) * rows, :]
        parts = [
            jnp.sum(jnp.where(place == lane, mine[:, k : k + 1], 0.0), axis=0, keepdims=True) for k in range(3)
        ]
        lines.append(jnp.concatenate(parts + [jnp.zeros((1, width - 384), F32)], axis=1))
    lines.append(jnp.zeros((16 - local, width), F32))
    out_ref[total:, :] = jnp.concatenate(lines, axis=0).astype(BF16)


def regroup_gated(slots, rows, capacity, after=()):
    width = slots.shape[-1]
    return pl.pallas_call(
        functools.partial(regroup_gated_kernel, capacity),
        in_specs=[ANYWHERE] * len(after) + [WHOLE],
        out_specs=WHOLE,
        out_shape=jax.ShapeDtypeStruct((rows + 16, width), BF16),
        compiler_params=params(60),
        cost_estimate=cost(),
    )(*after, slots)


def band_bias(vector_ref, head):
    wide = jnp.broadcast_to(vector_ref[head], (ROWS, vector_ref.shape[-1]))
    return pltpu.roll(wide, 0, 1, stride=1, stride_axis=0)


def band_slice(block, length):
    start = length - ROWS * (block + 1)
    return slice(start, start + length)


def attn_kernel(batch, waits, *refs):
    refs = refs[waits:]
    len_ref, tok_ref, gain_ref, wq_ref, wk_ref, wv_ref, vec_ref, qkv_ref, mixed_ref, lse_ref, bands_ref, probs_ref, mixed_t_ref = refs
    length, width = tok_ref.shape[2:]
    count = len_ref[batch]
    tokens = tok_ref[0, 0].astype(F32)
    inverse = lax.rsqrt(jnp.mean(tokens * tokens, axis=-1, keepdims=True) + epsilon)
    normed = (tokens * inverse * gain_ref[...]).astype(BF16)
    for which, w_ref in enumerate((wq_ref, wk_ref, wv_ref)):
        for part in range(width // 256):
            rows = dot(normed, w_ref[:, 256 * part : 256 * part + 256]).astype(BF16)
            qkv_ref[which, 2 * part] = rows[:, :PAIR]
            qkv_ref[which, 2 * part + 1] = rows[:, PAIR:]
    mask = jnp.where(iota((1, length), 1) < count, 0.0, negative)
    lane = iota((ROWS, PAIR), 1)
    lse_ref[...] = jnp.zeros_like(lse_ref)

    def one_pair(pair, carry):
        keys = qkv_ref[1, pair]
        values_t = qkv_ref[2, pair].T
        for side in range(2):
            head = 2 * pair + side
            bands_ref[side] = band_bias(vec_ref, head)
            mine = (lane >= HEAD_DIM) if side else (lane < HEAD_DIM)
            for block in range(length // ROWS):
                here = slice(ROWS * block, ROWS * (block + 1))
                queries = qkv_ref[0, pair, here, :] * 0.125
                queries = jnp.where(mine, queries, jnp.zeros_like(queries))
                scores = dot_t(queries, keys) + bands_ref[side, :, band_slice(block, length)] + mask
                highest = jnp.max(scores, axis=-1, keepdims=True)
                powers = jnp.exp(scores - highest)
                total = jnp.sum(powers, axis=-1, keepdims=True)
                probs_ref[side, here, :] = (powers * (1.0 / total)).astype(BF16)
                column = iota((ROWS, lse_ref.shape[1]), 1)
                lse_ref[here, :] = jnp.where(column == head, highest + jnp.log(total), lse_ref[here, :])
            rows = slice(HEAD_DIM * side, HEAD_DIM * (side + 1))
            mixed_t_ref[rows, :] = dot_t(values_t[rows, :], probs_ref[side])
        mixed_ref[pair] = mixed_t_ref[...].T.astype(BF16)
        return carry

    lax.fori_loop(0, PAIRS, one_pair, 0)


def attention_forward(batch, after, counts, tokens, gain, wq, wk, wv, vector):
    length = tokens.shape[2]
    return pl.pallas_call(
        functools.partial(attn_kernel, batch, len(after)),
        grid=(1,),
        in_specs=[ANYWHERE] * len(after) + [SCALARS, batch_block(tokens, batch)] + [WHOLE] * 5,
        out_specs=[WHOLE] * 3,
        out_shape=[
            jax.ShapeDtypeStruct((3, PAIRS, length, PAIR), BF16),
            jax.ShapeDtypeStruct((PAIRS, length, PAIR), BF16),
            jax.ShapeDtypeStruct((length, 128), F32),
        ],
        scratch_shapes=[
            pltpu.VMEM((2, ROWS, vector.shape[-1]), F32),
            pltpu.VMEM((2, length, length), BF16),
            pltpu.VMEM((PAIR, length), F32),
        ],
        compiler_params=params(60),
        cost_estimate=cost(),
    )(*after, counts, tokens, gain, wq, wk, wv, vector)


def route_kernel(per, gated, waits, *refs):
    refs = refs[waits:]
    tok_ref, cot_ref, mixed_ref, wo_ref, gffn_ref, wr_ref, srow_ref, rcol_ref, res_ref, probs_ref, *out_refs = refs
    length, width = tok_ref.shape[2:]
    mixed_all = jnp.concatenate([mixed_ref[p] for p in range(PAIRS)], axis=1)
    residual = tok_ref[0, 0].astype(F32) + dot(mixed_all, wo_ref[...])
    res_ref[...] = residual
    inverse = lax.rsqrt(jnp.mean(residual * residual, axis=-1, keepdims=True) + epsilon)
    routed = (residual * inverse * gffn_ref[...]).astype(BF16)
    logits = dot_t(routed, wr_ref[...])
    powers = jnp.exp(logits - jnp.max(logits, axis=-1, keepdims=True))
    probs = powers / jnp.sum(powers, axis=-1, keepdims=True)
    probs_ref[...] = probs
    gate = jnp.sum(jnp.where(iota(probs.shape, 1) == rcol_ref[0], probs, 0.0), axis=-1, keepdims=True)
    groups, message, _ = out_refs[0].shape
    places = iota((groups * message, length), 0)
    if gated:
        grads = (gate * cot_ref[0, 0].astype(F32)).astype(BF16)
        half = per // 2
        for which, out_ref in enumerate(out_refs):
            place = spread_slots(srow_ref[0], per, message, which * half, (which + 1) * half)
            rows = dot(one_hot(places == place), grads)
            rows = rows + dot(one_hot(places == jnp.where(place < 0, -1, place + half)), routed)
            out_ref[...] = rows.astype(BF16).reshape(out_ref.shape)
        return
    slots_ref = out_refs[0]
    dispatch = one_hot(places == spread_slots(srow_ref[0], per, message))
    slots_ref[...] = dot(dispatch, routed).astype(BF16).reshape(slots_ref.shape)
    first = gate.astype(BF16).astype(F32)
    second = (gate - first).astype(BF16).astype(F32)
    third = gate - first - second
    column = iota((length, PAIR), 1)
    pieces = jnp.where(column == 0, first, jnp.where(column == 1, second, jnp.where(column == 2, third, 0.0)))
    sorted_gates = dot(dispatch, pieces.astype(BF16))
    data = message - 16
    place = iota((data, 128), 0)
    lane = iota((data, 128), 1)
    for g in range(groups):
        mine = sorted_gates[g * message : g * message + data, :]
        parts = [
            jnp.sum(jnp.where(place == lane, mine[:, k : k + 1], 0.0), axis=0, keepdims=True) for k in range(3)
        ]
        line = jnp.concatenate(parts + [jnp.zeros((1, width - 384), F32)], axis=1)
        slots_ref[g, data:message, :] = jnp.broadcast_to(line, (16, width)).astype(BF16)


def route(batch, after, tokens, cot, mixed, wo, gain_ffn, w_router, srow, rcol, groups, per, gated):
    length, width = tokens.shape[2:]
    experts = w_router.shape[0]
    message = padded(per) if gated else padded(per) + 16
    return pl.pallas_call(
        functools.partial(route_kernel, per, gated, len(after)),
        grid=(1,),
        in_specs=[ANYWHERE] * len(after)
        + [batch_block(tokens, batch), batch_block(cot, batch)]
        + [WHOLE] * 4
        + [batch_block(srow, batch), batch_block(rcol, batch)],
        out_specs=[WHOLE] * (4 if gated else 3),
        out_shape=[
            jax.ShapeDtypeStruct((length, width), F32),
            jax.ShapeDtypeStruct((length, experts), F32),
        ]
        + [jax.ShapeDtypeStruct((groups, message, width), BF16)] * (2 if gated else 1),
        compiler_params=params(60),
        cost_estimate=cost(),
    )(*after, tokens, cot, mixed, wo, gain_ffn, w_router, srow, rcol)


GELU_SCALE = 0.7978845608028654
GELU_CUBIC = 0.044715


def expert_kernel(planes, gated, first_expert, waits, *refs):
    pieces = 2 * planes - 1
    refs = refs[waits:]
    plane = refs[0][0]
    x_refs, refs = refs[1 : 1 + pieces], refs[1 + pieces :]
    c_refs, refs = refs[:pieces], refs[pieces:]
    gate_refs = ()
    if not gated:
        gate_refs, refs = refs[:pieces], refs[pieces:]
    wi_ref, wo_ref, *refs = refs
    sum_refs = refs[:planes]
    act_ref, pre_ref, x_ref, c_ref = refs[planes:]
    rows = x_refs[0].shape[0]

    def assemble(parts):
        found = [parts[0][...]]
        for k in range(1, planes):
            from_above = plane + k < planes
            found.append(jnp.where(from_above, parts[k][...], parts[2 * planes - 1 - k][...]))
        return found

    inputs = jnp.concatenate(assemble(x_refs), axis=0)
    grads = assemble(c_refs)
    if not gated:
        place = iota((rows, 128), 0)
        lane = iota((rows, 128), 1)
        expert = first_expert + pl.program_id(0)
        for k, lines in enumerate(assemble(gate_refs)):
            lines = jnp.where(iota(lines.shape, 0) == expert, lines.astype(F32), 0.0)
            line = jnp.sum(lines, axis=0, keepdims=True)
            line = line[:, :128] + line[:, 128:256] + line[:, 256:384]
            gate = jnp.sum(jnp.where(place == lane, line, 0.0), axis=1, keepdims=True)
            grads[k] = (grads[k].astype(F32) * gate).astype(BF16)
    grads = jnp.concatenate(grads, axis=0)
    x_ref[0] = inputs
    c_ref[0] = grads
    pre = dot(inputs, wi_ref[0])
    square = pre * pre
    curve = jnp.tanh(GELU_SCALE * pre * (1.0 + GELU_CUBIC * square))
    half = 0.5 * (1.0 + curve)
    act = (pre * half).astype(BF16)
    slope = half + 0.5 * pre * (1.0 - curve * curve) * (GELU_SCALE * (1.0 + 3.0 * GELU_CUBIC * square))
    act_ref[0] = act
    outs = dot(act, wo_ref[0]).astype(BF16)
    pre_grad = (slope * dot_t(grads, wo_ref[0])).astype(BF16)
    pre_ref[0] = pre_grad
    ins = dot_t(pre_grad, wi_ref[0]).astype(BF16)
    for k in range(planes):
        sum_refs[k][0] = outs[k * rows : (k + 1) * rows]
        sum_refs[k][1] = ins[k * rows : (k + 1) * rows]


def experts_half(which, after, plane, messages, w_inner, w_outer, xs=None, cs=None):
    local, width, hidden = w_inner.shape
    mine = local // 2
    first = which * mine
    gated = messages is not None
    pieces = len(messages if gated else xs)
    planes = (pieces + 1) // 2
    if gated:
        rows = messages[0].shape[1] // mine
        x_block = pl.BlockSpec((None, rows, width), lambda e: (1, e, 0))
        c_block = pl.BlockSpec((None, rows, width), lambda e: (0, e, 0))
        arrays = (*messages, *messages)
        blocks = [x_block] * pieces + [c_block] * pieces
    else:
        rows = cs[0].shape[0] // local
        slab = pl.BlockSpec((rows, width), lambda e: (first + e, 0))
        lines = pl.BlockSpec((16, width), lambda e: (local * rows // 16, 0))
        arrays = (*xs, *cs, *xs)
        blocks = [slab] * (2 * pieces) + [lines] * pieces
    weight = lambda a, b: pl.BlockSpec((1, a, b), lambda e: (first + e, 0, 0))
    mat = lambda a, b: pl.BlockSpec((1, a, b), lambda e: (e, 0, 0))
    total = planes * rows
    kept = lambda n: jax.ShapeDtypeStruct((mine, total, n), BF16)
    return pl.pallas_call(
        functools.partial(expert_kernel, planes, gated, first, len(after)),
        grid=(mine,),
        in_specs=[ANYWHERE] * len(after) + [SCALARS] + blocks + [weight(width, hidden), weight(hidden, width)],
        out_specs=[pl.BlockSpec((2, rows, width), lambda e: (0, e, 0))] * planes
        + [mat(total, hidden), mat(total, hidden), mat(total, width), mat(total, width)],
        out_shape=[jax.ShapeDtypeStruct((2, mine * rows, width), BF16)] * planes
        + [kept(hidden), kept(hidden), kept(width), kept(width)],
        compiler_params=params(60),
        cost_estimate=cost(),
    )(*after, plane, *arrays, w_inner, w_outer)


def expert_grad_kernel(batches, waits, *refs):
    xs, cs, acts, pres = (refs[waits + k * batches : waits + (k + 1) * batches] for k in range(4))
    outer_ref, inner_ref = refs[-2:]
    whole = lambda refs: jnp.concatenate([ref[0] for ref in refs], axis=0)
    outer_ref[0] = t_dot(whole(acts), whole(cs))
    inner_ref[0] = t_dot(whole(xs), whole(pres))


def expert_grads(which, after, past, local, xs, cs, acts, pres):
    batches = len(xs)
    mine, total, width = xs[0].shape
    hidden = acts[0].shape[2]
    first = which * mine
    mat = lambda a, b: pl.BlockSpec((1, a, b), lambda e: (e, 0, 0))
    out = lambda a, b: pl.BlockSpec((1, a, b), lambda e: (first + e, 0, 0))
    behind = len(after) + 4 * batches
    return pl.pallas_call(
        functools.partial(expert_grad_kernel, batches, len(after)),
        grid=(mine,),
        in_specs=[ANYWHERE] * len(after)
        + [mat(total, width)] * (2 * batches)
        + [mat(total, hidden)] * (2 * batches)
        + [ANYWHERE] * len(past),
        out_specs=[out(hidden, width), out(width, hidden)],
        out_shape=[
            jax.ShapeDtypeStruct((local, hidden, width), F32),
            jax.ShapeDtypeStruct((local, width, hidden), F32),
        ],
        input_output_aliases={behind + k: k for k in range(len(past))},
        compiler_params=params(60),
        cost_estimate=cost(),
    )(*after, *xs, *cs, *acts, *pres, *past)


def combine_kernel(per, batch, waits, *refs):
    refs = refs[waits:]
    len_ref, low_ref, high_ref, scol_ref, rcol_ref, res_ref, probs_ref, cot_ref, gffn_ref, wr_ref, wo_ref, mixed_ref, *refs = refs
    past_ref = refs.pop(0) if batch else None
    layer_ref, resgrad_ref, mgrad_ref, shared_ref, *buffers, sems = refs
    fetched = [res_ref, cot_ref.at[batch, 0], mixed_ref, wo_ref] + ([past_ref] if batch else [])
    copies = [pltpu.make_async_copy(ref, buffer, sems.at[k]) for k, (ref, buffer) in enumerate(zip(fetched, buffers))]
    for copy in copies:
        copy.start()
    res_ref, cot_ref, mixed_ref, wo_ref = buffers[:4]
    if batch:
        past_ref = buffers[4]
    length, width = cot_ref.shape
    experts = wr_ref.shape[0]
    groups, message, _ = low_ref.shape
    valid = iota((length, 1), 0) < len_ref[batch]
    places = iota((length, groups * message), 1)
    half = per // 2
    returned = input_grad = None
    for which, ref in enumerate((low_ref, high_ref)):
        place = spread_slots(scol_ref[0], per, message, which * half, (which + 1) * half)
        rows = ref[...].reshape(groups * message, width)
        out_part = dot(one_hot(places == place), rows)
        in_part = dot(one_hot(places == jnp.where(place < 0, -1, place + half)), rows)
        returned = out_part if returned is None else returned + out_part
        input_grad = in_part if input_grad is None else input_grad + in_part
    copies[0].wait()
    copies[1].wait()
    residual = res_ref[...]
    probs = probs_ref[...]
    chosen = iota(probs.shape, 1) == rcol_ref[0]
    gate = jnp.sum(jnp.where(chosen, probs, 0.0), axis=-1, keepdims=True)
    layer_ref[...] = jnp.where(valid, residual + gate * returned, 0.0).astype(BF16)
    out_grad = jnp.where(valid, cot_ref[...].astype(F32), 0.0)
    gate_grad = jnp.sum(out_grad * returned, axis=-1, keepdims=True)
    prob_grad = jnp.where(chosen, gate_grad, 0.0)
    logit_grad = (probs * (prob_grad - jnp.sum(probs * prob_grad, axis=-1, keepdims=True))).astype(BF16)
    inverse = lax.rsqrt(jnp.mean(residual * residual, axis=-1, keepdims=True) + epsilon)
    gain = gffn_ref[...]
    scaled = residual * inverse
    routed = (scaled * gain).astype(BF16)

    def share(first, whole_rows):
        for side in range(2):
            rows = whole_rows[:, side * width // 2 : (side + 1) * width // 2]
            here = slice(side * shared_ref.shape[0] // 2 + first, side * shared_ref.shape[0] // 2 + first + rows.shape[0])
            if past_ref is not None:
                rows = rows + past_ref[here, :]
            shared_ref[here, :] = rows.astype(shared_ref.dtype)

    for copy in copies[2:]:
        copy.wait()
    share(width, t_dot(logit_grad, routed))
    routed_grad = dot(logit_grad, wr_ref[...]) + input_grad
    gain_part = jnp.sum(routed_grad * scaled, axis=0, keepdims=True)
    left = shared_ref.shape[0] // 2 - width - experts
    share(width + experts, jnp.where(iota((left, width), 0) == 0, gain_part, 0.0))
    upstream = routed_grad * gain
    middle = jnp.mean(upstream * scaled, axis=-1, keepdims=True)
    residual_grad = out_grad + inverse * (upstream - scaled * middle)
    resgrad_ref[...] = residual_grad
    attended = residual_grad.astype(BF16)
    mixed_all = jnp.concatenate([mixed_ref[p] for p in range(PAIRS)], axis=1)
    share(0, t_dot(mixed_all, attended))
    mixed_grad = dot_t(attended, wo_ref[...]).astype(BF16)
    for pair in range(PAIRS):
        mgrad_ref[pair] = mixed_grad[:, pair * PAIR : (pair + 1) * PAIR]


def combine(
    batch, last, after, counts, low, high, scol, rcol, residual, probs, cot, gain_ffn, w_router, w_output, mixed, past, per, shared
):
    length, width = cot.shape[2:]
    return pl.pallas_call(
        functools.partial(combine_kernel, per, batch, len(after)),
        grid=(1,),
        in_specs=[ANYWHERE] * len(after)
        + [SCALARS, WHOLE, WHOLE, batch_block(scol, batch), batch_block(rcol, batch), ANYWHERE, WHOLE, ANYWHERE]
        + [WHOLE] * 2
        + [ANYWHERE] * (2 + len(past)),
        out_specs=[WHOLE] * 4,
        out_shape=[
            jax.ShapeDtypeStruct((length, width), BF16),
            jax.ShapeDtypeStruct((length, width), F32),
            jax.ShapeDtypeStruct((PAIRS, length, PAIR), BF16),
            jax.ShapeDtypeStruct((shared, width // 2), BF16 if last else F32),
        ],
        scratch_shapes=[
            pltpu.VMEM(residual.shape, residual.dtype),
            pltpu.VMEM((length, width), BF16),
            *(pltpu.VMEM(array.shape, array.dtype) for array in (mixed, w_output, *past)),
            pltpu.SemaphoreType.DMA((4 + len(past),)),
        ],
        compiler_params=params(60),
        cost_estimate=cost(),
    )(
        *after, counts, low, high, scol, rcol, residual, probs, cot, gain_ffn, w_router, w_output, mixed, *past
    )


def attn_back_kernel(batch, which, waits, *refs):
    refs = refs[waits:]
    len_ref, qkv_ref, lse_ref, vec_ref, sel_ref, mgrad_ref, tok_ref, gain_ref, wq_ref, wk_ref, wv_ref, *refs = refs
    past_ref = refs.pop(0) if batch else None
    if which:
        seen_ref, part_ref, resgrad_ref, *refs = refs
        shared_ref, tgrad_ref, *refs = refs
    else:
        early_ref = refs.pop(0) if batch else None
        shared_ref, diag_out_ref, part_out_ref, *refs = refs
    bands_ref, probs_ref, sgrad_ref, spread_ref, low_ref, qt_ref, kt_ref, vt_ref, diag_ref, stage_ref, rest_ref, *buffers = refs
    *buffers, sems, out_sems = buffers
    half = wq_ref.shape[0] // 2
    columns = pl.ds(which * half, half)
    fetched = [tok_ref.at[batch, 0]] + [ref.at[:, columns] for ref in (wq_ref, wk_ref, wv_ref)]
    if past_ref is not None:
        fetched.append(past_ref)
    if which:
        fetched += [part_ref, resgrad_ref]
    elif batch:
        fetched.append(early_ref)
    copies = [pltpu.make_async_copy(ref, buffer, sems.at[k]) for k, (ref, buffer) in enumerate(zip(fetched, buffers))]
    for copy in copies:
        copy.start()
    going = []
    offset = 0 if which or shared_ref.dtype == F32 else early_ref.shape[0]
    tok_ref, wq_ref, wk_ref, wv_ref, *buffers = buffers
    if past_ref is not None:
        past_ref = buffers.pop(0)
    if which:
        part_ref, resgrad_ref = buffers
    elif batch:
        early_ref = buffers[0]
    length, width = tok_ref.shape
    first_pair = which * (PAIRS // 2)
    mask = jnp.where(iota((1, length), 1) < len_ref[batch], 0.0, negative)
    lane = iota((ROWS, PAIR), 1)
    diag_ref[...] = seen_ref[...] if which else jnp.zeros_like(diag_ref)

    def one_pair(step, carry):
        pair = first_pair + step
        keys = qkv_ref[1, step]
        values = qkv_ref[2, step]
        queries_t = qkv_ref[0, step].T
        keys_t = qkv_ref[1, step].T
        grads_t = mgrad_ref[step].T
        for side in range(2):
            head = 2 * pair + side
            bands_ref[side] = band_bias(vec_ref, head)
            spread_ref[side] = jnp.zeros(spread_ref.shape[1:], F32)
            mine = (lane >= HEAD_DIM) if side else (lane < HEAD_DIM)
            for block in range(length // ROWS):
                here = slice(ROWS * block, ROWS * (block + 1))
                window = band_slice(block, length)
                queries = qkv_ref[0, step, here, :] * 0.125
                queries = jnp.where(mine, queries, jnp.zeros_like(queries))
                grads = mgrad_ref[step, here, :]
                grads = jnp.where(mine, grads, jnp.zeros_like(grads))
                column = iota((ROWS, lse_ref.shape[1]), 1)
                log_total = jnp.sum(jnp.where(column == head, lse_ref[here, :], 0.0), axis=-1, keepdims=True)
                scores = dot_t(queries, keys) + bands_ref[side, :, window] + mask
                probs = jnp.exp(scores - log_total)
                probs_ref[side, here, :] = probs.astype(BF16)
                weighted = probs * dot_t(grads, values)
                score_grad = weighted - probs * jnp.sum(weighted, axis=-1, keepdims=True)
                spread_ref[side, :, window] += score_grad
                sgrad_ref[side, here, :] = score_grad.astype(BF16)
            rows = slice(HEAD_DIM * side, HEAD_DIM * (side + 1))
            qt_ref[rows, :] = dot_t(keys_t[rows, :], sgrad_ref[side]) * 0.125
            kt_ref[rows, :] = dot(queries_t[rows, :], sgrad_ref[side]) * 0.125
            vt_ref[rows, :] = dot(grads_t[rows, :], probs_ref[side])
            size = spread_ref.shape[2]
            eight = spread_ref[side, 0:8, :]
            for move in range(8, ROWS, 8):
                eight = eight + pltpu.roll(spread_ref[side, move : move + 8, :], size - move, 1)
            diagonal = eight[0:1, :]
            for move in range(1, 8):
                diagonal = diagonal + pltpu.roll(eight[move : move + 1, :], size - move, 1)
            diag_ref[...] = jnp.where(iota(diag_ref.shape, 0) == head, diagonal, diag_ref[...])
        low_ref[0, step] = qt_ref[...].T.astype(BF16)
        low_ref[1, step] = kt_ref[...].T.astype(BF16)
        low_ref[2, step] = vt_ref[...].T.astype(BF16)
        return carry

    lax.fori_loop(0, PAIRS // 2, one_pair, 0)
    for copy in copies:
        copy.wait()

    def send(source, first, place):
        target = shared_ref.at[pl.ds(offset + first, source.shape[0])]
        going.append(pltpu.make_async_copy(source, target, out_sems.at[place]))
        going[-1].start()

    if offset:
        going.append(pltpu.make_async_copy(early_ref, shared_ref.at[pl.ds(0, offset)], out_sems.at[0]))
        going[0].start()

    def past(first, count):
        return 0.0 if past_ref is None else past_ref[first : first + count, :]

    tokens = tok_ref[...].astype(F32)
    inverse = lax.rsqrt(jnp.mean(tokens * tokens, axis=-1, keepdims=True) + epsilon)
    gain = gain_ref[...]
    scaled = tokens * inverse
    normed_t = (scaled * gain).astype(BF16).T
    normed_grad = part_ref[...] if which else jnp.zeros((length, width), F32)
    for matrix, w_ref in enumerate((wq_ref, wk_ref, wv_ref)):
        low = jnp.concatenate([low_ref[matrix, p] for p in range(PAIRS // 2)], axis=1)
        stage_ref[matrix] = (dot(normed_t, low) + past(matrix * width, width)).astype(stage_ref.dtype)
        send(stage_ref.at[matrix], matrix * width, 1 + matrix)
        normed_grad = normed_grad + dot_t(low, w_ref[...])
    left = rest_ref.shape[0]
    if which:
        gain_part = jnp.sum(normed_grad * scaled, axis=0, keepdims=True)
        bias_part = lax.dot_general(
            diag_ref[...],
            sel_ref[...],
            (((1,), (0,)), ((), ())),
            precision=lax.Precision.HIGHEST,
            preferred_element_type=F32,
        )
        row = iota((8, half), 0)
        gains = jnp.where(row == 0, gain_part[:, :half], jnp.where(row == 1, gain_part[:, half:], 0.0))
        wide = jnp.concatenate([bias_part, jnp.zeros((16, half - bias_part.shape[1]), F32)], axis=1)
        last = [gains, wide] + ([jnp.zeros((left - 24, half), F32)] if left > 24 else [])
        rest_ref[...] = (jnp.concatenate(last, axis=0) + past(3 * width, left)).astype(rest_ref.dtype)
        send(rest_ref, 3 * width, 4)
        upstream = normed_grad * gain
        middle = jnp.mean(upstream * scaled, axis=-1, keepdims=True)
        tgrad_ref[...] = (resgrad_ref[...] + inverse * (upstream - scaled * middle)).astype(BF16)
    else:
        if offset and offset + 3 * width < shared_ref.shape[0]:
            rest_ref[...] = jnp.zeros_like(rest_ref)
            send(rest_ref, 3 * width, 4)
        diag_out_ref[...] = diag_ref[...]
        part_out_ref[...] = normed_grad
    for copy in going:
        copy.wait()


def attention_backward(batch, which, last, after, counts, qkv, lse, vector, selector, mixed_grad, tokens, gain, wq, wk, wv, past, more, rows):
    length, width = tokens.shape[2:]
    half = width // 2
    size = vector.shape[-1]
    late = (*past, *(more[1:] if which else more))
    buffers = [((length, width), BF16)] + [((width, half), BF16)] * 3 + [(array.shape, array.dtype) for array in late]
    sent = 0 if which or not last else more[0].shape[0]
    rest = max(rows - sent - 3 * width, 16)
    shared = jax.ShapeDtypeStruct((rows, half), BF16 if last else F32)
    if which:
        outs = [shared, jax.ShapeDtypeStruct((length, width), BF16)]
    else:
        outs = [shared, jax.ShapeDtypeStruct((16, size), F32), jax.ShapeDtypeStruct((length, width), F32)]
    return pl.pallas_call(
        functools.partial(attn_back_kernel, batch, which, len(after)),
        grid=(1,),
        in_specs=[ANYWHERE] * len(after)
        + [SCALARS, pl.BlockSpec((3, PAIRS // 2, length, PAIR), lambda _: (0, which, 0, 0))]
        + [WHOLE] * 3
        + [pl.BlockSpec((PAIRS // 2, length, PAIR), lambda _: (which, 0, 0))]
        + [ANYWHERE, WHOLE]
        + [ANYWHERE] * (3 + len(past))
        + [WHOLE if which and k == 0 else ANYWHERE for k in range(len(more))],
        out_specs=[ANYWHERE] + [WHOLE] * (len(outs) - 1),
        out_shape=outs,
        scratch_shapes=[
            pltpu.VMEM((2, ROWS, size), F32),
            pltpu.VMEM((2, length, length), BF16),
            pltpu.VMEM((2, length, length), BF16),
            pltpu.VMEM((2, ROWS, size), F32),
            pltpu.VMEM((3, PAIRS // 2, length, PAIR), BF16),
            pltpu.VMEM((PAIR, length), F32),
            pltpu.VMEM((PAIR, length), F32),
            pltpu.VMEM((PAIR, length), F32),
            pltpu.VMEM((16, size), F32),
            pltpu.VMEM((3, width, half), shared.dtype),
            pltpu.VMEM((rest, half), shared.dtype),
            *(pltpu.VMEM(shape, kind) for shape, kind in buffers),
            pltpu.SemaphoreType.DMA((len(buffers),)),
            pltpu.SemaphoreType.DMA((5,)),
        ],
        compiler_params=params(60),
        cost_estimate=cost(),
    )(*after, counts, qkv, lse, vector, selector, mixed_grad, tokens, gain, wq, wk, wv, *past, *more)


def unpack_kernel(early, side_ref, first_ref, first_other_ref, second_ref, second_other_ref, *refs):
    q_ref, k_ref, v_ref, output_ref, router_ref, gain_f_ref, gain_a_ref, bias_ref = refs
    swapped = side_ref[0] == 1

    def whole(mine_ref, other_ref):
        mine, other = mine_ref[...], other_ref[...]
        parts = [jnp.where(swapped, other, mine), jnp.where(swapped, mine, other)]
        return jnp.concatenate(parts, axis=0).astype(F32)

    rows = whole(first_ref, first_other_ref)
    width = 2 * rows.shape[1]
    half = rows.shape[1]
    last = early - 16
    output_ref[...] = jnp.concatenate([rows[:width], rows[early : early + width]], axis=1)
    router_ref[...] = jnp.concatenate([rows[width:last], rows[early + width : early + last]], axis=1)
    gain_f_ref[...] = jnp.concatenate([rows[last], rows[early + last]])
    for k, ref in enumerate((q_ref, k_ref, v_ref)):
        ref[:, :half] = rows[2 * early + k * width : 2 * early + (k + 1) * width]
    rows = whole(second_ref, second_other_ref)
    gain_a_ref[...] = jnp.concatenate([rows[3 * width], rows[3 * width + 1]])
    bias_ref[...] = rows[3 * width + 8 : 3 * width + 8 + HEADS, :BUCKETS]
    for k, ref in enumerate((q_ref, k_ref, v_ref)):
        ref[:, half:] = rows[k * width : (k + 1) * width]


def unpack(early, experts, side, first, first_other, second, second_other):
    width = 2 * first.shape[1]
    matrix = jax.ShapeDtypeStruct((width, width), F32)
    line = jax.ShapeDtypeStruct((width,), F32)
    return pl.pallas_call(
        functools.partial(unpack_kernel, early),
        in_specs=[SCALARS] + [WHOLE] * 4,
        out_specs=[WHOLE] * 8,
        out_shape=[matrix] * 4
        + [jax.ShapeDtypeStruct((experts, width), F32), line, line, jax.ShapeDtypeStruct((HEADS, BUCKETS), F32)],
        compiler_params=params(60),
        cost_estimate=cost(),
    )(side, first, first_other, second, second_other)


def upward(planes, first, last):
    return [(k, k + 1) for k in range(first, last)]


def downward(planes, first, last):
    return [(planes - 1 - k, planes - 2 - k) for k in range(first, last)]


def mix_kernel(both, planes, step, waits, here_ref, up_ref, down_ref, upsum_ref, downsum_ref, *refs):
    to_up, to_down = refs[waits:]
    for moving, sums, out, place in (
        (up_ref, upsum_ref, to_up, here_ref[0]),
        (down_ref, downsum_ref, to_down, planes - 1 - here_ref[0]),
    ):
        total = moving[...] + sums[...]
        out[...] = jnp.where(place <= step, total, moving[...]) if both else total


def mix(both, planes, step, here, up, down, upsum, downsum, after):
    kinds, rows, width = up.shape
    block = pl.BlockSpec((1, rows // 2, width), lambda i, j: (i, j, 0))
    return pl.pallas_call(
        functools.partial(mix_kernel, both, planes, step, len(after)),
        grid=(kinds, 2),
        in_specs=[SCALARS] + [block] * 4 + [ANYWHERE] * len(after),
        out_specs=[block] * 2,
        out_shape=[jax.ShapeDtypeStruct(up.shape, BF16)] * 2,
        compiler_params=params(32),
        cost_estimate=cost(),
    )(here, up, down, upsum, downsum, *after)


def gate_kernel(*refs):
    pass


def gate(arrays, after):
    count = len(arrays)
    return pl.pallas_call(
        gate_kernel,
        in_specs=[ANYWHERE] * (count + len(after)),
        out_specs=[ANYWHERE] * count,
        out_shape=[jax.ShapeDtypeStruct(array.shape, array.dtype) for array in arrays],
        input_output_aliases={k: k for k in range(count)},
        cost_estimate=cost(),
    )(*arrays, *after)


class Chain:
    def __init__(self, planes, own=None, sums=None):
        self.planes, self.own, self.sums = planes, own, sums
        self.here = lax.axis_index("hidden")[None]
        self.from_below, self.from_above = [], []
        if own is not None:
            self.up = self.down = own
        else:
            self.up, self.down = sums[planes - 1], sums[1]
        self.count = 0
        self.steps = planes if own is not None and sums is not None else planes - 1

    def send(self):
        planes, s = self.planes, self.count
        if self.own is not None and self.sums is not None:
            first, last = 0, planes - 1
        elif self.own is not None:
            first, last = s, planes - 1
        else:
            first, last = 0, s + 1
        self.up = lax.ppermute(self.up, "hidden", upward(planes, first, last))
        self.down = lax.ppermute(self.down, "hidden", downward(planes, first, last))
        self.count += 1
        if self.own is not None and s < planes - 1:
            self.from_below.append(self.up)
            self.from_above.append(self.down)

    def mix(self, *after):
        planes, s = self.planes, self.count - 1
        both = self.own is not None
        offset = 1 if both else 2
        self.up, self.down = mix(
            both, planes, s, self.here, self.up, self.down, self.sums[planes - offset - s], self.sums[s + offset], after
        )
        self.mixed = self.up

    def gate(self, *after):
        self.up, self.down = gate((self.up, self.down), after)
        self.from_below[-1], self.from_above[-1] = self.up, self.down

    def run(self):
        while self.count < self.steps:
            self.send()
        return self

    def gathered(self):
        return (self.own, *self.from_above, *self.from_below)

    def scattered(self):
        return (self.sums[0], self.up, self.down)


def swap(values, axis, distance):
    return lax.ppermute(values, axis, [(k, k ^ distance) for k in range(lax.axis_size(axis))])


def share_sums(values, axis, near, count):
    me = lax.axis_index(axis) // near
    parts = values.reshape(count, values.shape[0] // count, values.shape[1])
    total = lax.dynamic_index_in_dim(parts, me, 0, keepdims=False).astype(F32)
    for k in range(1, count):
        part = lax.dynamic_index_in_dim(parts, me ^ k, 0, keepdims=False)
        total = total + swap(part, axis, k * near).astype(F32)
    return total.astype(BF16)


def join_sums(values, axis, near, count):
    me = lax.axis_index(axis) // near
    found = [values] + [swap(values, axis, k * near) for k in range(1, count)]
    joined = []
    for j in range(count):
        piece = found[count - 1]
        for k in range(count - 2, -1, -1):
            piece = jnp.where(me ^ k == j, found[k], piece)
        joined.append(piece)
    return jnp.concatenate(joined)


def sum_everywhere(values):
    size = lax.axis_size("expert")
    planes = lax.axis_size("hidden")
    values = share_sums(values, "expert", 2, size // 2)
    values = share_sums(values, "hidden", 1, planes)
    values = join_sums(values, "hidden", 1, planes)
    values = join_sums(values, "expert", 2, size // 2)
    return values, swap(values, "expert", 1)


def share_half(values):
    side = lax.axis_index("expert") % 2
    parts = values.reshape(2, values.shape[0] // 2, values.shape[1])
    mine = lax.dynamic_index_in_dim(parts, side, 0, keepdims=False)
    other = lax.dynamic_index_in_dim(parts, 1 - side, 0, keepdims=False)
    return mine + swap(other, "expert", 1)


def offset_selector(length):
    place = np.arange(2 * length)
    offsets = np.where(place < 2 * length - ROWS, place, place - 2 * length) - (length - ROWS)
    offsets = np.clip(offsets, -(length - 1), length - 1)
    return (offset_bucket(offsets)[:, None] == np.arange(BUCKETS)[None, :]).astype(np.float32)


def shards(
    tokens,
    cotangent,
    lengths,
    routes,
    gain_attn,
    w_query,
    w_key,
    w_value,
    w_output,
    bucket_head_bias,
    gain_ffn,
    w_router,
    w_inner,
    w_outer,
):
    batches, _, length, width = tokens.shape
    experts = w_router.shape[1]
    local = w_inner.shape[0]
    groups = lax.axis_size("expert")
    planes = lax.axis_size("hidden")
    capacity = (5 * length + 4 * experts - 1) // (4 * experts)
    per = local * capacity
    rows = groups * capacity
    message = padded(per)
    in_groups = (groups, capacity, message)
    selector = jnp.asarray(offset_selector(length))
    vector = lax.dot_general(
        bucket_head_bias, selector, (((0,), (1,)), ((), ())), precision=lax.Precision.HIGHEST
    )[:, None, :]
    gain_a = gain_attn[None, :]
    gain_f = gain_ffn[None, :]
    router_rows = w_router.T
    counts = lengths[:, 0]
    plane = lax.axis_index("hidden")[None]

    def to_groups(values):
        return lax.all_to_all(values, "expert", split_axis=0, concat_axis=0, tiled=True)

    def leaving(values, *after):
        return regroup(False, [to_groups(values)], (2, local // 2 * rows, width), 2, local // 2, *in_groups, after)

    def returning(chain, *after):
        shape = (groups, message, width)
        return regroup(True, chain.scattered(), shape, 2, local // 2, *in_groups, after)

    def arriving(chain, *after):
        return to_groups(returning(chain, *after))

    def attend(b, *after):
        return attention_forward(b, after, counts, tokens, gain_a, w_query, w_key, w_value, vector)

    def routing(b, *after):
        return route(
            b, after, tokens, cotangent, forward[b][1], w_output, gain_f, router_rows, srow, rcol, groups, per, b > 0
        )

    srow, scol, cot_slots = prep(counts, routes.reshape(batches, length), cotangent, groups, per, capacity)
    rcol = routes.reshape(batches, length, 1)
    early_rows = width + experts + 16
    unit = 16 * groups * planes
    first_rows = 2 * early_rows + 3 * width
    first_rows = first_rows + -first_rows % unit
    second_rows = 3 * width + 24
    second_rows = second_rows + -second_rows % unit
    kept, layer_rows, token_grads = [], [], []
    early_part, first_part, second_part = (), (), ()

    def back_tokens(b, after, low, high):
        return combine(
            b,
            b + 1 == batches,
            after,
            counts,
            low,
            high,
            scol,
            rcol,
            *routed[b][:2],
            cotangent,
            gain_f,
            router_rows,
            w_output,
            forward[b][1],
            early_part,
            per,
            2 * early_rows,
        )

    def back_half(b, which, after, mixed_grad, more):
        qkv, _, lse = forward[b]
        last = b + 1 == batches
        return attention_backward(
            b,
            which,
            last,
            after,
            counts,
            qkv,
            lse,
            vector,
            selector,
            mixed_grad,
            tokens,
            gain_a,
            w_query,
            w_key,
            w_value,
            second_part if which else first_part,
            more,
            second_rows if which else first_rows if last else 3 * width,
        )

    def grads_half(h, after, past):
        return expert_grads(h, after, past, local, *([k[h][part] for k in kept] for part in (2, 3, 0, 1)))

    forward = [attend(0, cot_slots)]
    routed = [routing(0)]
    grads = regroup(False, [to_groups(cot_slots)], (local * rows, width), 1, local, *in_groups, (routed[0][2],))
    grad_chain = Chain(planes, grads)
    grad_chain.send()
    inputs = regroup_gated(to_groups(routed[0][2]), local * rows, capacity, (grads,))
    input_chain = Chain(planes, inputs)
    input_chain.send()
    forward.append(attend(1, inputs, grad_chain.up, grad_chain.down))
    grad_chain.send()
    routed.append(routing(1, grad_chain.up, grad_chain.down))
    grad_chain.run()
    input_chain.gate(forward[1][1])
    input_chain.send()
    held = (input_chain.up, input_chain.down, grad_chain.up, grad_chain.down)
    input_chain.run()
    halves = range(2)
    chains = [None, None]
    for b in range(batches):
        last = b + 1 == batches
        before = chains
        messages = [None, None]
        ready = ()
        if not last:
            if b:
                forward.append(attend(b + 1))
                routed.append(routing(b + 1))
            messages = [leaving(m, *held) for m in routed[b + 1][2:]]
            held = ()
            ready = tuple(messages)
        chains, worked = [], []
        for h in halves:
            if b == 0:
                done = experts_half(
                    h, ready, plane, None, w_inner, w_outer, input_chain.gathered(), grad_chain.gathered()
                )
            else:
                before[h].mix(*(w[0] for w in worked))
                tied = (before[h].up, before[h].down)
                if h:
                    tied += (before[0].up, before[0].down)
                done = experts_half(h, ready + tied, plane, before[h].gathered(), w_inner, w_outer)
                before[h].send()
            worked.append(done)
            chains.append(Chain(planes, messages[h], done[:planes]))
            chains[h].send()
        kept.append([w[planes:] for w in worked])
        low_chain, high_chain = chains
        if not last:
            for step in range(1, planes):
                for chain in chains:
                    if step > 1:
                        chain.send()
                    if step < planes - 1:
                        chain.mix()
            if b == 0:
                continue
            low, high = (arriving(chain) for chain in before)
            layer, res_grad, mixed_grad, early_part = back_tokens(b - 1, (), low, high)
            first_part, *more = back_half(b - 1, 0, (), mixed_grad, (early_part,) if b > 1 else ())
            second_part, token_grad = back_half(b - 1, 1, (), mixed_grad, (*more, res_grad))
        else:
            low = arriving(before[0], before[1].up, before[1].down)
            high = arriving(before[1])
            low_chain.mix()
            low_chain.send()
            totals = grads_half(0, (low_chain.mixed,), ())
            high_chain.mix(totals[0])
            high_chain.send()
            low_chain.mix(high)
            low_chain.send()
            layer, res_grad, mixed_grad, early_part = back_tokens(b - 1, (low_chain.mixed,), low, high)
            high_chain.mix(mixed_grad)
            high_chain.send()
            first_part, *more = back_half(
                b - 1, 0, (high_chain.mixed,), mixed_grad, (early_part,) if b > 1 else ()
            )
            low = returning(low_chain, first_part)
            second_part, token_grad = back_half(b - 1, 1, (low,), mixed_grad, (*more, res_grad))
            low = to_groups(low)
            high = returning(high_chain, second_part, low)
            totals = grads_half(1, (high,), totals)
            high = to_groups(high)
        layer_rows.append(layer)
        token_grads.append(token_grad)
        early_part, first_part, second_part = (early_part,), (first_part,), (second_part,)
    layer, res_grad, mixed_grad, early_part = back_tokens(batches - 1, (totals[0],), low, high)
    first_part, *more = back_half(batches - 1, 0, (), mixed_grad, (early_part,))
    side = (lax.axis_index("expert") % 2)[None]
    first_half = share_half(first_part)
    second_part, token_grad = back_half(batches - 1, 1, (first_half,), mixed_grad, (*more, res_grad))
    mine, other = sum_everywhere(first_half)
    mine_second, other_second = sum_everywhere(share_half(second_part))
    layer_rows.append(layer)
    token_grads.append(token_grad)
    query_grad, key_grad, value_grad, output_grad, router_grad, gain_f_grad, gain_a_grad, bias_grad = unpack(
        early_rows, experts, side, mine, other, mine_second, other_second
    )
    return (
        jnp.stack(layer_rows)[:, None],
        jnp.stack(token_grads)[:, None],
        gain_a_grad,
        query_grad,
        key_grad,
        value_grad,
        output_grad,
        bias_grad.T,
        gain_f_grad,
        router_grad.T,
        totals[1],
        totals[0],
    )


def solution(mesh):
    token = P(None, ("expert", "hidden"), None, None)
    placed = (
        token,
        token,
        P(None, ("expert", "hidden")),
        token,
        *(P() for _ in range(8)),
        P("expert", None, "hidden"),
        P("expert", "hidden", None),
    )
    return jax.shard_map(
        shards,
        mesh=mesh,
        in_specs=placed,
        out_specs=(
            token,
            token,
            *(P() for _ in range(8)),
            P("expert", None, "hidden"),
            P("expert", "hidden", None),
        ),
        check_vma=False,
    )
```

```python
import functools

import jax
import jax.numpy as jnp
import numpy as np
from jax import lax
from jax.experimental import pallas as pl
from jax.experimental.pallas import tpu as pltpu
from jax.sharding import PartitionSpec as P

HEADS = 12
HEAD_DIM = 64
BUCKETS = 32
MAXDIST = 128
PAIR = 2 * HEAD_DIM
PAIRS = HEADS // 2
ROWS = 128

epsilon = 1e-06
negative = -1e30
F32 = jnp.float32
BF16 = jnp.bfloat16
MIB = 1 << 20


def params(mib):
    return pltpu.CompilerParams(vmem_limit_bytes=mib * MIB)


def cost():
    return pl.CostEstimate(flops=1, bytes_accessed=1, transcendentals=0)


def offset_bucket(offsets):
    halfway = BUCKETS // 2
    exact_count = halfway // 2
    relative_distance = np.abs(offsets)
    scaled = (
        np.log(np.maximum(relative_distance, 1) / exact_count)
        / np.log(MAXDIST / exact_count)
        * (halfway - exact_count)
    )
    far_bucket = np.minimum(exact_count + np.floor(scaled).astype(np.int64), halfway - 1)
    near_bucket = np.where(relative_distance < exact_count, relative_distance, far_bucket)
    return (np.where(offsets > 0, halfway, 0) + near_bucket).astype(np.int32)


def dot(a, b):
    return lax.dot_general(a, b, (((1,), (0,)), ((), ())), preferred_element_type=F32)


def dot_t(a, b):
    return lax.dot_general(a, b, (((1,), (1,)), ((), ())), preferred_element_type=F32)


def t_dot(a, b):
    return lax.dot_general(a, b, (((0,), (0,)), ((), ())), preferred_element_type=F32)


def one_hot(condition):
    return jnp.where(condition, 1.0, 0.0).astype(BF16)


def batch_block(array, b):
    rest = array.shape[1:]
    return pl.BlockSpec((1,) + rest, lambda *_: (b,) + (0,) * len(rest))


ANYWHERE = pl.BlockSpec(memory_space=pl.ANY)
WHOLE = pl.BlockSpec(memory_space=pltpu.VMEM)
SCALARS = pl.BlockSpec(memory_space=pltpu.SMEM)


def iota(shape, axis):
    return lax.broadcasted_iota(jnp.int32, shape, axis)


def padded(rows):
    return -(-rows // 16) * 16


def spread_slots(slot, per, message, first=0, last=None):
    last = per if last is None else last
    group = lax.div(jnp.maximum(slot, 0), per)
    inside = slot - group * per
    held = (slot >= 0) & (inside >= first) & (inside < last)
    return jnp.where(held, group * message + inside - first, -1)


def prep_kernel(per, capacity, len_ref, row_ref, col_ref, cot_ref, srow_ref, scol_ref, slots_ref):
    batches, _, length = row_ref.shape
    groups, message, width = slots_ref.shape
    experts = groups * per // capacity
    before = one_hot(iota((length, length), 0) < iota((length, length), 1))
    after = one_hot(iota((length, length), 1) < iota((length, length), 0))
    for b in range(batches):
        count = len_ref[b]
        row = row_ref[b]
        col = col_ref[b]
        valid_row = iota((1, length), 1) < count
        valid_col = iota((length, 1), 0) < count
        chosen_row = iota((experts, length), 0) == row
        chosen_col = iota((length, experts), 1) == col
        earlier_row = dot(one_hot(chosen_row & valid_row), before)
        rank_row = jnp.sum(jnp.where(chosen_row, earlier_row, 0.0), axis=0, keepdims=True).astype(jnp.int32)
        earlier_col = dot(after, one_hot(chosen_col & valid_col))
        rank_col = jnp.sum(jnp.where(chosen_col, earlier_col, 0.0), axis=1, keepdims=True).astype(jnp.int32)
        slot_row = jnp.where(valid_row & (rank_row < capacity), row * capacity + rank_row, -1)
        srow_ref[b] = slot_row
        scol_ref[b] = jnp.where(valid_col & (rank_col < capacity), col * capacity + rank_col, -1)
        if b == 0:
            dispatch = one_hot(iota((groups * message, length), 0) == spread_slots(slot_row, per, message))
            slots_ref[...] = dot(dispatch, cot_ref[0, 0]).astype(BF16).reshape(groups, message, width)


def prep(lengths, routes, cot, groups, per, capacity):
    batches, length = routes.shape
    width = cot.shape[-1]
    vmem = WHOLE
    message = padded(per)
    return pl.pallas_call(
        functools.partial(prep_kernel, per, capacity),
        grid=(1,),
        in_specs=[SCALARS, vmem, vmem, batch_block(cot, 0)],
        out_specs=[vmem] * 3,
        out_shape=[
            jax.ShapeDtypeStruct((batches, 1, length), jnp.int32),
            jax.ShapeDtypeStruct((batches, length, 1), jnp.int32),
            jax.ShapeDtypeStruct((groups, message, width), BF16),
        ],
        compiler_params=params(60),
        cost_estimate=cost(),
    )(lengths, routes.reshape(batches, 1, length), routes.reshape(batches, length, 1), cot)


def slot_places(kinds, local, groups, capacity, message):
    row = iota((1, kinds * local * groups * capacity), 1)
    slot = lax.rem(row, capacity)
    row = lax.div(row, capacity)
    group = lax.rem(row, groups)
    return group * message + lax.div(row, groups) * capacity + slot


def regroup_kernel(back, kinds, local, groups, capacity, message, waits, *refs):
    refs = refs[waits:]
    out_ref = refs[-1]
    total = refs[0][...].astype(F32)
    for ref in refs[1:-1]:
        total = total + ref[...].astype(F32)
    places = slot_places(kinds, local, groups, capacity, message)
    move = one_hot(iota((groups * message, places.shape[1]), 0) == places)
    if back:
        rows = dot(move, total.astype(BF16).reshape(places.shape[1], -1))
    else:
        rows = t_dot(move, total.astype(BF16).reshape(groups * message, -1))
    out_ref[...] = rows.astype(BF16).reshape(out_ref.shape)


def regroup(back, arrays, shape, kinds, local, groups, capacity, message, after=()):
    return pl.pallas_call(
        functools.partial(regroup_kernel, back, kinds, local, groups, capacity, message, len(after)),
        in_specs=[ANYWHERE] * len(after) + [WHOLE] * len(arrays),
        out_specs=WHOLE,
        out_shape=jax.ShapeDtypeStruct(shape, BF16),
        compiler_params=params(60),
        cost_estimate=cost(),
    )(*after, *arrays)


def regroup_gated_kernel(capacity, *refs):
    in_ref, out_ref = refs[-2:]
    groups, message, width = in_ref.shape
    total = out_ref.shape[0] - 16
    local = total // (groups * capacity)
    rows = groups * capacity
    flat = in_ref[...].reshape(groups * message, width)
    places = slot_places(1, local, groups, capacity, message)
    move = one_hot(iota((groups * message, total), 0) == places)
    out_ref[:total, :] = t_dot(move, flat).astype(BF16)
    place = iota((message, 128), 0)
    lane = iota((message, 128), 1)
    columns = []
    for g in range(groups):
        gates = in_ref[g, message - 16 : message, :].astype(F32)[0:1, :]
        parts = [
            jnp.sum(jnp.where(place == lane, gates[:, 128 * k : 128 * (k + 1)], 0.0), axis=1, keepdims=True)
            for k in range(3)
        ]
        wide = iota((message, 128), 1)
        columns.append(jnp.where(wide == 0, parts[0], jnp.where(wide == 1, parts[1], jnp.where(wide == 2, parts[2], 0.0))))
    column = jnp.concatenate(columns, axis=0).astype(BF16)
    moved = t_dot(move, column)
    place = iota((rows, 128), 0)
    lane = iota((rows, 128), 1)
    lines = []
    for l in range(local):
        mine = moved[l * rows : (l + 1) * rows, :]
        parts = [
            jnp.sum(jnp.where(place == lane, mine[:, k : k + 1], 0.0), axis=0, keepdims=True) for k in range(3)
        ]
        lines.append(jnp.concatenate(parts + [jnp.zeros((1, width - 384), F32)], axis=1))
    lines.append(jnp.zeros((16 - local, width), F32))
    out_ref[total:, :] = jnp.concatenate(lines, axis=0).astype(BF16)


def regroup_gated(slots, rows, capacity, after=()):
    width = slots.shape[-1]
    return pl.pallas_call(
        functools.partial(regroup_gated_kernel, capacity),
        in_specs=[ANYWHERE] * len(after) + [WHOLE],
        out_specs=WHOLE,
        out_shape=jax.ShapeDtypeStruct((rows + 16, width), BF16),
        compiler_params=params(60),
        cost_estimate=cost(),
    )(*after, slots)


def band_bias(vector_ref, head):
    wide = jnp.broadcast_to(vector_ref[head], (ROWS, vector_ref.shape[-1]))
    return pltpu.roll(wide, 0, 1, stride=1, stride_axis=0)


def band_slice(block, length):
    start = length - ROWS * (block + 1)
    return slice(start, start + length)


def attn_kernel(batch, waits, *refs):
    refs = refs[waits:]
    len_ref, tok_ref, gain_ref, wq_ref, wk_ref, wv_ref, vec_ref, qkv_ref, mixed_ref, lse_ref, bands_ref, probs_ref, mixed_t_ref = refs
    length, width = tok_ref.shape[2:]
    count = len_ref[batch]
    tokens = tok_ref[0, 0].astype(F32)
    inverse = lax.rsqrt(jnp.mean(tokens * tokens, axis=-1, keepdims=True) + epsilon)
    normed = (tokens * inverse * gain_ref[...]).astype(BF16)
    for which, w_ref in enumerate((wq_ref, wk_ref, wv_ref)):
        for part in range(width // 256):
            rows = dot(normed, w_ref[:, 256 * part : 256 * part + 256]).astype(BF16)
            qkv_ref[which, 2 * part] = rows[:, :PAIR]
            qkv_ref[which, 2 * part + 1] = rows[:, PAIR:]
    mask = jnp.where(iota((1, length), 1) < count, 0.0, negative)
    lane = iota((ROWS, PAIR), 1)
    lse_ref[...] = jnp.zeros_like(lse_ref)

    def one_pair(pair, carry):
        keys = qkv_ref[1, pair]
        values_t = qkv_ref[2, pair].T
        for side in range(2):
            head = 2 * pair + side
            bands_ref[side] = band_bias(vec_ref, head)
            mine = (lane >= HEAD_DIM) if side else (lane < HEAD_DIM)
            for block in range(length // ROWS):
                here = slice(ROWS * block, ROWS * (block + 1))
                queries = qkv_ref[0, pair, here, :] * 0.125
                queries = jnp.where(mine, queries, jnp.zeros_like(queries))
                scores = dot_t(queries, keys) + bands_ref[side, :, band_slice(block, length)] + mask
                highest = jnp.max(scores, axis=-1, keepdims=True)
                powers = jnp.exp(scores - highest)
                total = jnp.sum(powers, axis=-1, keepdims=True)
                probs_ref[side, here, :] = (powers * (1.0 / total)).astype(BF16)
                column = iota((ROWS, lse_ref.shape[1]), 1)
                lse_ref[here, :] = jnp.where(column == head, highest + jnp.log(total), lse_ref[here, :])
            rows = slice(HEAD_DIM * side, HEAD_DIM * (side + 1))
            mixed_t_ref[rows, :] = dot_t(values_t[rows, :], probs_ref[side])
        mixed_ref[pair] = mixed_t_ref[...].T.astype(BF16)
        return carry

    lax.fori_loop(0, PAIRS, one_pair, 0)


def attention_forward(batch, after, counts, tokens, gain, wq, wk, wv, vector):
    length = tokens.shape[2]
    return pl.pallas_call(
        functools.partial(attn_kernel, batch, len(after)),
        grid=(1,),
        in_specs=[ANYWHERE] * len(after) + [SCALARS, batch_block(tokens, batch)] + [WHOLE] * 5,
        out_specs=[WHOLE] * 3,
        out_shape=[
            jax.ShapeDtypeStruct((3, PAIRS, length, PAIR), BF16),
            jax.ShapeDtypeStruct((PAIRS, length, PAIR), BF16),
            jax.ShapeDtypeStruct((length, 128), F32),
        ],
        scratch_shapes=[
            pltpu.VMEM((2, ROWS, vector.shape[-1]), F32),
            pltpu.VMEM((2, length, length), BF16),
            pltpu.VMEM((PAIR, length), F32),
        ],
        compiler_params=params(60),
        cost_estimate=cost(),
    )(*after, counts, tokens, gain, wq, wk, wv, vector)


def route_kernel(per, gated, waits, *refs):
    refs = refs[waits:]
    tok_ref, cot_ref, mixed_ref, wo_ref, gffn_ref, wr_ref, srow_ref, rcol_ref, res_ref, probs_ref, *out_refs = refs
    length, width = tok_ref.shape[2:]
    mixed_all = jnp.concatenate([mixed_ref[p] for p in range(PAIRS)], axis=1)
    residual = tok_ref[0, 0].astype(F32) + dot(mixed_all, wo_ref[...])
    res_ref[...] = residual
    inverse = lax.rsqrt(jnp.mean(residual * residual, axis=-1, keepdims=True) + epsilon)
    routed = (residual * inverse * gffn_ref[...]).astype(BF16)
    logits = dot_t(routed, wr_ref[...])
    powers = jnp.exp(logits - jnp.max(logits, axis=-1, keepdims=True))
    probs = powers / jnp.sum(powers, axis=-1, keepdims=True)
    probs_ref[...] = probs
    gate = jnp.sum(jnp.where(iota(probs.shape, 1) == rcol_ref[0], probs, 0.0), axis=-1, keepdims=True)
    groups, message, _ = out_refs[0].shape
    places = iota((groups * message, length), 0)
    if gated:
        grads = (gate * cot_ref[0, 0].astype(F32)).astype(BF16)
        half = per // 2
        for which, out_ref in enumerate(out_refs):
            place = spread_slots(srow_ref[0], per, message, which * half, (which + 1) * half)
            rows = dot(one_hot(places == place), grads)
            rows = rows + dot(one_hot(places == jnp.where(place < 0, -1, place + half)), routed)
            out_ref[...] = rows.astype(BF16).reshape(out_ref.shape)
        return
    slots_ref = out_refs[0]
    dispatch = one_hot(places == spread_slots(srow_ref[0], per, message))
    slots_ref[...] = dot(dispatch, routed).astype(BF16).reshape(slots_ref.shape)
    first = gate.astype(BF16).astype(F32)
    second = (gate - first).astype(BF16).astype(F32)
    third = gate - first - second
    column = iota((length, PAIR), 1)
    pieces = jnp.where(column == 0, first, jnp.where(column == 1, second, jnp.where(column == 2, third, 0.0)))
    sorted_gates = dot(dispatch, pieces.astype(BF16))
    data = message - 16
    place = iota((data, 128), 0)
    lane = iota((data, 128), 1)
    for g in range(groups):
        mine = sorted_gates[g * message : g * message + data, :]
        parts = [
            jnp.sum(jnp.where(place == lane, mine[:, k : k + 1], 0.0), axis=0, keepdims=True) for k in range(3)
        ]
        line = jnp.concatenate(parts + [jnp.zeros((1, width - 384), F32)], axis=1)
        slots_ref[g, data:message, :] = jnp.broadcast_to(line, (16, width)).astype(BF16)


def route(batch, after, tokens, cot, mixed, wo, gain_ffn, w_router, srow, rcol, groups, per, gated):
    length, width = tokens.shape[2:]
    experts = w_router.shape[0]
    message = padded(per) if gated else padded(per) + 16
    return pl.pallas_call(
        functools.partial(route_kernel, per, gated, len(after)),
        grid=(1,),
        in_specs=[ANYWHERE] * len(after)
        + [batch_block(tokens, batch), batch_block(cot, batch)]
        + [WHOLE] * 4
        + [batch_block(srow, batch), batch_block(rcol, batch)],
        out_specs=[WHOLE] * (4 if gated else 3),
        out_shape=[
            jax.ShapeDtypeStruct((length, width), F32),
            jax.ShapeDtypeStruct((length, experts), F32),
        ]
        + [jax.ShapeDtypeStruct((groups, message, width), BF16)] * (2 if gated else 1),
        compiler_params=params(60),
        cost_estimate=cost(),
    )(*after, tokens, cot, mixed, wo, gain_ffn, w_router, srow, rcol)


GELU_SCALE = 0.7978845608028654
GELU_CUBIC = 0.044715


def expert_kernel(planes, gated, first_expert, waits, *refs):
    pieces = 2 * planes - 1
    refs = refs[waits:]
    plane = refs[0][0]
    x_refs, refs = refs[1 : 1 + pieces], refs[1 + pieces :]
    c_refs, refs = refs[:pieces], refs[pieces:]
    gate_refs = ()
    if not gated:
        gate_refs, refs = refs[:pieces], refs[pieces:]
    wi_ref, wo_ref, *refs = refs
    sum_refs = refs[:planes]
    act_ref, pre_ref, x_ref, c_ref = refs[planes:]
    rows = x_refs[0].shape[0]

    def assemble(parts):
        found = [parts[0][...]]
        for k in range(1, planes):
            from_above = plane + k < planes
            found.append(jnp.where(from_above, parts[k][...], parts[2 * planes - 1 - k][...]))
        return found

    inputs = jnp.concatenate(assemble(x_refs), axis=0)
    grads = assemble(c_refs)
    if not gated:
        place = iota((rows, 128), 0)
        lane = iota((rows, 128), 1)
        expert = first_expert + pl.program_id(0)
        for k, lines in enumerate(assemble(gate_refs)):
            lines = jnp.where(iota(lines.shape, 0) == expert, lines.astype(F32), 0.0)
            line = jnp.sum(lines, axis=0, keepdims=True)
            line = line[:, :128] + line[:, 128:256] + line[:, 256:384]
            gate = jnp.sum(jnp.where(place == lane, line, 0.0), axis=1, keepdims=True)
            grads[k] = (grads[k].astype(F32) * gate).astype(BF16)
    grads = jnp.concatenate(grads, axis=0)
    x_ref[0] = inputs
    c_ref[0] = grads
    pre = dot(inputs, wi_ref[0])
    square = pre * pre
    curve = jnp.tanh(GELU_SCALE * pre * (1.0 + GELU_CUBIC * square))
    half = 0.5 * (1.0 + curve)
    act = (pre * half).astype(BF16)
    slope = half + 0.5 * pre * (1.0 - curve * curve) * (GELU_SCALE * (1.0 + 3.0 * GELU_CUBIC * square))
    act_ref[0] = act
    outs = dot(act, wo_ref[0]).astype(BF16)
    pre_grad = (slope * dot_t(grads, wo_ref[0])).astype(BF16)
    pre_ref[0] = pre_grad
    ins = dot_t(pre_grad, wi_ref[0]).astype(BF16)
    for k in range(planes):
        sum_refs[k][0] = outs[k * rows : (k + 1) * rows]
        sum_refs[k][1] = ins[k * rows : (k + 1) * rows]


def experts_half(which, after, plane, messages, w_inner, w_outer, xs=None, cs=None):
    local, width, hidden = w_inner.shape
    mine = local // 2
    first = which * mine
    gated = messages is not None
    pieces = len(messages if gated else xs)
    planes = (pieces + 1) // 2
    if gated:
        rows = messages[0].shape[1] // mine
        x_block = pl.BlockSpec((None, rows, width), lambda e: (1, e, 0))
        c_block = pl.BlockSpec((None, rows, width), lambda e: (0, e, 0))
        arrays = (*messages, *messages)
        blocks = [x_block] * pieces + [c_block] * pieces
    else:
        rows = cs[0].shape[0] // local
        slab = pl.BlockSpec((rows, width), lambda e: (first + e, 0))
        lines = pl.BlockSpec((16, width), lambda e: (local * rows // 16, 0))
        arrays = (*xs, *cs, *xs)
        blocks = [slab] * (2 * pieces) + [lines] * pieces
    weight = lambda a, b: pl.BlockSpec((1, a, b), lambda e: (first + e, 0, 0))
    mat = lambda a, b: pl.BlockSpec((1, a, b), lambda e: (e, 0, 0))
    total = planes * rows
    kept = lambda n: jax.ShapeDtypeStruct((mine, total, n), BF16)
    return pl.pallas_call(
        functools.partial(expert_kernel, planes, gated, first, len(after)),
        grid=(mine,),
        in_specs=[ANYWHERE] * len(after) + [SCALARS] + blocks + [weight(width, hidden), weight(hidden, width)],
        out_specs=[pl.BlockSpec((2, rows, width), lambda e: (0, e, 0))] * planes
        + [mat(total, hidden), mat(total, hidden), mat(total, width), mat(total, width)],
        out_shape=[jax.ShapeDtypeStruct((2, mine * rows, width), BF16)] * planes
        + [kept(hidden), kept(hidden), kept(width), kept(width)],
        compiler_params=params(60),
        cost_estimate=cost(),
    )(*after, plane, *arrays, w_inner, w_outer)


def expert_grad_kernel(batches, waits, *refs):
    xs, cs, acts, pres = (refs[waits + k * batches : waits + (k + 1) * batches] for k in range(4))
    outer_ref, inner_ref = refs[-2:]
    whole = lambda refs: jnp.concatenate([ref[0] for ref in refs], axis=0)
    outer_ref[0] = t_dot(whole(acts), whole(cs))
    inner_ref[0] = t_dot(whole(xs), whole(pres))


def expert_grads(which, after, past, local, xs, cs, acts, pres):
    batches = len(xs)
    mine, total, width = xs[0].shape
    hidden = acts[0].shape[2]
    first = which * mine
    mat = lambda a, b: pl.BlockSpec((1, a, b), lambda e: (e, 0, 0))
    out = lambda a, b: pl.BlockSpec((1, a, b), lambda e: (first + e, 0, 0))
    behind = len(after) + 4 * batches
    return pl.pallas_call(
        functools.partial(expert_grad_kernel, batches, len(after)),
        grid=(mine,),
        in_specs=[ANYWHERE] * len(after)
        + [mat(total, width)] * (2 * batches)
        + [mat(total, hidden)] * (2 * batches)
        + [ANYWHERE] * len(past),
        out_specs=[out(hidden, width), out(width, hidden)],
        out_shape=[
            jax.ShapeDtypeStruct((local, hidden, width), F32),
            jax.ShapeDtypeStruct((local, width, hidden), F32),
        ],
        input_output_aliases={behind + k: k for k in range(len(past))},
        compiler_params=params(60),
        cost_estimate=cost(),
    )(*after, *xs, *cs, *acts, *pres, *past)


def combine_kernel(per, batch, waits, *refs):
    refs = refs[waits:]
    len_ref, low_ref, high_ref, scol_ref, rcol_ref, res_ref, probs_ref, cot_ref, gffn_ref, wr_ref, wo_ref, mixed_ref, *refs = refs
    past_ref = refs.pop(0) if batch else None
    layer_ref, resgrad_ref, mgrad_ref, shared_ref, *buffers, sems = refs
    fetched = [res_ref, cot_ref.at[batch, 0], mixed_ref, wo_ref] + ([past_ref] if batch else [])
    copies = [pltpu.make_async_copy(ref, buffer, sems.at[k]) for k, (ref, buffer) in enumerate(zip(fetched, buffers))]
    for copy in copies:
        copy.start()
    res_ref, cot_ref, mixed_ref, wo_ref = buffers[:4]
    if batch:
        past_ref = buffers[4]
    length, width = cot_ref.shape
    experts = wr_ref.shape[0]
    groups, message, _ = low_ref.shape
    valid = iota((length, 1), 0) < len_ref[batch]
    places = iota((length, groups * message), 1)
    half = per // 2
    returned = input_grad = None
    for which, ref in enumerate((low_ref, high_ref)):
        place = spread_slots(scol_ref[0], per, message, which * half, (which + 1) * half)
        rows = ref[...].reshape(groups * message, width)
        out_part = dot(one_hot(places == place), rows)
        in_part = dot(one_hot(places == jnp.where(place < 0, -1, place + half)), rows)
        returned = out_part if returned is None else returned + out_part
        input_grad = in_part if input_grad is None else input_grad + in_part
    copies[0].wait()
    copies[1].wait()
    residual = res_ref[...]
    probs = probs_ref[...]
    chosen = iota(probs.shape, 1) == rcol_ref[0]
    gate = jnp.sum(jnp.where(chosen, probs, 0.0), axis=-1, keepdims=True)
    layer_ref[0, 0] = jnp.where(valid, residual + gate * returned, 0.0).astype(BF16)
    out_grad = jnp.where(valid, cot_ref[...].astype(F32), 0.0)
    gate_grad = jnp.sum(out_grad * returned, axis=-1, keepdims=True)
    prob_grad = jnp.where(chosen, gate_grad, 0.0)
    logit_grad = (probs * (prob_grad - jnp.sum(probs * prob_grad, axis=-1, keepdims=True))).astype(BF16)
    inverse = lax.rsqrt(jnp.mean(residual * residual, axis=-1, keepdims=True) + epsilon)
    gain = gffn_ref[...]
    scaled = residual * inverse
    routed = (scaled * gain).astype(BF16)

    def share(first, whole_rows):
        for side in range(2):
            rows = whole_rows[:, side * width // 2 : (side + 1) * width // 2]
            here = slice(side * shared_ref.shape[0] // 2 + first, side * shared_ref.shape[0] // 2 + first + rows.shape[0])
            if past_ref is not None:
                rows = rows + past_ref[here, :]
            shared_ref[here, :] = rows.astype(shared_ref.dtype)

    for copy in copies[2:]:
        copy.wait()
    share(width, t_dot(logit_grad, routed))
    routed_grad = dot(logit_grad, wr_ref[...]) + input_grad
    gain_part = jnp.sum(routed_grad * scaled, axis=0, keepdims=True)
    left = shared_ref.shape[0] // 2 - width - experts
    share(width + experts, jnp.where(iota((left, width), 0) == 0, gain_part, 0.0))
    upstream = routed_grad * gain
    middle = jnp.mean(upstream * scaled, axis=-1, keepdims=True)
    residual_grad = out_grad + inverse * (upstream - scaled * middle)
    resgrad_ref[...] = residual_grad
    attended = residual_grad.astype(BF16)
    mixed_all = jnp.concatenate([mixed_ref[p] for p in range(PAIRS)], axis=1)
    share(0, t_dot(mixed_all, attended))
    mixed_grad = dot_t(attended, wo_ref[...]).astype(BF16)
    for pair in range(PAIRS):
        mgrad_ref[pair] = mixed_grad[:, pair * PAIR : (pair + 1) * PAIR]


def combine(
    batch, last, after, layers, counts, low, high, scol, rcol, residual, probs, cot, gain_ffn, w_router, w_output, mixed, past, per, shared
):
    length, width = cot.shape[2:]
    return pl.pallas_call(
        functools.partial(combine_kernel, per, batch, len(after) + len(layers)),
        grid=(1,),
        in_specs=[ANYWHERE] * (len(after) + len(layers))
        + [SCALARS, WHOLE, WHOLE, batch_block(scol, batch), batch_block(rcol, batch), ANYWHERE, WHOLE, ANYWHERE]
        + [WHOLE] * 2
        + [ANYWHERE] * (2 + len(past)),
        out_specs=[batch_block(cot, batch)] + [WHOLE] * 3,
        out_shape=[
            jax.ShapeDtypeStruct(cot.shape, BF16),
            jax.ShapeDtypeStruct((length, width), F32),
            jax.ShapeDtypeStruct((PAIRS, length, PAIR), BF16),
            jax.ShapeDtypeStruct((shared, width // 2), BF16 if last else F32),
        ],
        scratch_shapes=[
            pltpu.VMEM(residual.shape, residual.dtype),
            pltpu.VMEM((length, width), BF16),
            *(pltpu.VMEM(array.shape, array.dtype) for array in (mixed, w_output, *past)),
            pltpu.SemaphoreType.DMA((4 + len(past),)),
        ],
        input_output_aliases={len(after): 0} if layers else {},
        compiler_params=params(60),
        cost_estimate=cost(),
    )(
        *after, *layers, counts, low, high, scol, rcol, residual, probs, cot, gain_ffn, w_router, w_output, mixed, *past
    )


def attn_back_kernel(batch, which, last, waits, *refs):
    refs = refs[waits:]
    side_ref, len_ref, qkv_ref, lse_ref, vec_ref, sel_ref, mgrad_ref, tok_ref, gain_ref, wq_ref, wk_ref, wv_ref, *refs = refs
    past_ref = refs.pop(0) if batch else None
    if which:
        seen_ref, part_ref, resgrad_ref, *refs = refs
        tgrad_ref, *refs = refs
    else:
        early_ref = refs.pop(0) if batch else None
        diag_out_ref, part_out_ref, *refs = refs
    shared_refs, refs = refs[: 1 + last], refs[1 + last :]
    bands_ref, probs_ref, sgrad_ref, spread_ref, low_ref, qt_ref, kt_ref, vt_ref, diag_ref, stage_ref, rest_ref, *buffers = refs
    *buffers, sems, out_sems = buffers
    half = wq_ref.shape[0] // 2
    columns = pl.ds(which * half, half)
    fetched = [tok_ref.at[batch, 0]] + [ref.at[:, columns] for ref in (wq_ref, wk_ref, wv_ref)]
    if past_ref is not None:
        fetched.append(past_ref)
    if which:
        fetched += [part_ref, resgrad_ref]
    elif batch:
        fetched.append(early_ref)
    copies = [pltpu.make_async_copy(ref, buffer, sems.at[k]) for k, (ref, buffer) in enumerate(zip(fetched, buffers))]
    for copy in copies:
        copy.start()
    going = []
    offset = early_ref.shape[0] if last and not which else 0
    part_rows = shared_refs[0].shape[0]
    tok_ref, wq_ref, wk_ref, wv_ref, *buffers = buffers
    if past_ref is not None:
        past_ref = buffers.pop(0)
    if which:
        part_ref, resgrad_ref = buffers
    elif batch:
        early_ref = buffers[0]
    length, width = tok_ref.shape
    first_pair = which * (PAIRS // 2)
    mask = jnp.where(iota((1, length), 1) < len_ref[batch], 0.0, negative)
    lane = iota((ROWS, PAIR), 1)
    diag_ref[...] = seen_ref[...] if which else jnp.zeros_like(diag_ref)

    def one_pair(step, carry):
        pair = first_pair + step
        keys = qkv_ref[1, step]
        values = qkv_ref[2, step]
        queries_t = qkv_ref[0, step].T
        keys_t = qkv_ref[1, step].T
        grads_t = mgrad_ref[step].T
        for side in range(2):
            head = 2 * pair + side
            bands_ref[side] = band_bias(vec_ref, head)
            spread_ref[side] = jnp.zeros(spread_ref.shape[1:], F32)
            mine = (lane >= HEAD_DIM) if side else (lane < HEAD_DIM)
            for block in range(length // ROWS):
                here = slice(ROWS * block, ROWS * (block + 1))
                window = band_slice(block, length)
                queries = qkv_ref[0, step, here, :] * 0.125
                queries = jnp.where(mine, queries, jnp.zeros_like(queries))
                grads = mgrad_ref[step, here, :]
                grads = jnp.where(mine, grads, jnp.zeros_like(grads))
                column = iota((ROWS, lse_ref.shape[1]), 1)
                log_total = jnp.sum(jnp.where(column == head, lse_ref[here, :], 0.0), axis=-1, keepdims=True)
                scores = dot_t(queries, keys) + bands_ref[side, :, window] + mask
                probs = jnp.exp(scores - log_total)
                probs_ref[side, here, :] = probs.astype(BF16)
                weighted = probs * dot_t(grads, values)
                score_grad = weighted - probs * jnp.sum(weighted, axis=-1, keepdims=True)
                spread_ref[side, :, window] += score_grad
                sgrad_ref[side, here, :] = score_grad.astype(BF16)
            rows = slice(HEAD_DIM * side, HEAD_DIM * (side + 1))
            qt_ref[rows, :] = dot_t(keys_t[rows, :], sgrad_ref[side]) * 0.125
            kt_ref[rows, :] = dot(queries_t[rows, :], sgrad_ref[side]) * 0.125
            vt_ref[rows, :] = dot(grads_t[rows, :], probs_ref[side])
            size = spread_ref.shape[2]
            eight = spread_ref[side, 0:8, :]
            for move in range(8, ROWS, 8):
                eight = eight + pltpu.roll(spread_ref[side, move : move + 8, :], size - move, 1)
            diagonal = eight[0:1, :]
            for move in range(1, 8):
                diagonal = diagonal + pltpu.roll(eight[move : move + 1, :], size - move, 1)
            diag_ref[...] = jnp.where(iota(diag_ref.shape, 0) == head, diagonal, diag_ref[...])
        low_ref[0, step] = qt_ref[...].T.astype(BF16)
        low_ref[1, step] = kt_ref[...].T.astype(BF16)
        low_ref[2, step] = vt_ref[...].T.astype(BF16)
        return carry

    lax.fori_loop(0, PAIRS // 2, one_pair, 0)
    for copy in copies:
        copy.wait()

    def send(source, first, place):
        count = source.shape[0]
        for k in range(1 + last):
            low, high = max(first, k * part_rows), min(first + count, (k + 1) * part_rows)
            if low >= high:
                continue
            part = source.at[pl.ds(low - first, high - low)]
            for turn in range(1 + last):
                there = shared_refs[turn].at[pl.ds(low - k * part_rows, high - low)]
                copy = pltpu.make_async_copy(part, there, out_sems.at[place, k])
                going.append((copy, k ^ turn))

                @pl.when(side_ref[0] == (k ^ turn) if last else True)
                def _():
                    copy.start()

    if offset:
        send(early_ref, 0, 0)

    def past(first, count):
        return 0.0 if past_ref is None else past_ref[first : first + count, :]

    tokens = tok_ref[...].astype(F32)
    inverse = lax.rsqrt(jnp.mean(tokens * tokens, axis=-1, keepdims=True) + epsilon)
    gain = gain_ref[...]
    scaled = tokens * inverse
    normed_t = (scaled * gain).astype(BF16).T
    normed_grad = part_ref[...] if which else jnp.zeros((length, width), F32)
    for matrix, w_ref in enumerate((wq_ref, wk_ref, wv_ref)):
        low = jnp.concatenate([low_ref[matrix, p] for p in range(PAIRS // 2)], axis=1)
        stage_ref[matrix] = (dot(normed_t, low) + past(matrix * width, width)).astype(stage_ref.dtype)
        send(stage_ref.at[matrix], offset + matrix * width, 1 + matrix)
        normed_grad = normed_grad + dot_t(low, w_ref[...])
    left = rest_ref.shape[0]
    if which:
        gain_part = jnp.sum(normed_grad * scaled, axis=0, keepdims=True)
        bias_part = lax.dot_general(
            diag_ref[...],
            sel_ref[...],
            (((1,), (0,)), ((), ())),
            precision=lax.Precision.HIGHEST,
            preferred_element_type=F32,
        )
        row = iota((8, half), 0)
        gains = jnp.where(row == 0, gain_part[:, :half], jnp.where(row == 1, gain_part[:, half:], 0.0))
        wide = jnp.concatenate([bias_part, jnp.zeros((16, half - bias_part.shape[1]), F32)], axis=1)
        tail = [gains, wide] + ([jnp.zeros((left - 24, half), F32)] if left > 24 else [])
        rest_ref[...] = (jnp.concatenate(tail, axis=0) + past(3 * width, left)).astype(rest_ref.dtype)
        send(rest_ref, 3 * width, 4)
        upstream = normed_grad * gain
        middle = jnp.mean(upstream * scaled, axis=-1, keepdims=True)
        tgrad_ref[0, 0] = (resgrad_ref[...] + inverse * (upstream - scaled * middle)).astype(BF16)
    else:
        if offset and offset + 3 * width < 2 * part_rows:
            rest_ref[...] = jnp.zeros_like(rest_ref)
            send(rest_ref, offset + 3 * width, 4)
        diag_out_ref[...] = diag_ref[...]
        part_out_ref[...] = normed_grad
    for copy, turn in going:

        @pl.when(side_ref[0] == turn if last else True)
        def _():
            copy.wait()


def attention_backward(batch, which, last, after, grads, side, counts, qkv, lse, vector, selector, mixed_grad, tokens, gain, wq, wk, wv, past, more, rows):
    length, width = tokens.shape[2:]
    half = width // 2
    size = vector.shape[-1]
    late = (*past, *(more[1:] if which else more))
    buffers = [((length, width), BF16)] + [((width, half), BF16)] * 3 + [(array.shape, array.dtype) for array in late]
    sent = 0 if which or not last else more[0].shape[0]
    rest = max(rows - sent - 3 * width, 16)
    shared = jax.ShapeDtypeStruct((rows // 2 if last else rows, half), BF16 if last else F32)
    if which:
        outs = [jax.ShapeDtypeStruct(tokens.shape, BF16)]
        out_specs = [batch_block(tokens, batch)]
    else:
        outs = [jax.ShapeDtypeStruct((16, size), F32), jax.ShapeDtypeStruct((length, width), F32)]
        out_specs = [WHOLE] * 2
    outs += [shared] * (2 if last else 1)
    out_specs += [ANYWHERE] * (2 if last else 1)
    return pl.pallas_call(
        functools.partial(attn_back_kernel, batch, which, last, len(after) + len(grads)),
        grid=(1,),
        in_specs=[ANYWHERE] * (len(after) + len(grads))
        + [SCALARS, SCALARS, pl.BlockSpec((3, PAIRS // 2, length, PAIR), lambda _: (0, which, 0, 0))]
        + [WHOLE] * 3
        + [pl.BlockSpec((PAIRS // 2, length, PAIR), lambda _: (which, 0, 0))]
        + [ANYWHERE, WHOLE]
        + [ANYWHERE] * (3 + len(past))
        + [WHOLE if which and k == 0 else ANYWHERE for k in range(len(more))],
        out_specs=out_specs,
        out_shape=outs,
        input_output_aliases={len(after): 0} if grads else {},
        scratch_shapes=[
            pltpu.VMEM((2, ROWS, size), F32),
            pltpu.VMEM((2, length, length), BF16),
            pltpu.VMEM((2, length, length), BF16),
            pltpu.VMEM((2, ROWS, size), F32),
            pltpu.VMEM((3, PAIRS // 2, length, PAIR), BF16),
            pltpu.VMEM((PAIR, length), F32),
            pltpu.VMEM((PAIR, length), F32),
            pltpu.VMEM((PAIR, length), F32),
            pltpu.VMEM((16, size), F32),
            pltpu.VMEM((3, width, half), shared.dtype),
            pltpu.VMEM((rest, half), shared.dtype),
            *(pltpu.VMEM(shape, kind) for shape, kind in buffers),
            pltpu.SemaphoreType.DMA((len(buffers),)),
            pltpu.SemaphoreType.DMA((5, 2)),
        ],
        compiler_params=params(60),
        cost_estimate=cost(),
    )(*after, *grads, side, counts, qkv, lse, vector, selector, mixed_grad, tokens, gain, wq, wk, wv, *past, *more)


def unpack_kernel(early, side_ref, *refs):
    arrived, refs = refs[:4], refs[4:]
    q_ref, k_ref, v_ref, output_ref, router_ref, gain_f_ref, gain_a_ref, bias_ref, *refs = refs
    buffers, (stage_ref, in_sems, out_sems) = refs[:4], refs[4:]
    copies = [
        pltpu.make_async_copy(ref, buffer, in_sems.at[k]) for k, (ref, buffer) in enumerate(zip(arrived, buffers))
    ]
    for copy in copies:
        copy.start()
    swapped = side_ref[0] == 1

    def whole(k):
        copies[k].wait()
        copies[k + 1].wait()
        mine, other = buffers[k][...], buffers[k + 1][...]
        parts = [jnp.where(swapped, other, mine), jnp.where(swapped, mine, other)]
        return jnp.concatenate(parts, axis=0).astype(F32)

    leaving = [
        pltpu.make_async_copy(stage_ref.at[k], ref, out_sems.at[k])
        for k, ref in enumerate((q_ref, k_ref, v_ref, output_ref))
    ]
    rows = whole(0)
    half = rows.shape[1]
    width = 2 * half
    last = early - 16
    stage_ref[3, :, :half] = rows[:width]
    stage_ref[3, :, half:] = rows[early : early + width]
    leaving[3].start()
    router_ref[...] = jnp.concatenate([rows[width:last], rows[early + width : early + last]], axis=1)
    gain_f_ref[...] = jnp.concatenate([rows[last], rows[early + last]])
    for k in range(3):
        stage_ref[k, :, :half] = rows[2 * early + k * width : 2 * early + (k + 1) * width]
    rows = whole(2)
    for k in range(3):
        stage_ref[k, :, half:] = rows[k * width : (k + 1) * width]
        leaving[k].start()
    gain_a_ref[...] = jnp.concatenate([rows[3 * width], rows[3 * width + 1]])
    bias_ref[...] = rows[3 * width + 8 : 3 * width + 8 + HEADS, :BUCKETS]
    for copy in leaving:
        copy.wait()


def unpack(early, experts, side, first, first_other, second, second_other):
    width = 2 * first.shape[1]
    matrix = jax.ShapeDtypeStruct((width, width), F32)
    line = jax.ShapeDtypeStruct((width,), F32)
    arrays = (first, first_other, second, second_other)
    return pl.pallas_call(
        functools.partial(unpack_kernel, early),
        in_specs=[SCALARS] + [ANYWHERE] * 4,
        out_specs=[ANYWHERE] * 4 + [WHOLE] * 4,
        out_shape=[matrix] * 4
        + [jax.ShapeDtypeStruct((experts, width), F32), line, line, jax.ShapeDtypeStruct((HEADS, BUCKETS), F32)],
        scratch_shapes=[pltpu.VMEM(array.shape, array.dtype) for array in arrays]
        + [pltpu.VMEM((4, width, width), F32), pltpu.SemaphoreType.DMA((4,)), pltpu.SemaphoreType.DMA((4,))],
        compiler_params=params(60),
        cost_estimate=cost(),
    )(side, *arrays)


def upward(planes, first, last):
    return [(k, k + 1) for k in range(first, last)]


def downward(planes, first, last):
    return [(planes - 1 - k, planes - 2 - k) for k in range(first, last)]


def mix_kernel(both, planes, step, waits, here_ref, up_ref, down_ref, upsum_ref, downsum_ref, *refs):
    to_up, to_down = refs[waits:]
    for moving, sums, out, place in (
        (up_ref, upsum_ref, to_up, here_ref[0]),
        (down_ref, downsum_ref, to_down, planes - 1 - here_ref[0]),
    ):
        total = moving[...] + sums[...]
        out[...] = jnp.where(place <= step, total, moving[...]) if both else total


def mix(both, planes, step, here, up, down, upsum, downsum, after):
    kinds, rows, width = up.shape
    block = pl.BlockSpec((1, rows // 2, width), lambda i, j: (i, j, 0))
    return pl.pallas_call(
        functools.partial(mix_kernel, both, planes, step, len(after)),
        grid=(kinds, 2),
        in_specs=[SCALARS] + [block] * 4 + [ANYWHERE] * len(after),
        out_specs=[block] * 2,
        out_shape=[jax.ShapeDtypeStruct(up.shape, BF16)] * 2,
        compiler_params=params(32),
        cost_estimate=cost(),
    )(here, up, down, upsum, downsum, *after)


def gate_kernel(*refs):
    pass


def gate(arrays, after):
    count = len(arrays)
    return pl.pallas_call(
        gate_kernel,
        in_specs=[ANYWHERE] * (count + len(after)),
        out_specs=[ANYWHERE] * count,
        out_shape=[jax.ShapeDtypeStruct(array.shape, array.dtype) for array in arrays],
        input_output_aliases={k: k for k in range(count)},
        cost_estimate=cost(),
    )(*arrays, *after)


class Chain:
    def __init__(self, planes, own=None, sums=None):
        self.planes, self.own, self.sums = planes, own, sums
        self.here = lax.axis_index("hidden")[None]
        self.from_below, self.from_above = [], []
        if own is not None:
            self.up = self.down = own
        else:
            self.up, self.down = sums[planes - 1], sums[1]
        self.count = 0
        self.steps = planes if own is not None and sums is not None else planes - 1

    def send(self):
        planes, s = self.planes, self.count
        if self.own is not None and self.sums is not None:
            first, last = 0, planes - 1
        elif self.own is not None:
            first, last = s, planes - 1
        else:
            first, last = 0, s + 1
        self.up = lax.ppermute(self.up, "hidden", upward(planes, first, last))
        self.down = lax.ppermute(self.down, "hidden", downward(planes, first, last))
        self.count += 1
        if self.own is not None and s < planes - 1:
            self.from_below.append(self.up)
            self.from_above.append(self.down)

    def mix(self, *after):
        planes, s = self.planes, self.count - 1
        both = self.own is not None
        offset = 1 if both else 2
        self.up, self.down = mix(
            both, planes, s, self.here, self.up, self.down, self.sums[planes - offset - s], self.sums[s + offset], after
        )
        self.mixed = self.up

    def gate(self, *after):
        self.up, self.down = gate((self.up, self.down), after)
        self.from_below[-1], self.from_above[-1] = self.up, self.down

    def run(self):
        while self.count < self.steps:
            self.send()
        return self

    def gathered(self):
        return (self.own, *self.from_above, *self.from_below)

    def scattered(self):
        return (self.sums[0], self.up, self.down)


def swap(values, axis, distance):
    return lax.ppermute(values, axis, [(k, k ^ distance) for k in range(lax.axis_size(axis))])


def share_sums(values, axis, near, count):
    me = lax.axis_index(axis) // near
    parts = values.reshape(count, values.shape[0] // count, values.shape[1])
    total = lax.dynamic_index_in_dim(parts, me, 0, keepdims=False).astype(F32)
    for k in range(1, count):
        part = lax.dynamic_index_in_dim(parts, me ^ k, 0, keepdims=False)
        total = total + swap(part, axis, k * near).astype(F32)
    return total.astype(BF16)


def join_sums(values, axis, near, count):
    me = lax.axis_index(axis) // near
    found = [values] + [swap(values, axis, k * near) for k in range(1, count)]
    joined = []
    for j in range(count):
        piece = found[count - 1]
        for k in range(count - 2, -1, -1):
            piece = jnp.where(me ^ k == j, found[k], piece)
        joined.append(piece)
    return jnp.concatenate(joined)


def sum_everywhere(values):
    size = lax.axis_size("expert")
    planes = lax.axis_size("hidden")
    values = share_sums(values, "expert", 2, size // 2)
    values = share_sums(values, "hidden", 1, planes)
    values = join_sums(values, "hidden", 1, planes)
    values = join_sums(values, "expert", 2, size // 2)
    return values, swap(values, "expert", 1)


def add_half(mine, other):
    return mine + swap(other, "expert", 1)


def offset_selector(length):
    place = np.arange(2 * length)
    offsets = np.where(place < 2 * length - ROWS, place, place - 2 * length) - (length - ROWS)
    offsets = np.clip(offsets, -(length - 1), length - 1)
    return (offset_bucket(offsets)[:, None] == np.arange(BUCKETS)[None, :]).astype(np.float32)


def shards(
    tokens,
    cotangent,
    lengths,
    routes,
    gain_attn,
    w_query,
    w_key,
    w_value,
    w_output,
    bucket_head_bias,
    gain_ffn,
    w_router,
    w_inner,
    w_outer,
):
    batches, _, length, width = tokens.shape
    experts = w_router.shape[1]
    local = w_inner.shape[0]
    groups = lax.axis_size("expert")
    planes = lax.axis_size("hidden")
    capacity = (5 * length + 4 * experts - 1) // (4 * experts)
    per = local * capacity
    rows = groups * capacity
    message = padded(per)
    in_groups = (groups, capacity, message)
    selector = jnp.asarray(offset_selector(length))
    vector = lax.dot_general(
        bucket_head_bias, selector, (((0,), (1,)), ((), ())), precision=lax.Precision.HIGHEST
    )[:, None, :]
    gain_a = gain_attn[None, :]
    gain_f = gain_ffn[None, :]
    router_rows = w_router.T
    counts = lengths[:, 0]
    plane = lax.axis_index("hidden")[None]

    def to_groups(values):
        return lax.all_to_all(values, "expert", split_axis=0, concat_axis=0, tiled=True)

    def leaving(values, *after):
        return regroup(False, [to_groups(values)], (2, local // 2 * rows, width), 2, local // 2, *in_groups, after)

    def returning(chain, *after):
        shape = (groups, message, width)
        return regroup(True, chain.scattered(), shape, 2, local // 2, *in_groups, after)

    def arriving(chain, *after):
        return to_groups(returning(chain, *after))

    def attend(b, *after):
        return attention_forward(b, after, counts, tokens, gain_a, w_query, w_key, w_value, vector)

    def routing(b, *after):
        return route(
            b, after, tokens, cotangent, forward[b][1], w_output, gain_f, router_rows, srow, rcol, groups, per, b > 0
        )

    srow, scol, cot_slots = prep(counts, routes.reshape(batches, length), cotangent, groups, per, capacity)
    rcol = routes.reshape(batches, length, 1)
    early_rows = width + experts + 16
    unit = 16 * groups * planes
    first_rows = 2 * early_rows + 3 * width
    first_rows = first_rows + -first_rows % unit
    second_rows = 3 * width + 24
    second_rows = second_rows + -second_rows % unit
    kept, layers, token_grads = [], (), ()
    side = (lax.axis_index("expert") % 2)[None]
    early_part, first_part, second_part = (), (), ()

    def back_tokens(b, after, low, high):
        return combine(
            b,
            b + 1 == batches,
            after,
            layers,
            counts,
            low,
            high,
            scol,
            rcol,
            *routed[b][:2],
            cotangent,
            gain_f,
            router_rows,
            w_output,
            forward[b][1],
            early_part,
            per,
            2 * early_rows,
        )

    def back_half(b, which, after, mixed_grad, more):
        qkv, _, lse = forward[b]
        last = b + 1 == batches
        return attention_backward(
            b,
            which,
            last,
            after,
            token_grads if which else (),
            side,
            counts,
            qkv,
            lse,
            vector,
            selector,
            mixed_grad,
            tokens,
            gain_a,
            w_query,
            w_key,
            w_value,
            second_part if which else first_part,
            more,
            second_rows if which else first_rows if last else 3 * width,
        )

    def grads_half(h, after, past):
        return expert_grads(h, after, past, local, *([k[h][part] for k in kept] for part in (2, 3, 0, 1)))

    forward = [attend(0, cot_slots)]
    routed = [routing(0)]
    grads = regroup(False, [to_groups(cot_slots)], (local * rows, width), 1, local, *in_groups, (routed[0][2],))
    grad_chain = Chain(planes, grads)
    grad_chain.send()
    inputs = regroup_gated(to_groups(routed[0][2]), local * rows, capacity, (grads,))
    input_chain = Chain(planes, inputs)
    input_chain.send()
    forward.append(attend(1, inputs, grad_chain.up, grad_chain.down))
    grad_chain.send()
    routed.append(routing(1, grad_chain.up, grad_chain.down))
    grad_chain.run()
    input_chain.gate(forward[1][1])
    input_chain.send()
    held = (input_chain.up, input_chain.down, grad_chain.up, grad_chain.down)
    input_chain.run()
    halves = range(2)
    chains = [None, None]
    for b in range(batches):
        last = b + 1 == batches
        before = chains
        messages = [None, None]
        ready = ()
        if not last:
            if b:
                forward.append(attend(b + 1))
                routed.append(routing(b + 1))
            messages = [leaving(m, *held) for m in routed[b + 1][2:]]
            held = ()
            ready = tuple(messages)
        chains, worked = [], []
        for h in halves:
            if b == 0:
                done = experts_half(
                    h, ready, plane, None, w_inner, w_outer, input_chain.gathered(), grad_chain.gathered()
                )
            else:
                before[h].mix(*(w[0] for w in worked))
                tied = (before[h].up, before[h].down)
                if h:
                    tied += (before[0].up, before[0].down)
                done = experts_half(h, ready + tied, plane, before[h].gathered(), w_inner, w_outer)
                before[h].send()
            worked.append(done)
            chains.append(Chain(planes, messages[h], done[:planes]))
            chains[h].send()
        kept.append([w[planes:] for w in worked])
        low_chain, high_chain = chains
        if not last:
            for step in range(1, planes):
                for chain in chains:
                    if step > 1:
                        chain.send()
                    if step < planes - 1:
                        chain.mix()
            if b == 0:
                continue
            low, high = (arriving(chain) for chain in before)
            layer, res_grad, mixed_grad, early_part = back_tokens(b - 1, (), low, high)
            *more, first_part = back_half(b - 1, 0, (), mixed_grad, (early_part,) if b > 1 else ())
            token_grad, second_part = back_half(b - 1, 1, (), mixed_grad, (*more, res_grad))
        else:
            low = arriving(before[0], before[1].up, before[1].down)
            high = arriving(before[1])
            low_chain.mix()
            low_chain.send()
            totals = grads_half(0, (low_chain.mixed,), ())
            high_chain.mix(totals[0])
            high_chain.send()
            low_chain.mix(high)
            low_chain.send()
            layer, res_grad, mixed_grad, early_part = back_tokens(b - 1, (low_chain.mixed,), low, high)
            high_chain.mix(mixed_grad)
            high_chain.send()
            *more, first_part = back_half(
                b - 1, 0, (high_chain.mixed,), mixed_grad, (early_part,) if b > 1 else ()
            )
            low = returning(low_chain, first_part)
            token_grad, second_part = back_half(b - 1, 1, (low,), mixed_grad, (*more, res_grad))
            low = to_groups(low)
            high = returning(high_chain, second_part, low)
            totals = grads_half(1, (high,), totals)
            high = to_groups(high)
        layers, token_grads = (layer,), (token_grad,)
        early_part, first_part, second_part = (early_part,), (first_part,), (second_part,)
    layer, res_grad, mixed_grad, early_part = back_tokens(batches - 1, (totals[0],), low, high)
    diagonal, part, *first_part = back_half(batches - 1, 0, (), mixed_grad, (early_part,))
    first_half = add_half(*first_part)
    token_grad, *second_part = back_half(batches - 1, 1, (first_half,), mixed_grad, (diagonal, part, res_grad))
    mine, other = sum_everywhere(first_half)
    mine_second, other_second = sum_everywhere(add_half(*second_part))
    query_grad, key_grad, value_grad, output_grad, router_grad, gain_f_grad, gain_a_grad, bias_grad = unpack(
        early_rows, experts, side, mine, other, mine_second, other_second
    )
    return (
        layer,
        token_grad,
        gain_a_grad,
        query_grad,
        key_grad,
        value_grad,
        output_grad,
        bias_grad.T,
        gain_f_grad,
        router_grad.T,
        totals[1],
        totals[0],
    )


def solution(mesh):
    token = P(None, ("expert", "hidden"), None, None)
    placed = (
        token,
        token,
        P(None, ("expert", "hidden")),
        token,
        *(P() for _ in range(8)),
        P("expert", None, "hidden"),
        P("expert", "hidden", None),
    )
    return jax.shard_map(
        shards,
        mesh=mesh,
        in_specs=placed,
        out_specs=(
            token,
            token,
            *(P() for _ in range(8)),
            P("expert", None, "hidden"),
            P("expert", "hidden", None),
        ),
        check_vma=False,
    )
```

```python
import functools

import jax
import jax.numpy as jnp
import numpy as np
from jax import lax
from jax.experimental import pallas as pl
from jax.experimental.pallas import tpu as pltpu
from jax.sharding import PartitionSpec as P

HEADS = 12
HEAD_DIM = 64
BUCKETS = 32
MAXDIST = 128
PAIR = 2 * HEAD_DIM
PAIRS = HEADS // 2
ROWS = 128

epsilon = 1e-06
negative = -1e30
F32 = jnp.float32
BF16 = jnp.bfloat16
MIB = 1 << 20


def params(mib):
    return pltpu.CompilerParams(vmem_limit_bytes=mib * MIB)


def cost():
    return pl.CostEstimate(flops=1, bytes_accessed=1, transcendentals=0)


def offset_bucket(offsets):
    halfway = BUCKETS // 2
    exact_count = halfway // 2
    relative_distance = np.abs(offsets)
    scaled = (
        np.log(np.maximum(relative_distance, 1) / exact_count)
        / np.log(MAXDIST / exact_count)
        * (halfway - exact_count)
    )
    far_bucket = np.minimum(exact_count + np.floor(scaled).astype(np.int64), halfway - 1)
    near_bucket = np.where(relative_distance < exact_count, relative_distance, far_bucket)
    return (np.where(offsets > 0, halfway, 0) + near_bucket).astype(np.int32)


def dot(a, b):
    return lax.dot_general(a, b, (((1,), (0,)), ((), ())), preferred_element_type=F32)


def dot_t(a, b):
    return lax.dot_general(a, b, (((1,), (1,)), ((), ())), preferred_element_type=F32)


def t_dot(a, b):
    return lax.dot_general(a, b, (((0,), (0,)), ((), ())), preferred_element_type=F32)


def one_hot(condition):
    return jnp.where(condition, 1.0, 0.0).astype(BF16)


def batch_block(array, b):
    rest = array.shape[1:]
    return pl.BlockSpec((1,) + rest, lambda *_: (b,) + (0,) * len(rest))


ANYWHERE = pl.BlockSpec(memory_space=pl.ANY)
WHOLE = pl.BlockSpec(memory_space=pltpu.VMEM)
SCALARS = pl.BlockSpec(memory_space=pltpu.SMEM)


def iota(shape, axis):
    return lax.broadcasted_iota(jnp.int32, shape, axis)


def padded(rows):
    return -(-rows // 16) * 16


def spread_slots(slot, per, message, first=0, last=None):
    last = per if last is None else last
    group = lax.div(jnp.maximum(slot, 0), per)
    inside = slot - group * per
    held = (slot >= 0) & (inside >= first) & (inside < last)
    return jnp.where(held, group * message + inside - first, -1)


def prep_kernel(batch, experts, capacity, waits, *refs):
    refs = refs[waits:]
    len_ref, row_ref, col_ref, *refs = refs
    length = row_ref.shape[-1]
    before = one_hot(iota((length, length), 0) < iota((length, length), 1))
    after = one_hot(iota((length, length), 1) < iota((length, length), 0))
    count = len_ref[batch]
    row = row_ref[0]
    col = col_ref[0]
    valid_row = iota((1, length), 1) < count
    valid_col = iota((length, 1), 0) < count
    chosen_row = iota((experts, length), 0) == row
    chosen_col = iota((length, experts), 1) == col
    earlier_row = dot(one_hot(chosen_row & valid_row), before)
    rank_row = jnp.sum(jnp.where(chosen_row, earlier_row, 0.0), axis=0, keepdims=True).astype(jnp.int32)
    earlier_col = dot(after, one_hot(chosen_col & valid_col))
    rank_col = jnp.sum(jnp.where(chosen_col, earlier_col, 0.0), axis=1, keepdims=True).astype(jnp.int32)
    slot_row = jnp.where(valid_row & (rank_row < capacity), row * capacity + rank_row, -1)
    if batch:
        srow_ref, scol_ref = refs
    else:
        cot_ref, srow_ref, scol_ref, slots_ref = refs
        groups, message, width = slots_ref.shape
        place = spread_slots(slot_row, experts * capacity // groups, message)
        dispatch = one_hot(iota((groups * message, length), 0) == place)
        slots_ref[...] = dot(dispatch, cot_ref[0, 0]).astype(BF16).reshape(groups, message, width)
    srow_ref[0] = slot_row
    scol_ref[0] = jnp.where(valid_col & (rank_col < capacity), col * capacity + rank_col, -1)


def prep(batch, after, lengths, routes, cot, groups, experts, capacity):
    batches, length = routes.shape
    width = cot.shape[-1]
    rows = routes.reshape(batches, 1, length)
    columns = routes.reshape(batches, length, 1)
    first = batch == 0
    message = padded(experts // groups * capacity)
    return pl.pallas_call(
        functools.partial(prep_kernel, batch, experts, capacity, len(after)),
        grid=(1,),
        in_specs=[ANYWHERE] * len(after)
        + [SCALARS, batch_block(rows, batch), batch_block(columns, batch)]
        + ([batch_block(cot, 0)] if first else []),
        out_specs=[WHOLE] * (3 if first else 2),
        out_shape=[jax.ShapeDtypeStruct((1, 1, length), jnp.int32), jax.ShapeDtypeStruct((1, length, 1), jnp.int32)]
        + ([jax.ShapeDtypeStruct((groups, message, width), BF16)] if first else []),
        compiler_params=params(60),
        cost_estimate=cost(),
    )(*after, lengths, rows, columns, *((cot,) if first else ()))


def slot_places(kinds, local, groups, capacity, message):
    row = iota((1, kinds * local * groups * capacity), 1)
    slot = lax.rem(row, capacity)
    row = lax.div(row, capacity)
    group = lax.rem(row, groups)
    return group * message + lax.div(row, groups) * capacity + slot


def regroup_kernel(back, kinds, local, groups, capacity, message, waits, *refs):
    refs = refs[waits:]
    out_ref = refs[-1]
    total = refs[0][...].astype(F32)
    for ref in refs[1:-1]:
        total = total + ref[...].astype(F32)
    places = slot_places(kinds, local, groups, capacity, message)
    move = one_hot(iota((groups * message, places.shape[1]), 0) == places)
    if back:
        rows = dot(move, total.astype(BF16).reshape(places.shape[1], -1))
    else:
        rows = t_dot(move, total.astype(BF16).reshape(groups * message, -1))
    out_ref[...] = rows.astype(BF16).reshape(out_ref.shape)


def regroup(back, arrays, shape, kinds, local, groups, capacity, message, after=()):
    return pl.pallas_call(
        functools.partial(regroup_kernel, back, kinds, local, groups, capacity, message, len(after)),
        in_specs=[ANYWHERE] * len(after) + [WHOLE] * len(arrays),
        out_specs=WHOLE,
        out_shape=jax.ShapeDtypeStruct(shape, BF16),
        compiler_params=params(60),
        cost_estimate=cost(),
    )(*after, *arrays)


def regroup_gated_kernel(capacity, *refs):
    in_ref, out_ref = refs[-2:]
    groups, message, width = in_ref.shape
    total = out_ref.shape[0] - 16
    local = total // (groups * capacity)
    rows = groups * capacity
    flat = in_ref[...].reshape(groups * message, width)
    places = slot_places(1, local, groups, capacity, message)
    move = one_hot(iota((groups * message, total), 0) == places)
    out_ref[:total, :] = t_dot(move, flat).astype(BF16)
    place = iota((message, 128), 0)
    lane = iota((message, 128), 1)
    columns = []
    for g in range(groups):
        gates = in_ref[g, message - 16 : message, :].astype(F32)[0:1, :]
        parts = [
            jnp.sum(jnp.where(place == lane, gates[:, 128 * k : 128 * (k + 1)], 0.0), axis=1, keepdims=True)
            for k in range(3)
        ]
        wide = iota((message, 128), 1)
        columns.append(jnp.where(wide == 0, parts[0], jnp.where(wide == 1, parts[1], jnp.where(wide == 2, parts[2], 0.0))))
    column = jnp.concatenate(columns, axis=0).astype(BF16)
    moved = t_dot(move, column)
    place = iota((rows, 128), 0)
    lane = iota((rows, 128), 1)
    lines = []
    for l in range(local):
        mine = moved[l * rows : (l + 1) * rows, :]
        parts = [
            jnp.sum(jnp.where(place == lane, mine[:, k : k + 1], 0.0), axis=0, keepdims=True) for k in range(3)
        ]
        lines.append(jnp.concatenate(parts + [jnp.zeros((1, width - 384), F32)], axis=1))
    lines.append(jnp.zeros((16 - local, width), F32))
    out_ref[total:, :] = jnp.concatenate(lines, axis=0).astype(BF16)


def regroup_gated(slots, rows, capacity, after=()):
    width = slots.shape[-1]
    return pl.pallas_call(
        functools.partial(regroup_gated_kernel, capacity),
        in_specs=[ANYWHERE] * len(after) + [WHOLE],
        out_specs=WHOLE,
        out_shape=jax.ShapeDtypeStruct((rows + 16, width), BF16),
        compiler_params=params(60),
        cost_estimate=cost(),
    )(*after, slots)


def band_bias(vector_ref, head):
    wide = jnp.broadcast_to(vector_ref[head], (ROWS, vector_ref.shape[-1]))
    return pltpu.roll(wide, 0, 1, stride=1, stride_axis=0)


def band_slice(block, length):
    start = length - ROWS * (block + 1)
    return slice(start, start + length)


def attn_kernel(batch, waits, *refs):
    refs = refs[waits:]
    len_ref, tok_ref, gain_ref, wq_ref, wk_ref, wv_ref, vec_ref, qkv_ref, mixed_ref, lse_ref, bands_ref, probs_ref, mixed_t_ref = refs
    length, width = tok_ref.shape[2:]
    count = len_ref[batch]
    tokens = tok_ref[0, 0].astype(F32)
    inverse = lax.rsqrt(jnp.mean(tokens * tokens, axis=-1, keepdims=True) + epsilon)
    normed = (tokens * inverse * gain_ref[...]).astype(BF16)
    for which, w_ref in enumerate((wq_ref, wk_ref, wv_ref)):
        for part in range(width // 256):
            rows = dot(normed, w_ref[:, 256 * part : 256 * part + 256]).astype(BF16)
            qkv_ref[which, 2 * part] = rows[:, :PAIR]
            qkv_ref[which, 2 * part + 1] = rows[:, PAIR:]
    mask = jnp.where(iota((1, length), 1) < count, 0.0, negative)
    lane = iota((ROWS, PAIR), 1)
    lse_ref[...] = jnp.zeros_like(lse_ref)

    def one_pair(pair, carry):
        keys = qkv_ref[1, pair]
        values_t = qkv_ref[2, pair].T
        for side in range(2):
            head = 2 * pair + side
            bands_ref[side] = band_bias(vec_ref, head)
            mine = (lane >= HEAD_DIM) if side else (lane < HEAD_DIM)
            for block in range(length // ROWS):
                here = slice(ROWS * block, ROWS * (block + 1))
                queries = qkv_ref[0, pair, here, :] * 0.125
                queries = jnp.where(mine, queries, jnp.zeros_like(queries))
                scores = dot_t(queries, keys) + bands_ref[side, :, band_slice(block, length)] + mask
                highest = jnp.max(scores, axis=-1, keepdims=True)
                powers = jnp.exp(scores - highest)
                total = jnp.sum(powers, axis=-1, keepdims=True)
                probs_ref[side, here, :] = (powers * (1.0 / total)).astype(BF16)
                column = iota((ROWS, lse_ref.shape[1]), 1)
                lse_ref[here, :] = jnp.where(column == head, highest + jnp.log(total), lse_ref[here, :])
            rows = slice(HEAD_DIM * side, HEAD_DIM * (side + 1))
            mixed_t_ref[rows, :] = dot_t(values_t[rows, :], probs_ref[side])
        mixed_ref[pair] = mixed_t_ref[...].T.astype(BF16)
        return carry

    lax.fori_loop(0, PAIRS, one_pair, 0, unroll=3)


def attention_forward(batch, after, counts, tokens, gain, wq, wk, wv, vector):
    length = tokens.shape[2]
    return pl.pallas_call(
        functools.partial(attn_kernel, batch, len(after)),
        grid=(1,),
        in_specs=[ANYWHERE] * len(after) + [SCALARS, batch_block(tokens, batch)] + [WHOLE] * 5,
        out_specs=[WHOLE] * 3,
        out_shape=[
            jax.ShapeDtypeStruct((3, PAIRS, length, PAIR), BF16),
            jax.ShapeDtypeStruct((PAIRS, length, PAIR), BF16),
            jax.ShapeDtypeStruct((length, 128), F32),
        ],
        scratch_shapes=[
            pltpu.VMEM((2, ROWS, vector.shape[-1]), F32),
            pltpu.VMEM((2, length, length), BF16),
            pltpu.VMEM((PAIR, length), F32),
        ],
        compiler_params=params(60),
        cost_estimate=cost(),
    )(*after, counts, tokens, gain, wq, wk, wv, vector)


def route_kernel(per, gated, waits, *refs):
    refs = refs[waits:]
    tok_ref, cot_ref, mixed_ref, wo_ref, gffn_ref, wr_ref, srow_ref, rcol_ref, res_ref, probs_ref, *out_refs = refs
    length, width = tok_ref.shape[2:]
    mixed_all = jnp.concatenate([mixed_ref[p] for p in range(PAIRS)], axis=1)
    residual = tok_ref[0, 0].astype(F32) + dot(mixed_all, wo_ref[...])
    res_ref[...] = residual
    inverse = lax.rsqrt(jnp.mean(residual * residual, axis=-1, keepdims=True) + epsilon)
    routed = (residual * inverse * gffn_ref[...]).astype(BF16)
    logits = dot_t(routed, wr_ref[...])
    powers = jnp.exp(logits - jnp.max(logits, axis=-1, keepdims=True))
    probs = powers / jnp.sum(powers, axis=-1, keepdims=True)
    probs_ref[...] = probs
    gate = jnp.sum(jnp.where(iota(probs.shape, 1) == rcol_ref[0], probs, 0.0), axis=-1, keepdims=True)
    groups, message, _ = out_refs[0].shape
    places = iota((groups * message, length), 0)
    if gated:
        grads = (gate * cot_ref[0, 0].astype(F32)).astype(BF16)
        half = per // 2
        for which, out_ref in enumerate(out_refs):
            place = spread_slots(srow_ref[0], per, message, which * half, (which + 1) * half)
            rows = dot(one_hot(places == place), grads)
            rows = rows + dot(one_hot(places == jnp.where(place < 0, -1, place + half)), routed)
            out_ref[...] = rows.astype(BF16).reshape(out_ref.shape)
        return
    slots_ref = out_refs[0]
    dispatch = one_hot(places == spread_slots(srow_ref[0], per, message))
    slots_ref[...] = dot(dispatch, routed).astype(BF16).reshape(slots_ref.shape)
    first = gate.astype(BF16).astype(F32)
    second = (gate - first).astype(BF16).astype(F32)
    third = gate - first - second
    column = iota((length, PAIR), 1)
    pieces = jnp.where(column == 0, first, jnp.where(column == 1, second, jnp.where(column == 2, third, 0.0)))
    sorted_gates = dot(dispatch, pieces.astype(BF16))
    data = message - 16
    place = iota((data, 128), 0)
    lane = iota((data, 128), 1)
    for g in range(groups):
        mine = sorted_gates[g * message : g * message + data, :]
        parts = [
            jnp.sum(jnp.where(place == lane, mine[:, k : k + 1], 0.0), axis=0, keepdims=True) for k in range(3)
        ]
        line = jnp.concatenate(parts + [jnp.zeros((1, width - 384), F32)], axis=1)
        slots_ref[g, data:message, :] = jnp.broadcast_to(line, (16, width)).astype(BF16)


def route(batch, after, tokens, cot, mixed, wo, gain_ffn, w_router, srow, rcol, groups, per, gated):
    length, width = tokens.shape[2:]
    experts = w_router.shape[0]
    message = padded(per) if gated else padded(per) + 16
    return pl.pallas_call(
        functools.partial(route_kernel, per, gated, len(after)),
        grid=(1,),
        in_specs=[ANYWHERE] * len(after)
        + [batch_block(tokens, batch), batch_block(cot, batch) if gated else ANYWHERE]
        + [WHOLE] * 5
        + [batch_block(rcol, batch)],
        out_specs=[WHOLE] * (4 if gated else 3),
        out_shape=[
            jax.ShapeDtypeStruct((length, width), F32),
            jax.ShapeDtypeStruct((length, experts), F32),
        ]
        + [jax.ShapeDtypeStruct((groups, message, width), BF16)] * (2 if gated else 1),
        compiler_params=params(60),
        cost_estimate=cost(),
    )(*after, tokens, cot, mixed, wo, gain_ffn, w_router, srow, rcol)


GELU_SCALE = 0.7978845608028654
GELU_CUBIC = 0.044715


def expert_kernel(planes, gated, first_expert, waits, *refs):
    pieces = 2 * planes - 1
    refs = refs[waits:]
    plane = refs[0][0]
    x_refs, refs = refs[1 : 1 + pieces], refs[1 + pieces :]
    c_refs, refs = refs[:pieces], refs[pieces:]
    gate_refs = ()
    if not gated:
        gate_refs, refs = refs[:pieces], refs[pieces:]
    wi_ref, wo_ref, *refs = refs
    sum_refs = refs[:planes]
    act_ref, pre_ref, x_ref, c_ref = refs[planes:]
    rows = x_refs[0].shape[0]

    def assemble(parts):
        found = [parts[0][...]]
        for k in range(1, planes):
            from_above = plane + k < planes
            found.append(jnp.where(from_above, parts[k][...], parts[2 * planes - 1 - k][...]))
        return found

    inputs = jnp.concatenate(assemble(x_refs), axis=0)
    grads = assemble(c_refs)
    if not gated:
        place = iota((rows, 128), 0)
        lane = iota((rows, 128), 1)
        expert = first_expert + pl.program_id(0)
        for k, lines in enumerate(assemble(gate_refs)):
            lines = jnp.where(iota(lines.shape, 0) == expert, lines.astype(F32), 0.0)
            line = jnp.sum(lines, axis=0, keepdims=True)
            line = line[:, :128] + line[:, 128:256] + line[:, 256:384]
            gate = jnp.sum(jnp.where(place == lane, line, 0.0), axis=1, keepdims=True)
            grads[k] = (grads[k].astype(F32) * gate).astype(BF16)
    grads = jnp.concatenate(grads, axis=0)
    x_ref[0] = inputs
    c_ref[0] = grads
    pre = dot(inputs, wi_ref[0])
    square = pre * pre
    curve = jnp.tanh(GELU_SCALE * pre * (1.0 + GELU_CUBIC * square))
    half = 0.5 * (1.0 + curve)
    act = (pre * half).astype(BF16)
    slope = half + 0.5 * pre * (1.0 - curve * curve) * (GELU_SCALE * (1.0 + 3.0 * GELU_CUBIC * square))
    act_ref[0] = act
    outs = dot(act, wo_ref[0]).astype(BF16)
    pre_grad = (slope * dot_t(grads, wo_ref[0])).astype(BF16)
    pre_ref[0] = pre_grad
    ins = dot_t(pre_grad, wi_ref[0]).astype(BF16)
    for k in range(planes):
        sum_refs[k][0] = outs[k * rows : (k + 1) * rows]
        sum_refs[k][1] = ins[k * rows : (k + 1) * rows]


def experts_half(which, after, plane, messages, w_inner, w_outer, xs=None, cs=None):
    local, width, hidden = w_inner.shape
    mine = local // 2
    first = which * mine
    gated = messages is not None
    pieces = len(messages if gated else xs)
    planes = (pieces + 1) // 2
    if gated:
        rows = messages[0].shape[1] // mine
        x_block = pl.BlockSpec((None, rows, width), lambda e: (1, e, 0))
        c_block = pl.BlockSpec((None, rows, width), lambda e: (0, e, 0))
        arrays = (*messages, *messages)
        blocks = [x_block] * pieces + [c_block] * pieces
    else:
        rows = cs[0].shape[0] // local
        slab = pl.BlockSpec((rows, width), lambda e: (first + e, 0))
        lines = pl.BlockSpec((16, width), lambda e: (local * rows // 16, 0))
        arrays = (*xs, *cs, *xs)
        blocks = [slab] * (2 * pieces) + [lines] * pieces
    weight = lambda a, b: pl.BlockSpec((1, a, b), lambda e: (first + e, 0, 0))
    mat = lambda a, b: pl.BlockSpec((1, a, b), lambda e: (e, 0, 0))
    total = planes * rows
    kept = lambda n: jax.ShapeDtypeStruct((mine, total, n), BF16)
    return pl.pallas_call(
        functools.partial(expert_kernel, planes, gated, first, len(after)),
        grid=(mine,),
        in_specs=[ANYWHERE] * len(after) + [SCALARS] + blocks + [weight(width, hidden), weight(hidden, width)],
        out_specs=[pl.BlockSpec((2, rows, width), lambda e: (0, e, 0))] * planes
        + [mat(total, hidden), mat(total, hidden), mat(total, width), mat(total, width)],
        out_shape=[jax.ShapeDtypeStruct((2, mine * rows, width), BF16)] * planes
        + [kept(hidden), kept(hidden), kept(width), kept(width)],
        compiler_params=params(60),
        cost_estimate=cost(),
    )(*after, plane, *arrays, w_inner, w_outer)


def expert_grad_kernel(batches, waits, *refs):
    xs, cs, acts, pres = (refs[waits + k * batches : waits + (k + 1) * batches] for k in range(4))
    outer_ref, inner_ref = refs[-2:]
    whole = lambda refs: jnp.concatenate([ref[0] for ref in refs], axis=0)
    outer_ref[0] = t_dot(whole(acts), whole(cs))
    inner_ref[0] = t_dot(whole(xs), whole(pres))


def expert_grads(which, after, past, local, xs, cs, acts, pres):
    batches = len(xs)
    mine, total, width = xs[0].shape
    hidden = acts[0].shape[2]
    first = which * mine
    mat = lambda a, b: pl.BlockSpec((1, a, b), lambda e: (e, 0, 0))
    out = lambda a, b: pl.BlockSpec((1, a, b), lambda e: (first + e, 0, 0))
    behind = len(after) + 4 * batches
    return pl.pallas_call(
        functools.partial(expert_grad_kernel, batches, len(after)),
        grid=(mine,),
        in_specs=[ANYWHERE] * len(after)
        + [mat(total, width)] * (2 * batches)
        + [mat(total, hidden)] * (2 * batches)
        + [ANYWHERE] * len(past),
        out_specs=[out(hidden, width), out(width, hidden)],
        out_shape=[
            jax.ShapeDtypeStruct((local, hidden, width), F32),
            jax.ShapeDtypeStruct((local, width, hidden), F32),
        ],
        input_output_aliases={behind + k: k for k in range(len(past))},
        compiler_params=params(60),
        cost_estimate=cost(),
    )(*after, *xs, *cs, *acts, *pres, *past)


def combine_kernel(per, batch, waits, *refs):
    refs = refs[waits:]
    len_ref, low_ref, high_ref, scol_ref, rcol_ref, res_ref, probs_ref, cot_ref, gffn_ref, wr_ref, wo_ref, mixed_ref, *refs = refs
    past_ref = refs.pop(0) if batch else None
    layer_ref, resgrad_ref, mgrad_ref, shared_ref, *buffers, sems = refs
    fetched = [res_ref, cot_ref.at[batch, 0], mixed_ref, wo_ref] + ([past_ref] if batch else [])
    copies = [pltpu.make_async_copy(ref, buffer, sems.at[k]) for k, (ref, buffer) in enumerate(zip(fetched, buffers))]
    for copy in copies:
        copy.start()
    res_ref, cot_ref, mixed_ref, wo_ref = buffers[:4]
    if batch:
        past_ref = buffers[4]
    length, width = cot_ref.shape
    experts = wr_ref.shape[0]
    groups, message, _ = low_ref.shape
    valid = iota((length, 1), 0) < len_ref[batch]
    places = iota((length, groups * message), 1)
    half = per // 2
    returned = input_grad = None
    for which, ref in enumerate((low_ref, high_ref)):
        place = spread_slots(scol_ref[0], per, message, which * half, (which + 1) * half)
        rows = ref[...].reshape(groups * message, width)
        out_part = dot(one_hot(places == place), rows)
        in_part = dot(one_hot(places == jnp.where(place < 0, -1, place + half)), rows)
        returned = out_part if returned is None else returned + out_part
        input_grad = in_part if input_grad is None else input_grad + in_part
    copies[0].wait()
    copies[1].wait()
    residual = res_ref[...]
    probs = probs_ref[...]
    chosen = iota(probs.shape, 1) == rcol_ref[0]
    gate = jnp.sum(jnp.where(chosen, probs, 0.0), axis=-1, keepdims=True)
    layer_ref[0, 0] = jnp.where(valid, residual + gate * returned, 0.0).astype(BF16)
    out_grad = jnp.where(valid, cot_ref[...].astype(F32), 0.0)
    gate_grad = jnp.sum(out_grad * returned, axis=-1, keepdims=True)
    prob_grad = jnp.where(chosen, gate_grad, 0.0)
    logit_grad = (probs * (prob_grad - jnp.sum(probs * prob_grad, axis=-1, keepdims=True))).astype(BF16)
    inverse = lax.rsqrt(jnp.mean(residual * residual, axis=-1, keepdims=True) + epsilon)
    gain = gffn_ref[...]
    scaled = residual * inverse
    routed = (scaled * gain).astype(BF16)

    def share(first, whole_rows):
        for side in range(2):
            rows = whole_rows[:, side * width // 2 : (side + 1) * width // 2]
            here = slice(side * shared_ref.shape[0] // 2 + first, side * shared_ref.shape[0] // 2 + first + rows.shape[0])
            if past_ref is not None:
                rows = rows + past_ref[here, :]
            shared_ref[here, :] = rows.astype(shared_ref.dtype)

    for copy in copies[2:]:
        copy.wait()
    share(width, t_dot(logit_grad, routed))
    routed_grad = dot(logit_grad, wr_ref[...]) + input_grad
    gain_part = jnp.sum(routed_grad * scaled, axis=0, keepdims=True)
    left = shared_ref.shape[0] // 2 - width - experts
    share(width + experts, jnp.where(iota((left, width), 0) == 0, gain_part, 0.0))
    upstream = routed_grad * gain
    middle = jnp.mean(upstream * scaled, axis=-1, keepdims=True)
    residual_grad = out_grad + inverse * (upstream - scaled * middle)
    resgrad_ref[...] = residual_grad
    attended = residual_grad.astype(BF16)
    mixed_all = jnp.concatenate([mixed_ref[p] for p in range(PAIRS)], axis=1)
    share(0, t_dot(mixed_all, attended))
    mixed_grad = dot_t(attended, wo_ref[...]).astype(BF16)
    for pair in range(PAIRS):
        mgrad_ref[pair] = mixed_grad[:, pair * PAIR : (pair + 1) * PAIR]


def combine(
    batch, last, after, layers, counts, low, high, scol, rcol, residual, probs, cot, gain_ffn, w_router, w_output, mixed, past, per, shared
):
    length, width = cot.shape[2:]
    return pl.pallas_call(
        functools.partial(combine_kernel, per, batch, len(after) + len(layers)),
        grid=(1,),
        in_specs=[ANYWHERE] * (len(after) + len(layers))
        + [SCALARS, WHOLE, WHOLE, WHOLE, batch_block(rcol, batch), ANYWHERE, WHOLE, ANYWHERE]
        + [WHOLE] * 2
        + [ANYWHERE] * (2 + len(past)),
        out_specs=[batch_block(cot, batch)] + [WHOLE] * 3,
        out_shape=[
            jax.ShapeDtypeStruct(cot.shape, BF16),
            jax.ShapeDtypeStruct((length, width), F32),
            jax.ShapeDtypeStruct((PAIRS, length, PAIR), BF16),
            jax.ShapeDtypeStruct((shared, width // 2), BF16 if last else F32),
        ],
        scratch_shapes=[
            pltpu.VMEM(residual.shape, residual.dtype),
            pltpu.VMEM((length, width), BF16),
            *(pltpu.VMEM(array.shape, array.dtype) for array in (mixed, w_output, *past)),
            pltpu.SemaphoreType.DMA((4 + len(past),)),
        ],
        input_output_aliases={len(after): 0} if layers else {},
        compiler_params=params(60),
        cost_estimate=cost(),
    )(
        *after, *layers, counts, low, high, scol, rcol, residual, probs, cot, gain_ffn, w_router, w_output, mixed, *past
    )


def attn_back_kernel(batch, which, last, waits, *refs):
    refs = refs[waits:]
    side_ref, len_ref, qkv_ref, lse_ref, vec_ref, sel_ref, mgrad_ref, tok_ref, gain_ref, wq_ref, wk_ref, wv_ref, *refs = refs
    past_ref = refs.pop(0) if batch else None
    if which:
        seen_ref, part_ref, resgrad_ref, *refs = refs
        tgrad_ref, *refs = refs
    else:
        early_ref = refs.pop(0) if batch else None
        diag_out_ref, part_out_ref, *refs = refs
    shared_refs, refs = refs[: 1 + last], refs[1 + last :]
    bands_ref, probs_ref, sgrad_ref, spread_ref, low_ref, qt_ref, kt_ref, vt_ref, diag_ref, stage_ref, rest_ref, *buffers = refs
    *buffers, sems, out_sems = buffers
    half = wq_ref.shape[0] // 2
    columns = pl.ds(which * half, half)
    fetched = [tok_ref.at[batch, 0]] + [ref.at[:, columns] for ref in (wq_ref, wk_ref, wv_ref)]
    if past_ref is not None:
        fetched.append(past_ref)
    if which:
        fetched += [part_ref, resgrad_ref]
    elif batch:
        fetched.append(early_ref)
    copies = [pltpu.make_async_copy(ref, buffer, sems.at[k]) for k, (ref, buffer) in enumerate(zip(fetched, buffers))]
    for copy in copies:
        copy.start()
    going = []
    offset = early_ref.shape[0] if last and not which else 0
    part_rows = shared_refs[0].shape[0]
    tok_ref, wq_ref, wk_ref, wv_ref, *buffers = buffers
    if past_ref is not None:
        past_ref = buffers.pop(0)
    if which:
        part_ref, resgrad_ref = buffers
    elif batch:
        early_ref = buffers[0]
    length, width = tok_ref.shape
    first_pair = which * (PAIRS // 2)
    mask = jnp.where(iota((1, length), 1) < len_ref[batch], 0.0, negative)
    lane = iota((ROWS, PAIR), 1)
    diag_ref[...] = seen_ref[...] if which else jnp.zeros_like(diag_ref)

    def one_pair(step, carry):
        pair = first_pair + step
        keys = qkv_ref[1, step]
        values = qkv_ref[2, step]
        queries_t = qkv_ref[0, step].T
        keys_t = qkv_ref[1, step].T
        grads_t = mgrad_ref[step].T
        for side in range(2):
            head = 2 * pair + side
            bands_ref[side] = band_bias(vec_ref, head)
            spread_ref[side] = jnp.zeros(spread_ref.shape[1:], F32)
            mine = (lane >= HEAD_DIM) if side else (lane < HEAD_DIM)
            for block in range(length // ROWS):
                here = slice(ROWS * block, ROWS * (block + 1))
                window = band_slice(block, length)
                queries = qkv_ref[0, step, here, :] * 0.125
                queries = jnp.where(mine, queries, jnp.zeros_like(queries))
                grads = mgrad_ref[step, here, :]
                grads = jnp.where(mine, grads, jnp.zeros_like(grads))
                column = iota((ROWS, lse_ref.shape[1]), 1)
                log_total = jnp.sum(jnp.where(column == head, lse_ref[here, :], 0.0), axis=-1, keepdims=True)
                scores = dot_t(queries, keys) + bands_ref[side, :, window] + mask
                probs = jnp.exp(scores - log_total)
                probs_ref[side, here, :] = probs.astype(BF16)
                weighted = probs * dot_t(grads, values)
                score_grad = weighted - probs * jnp.sum(weighted, axis=-1, keepdims=True)
                spread_ref[side, :, window] += score_grad
                sgrad_ref[side, here, :] = score_grad.astype(BF16)
            rows = slice(HEAD_DIM * side, HEAD_DIM * (side + 1))
            qt_ref[rows, :] = dot_t(keys_t[rows, :], sgrad_ref[side]) * 0.125
            kt_ref[rows, :] = dot(queries_t[rows, :], sgrad_ref[side]) * 0.125
            vt_ref[rows, :] = dot(grads_t[rows, :], probs_ref[side])
            size = spread_ref.shape[2]
            eight = spread_ref[side, 0:8, :]
            for move in range(8, ROWS, 8):
                eight = eight + pltpu.roll(spread_ref[side, move : move + 8, :], size - move, 1)
            diagonal = eight[0:1, :]
            for move in range(1, 8):
                diagonal = diagonal + pltpu.roll(eight[move : move + 1, :], size - move, 1)
            diag_ref[...] = jnp.where(iota(diag_ref.shape, 0) == head, diagonal, diag_ref[...])
        low_ref[0, step] = qt_ref[...].T.astype(BF16)
        low_ref[1, step] = kt_ref[...].T.astype(BF16)
        low_ref[2, step] = vt_ref[...].T.astype(BF16)
        return carry

    lax.fori_loop(0, PAIRS // 2, one_pair, 0)
    for copy in copies:
        copy.wait()

    def send(source, first, place):
        count = source.shape[0]
        for k in range(1 + last):
            low, high = max(first, k * part_rows), min(first + count, (k + 1) * part_rows)
            if low >= high:
                continue
            part = source.at[pl.ds(low - first, high - low)]
            for turn in range(1 + last):
                there = shared_refs[turn].at[pl.ds(low - k * part_rows, high - low)]
                copy = pltpu.make_async_copy(part, there, out_sems.at[place, k])
                going.append((copy, k ^ turn))

                @pl.when(side_ref[0] == (k ^ turn) if last else True)
                def _():
                    copy.start()

    if offset:
        send(early_ref, 0, 0)

    def past(first, count):
        return 0.0 if past_ref is None else past_ref[first : first + count, :]

    tokens = tok_ref[...].astype(F32)
    inverse = lax.rsqrt(jnp.mean(tokens * tokens, axis=-1, keepdims=True) + epsilon)
    gain = gain_ref[...]
    scaled = tokens * inverse
    normed_t = (scaled * gain).astype(BF16).T
    normed_grad = part_ref[...] if which else jnp.zeros((length, width), F32)
    for matrix, w_ref in enumerate((wq_ref, wk_ref, wv_ref)):
        low = jnp.concatenate([low_ref[matrix, p] for p in range(PAIRS // 2)], axis=1)
        stage_ref[matrix] = (dot(normed_t, low) + past(matrix * width, width)).astype(stage_ref.dtype)
        send(stage_ref.at[matrix], offset + matrix * width, 1 + matrix)
        normed_grad = normed_grad + dot_t(low, w_ref[...])
    left = rest_ref.shape[0]
    if which:
        gain_part = jnp.sum(normed_grad * scaled, axis=0, keepdims=True)
        bias_part = lax.dot_general(
            diag_ref[...],
            sel_ref[...],
            (((1,), (0,)), ((), ())),
            precision=lax.Precision.HIGHEST,
            preferred_element_type=F32,
        )
        row = iota((8, half), 0)
        gains = jnp.where(row == 0, gain_part[:, :half], jnp.where(row == 1, gain_part[:, half:], 0.0))
        wide = jnp.concatenate([bias_part, jnp.zeros((16, half - bias_part.shape[1]), F32)], axis=1)
        tail = [gains, wide] + ([jnp.zeros((left - 24, half), F32)] if left > 24 else [])
        rest_ref[...] = (jnp.concatenate(tail, axis=0) + past(3 * width, left)).astype(rest_ref.dtype)
        send(rest_ref, 3 * width, 4)
        upstream = normed_grad * gain
        middle = jnp.mean(upstream * scaled, axis=-1, keepdims=True)
        tgrad_ref[0, 0] = (resgrad_ref[...] + inverse * (upstream - scaled * middle)).astype(BF16)
    else:
        if offset and offset + 3 * width < 2 * part_rows:
            rest_ref[...] = jnp.zeros_like(rest_ref)
            send(rest_ref, offset + 3 * width, 4)
        diag_out_ref[...] = diag_ref[...]
        part_out_ref[...] = normed_grad
    for copy, turn in going:

        @pl.when(side_ref[0] == turn if last else True)
        def _():
            copy.wait()


def attention_backward(batch, which, last, after, grads, side, counts, qkv, lse, vector, selector, mixed_grad, tokens, gain, wq, wk, wv, past, more, rows):
    length, width = tokens.shape[2:]
    half = width // 2
    size = vector.shape[-1]
    late = (*past, *(more[1:] if which else more))
    buffers = [((length, width), BF16)] + [((width, half), BF16)] * 3 + [(array.shape, array.dtype) for array in late]
    sent = 0 if which or not last else more[0].shape[0]
    rest = max(rows - sent - 3 * width, 16)
    shared = jax.ShapeDtypeStruct((rows // 2 if last else rows, half), BF16 if last else F32)
    if which:
        outs = [jax.ShapeDtypeStruct(tokens.shape, BF16)]
        out_specs = [batch_block(tokens, batch)]
    else:
        outs = [jax.ShapeDtypeStruct((16, size), F32), jax.ShapeDtypeStruct((length, width), F32)]
        out_specs = [WHOLE] * 2
    outs += [shared] * (2 if last else 1)
    out_specs += [ANYWHERE] * (2 if last else 1)
    return pl.pallas_call(
        functools.partial(attn_back_kernel, batch, which, last, len(after) + len(grads)),
        grid=(1,),
        in_specs=[ANYWHERE] * (len(after) + len(grads))
        + [SCALARS, SCALARS, pl.BlockSpec((3, PAIRS // 2, length, PAIR), lambda _: (0, which, 0, 0))]
        + [WHOLE] * 3
        + [pl.BlockSpec((PAIRS // 2, length, PAIR), lambda _: (which, 0, 0))]
        + [ANYWHERE, WHOLE]
        + [ANYWHERE] * (3 + len(past))
        + [WHOLE if which and k == 0 else ANYWHERE for k in range(len(more))],
        out_specs=out_specs,
        out_shape=outs,
        input_output_aliases={len(after): 0} if grads else {},
        scratch_shapes=[
            pltpu.VMEM((2, ROWS, size), F32),
            pltpu.VMEM((2, length, length), BF16),
            pltpu.VMEM((2, length, length), BF16),
            pltpu.VMEM((2, ROWS, size), F32),
            pltpu.VMEM((3, PAIRS // 2, length, PAIR), BF16),
            pltpu.VMEM((PAIR, length), F32),
            pltpu.VMEM((PAIR, length), F32),
            pltpu.VMEM((PAIR, length), F32),
            pltpu.VMEM((16, size), F32),
            pltpu.VMEM((3, width, half), shared.dtype),
            pltpu.VMEM((rest, half), shared.dtype),
            *(pltpu.VMEM(shape, kind) for shape, kind in buffers),
            pltpu.SemaphoreType.DMA((len(buffers),)),
            pltpu.SemaphoreType.DMA((5, 2)),
        ],
        compiler_params=params(60),
        cost_estimate=cost(),
    )(*after, *grads, side, counts, qkv, lse, vector, selector, mixed_grad, tokens, gain, wq, wk, wv, *past, *more)


def unpack_kernel(early, side_ref, *refs):
    arrived, refs = refs[:4], refs[4:]
    q_ref, k_ref, v_ref, output_ref, router_ref, gain_f_ref, gain_a_ref, bias_ref, *refs = refs
    buffers, (stage_ref, in_sems, out_sems) = refs[:4], refs[4:]
    copies = [
        pltpu.make_async_copy(ref, buffer, in_sems.at[k]) for k, (ref, buffer) in enumerate(zip(arrived, buffers))
    ]
    for copy in copies:
        copy.start()
    swapped = side_ref[0] == 1

    def whole(k):
        copies[k].wait()
        copies[k + 1].wait()
        mine, other = buffers[k][...], buffers[k + 1][...]
        parts = [jnp.where(swapped, other, mine), jnp.where(swapped, mine, other)]
        return jnp.concatenate(parts, axis=0).astype(F32)

    leaving = [
        pltpu.make_async_copy(stage_ref.at[k], ref, out_sems.at[k])
        for k, ref in enumerate((q_ref, k_ref, v_ref, output_ref))
    ]
    rows = whole(0)
    half = rows.shape[1]
    width = 2 * half
    last = early - 16
    stage_ref[3, :, :half] = rows[:width]
    stage_ref[3, :, half:] = rows[early : early + width]
    leaving[3].start()
    router_ref[...] = jnp.concatenate([rows[width:last], rows[early + width : early + last]], axis=1)
    gain_f_ref[...] = jnp.concatenate([rows[last], rows[early + last]])
    for k in range(3):
        stage_ref[k, :, :half] = rows[2 * early + k * width : 2 * early + (k + 1) * width]
    rows = whole(2)
    for k in range(3):
        stage_ref[k, :, half:] = rows[k * width : (k + 1) * width]
        leaving[k].start()
    gain_a_ref[...] = jnp.concatenate([rows[3 * width], rows[3 * width + 1]])
    bias_ref[...] = rows[3 * width + 8 : 3 * width + 8 + HEADS, :BUCKETS]
    for copy in leaving:
        copy.wait()


def unpack(early, experts, side, first, first_other, second, second_other):
    width = 2 * first.shape[1]
    matrix = jax.ShapeDtypeStruct((width, width), F32)
    line = jax.ShapeDtypeStruct((width,), F32)
    arrays = (first, first_other, second, second_other)
    return pl.pallas_call(
        functools.partial(unpack_kernel, early),
        in_specs=[SCALARS] + [ANYWHERE] * 4,
        out_specs=[ANYWHERE] * 4 + [WHOLE] * 4,
        out_shape=[matrix] * 4
        + [jax.ShapeDtypeStruct((experts, width), F32), line, line, jax.ShapeDtypeStruct((HEADS, BUCKETS), F32)],
        scratch_shapes=[pltpu.VMEM(array.shape, array.dtype) for array in arrays]
        + [pltpu.VMEM((4, width, width), F32), pltpu.SemaphoreType.DMA((4,)), pltpu.SemaphoreType.DMA((4,))],
        compiler_params=params(60),
        cost_estimate=cost(),
    )(side, *arrays)


def upward(planes, first, last):
    return [(k, k + 1) for k in range(first, last)]


def downward(planes, first, last):
    return [(planes - 1 - k, planes - 2 - k) for k in range(first, last)]


def mix_kernel(both, planes, step, waits, here_ref, up_ref, down_ref, upsum_ref, downsum_ref, *refs):
    to_up, to_down = refs[waits:]
    for moving, sums, out, place in (
        (up_ref, upsum_ref, to_up, here_ref[0]),
        (down_ref, downsum_ref, to_down, planes - 1 - here_ref[0]),
    ):
        total = moving[...] + sums[...]
        out[...] = jnp.where(place <= step, total, moving[...]) if both else total


def mix(both, planes, step, here, up, down, upsum, downsum, after):
    kinds, rows, width = up.shape
    block = pl.BlockSpec((1, rows // 2, width), lambda i, j: (i, j, 0))
    return pl.pallas_call(
        functools.partial(mix_kernel, both, planes, step, len(after)),
        grid=(kinds, 2),
        in_specs=[SCALARS] + [block] * 4 + [ANYWHERE] * len(after),
        out_specs=[block] * 2,
        out_shape=[jax.ShapeDtypeStruct(up.shape, BF16)] * 2,
        compiler_params=params(32),
        cost_estimate=cost(),
    )(here, up, down, upsum, downsum, *after)


def gate_kernel(*refs):
    pass


def gate(arrays, after):
    count = len(arrays)
    return pl.pallas_call(
        gate_kernel,
        in_specs=[ANYWHERE] * (count + len(after)),
        out_specs=[ANYWHERE] * count,
        out_shape=[jax.ShapeDtypeStruct(array.shape, array.dtype) for array in arrays],
        input_output_aliases={k: k for k in range(count)},
        cost_estimate=cost(),
    )(*arrays, *after)


class Chain:
    def __init__(self, planes, own=None, sums=None):
        self.planes, self.own, self.sums = planes, own, sums
        self.here = lax.axis_index("hidden")[None]
        self.from_below, self.from_above = [], []
        if own is not None:
            self.up = self.down = own
        else:
            self.up, self.down = sums[planes - 1], sums[1]
        self.count = 0
        self.steps = planes if own is not None and sums is not None else planes - 1

    def send(self):
        planes, s = self.planes, self.count
        if self.own is not None and self.sums is not None:
            first, last = 0, planes - 1
        elif self.own is not None:
            first, last = s, planes - 1
        else:
            first, last = 0, s + 1
        self.up = lax.ppermute(self.up, "hidden", upward(planes, first, last))
        self.down = lax.ppermute(self.down, "hidden", downward(planes, first, last))
        self.count += 1
        if self.own is not None and s < planes - 1:
            self.from_below.append(self.up)
            self.from_above.append(self.down)

    def mix(self, *after):
        planes, s = self.planes, self.count - 1
        both = self.own is not None
        offset = 1 if both else 2
        self.up, self.down = mix(
            both, planes, s, self.here, self.up, self.down, self.sums[planes - offset - s], self.sums[s + offset], after
        )
        self.mixed = self.up

    def gate(self, *after):
        self.up, self.down = gate((self.up, self.down), after)
        self.from_below[-1], self.from_above[-1] = self.up, self.down

    def run(self):
        while self.count < self.steps:
            self.send()
        return self

    def gathered(self):
        return (self.own, *self.from_above, *self.from_below)

    def scattered(self):
        return (self.sums[0], self.up, self.down)


def swap(values, axis, distance):
    return lax.ppermute(values, axis, [(k, k ^ distance) for k in range(lax.axis_size(axis))])


def share_sums(values, axis, near, count):
    me = lax.axis_index(axis) // near
    parts = values.reshape(count, values.shape[0] // count, values.shape[1])
    total = lax.dynamic_index_in_dim(parts, me, 0, keepdims=False).astype(F32)
    for k in range(1, count):
        part = lax.dynamic_index_in_dim(parts, me ^ k, 0, keepdims=False)
        total = total + swap(part, axis, k * near).astype(F32)
    return total.astype(BF16)


def join_sums(values, axis, near, count):
    me = lax.axis_index(axis) // near
    found = [values] + [swap(values, axis, k * near) for k in range(1, count)]
    joined = []
    for j in range(count):
        piece = found[count - 1]
        for k in range(count - 2, -1, -1):
            piece = jnp.where(me ^ k == j, found[k], piece)
        joined.append(piece)
    return jnp.concatenate(joined)


def sum_everywhere(values):
    size = lax.axis_size("expert")
    planes = lax.axis_size("hidden")
    values = share_sums(values, "expert", 2, size // 2)
    values = share_sums(values, "hidden", 1, planes)
    values = join_sums(values, "hidden", 1, planes)
    values = join_sums(values, "expert", 2, size // 2)
    return values, swap(values, "expert", 1)


def add_half(mine, other):
    return mine + swap(other, "expert", 1)


def offset_selector(length):
    place = np.arange(2 * length)
    offsets = np.where(place < 2 * length - ROWS, place, place - 2 * length) - (length - ROWS)
    offsets = np.clip(offsets, -(length - 1), length - 1)
    return (offset_bucket(offsets)[:, None] == np.arange(BUCKETS)[None, :]).astype(np.float32)


def shards(
    tokens,
    cotangent,
    lengths,
    routes,
    gain_attn,
    w_query,
    w_key,
    w_value,
    w_output,
    bucket_head_bias,
    gain_ffn,
    w_router,
    w_inner,
    w_outer,
):
    batches, _, length, width = tokens.shape
    experts = w_router.shape[1]
    local = w_inner.shape[0]
    groups = lax.axis_size("expert")
    planes = lax.axis_size("hidden")
    capacity = (5 * length + 4 * experts - 1) // (4 * experts)
    per = local * capacity
    rows = groups * capacity
    message = padded(per)
    in_groups = (groups, capacity, message)
    selector = jnp.asarray(offset_selector(length))
    vector = lax.dot_general(
        bucket_head_bias, selector, (((0,), (1,)), ((), ())), precision=lax.Precision.HIGHEST
    )[:, None, :]
    gain_a = gain_attn[None, :]
    gain_f = gain_ffn[None, :]
    router_rows = w_router.T
    counts = lengths[:, 0]
    plane = lax.axis_index("hidden")[None]

    def to_groups(values):
        return lax.all_to_all(values, "expert", split_axis=0, concat_axis=0, tiled=True)

    def leaving(values, *after):
        return regroup(False, [to_groups(values)], (2, local // 2 * rows, width), 2, local // 2, *in_groups, after)

    def returning(chain, *after):
        shape = (groups, message, width)
        return regroup(True, chain.scattered(), shape, 2, local // 2, *in_groups, after)

    def arriving(chain, *after):
        return to_groups(returning(chain, *after))

    def attend(b, *after):
        return attention_forward(b, after, counts, tokens, gain_a, w_query, w_key, w_value, vector)

    def routing(b, *after):
        return route(
            b, after, tokens, cotangent, forward[b][1], w_output, gain_f, router_rows, slots[b][0], rcol, groups, per, b > 0
        )

    def place(b, *after):
        return prep(b, after, counts, routes.reshape(batches, length), cotangent, groups, experts, capacity)

    *placed, cot_slots = place(0)
    slots = [placed]
    rcol = routes.reshape(batches, length, 1)
    early_rows = width + experts + 16
    unit = 16 * groups * planes
    first_rows = 2 * early_rows + 3 * width
    first_rows = first_rows + -first_rows % unit
    second_rows = 3 * width + 24
    second_rows = second_rows + -second_rows % unit
    kept, layers, token_grads = [], (), ()
    side = (lax.axis_index("expert") % 2)[None]
    early_part, first_part, second_part = (), (), ()

    def back_tokens(b, after, low, high):
        return combine(
            b,
            b + 1 == batches,
            after,
            layers,
            counts,
            low,
            high,
            slots[b][1],
            rcol,
            *routed[b][:2],
            cotangent,
            gain_f,
            router_rows,
            w_output,
            forward[b][1],
            early_part,
            per,
            2 * early_rows,
        )

    def back_half(b, which, after, mixed_grad, more):
        qkv, _, lse = forward[b]
        last = b + 1 == batches
        return attention_backward(
            b,
            which,
            last,
            after,
            token_grads if which else (),
            side,
            counts,
            qkv,
            lse,
            vector,
            selector,
            mixed_grad,
            tokens,
            gain_a,
            w_query,
            w_key,
            w_value,
            second_part if which else first_part,
            more,
            second_rows if which else first_rows if last else 3 * width,
        )

    def grads_half(h, after, past):
        return expert_grads(h, after, past, local, *([k[h][part] for k in kept] for part in (2, 3, 0, 1)))

    forward = [attend(0, cot_slots)]
    routed = [routing(0)]
    grads = regroup(False, [to_groups(cot_slots)], (local * rows, width), 1, local, *in_groups, (routed[0][2],))
    grad_chain = Chain(planes, grads)
    grad_chain.send()
    inputs = regroup_gated(to_groups(routed[0][2]), local * rows, capacity, (grads,))
    input_chain = Chain(planes, inputs)
    input_chain.send()
    slots.append(place(1, inputs))
    forward.append(attend(1, inputs, grad_chain.up, grad_chain.down))
    grad_chain.send()
    routed.append(routing(1, grad_chain.up, grad_chain.down))
    grad_chain.run()
    input_chain.gate(forward[1][1])
    input_chain.send()
    held = (input_chain.up, input_chain.down, grad_chain.up, grad_chain.down)
    input_chain.run()
    halves = range(2)
    chains = [None, None]
    for b in range(batches):
        last = b + 1 == batches
        before = chains
        messages = [None, None]
        ready = ()
        if not last:
            if b:
                slots.append(place(b + 1))
                forward.append(attend(b + 1))
                routed.append(routing(b + 1))
            messages = [leaving(m, *held) for m in routed[b + 1][2:]]
            held = ()
            ready = tuple(messages)
        chains, worked = [], []
        for h in halves:
            if b == 0:
                done = experts_half(
                    h, ready, plane, None, w_inner, w_outer, input_chain.gathered(), grad_chain.gathered()
                )
            else:
                before[h].mix(*(w[0] for w in worked))
                tied = (before[h].up, before[h].down)
                if h:
                    tied += (before[0].up, before[0].down)
                done = experts_half(h, ready + tied, plane, before[h].gathered(), w_inner, w_outer)
                before[h].send()
            worked.append(done)
            chains.append(Chain(planes, messages[h], done[:planes]))
            chains[h].send()
        kept.append([w[planes:] for w in worked])
        low_chain, high_chain = chains
        if not last:
            for step in range(1, planes):
                for chain in chains:
                    if step > 1:
                        chain.send()
                    if step < planes - 1:
                        chain.mix()
            if b == 0:
                continue
            low, high = (arriving(chain) for chain in before)
            layer, res_grad, mixed_grad, early_part = back_tokens(b - 1, (), low, high)
            *more, first_part = back_half(b - 1, 0, (), mixed_grad, (early_part,) if b > 1 else ())
            token_grad, second_part = back_half(b - 1, 1, (), mixed_grad, (*more, res_grad))
        else:
            low = arriving(before[0], before[1].up, before[1].down)
            high = arriving(before[1])
            low_chain.mix()
            low_chain.send()
            totals = grads_half(0, (low_chain.mixed,), ())
            high_chain.mix(totals[0])
            high_chain.send()
            low_chain.mix(high)
            low_chain.send()
            layer, res_grad, mixed_grad, early_part = back_tokens(b - 1, (low_chain.mixed,), low, high)
            high_chain.mix(mixed_grad)
            high_chain.send()
            *more, first_part = back_half(
                b - 1, 0, (high_chain.mixed,), mixed_grad, (early_part,) if b > 1 else ()
            )
            low = returning(low_chain, first_part)
            token_grad, second_part = back_half(b - 1, 1, (low,), mixed_grad, (*more, res_grad))
            low = to_groups(low)
            high = returning(high_chain, second_part, low)
            totals = grads_half(1, (high,), totals)
            high = to_groups(high)
        layers, token_grads = (layer,), (token_grad,)
        early_part, first_part, second_part = (early_part,), (first_part,), (second_part,)
    layer, res_grad, mixed_grad, early_part = back_tokens(batches - 1, (totals[0],), low, high)
    diagonal, part, *first_part = back_half(batches - 1, 0, (), mixed_grad, (early_part,))
    first_half = add_half(*first_part)
    token_grad, *second_part = back_half(batches - 1, 1, (first_half,), mixed_grad, (diagonal, part, res_grad))
    mine, other = sum_everywhere(first_half)
    mine_second, other_second = sum_everywhere(add_half(*second_part))
    query_grad, key_grad, value_grad, output_grad, router_grad, gain_f_grad, gain_a_grad, bias_grad = unpack(
        early_rows, experts, side, mine, other, mine_second, other_second
    )
    return (
        layer,
        token_grad,
        gain_a_grad,
        query_grad,
        key_grad,
        value_grad,
        output_grad,
        bias_grad.T,
        gain_f_grad,
        router_grad.T,
        totals[1],
        totals[0],
    )


def solution(mesh):
    token = P(None, ("expert", "hidden"), None, None)
    placed = (
        token,
        token,
        P(None, ("expert", "hidden")),
        token,
        *(P() for _ in range(8)),
        P("expert", None, "hidden"),
        P("expert", "hidden", None),
    )
    return jax.shard_map(
        shards,
        mesh=mesh,
        in_specs=placed,
        out_specs=(
            token,
            token,
            *(P() for _ in range(8)),
            P("expert", None, "hidden"),
            P("expert", "hidden", None),
        ),
        check_vma=False,
    )
```

```python
import functools

import jax
import jax.numpy as jnp
import numpy as np
from jax import lax
from jax.experimental import pallas as pl
from jax.experimental.pallas import tpu as pltpu
from jax.sharding import PartitionSpec as P

HEADS = 12
HEAD_DIM = 64
BUCKETS = 32
MAXDIST = 128
PAIR = 2 * HEAD_DIM
PAIRS = HEADS // 2
ROWS = 256

epsilon = 1e-06
negative = -1e30
F32 = jnp.float32
BF16 = jnp.bfloat16
MIB = 1 << 20


def params(mib):
    return pltpu.CompilerParams(vmem_limit_bytes=mib * MIB)


def cost():
    return pl.CostEstimate(flops=1, bytes_accessed=1, transcendentals=0)


def offset_bucket(offsets):
    halfway = BUCKETS // 2
    exact_count = halfway // 2
    relative_distance = np.abs(offsets)
    scaled = (
        np.log(np.maximum(relative_distance, 1) / exact_count)
        / np.log(MAXDIST / exact_count)
        * (halfway - exact_count)
    )
    far_bucket = np.minimum(exact_count + np.floor(scaled).astype(np.int64), halfway - 1)
    near_bucket = np.where(relative_distance < exact_count, relative_distance, far_bucket)
    return (np.where(offsets > 0, halfway, 0) + near_bucket).astype(np.int32)


def dot(a, b):
    return lax.dot_general(a, b, (((1,), (0,)), ((), ())), preferred_element_type=F32)


def dot_t(a, b):
    return lax.dot_general(a, b, (((1,), (1,)), ((), ())), preferred_element_type=F32)


def t_dot(a, b):
    return lax.dot_general(a, b, (((0,), (0,)), ((), ())), preferred_element_type=F32)


def one_hot(condition):
    return jnp.where(condition, 1.0, 0.0).astype(BF16)


def batch_block(array, b):
    rest = array.shape[1:]
    return pl.BlockSpec((1,) + rest, lambda *_: (b,) + (0,) * len(rest))


ANYWHERE = pl.BlockSpec(memory_space=pl.ANY)
WHOLE = pl.BlockSpec(memory_space=pltpu.VMEM)
SCALARS = pl.BlockSpec(memory_space=pltpu.SMEM)


def iota(shape, axis):
    return lax.broadcasted_iota(jnp.int32, shape, axis)


def padded(rows):
    return -(-rows // 16) * 16


def spread_slots(slot, per, message, first=0, last=None):
    last = per if last is None else last
    group = lax.div(jnp.maximum(slot, 0), per)
    inside = slot - group * per
    held = (slot >= 0) & (inside >= first) & (inside < last)
    return jnp.where(held, group * message + inside - first, -1)


def prep_kernel(batch, experts, capacity, waits, *refs):
    refs = refs[waits:]
    len_ref, row_ref, col_ref, *refs = refs
    length = row_ref.shape[-1]
    before = one_hot(iota((length, length), 0) < iota((length, length), 1))
    after = one_hot(iota((length, length), 1) < iota((length, length), 0))
    count = len_ref[batch]
    row = row_ref[0]
    col = col_ref[0]
    valid_row = iota((1, length), 1) < count
    valid_col = iota((length, 1), 0) < count
    chosen_row = iota((experts, length), 0) == row
    chosen_col = iota((length, experts), 1) == col
    earlier_row = dot(one_hot(chosen_row & valid_row), before)
    rank_row = jnp.sum(jnp.where(chosen_row, earlier_row, 0.0), axis=0, keepdims=True).astype(jnp.int32)
    earlier_col = dot(after, one_hot(chosen_col & valid_col))
    rank_col = jnp.sum(jnp.where(chosen_col, earlier_col, 0.0), axis=1, keepdims=True).astype(jnp.int32)
    slot_row = jnp.where(valid_row & (rank_row < capacity), row * capacity + rank_row, -1)
    if batch:
        srow_ref, scol_ref = refs
    else:
        cot_ref, srow_ref, scol_ref, slots_ref = refs
        groups, message, width = slots_ref.shape
        place = spread_slots(slot_row, experts * capacity // groups, message)
        dispatch = one_hot(iota((groups * message, length), 0) == place)
        slots_ref[...] = dot(dispatch, cot_ref[0, 0]).astype(BF16).reshape(groups, message, width)
    srow_ref[0] = slot_row
    scol_ref[0] = jnp.where(valid_col & (rank_col < capacity), col * capacity + rank_col, -1)


def prep(batch, after, lengths, routes, cot, groups, experts, capacity):
    batches, length = routes.shape
    width = cot.shape[-1]
    rows = routes.reshape(batches, 1, length)
    columns = routes.reshape(batches, length, 1)
    first = batch == 0
    message = padded(experts // groups * capacity)
    return pl.pallas_call(
        functools.partial(prep_kernel, batch, experts, capacity, len(after)),
        grid=(1,),
        in_specs=[ANYWHERE] * len(after)
        + [SCALARS, batch_block(rows, batch), batch_block(columns, batch)]
        + ([batch_block(cot, 0)] if first else []),
        out_specs=[WHOLE] * (3 if first else 2),
        out_shape=[jax.ShapeDtypeStruct((1, 1, length), jnp.int32), jax.ShapeDtypeStruct((1, length, 1), jnp.int32)]
        + ([jax.ShapeDtypeStruct((groups, message, width), BF16)] if first else []),
        compiler_params=params(60),
        cost_estimate=cost(),
    )(*after, lengths, rows, columns, *((cot,) if first else ()))


def slot_places(kinds, local, groups, capacity, message):
    row = iota((1, kinds * local * groups * capacity), 1)
    slot = lax.rem(row, capacity)
    row = lax.div(row, capacity)
    group = lax.rem(row, groups)
    return group * message + lax.div(row, groups) * capacity + slot


def regroup_kernel(back, kinds, local, groups, capacity, message, waits, *refs):
    refs = refs[waits:]
    out_ref = refs[-1]
    total = refs[0][...].astype(F32)
    for ref in refs[1:-1]:
        total = total + ref[...].astype(F32)
    places = slot_places(kinds, local, groups, capacity, message)
    move = one_hot(iota((groups * message, places.shape[1]), 0) == places)
    if back:
        rows = dot(move, total.astype(BF16).reshape(places.shape[1], -1))
    else:
        rows = t_dot(move, total.astype(BF16).reshape(groups * message, -1))
    out_ref[...] = rows.astype(BF16).reshape(out_ref.shape)


def regroup(back, arrays, shape, kinds, local, groups, capacity, message, after=()):
    return pl.pallas_call(
        functools.partial(regroup_kernel, back, kinds, local, groups, capacity, message, len(after)),
        in_specs=[ANYWHERE] * len(after) + [WHOLE] * len(arrays),
        out_specs=WHOLE,
        out_shape=jax.ShapeDtypeStruct(shape, BF16),
        compiler_params=params(60),
        cost_estimate=cost(),
    )(*after, *arrays)


def regroup_gated_kernel(capacity, *refs):
    in_ref, out_ref = refs[-2:]
    groups, message, width = in_ref.shape
    total = out_ref.shape[0] - 16
    local = total // (groups * capacity)
    rows = groups * capacity
    flat = in_ref[...].reshape(groups * message, width)
    places = slot_places(1, local, groups, capacity, message)
    move = one_hot(iota((groups * message, total), 0) == places)
    out_ref[:total, :] = t_dot(move, flat).astype(BF16)
    place = iota((message, 128), 0)
    lane = iota((message, 128), 1)
    columns = []
    for g in range(groups):
        gates = in_ref[g, message - 16 : message, :].astype(F32)[0:1, :]
        parts = [
            jnp.sum(jnp.where(place == lane, gates[:, 128 * k : 128 * (k + 1)], 0.0), axis=1, keepdims=True)
            for k in range(3)
        ]
        wide = iota((message, 128), 1)
        columns.append(jnp.where(wide == 0, parts[0], jnp.where(wide == 1, parts[1], jnp.where(wide == 2, parts[2], 0.0))))
    column = jnp.concatenate(columns, axis=0).astype(BF16)
    moved = t_dot(move, column)
    place = iota((rows, 128), 0)
    lane = iota((rows, 128), 1)
    lines = []
    for l in range(local):
        mine = moved[l * rows : (l + 1) * rows, :]
        parts = [
            jnp.sum(jnp.where(place == lane, mine[:, k : k + 1], 0.0), axis=0, keepdims=True) for k in range(3)
        ]
        lines.append(jnp.concatenate(parts + [jnp.zeros((1, width - 384), F32)], axis=1))
    lines.append(jnp.zeros((16 - local, width), F32))
    out_ref[total:, :] = jnp.concatenate(lines, axis=0).astype(BF16)


def regroup_gated(slots, rows, capacity, after=()):
    width = slots.shape[-1]
    return pl.pallas_call(
        functools.partial(regroup_gated_kernel, capacity),
        in_specs=[ANYWHERE] * len(after) + [WHOLE],
        out_specs=WHOLE,
        out_shape=jax.ShapeDtypeStruct((rows + 16, width), BF16),
        compiler_params=params(60),
        cost_estimate=cost(),
    )(*after, slots)


def band_bias(vector_ref, head):
    wide = jnp.broadcast_to(vector_ref[head], (ROWS, vector_ref.shape[-1]))
    return pltpu.roll(wide, 0, 1, stride=1, stride_axis=0)


def band_slice(block, length):
    start = length - ROWS * (block + 1)
    return slice(start, start + length)


def attn_kernel(batch, waits, *refs):
    refs = refs[waits:]
    len_ref, tok_ref, gain_ref, wq_ref, wk_ref, wv_ref, vec_ref, qkv_ref, mixed_ref, lse_ref, bands_ref, probs_ref, mixed_t_ref = refs
    length, width = tok_ref.shape[2:]
    count = len_ref[batch]
    tokens = tok_ref[0, 0].astype(F32)
    inverse = lax.rsqrt(jnp.mean(tokens * tokens, axis=-1, keepdims=True) + epsilon)
    normed = (tokens * inverse * gain_ref[...]).astype(BF16)
    for which, w_ref in enumerate((wq_ref, wk_ref, wv_ref)):
        for part in range(width // 256):
            rows = dot(normed, w_ref[:, 256 * part : 256 * part + 256]).astype(BF16)
            qkv_ref[which, 2 * part] = rows[:, :PAIR]
            qkv_ref[which, 2 * part + 1] = rows[:, PAIR:]
    mask = jnp.where(iota((1, length), 1) < count, 0.0, negative)
    lane = iota((ROWS, PAIR), 1)
    lse_ref[...] = jnp.zeros_like(lse_ref)

    def one_pair(pair, carry):
        keys = qkv_ref[1, pair]
        values_t = qkv_ref[2, pair].T
        for side in range(2):
            head = 2 * pair + side
            bands_ref[side] = band_bias(vec_ref, head)
            mine = (lane >= HEAD_DIM) if side else (lane < HEAD_DIM)
            for block in range(length // ROWS):
                here = slice(ROWS * block, ROWS * (block + 1))
                queries = qkv_ref[0, pair, here, :] * 0.125
                queries = jnp.where(mine, queries, jnp.zeros_like(queries))
                scores = dot_t(queries, keys) + bands_ref[side, :, band_slice(block, length)] + mask
                highest = jnp.max(scores, axis=-1, keepdims=True)
                powers = jnp.exp(scores - highest)
                total = jnp.sum(powers, axis=-1, keepdims=True)
                probs_ref[side, here, :] = (powers * (1.0 / total)).astype(BF16)
                column = iota((ROWS, lse_ref.shape[1]), 1)
                lse_ref[here, :] = jnp.where(column == head, highest + jnp.log(total), lse_ref[here, :])
            rows = slice(HEAD_DIM * side, HEAD_DIM * (side + 1))
            mixed_t_ref[rows, :] = dot_t(values_t[rows, :], probs_ref[side])
        mixed_ref[pair] = mixed_t_ref[...].T.astype(BF16)
        return carry

    lax.fori_loop(0, PAIRS, one_pair, 0, unroll=3)


def attention_forward(batch, after, counts, tokens, gain, wq, wk, wv, vector):
    length = tokens.shape[2]
    return pl.pallas_call(
        functools.partial(attn_kernel, batch, len(after)),
        grid=(1,),
        in_specs=[ANYWHERE] * len(after) + [SCALARS, batch_block(tokens, batch)] + [WHOLE] * 5,
        out_specs=[WHOLE] * 3,
        out_shape=[
            jax.ShapeDtypeStruct((3, PAIRS, length, PAIR), BF16),
            jax.ShapeDtypeStruct((PAIRS, length, PAIR), BF16),
            jax.ShapeDtypeStruct((length, 128), F32),
        ],
        scratch_shapes=[
            pltpu.VMEM((2, ROWS, vector.shape[-1]), F32),
            pltpu.VMEM((2, length, length), BF16),
            pltpu.VMEM((PAIR, length), F32),
        ],
        compiler_params=params(60),
        cost_estimate=cost(),
    )(*after, counts, tokens, gain, wq, wk, wv, vector)


def route_kernel(per, gated, waits, *refs):
    refs = refs[waits:]
    tok_ref, cot_ref, mixed_ref, wo_ref, gffn_ref, wr_ref, srow_ref, rcol_ref, res_ref, probs_ref, *out_refs = refs
    length, width = tok_ref.shape[2:]
    mixed_all = jnp.concatenate([mixed_ref[p] for p in range(PAIRS)], axis=1)
    residual = tok_ref[0, 0].astype(F32) + dot(mixed_all, wo_ref[...])
    res_ref[...] = residual
    inverse = lax.rsqrt(jnp.mean(residual * residual, axis=-1, keepdims=True) + epsilon)
    routed = (residual * inverse * gffn_ref[...]).astype(BF16)
    logits = dot_t(routed, wr_ref[...])
    powers = jnp.exp(logits - jnp.max(logits, axis=-1, keepdims=True))
    probs = powers / jnp.sum(powers, axis=-1, keepdims=True)
    probs_ref[...] = probs
    gate = jnp.sum(jnp.where(iota(probs.shape, 1) == rcol_ref[0], probs, 0.0), axis=-1, keepdims=True)
    groups, message, _ = out_refs[0].shape
    places = iota((groups * message, length), 0)
    if gated:
        grads = (gate * cot_ref[0, 0].astype(F32)).astype(BF16)
        half = per // 2
        for which, out_ref in enumerate(out_refs):
            place = spread_slots(srow_ref[0], per, message, which * half, (which + 1) * half)
            rows = dot(one_hot(places == place), grads)
            rows = rows + dot(one_hot(places == jnp.where(place < 0, -1, place + half)), routed)
            out_ref[...] = rows.astype(BF16).reshape(out_ref.shape)
        return
    slots_ref = out_refs[0]
    dispatch = one_hot(places == spread_slots(srow_ref[0], per, message))
    slots_ref[...] = dot(dispatch, routed).astype(BF16).reshape(slots_ref.shape)
    first = gate.astype(BF16).astype(F32)
    second = (gate - first).astype(BF16).astype(F32)
    third = gate - first - second
    column = iota((length, PAIR), 1)
    pieces = jnp.where(column == 0, first, jnp.where(column == 1, second, jnp.where(column == 2, third, 0.0)))
    sorted_gates = dot(dispatch, pieces.astype(BF16))
    data = message - 16
    place = iota((data, 128), 0)
    lane = iota((data, 128), 1)
    for g in range(groups):
        mine = sorted_gates[g * message : g * message + data, :]
        parts = [
            jnp.sum(jnp.where(place == lane, mine[:, k : k + 1], 0.0), axis=0, keepdims=True) for k in range(3)
        ]
        line = jnp.concatenate(parts + [jnp.zeros((1, width - 384), F32)], axis=1)
        slots_ref[g, data:message, :] = jnp.broadcast_to(line, (16, width)).astype(BF16)


def route(batch, after, tokens, cot, mixed, wo, gain_ffn, w_router, srow, rcol, groups, per, gated):
    length, width = tokens.shape[2:]
    experts = w_router.shape[0]
    message = padded(per) if gated else padded(per) + 16
    return pl.pallas_call(
        functools.partial(route_kernel, per, gated, len(after)),
        grid=(1,),
        in_specs=[ANYWHERE] * len(after)
        + [batch_block(tokens, batch), batch_block(cot, batch) if gated else ANYWHERE]
        + [WHOLE] * 5
        + [batch_block(rcol, batch)],
        out_specs=[WHOLE] * (4 if gated else 3),
        out_shape=[
            jax.ShapeDtypeStruct((length, width), F32),
            jax.ShapeDtypeStruct((length, experts), F32),
        ]
        + [jax.ShapeDtypeStruct((groups, message, width), BF16)] * (2 if gated else 1),
        compiler_params=params(60),
        cost_estimate=cost(),
    )(*after, tokens, cot, mixed, wo, gain_ffn, w_router, srow, rcol)


GELU_SCALE = 0.7978845608028654
GELU_CUBIC = 0.044715


def expert_kernel(planes, gated, first_expert, waits, *refs):
    pieces = 2 * planes - 1
    refs = refs[waits:]
    plane = refs[0][0]
    x_refs, refs = refs[1 : 1 + pieces], refs[1 + pieces :]
    c_refs, refs = refs[:pieces], refs[pieces:]
    gate_refs = ()
    if not gated:
        gate_refs, refs = refs[:pieces], refs[pieces:]
    wi_ref, wo_ref, *refs = refs
    sum_refs = refs[:planes]
    act_ref, pre_ref, x_ref, c_ref = refs[planes:]
    rows = x_refs[0].shape[0]

    def assemble(parts):
        found = [parts[0][...]]
        for k in range(1, planes):
            from_above = plane + k < planes
            found.append(jnp.where(from_above, parts[k][...], parts[2 * planes - 1 - k][...]))
        return found

    inputs = jnp.concatenate(assemble(x_refs), axis=0)
    grads = assemble(c_refs)
    if not gated:
        place = iota((rows, 128), 0)
        lane = iota((rows, 128), 1)
        expert = first_expert + pl.program_id(0)
        for k, lines in enumerate(assemble(gate_refs)):
            lines = jnp.where(iota(lines.shape, 0) == expert, lines.astype(F32), 0.0)
            line = jnp.sum(lines, axis=0, keepdims=True)
            line = line[:, :128] + line[:, 128:256] + line[:, 256:384]
            gate = jnp.sum(jnp.where(place == lane, line, 0.0), axis=1, keepdims=True)
            grads[k] = (grads[k].astype(F32) * gate).astype(BF16)
    grads = jnp.concatenate(grads, axis=0)
    x_ref[0] = inputs
    c_ref[0] = grads
    pre = dot(inputs, wi_ref[0])
    square = pre * pre
    curve = jnp.tanh(GELU_SCALE * pre * (1.0 + GELU_CUBIC * square))
    half = 0.5 * (1.0 + curve)
    act = (pre * half).astype(BF16)
    slope = half + 0.5 * pre * (1.0 - curve * curve) * (GELU_SCALE * (1.0 + 3.0 * GELU_CUBIC * square))
    act_ref[0] = act
    outs = dot(act, wo_ref[0]).astype(BF16)
    pre_grad = (slope * dot_t(grads, wo_ref[0])).astype(BF16)
    pre_ref[0] = pre_grad
    ins = dot_t(pre_grad, wi_ref[0]).astype(BF16)
    for k in range(planes):
        sum_refs[k][0] = outs[k * rows : (k + 1) * rows]
        sum_refs[k][1] = ins[k * rows : (k + 1) * rows]


def experts_half(which, after, plane, messages, w_inner, w_outer, xs=None, cs=None):
    local, width, hidden = w_inner.shape
    mine = local // 2
    first = which * mine
    gated = messages is not None
    pieces = len(messages if gated else xs)
    planes = (pieces + 1) // 2
    if gated:
        rows = messages[0].shape[1] // mine
        x_block = pl.BlockSpec((None, rows, width), lambda e: (1, e, 0))
        c_block = pl.BlockSpec((None, rows, width), lambda e: (0, e, 0))
        arrays = (*messages, *messages)
        blocks = [x_block] * pieces + [c_block] * pieces
    else:
        rows = cs[0].shape[0] // local
        slab = pl.BlockSpec((rows, width), lambda e: (first + e, 0))
        lines = pl.BlockSpec((16, width), lambda e: (local * rows // 16, 0))
        arrays = (*xs, *cs, *xs)
        blocks = [slab] * (2 * pieces) + [lines] * pieces
    weight = lambda a, b: pl.BlockSpec((1, a, b), lambda e: (first + e, 0, 0))
    mat = lambda a, b: pl.BlockSpec((1, a, b), lambda e: (e, 0, 0))
    total = planes * rows
    kept = lambda n: jax.ShapeDtypeStruct((mine, total, n), BF16)
    return pl.pallas_call(
        functools.partial(expert_kernel, planes, gated, first, len(after)),
        grid=(mine,),
        in_specs=[ANYWHERE] * len(after) + [SCALARS] + blocks + [weight(width, hidden), weight(hidden, width)],
        out_specs=[pl.BlockSpec((2, rows, width), lambda e: (0, e, 0))] * planes
        + [mat(total, hidden), mat(total, hidden), mat(total, width), mat(total, width)],
        out_shape=[jax.ShapeDtypeStruct((2, mine * rows, width), BF16)] * planes
        + [kept(hidden), kept(hidden), kept(width), kept(width)],
        compiler_params=params(60),
        cost_estimate=cost(),
    )(*after, plane, *arrays, w_inner, w_outer)


def expert_grad_kernel(batches, waits, *refs):
    xs, cs, acts, pres = (refs[waits + k * batches : waits + (k + 1) * batches] for k in range(4))
    outer_ref, inner_ref = refs[-2:]
    whole = lambda refs: jnp.concatenate([ref[0] for ref in refs], axis=0)
    outer_ref[0] = t_dot(whole(acts), whole(cs))
    inner_ref[0] = t_dot(whole(xs), whole(pres))


def expert_grads(which, after, past, local, xs, cs, acts, pres):
    batches = len(xs)
    mine, total, width = xs[0].shape
    hidden = acts[0].shape[2]
    first = which * mine
    mat = lambda a, b: pl.BlockSpec((1, a, b), lambda e: (e, 0, 0))
    out = lambda a, b: pl.BlockSpec((1, a, b), lambda e: (first + e, 0, 0))
    behind = len(after) + 4 * batches
    return pl.pallas_call(
        functools.partial(expert_grad_kernel, batches, len(after)),
        grid=(mine,),
        in_specs=[ANYWHERE] * len(after)
        + [mat(total, width)] * (2 * batches)
        + [mat(total, hidden)] * (2 * batches)
        + [ANYWHERE] * len(past),
        out_specs=[out(hidden, width), out(width, hidden)],
        out_shape=[
            jax.ShapeDtypeStruct((local, hidden, width), F32),
            jax.ShapeDtypeStruct((local, width, hidden), F32),
        ],
        input_output_aliases={behind + k: k for k in range(len(past))},
        compiler_params=params(60),
        cost_estimate=cost(),
    )(*after, *xs, *cs, *acts, *pres, *past)


def combine_kernel(per, batch, waits, *refs):
    refs = refs[waits:]
    len_ref, low_ref, high_ref, scol_ref, rcol_ref, res_ref, probs_ref, cot_ref, gffn_ref, wr_ref, wo_ref, mixed_ref, *refs = refs
    past_ref = refs.pop(0) if batch else None
    layer_ref, resgrad_ref, mgrad_ref, shared_ref, *buffers, sems = refs
    fetched = [res_ref, cot_ref.at[batch, 0], mixed_ref, wo_ref] + ([past_ref] if batch else [])
    copies = [pltpu.make_async_copy(ref, buffer, sems.at[k]) for k, (ref, buffer) in enumerate(zip(fetched, buffers))]
    for copy in copies:
        copy.start()
    res_ref, cot_ref, mixed_ref, wo_ref = buffers[:4]
    if batch:
        past_ref = buffers[4]
    length, width = cot_ref.shape
    experts = wr_ref.shape[0]
    groups, message, _ = low_ref.shape
    valid = iota((length, 1), 0) < len_ref[batch]
    places = iota((length, groups * message), 1)
    half = per // 2
    returned = input_grad = None
    for which, ref in enumerate((low_ref, high_ref)):
        place = spread_slots(scol_ref[0], per, message, which * half, (which + 1) * half)
        rows = ref[...].reshape(groups * message, width)
        out_part = dot(one_hot(places == place), rows)
        in_part = dot(one_hot(places == jnp.where(place < 0, -1, place + half)), rows)
        returned = out_part if returned is None else returned + out_part
        input_grad = in_part if input_grad is None else input_grad + in_part
    copies[0].wait()
    copies[1].wait()
    residual = res_ref[...]
    probs = probs_ref[...]
    chosen = iota(probs.shape, 1) == rcol_ref[0]
    gate = jnp.sum(jnp.where(chosen, probs, 0.0), axis=-1, keepdims=True)
    layer_ref[0, 0] = jnp.where(valid, residual + gate * returned, 0.0).astype(BF16)
    out_grad = jnp.where(valid, cot_ref[...].astype(F32), 0.0)
    gate_grad = jnp.sum(out_grad * returned, axis=-1, keepdims=True)
    prob_grad = jnp.where(chosen, gate_grad, 0.0)
    logit_grad = (probs * (prob_grad - jnp.sum(probs * prob_grad, axis=-1, keepdims=True))).astype(BF16)
    inverse = lax.rsqrt(jnp.mean(residual * residual, axis=-1, keepdims=True) + epsilon)
    gain = gffn_ref[...]
    scaled = residual * inverse
    routed = (scaled * gain).astype(BF16)

    def share(first, whole_rows):
        for side in range(2):
            rows = whole_rows[:, side * width // 2 : (side + 1) * width // 2]
            here = slice(side * shared_ref.shape[0] // 2 + first, side * shared_ref.shape[0] // 2 + first + rows.shape[0])
            if past_ref is not None:
                rows = rows + past_ref[here, :]
            shared_ref[here, :] = rows.astype(shared_ref.dtype)

    for copy in copies[2:]:
        copy.wait()
    share(width, t_dot(logit_grad, routed))
    routed_grad = dot(logit_grad, wr_ref[...]) + input_grad
    gain_part = jnp.sum(routed_grad * scaled, axis=0, keepdims=True)
    left = shared_ref.shape[0] // 2 - width - experts
    share(width + experts, jnp.where(iota((left, width), 0) == 0, gain_part, 0.0))
    upstream = routed_grad * gain
    middle = jnp.mean(upstream * scaled, axis=-1, keepdims=True)
    residual_grad = out_grad + inverse * (upstream - scaled * middle)
    resgrad_ref[...] = residual_grad
    attended = residual_grad.astype(BF16)
    mixed_all = jnp.concatenate([mixed_ref[p] for p in range(PAIRS)], axis=1)
    share(0, t_dot(mixed_all, attended))
    mixed_grad = dot_t(attended, wo_ref[...]).astype(BF16)
    for pair in range(PAIRS):
        mgrad_ref[pair] = mixed_grad[:, pair * PAIR : (pair + 1) * PAIR]


def combine(
    batch, last, after, layers, counts, low, high, scol, rcol, residual, probs, cot, gain_ffn, w_router, w_output, mixed, past, per, shared
):
    length, width = cot.shape[2:]
    return pl.pallas_call(
        functools.partial(combine_kernel, per, batch, len(after) + len(layers)),
        grid=(1,),
        in_specs=[ANYWHERE] * (len(after) + len(layers))
        + [SCALARS, WHOLE, WHOLE, WHOLE, batch_block(rcol, batch), ANYWHERE, WHOLE, ANYWHERE]
        + [WHOLE] * 2
        + [ANYWHERE] * (2 + len(past)),
        out_specs=[batch_block(cot, batch)] + [WHOLE] * 3,
        out_shape=[
            jax.ShapeDtypeStruct(cot.shape, BF16),
            jax.ShapeDtypeStruct((length, width), F32),
            jax.ShapeDtypeStruct((PAIRS, length, PAIR), BF16),
            jax.ShapeDtypeStruct((shared, width // 2), BF16 if last else F32),
        ],
        scratch_shapes=[
            pltpu.VMEM(residual.shape, residual.dtype),
            pltpu.VMEM((length, width), BF16),
            *(pltpu.VMEM(array.shape, array.dtype) for array in (mixed, w_output, *past)),
            pltpu.SemaphoreType.DMA((4 + len(past),)),
        ],
        input_output_aliases={len(after): 0} if layers else {},
        compiler_params=params(60),
        cost_estimate=cost(),
    )(
        *after, *layers, counts, low, high, scol, rcol, residual, probs, cot, gain_ffn, w_router, w_output, mixed, *past
    )


def attn_back_kernel(batch, which, last, waits, *refs):
    refs = refs[waits:]
    side_ref, len_ref, qkv_ref, lse_ref, vec_ref, sel_ref, mgrad_ref, tok_ref, gain_ref, wq_ref, wk_ref, wv_ref, *refs = refs
    past_ref = refs.pop(0) if batch else None
    if which:
        seen_ref, part_ref, resgrad_ref, *refs = refs
        tgrad_ref, *refs = refs
    else:
        early_ref = refs.pop(0) if batch else None
        diag_out_ref, part_out_ref, *refs = refs
    shared_refs, refs = refs[: 1 + last], refs[1 + last :]
    bands_ref, probs_ref, sgrad_ref, spread_ref, low_ref, qt_ref, kt_ref, vt_ref, diag_ref, stage_ref, rest_ref, *buffers = refs
    *buffers, sems, out_sems = buffers
    half = wq_ref.shape[0] // 2
    columns = pl.ds(which * half, half)
    fetched = [tok_ref.at[batch, 0]] + [ref.at[:, columns] for ref in (wq_ref, wk_ref, wv_ref)]
    if past_ref is not None:
        fetched.append(past_ref)
    if which:
        fetched += [part_ref, resgrad_ref]
    elif batch:
        fetched.append(early_ref)
    copies = [pltpu.make_async_copy(ref, buffer, sems.at[k]) for k, (ref, buffer) in enumerate(zip(fetched, buffers))]
    for copy in copies:
        copy.start()
    going = []
    offset = early_ref.shape[0] if last and not which else 0
    part_rows = shared_refs[0].shape[0]
    tok_ref, wq_ref, wk_ref, wv_ref, *buffers = buffers
    if past_ref is not None:
        past_ref = buffers.pop(0)
    if which:
        part_ref, resgrad_ref = buffers
    elif batch:
        early_ref = buffers[0]
    length, width = tok_ref.shape
    first_pair = which * (PAIRS // 2)
    mask = jnp.where(iota((1, length), 1) < len_ref[batch], 0.0, negative)
    lane = iota((ROWS, PAIR), 1)
    diag_ref[...] = seen_ref[...] if which else jnp.zeros_like(diag_ref)

    def one_pair(step, carry):
        pair = first_pair + step
        keys = qkv_ref[1, step]
        values = qkv_ref[2, step]
        queries_t = qkv_ref[0, step].T
        keys_t = qkv_ref[1, step].T
        grads_t = mgrad_ref[step].T
        for side in range(2):
            head = 2 * pair + side
            bands_ref[side] = band_bias(vec_ref, head)
            spread_ref[side] = jnp.zeros(spread_ref.shape[1:], F32)
            mine = (lane >= HEAD_DIM) if side else (lane < HEAD_DIM)
            for block in range(length // ROWS):
                here = slice(ROWS * block, ROWS * (block + 1))
                window = band_slice(block, length)
                queries = qkv_ref[0, step, here, :] * 0.125
                queries = jnp.where(mine, queries, jnp.zeros_like(queries))
                grads = mgrad_ref[step, here, :]
                grads = jnp.where(mine, grads, jnp.zeros_like(grads))
                column = iota((ROWS, lse_ref.shape[1]), 1)
                log_total = jnp.sum(jnp.where(column == head, lse_ref[here, :], 0.0), axis=-1, keepdims=True)
                scores = dot_t(queries, keys) + bands_ref[side, :, window] + mask
                probs = jnp.exp(scores - log_total)
                probs_ref[side, here, :] = probs.astype(BF16)
                weighted = probs * dot_t(grads, values)
                score_grad = weighted - probs * jnp.sum(weighted, axis=-1, keepdims=True)
                spread_ref[side, :, window] += score_grad
                sgrad_ref[side, here, :] = score_grad.astype(BF16)
            rows = slice(HEAD_DIM * side, HEAD_DIM * (side + 1))
            qt_ref[rows, :] = dot_t(keys_t[rows, :], sgrad_ref[side]) * 0.125
            kt_ref[rows, :] = dot(queries_t[rows, :], sgrad_ref[side]) * 0.125
            vt_ref[rows, :] = dot(grads_t[rows, :], probs_ref[side])
            size = spread_ref.shape[2]
            eight = spread_ref[side, 0:8, :]
            for move in range(8, ROWS, 8):
                eight = eight + pltpu.roll(spread_ref[side, move : move + 8, :], size - move, 1)
            diagonal = eight[0:1, :]
            for move in range(1, 8):
                diagonal = diagonal + pltpu.roll(eight[move : move + 1, :], size - move, 1)
            diag_ref[...] = jnp.where(iota(diag_ref.shape, 0) == head, diagonal, diag_ref[...])
        low_ref[0, step] = qt_ref[...].T.astype(BF16)
        low_ref[1, step] = kt_ref[...].T.astype(BF16)
        low_ref[2, step] = vt_ref[...].T.astype(BF16)
        return carry

    lax.fori_loop(0, PAIRS // 2, one_pair, 0)
    for copy in copies:
        copy.wait()

    def send(source, first, place):
        count = source.shape[0]
        for k in range(1 + last):
            low, high = max(first, k * part_rows), min(first + count, (k + 1) * part_rows)
            if low >= high:
                continue
            part = source.at[pl.ds(low - first, high - low)]
            for turn in range(1 + last):
                there = shared_refs[turn].at[pl.ds(low - k * part_rows, high - low)]
                copy = pltpu.make_async_copy(part, there, out_sems.at[place, k])
                going.append((copy, k ^ turn))

                @pl.when(side_ref[0] == (k ^ turn) if last else True)
                def _():
                    copy.start()

    if offset:
        send(early_ref, 0, 0)

    def past(first, count):
        return 0.0 if past_ref is None else past_ref[first : first + count, :]

    tokens = tok_ref[...].astype(F32)
    inverse = lax.rsqrt(jnp.mean(tokens * tokens, axis=-1, keepdims=True) + epsilon)
    gain = gain_ref[...]
    scaled = tokens * inverse
    normed_t = (scaled * gain).astype(BF16).T
    normed_grad = part_ref[...] if which else jnp.zeros((length, width), F32)
    for matrix, w_ref in enumerate((wq_ref, wk_ref, wv_ref)):
        low = jnp.concatenate([low_ref[matrix, p] for p in range(PAIRS // 2)], axis=1)
        stage_ref[matrix] = (dot(normed_t, low) + past(matrix * width, width)).astype(stage_ref.dtype)
        send(stage_ref.at[matrix], offset + matrix * width, 1 + matrix)
        normed_grad = normed_grad + dot_t(low, w_ref[...])
    left = rest_ref.shape[0]
    if which:
        gain_part = jnp.sum(normed_grad * scaled, axis=0, keepdims=True)
        bias_part = lax.dot_general(
            diag_ref[...],
            sel_ref[...],
            (((1,), (0,)), ((), ())),
            precision=lax.Precision.HIGHEST,
            preferred_element_type=F32,
        )
        row = iota((8, half), 0)
        gains = jnp.where(row == 0, gain_part[:, :half], jnp.where(row == 1, gain_part[:, half:], 0.0))
        wide = jnp.concatenate([bias_part, jnp.zeros((16, half - bias_part.shape[1]), F32)], axis=1)
        tail = [gains, wide] + ([jnp.zeros((left - 24, half), F32)] if left > 24 else [])
        rest_ref[...] = (jnp.concatenate(tail, axis=0) + past(3 * width, left)).astype(rest_ref.dtype)
        send(rest_ref, 3 * width, 4)
        upstream = normed_grad * gain
        middle = jnp.mean(upstream * scaled, axis=-1, keepdims=True)
        tgrad_ref[0, 0] = (resgrad_ref[...] + inverse * (upstream - scaled * middle)).astype(BF16)
    else:
        if offset and offset + 3 * width < 2 * part_rows:
            rest_ref[...] = jnp.zeros_like(rest_ref)
            send(rest_ref, offset + 3 * width, 4)
        diag_out_ref[...] = diag_ref[...]
        part_out_ref[...] = normed_grad
    for copy, turn in going:

        @pl.when(side_ref[0] == turn if last else True)
        def _():
            copy.wait()


def attention_backward(batch, which, last, after, grads, side, counts, qkv, lse, vector, selector, mixed_grad, tokens, gain, wq, wk, wv, past, more, rows):
    length, width = tokens.shape[2:]
    half = width // 2
    size = vector.shape[-1]
    late = (*past, *(more[1:] if which else more))
    buffers = [((length, width), BF16)] + [((width, half), BF16)] * 3 + [(array.shape, array.dtype) for array in late]
    sent = 0 if which or not last else more[0].shape[0]
    rest = max(rows - sent - 3 * width, 16)
    shared = jax.ShapeDtypeStruct((rows // 2 if last else rows, half), BF16 if last else F32)
    if which:
        outs = [jax.ShapeDtypeStruct(tokens.shape, BF16)]
        out_specs = [batch_block(tokens, batch)]
    else:
        outs = [jax.ShapeDtypeStruct((16, size), F32), jax.ShapeDtypeStruct((length, width), F32)]
        out_specs = [WHOLE] * 2
    outs += [shared] * (2 if last else 1)
    out_specs += [ANYWHERE] * (2 if last else 1)
    return pl.pallas_call(
        functools.partial(attn_back_kernel, batch, which, last, len(after) + len(grads)),
        grid=(1,),
        in_specs=[ANYWHERE] * (len(after) + len(grads))
        + [SCALARS, SCALARS, pl.BlockSpec((3, PAIRS // 2, length, PAIR), lambda _: (0, which, 0, 0))]
        + [WHOLE] * 3
        + [pl.BlockSpec((PAIRS // 2, length, PAIR), lambda _: (which, 0, 0))]
        + [ANYWHERE, WHOLE]
        + [ANYWHERE] * (3 + len(past))
        + [WHOLE if which and k == 0 else ANYWHERE for k in range(len(more))],
        out_specs=out_specs,
        out_shape=outs,
        input_output_aliases={len(after): 0} if grads else {},
        scratch_shapes=[
            pltpu.VMEM((2, ROWS, size), F32),
            pltpu.VMEM((2, length, length), BF16),
            pltpu.VMEM((2, length, length), BF16),
            pltpu.VMEM((2, ROWS, size), F32),
            pltpu.VMEM((3, PAIRS // 2, length, PAIR), BF16),
            pltpu.VMEM((PAIR, length), F32),
            pltpu.VMEM((PAIR, length), F32),
            pltpu.VMEM((PAIR, length), F32),
            pltpu.VMEM((16, size), F32),
            pltpu.VMEM((3, width, half), shared.dtype),
            pltpu.VMEM((rest, half), shared.dtype),
            *(pltpu.VMEM(shape, kind) for shape, kind in buffers),
            pltpu.SemaphoreType.DMA((len(buffers),)),
            pltpu.SemaphoreType.DMA((5, 2)),
        ],
        compiler_params=params(60),
        cost_estimate=cost(),
    )(*after, *grads, side, counts, qkv, lse, vector, selector, mixed_grad, tokens, gain, wq, wk, wv, *past, *more)


def unpack_kernel(early, side_ref, *refs):
    arrived, refs = refs[:4], refs[4:]
    q_ref, k_ref, v_ref, output_ref, router_ref, gain_f_ref, gain_a_ref, bias_ref, *refs = refs
    buffers, (stage_ref, in_sems, out_sems) = refs[:4], refs[4:]
    copies = [
        pltpu.make_async_copy(ref, buffer, in_sems.at[k]) for k, (ref, buffer) in enumerate(zip(arrived, buffers))
    ]
    for copy in copies:
        copy.start()
    swapped = side_ref[0] == 1

    def whole(k):
        copies[k].wait()
        copies[k + 1].wait()
        mine, other = buffers[k][...], buffers[k + 1][...]
        parts = [jnp.where(swapped, other, mine), jnp.where(swapped, mine, other)]
        return jnp.concatenate(parts, axis=0).astype(F32)

    leaving = [
        pltpu.make_async_copy(stage_ref.at[k], ref, out_sems.at[k])
        for k, ref in enumerate((q_ref, k_ref, v_ref, output_ref))
    ]
    rows = whole(0)
    half = rows.shape[1]
    width = 2 * half
    last = early - 16
    stage_ref[3, :, :half] = rows[:width]
    stage_ref[3, :, half:] = rows[early : early + width]
    leaving[3].start()
    router_ref[...] = jnp.concatenate([rows[width:last], rows[early + width : early + last]], axis=1)
    gain_f_ref[...] = jnp.concatenate([rows[last], rows[early + last]])
    for k in range(3):
        stage_ref[k, :, :half] = rows[2 * early + k * width : 2 * early + (k + 1) * width]
    rows = whole(2)
    for k in range(3):
        stage_ref[k, :, half:] = rows[k * width : (k + 1) * width]
        leaving[k].start()
    gain_a_ref[...] = jnp.concatenate([rows[3 * width], rows[3 * width + 1]])
    bias_ref[...] = rows[3 * width + 8 : 3 * width + 8 + HEADS, :BUCKETS]
    for copy in leaving:
        copy.wait()


def unpack(early, experts, side, first, first_other, second, second_other):
    width = 2 * first.shape[1]
    matrix = jax.ShapeDtypeStruct((width, width), F32)
    line = jax.ShapeDtypeStruct((width,), F32)
    arrays = (first, first_other, second, second_other)
    return pl.pallas_call(
        functools.partial(unpack_kernel, early),
        in_specs=[SCALARS] + [ANYWHERE] * 4,
        out_specs=[ANYWHERE] * 4 + [WHOLE] * 4,
        out_shape=[matrix] * 4
        + [jax.ShapeDtypeStruct((experts, width), F32), line, line, jax.ShapeDtypeStruct((HEADS, BUCKETS), F32)],
        scratch_shapes=[pltpu.VMEM(array.shape, array.dtype) for array in arrays]
        + [pltpu.VMEM((4, width, width), F32), pltpu.SemaphoreType.DMA((4,)), pltpu.SemaphoreType.DMA((4,))],
        compiler_params=params(60),
        cost_estimate=cost(),
    )(side, *arrays)


def upward(planes, first, last):
    return [(k, k + 1) for k in range(first, last)]


def downward(planes, first, last):
    return [(planes - 1 - k, planes - 2 - k) for k in range(first, last)]


def mix_kernel(both, planes, step, waits, here_ref, up_ref, down_ref, upsum_ref, downsum_ref, *refs):
    to_up, to_down = refs[waits:]
    for moving, sums, out, place in (
        (up_ref, upsum_ref, to_up, here_ref[0]),
        (down_ref, downsum_ref, to_down, planes - 1 - here_ref[0]),
    ):
        total = moving[...] + sums[...]
        out[...] = jnp.where(place <= step, total, moving[...]) if both else total


def mix(both, planes, step, here, up, down, upsum, downsum, after):
    kinds, rows, width = up.shape
    block = pl.BlockSpec((1, rows // 2, width), lambda i, j: (i, j, 0))
    return pl.pallas_call(
        functools.partial(mix_kernel, both, planes, step, len(after)),
        grid=(kinds, 2),
        in_specs=[SCALARS] + [block] * 4 + [ANYWHERE] * len(after),
        out_specs=[block] * 2,
        out_shape=[jax.ShapeDtypeStruct(up.shape, BF16)] * 2,
        compiler_params=params(32),
        cost_estimate=cost(),
    )(here, up, down, upsum, downsum, *after)


def gate_kernel(*refs):
    pass


def gate(arrays, after):
    count = len(arrays)
    return pl.pallas_call(
        gate_kernel,
        in_specs=[ANYWHERE] * (count + len(after)),
        out_specs=[ANYWHERE] * count,
        out_shape=[jax.ShapeDtypeStruct(array.shape, array.dtype) for array in arrays],
        input_output_aliases={k: k for k in range(count)},
        cost_estimate=cost(),
    )(*arrays, *after)


class Chain:
    def __init__(self, planes, own=None, sums=None):
        self.planes, self.own, self.sums = planes, own, sums
        self.here = lax.axis_index("hidden")[None]
        self.from_below, self.from_above = [], []
        if own is not None:
            self.up = self.down = own
        else:
            self.up, self.down = sums[planes - 1], sums[1]
        self.count = 0
        self.steps = planes if own is not None and sums is not None else planes - 1

    def send(self):
        planes, s = self.planes, self.count
        if self.own is not None and self.sums is not None:
            first, last = 0, planes - 1
        elif self.own is not None:
            first, last = s, planes - 1
        else:
            first, last = 0, s + 1
        self.up = lax.ppermute(self.up, "hidden", upward(planes, first, last))
        self.down = lax.ppermute(self.down, "hidden", downward(planes, first, last))
        self.count += 1
        if self.own is not None and s < planes - 1:
            self.from_below.append(self.up)
            self.from_above.append(self.down)

    def mix(self, *after):
        planes, s = self.planes, self.count - 1
        both = self.own is not None
        offset = 1 if both else 2
        self.up, self.down = mix(
            both, planes, s, self.here, self.up, self.down, self.sums[planes - offset - s], self.sums[s + offset], after
        )
        self.mixed = self.up

    def gate(self, *after):
        self.up, self.down = gate((self.up, self.down), after)
        self.from_below[-1], self.from_above[-1] = self.up, self.down

    def run(self):
        while self.count < self.steps:
            self.send()
        return self

    def gathered(self):
        return (self.own, *self.from_above, *self.from_below)

    def scattered(self):
        return (self.sums[0], self.up, self.down)


def swap(values, axis, distance):
    return lax.ppermute(values, axis, [(k, k ^ distance) for k in range(lax.axis_size(axis))])


def share_sums(values, axis, near, count):
    me = lax.axis_index(axis) // near
    parts = values.reshape(count, values.shape[0] // count, values.shape[1])
    total = lax.dynamic_index_in_dim(parts, me, 0, keepdims=False).astype(F32)
    for k in range(1, count):
        part = lax.dynamic_index_in_dim(parts, me ^ k, 0, keepdims=False)
        total = total + swap(part, axis, k * near).astype(F32)
    return total.astype(BF16)


def join_sums(values, axis, near, count):
    me = lax.axis_index(axis) // near
    found = [values] + [swap(values, axis, k * near) for k in range(1, count)]
    joined = []
    for j in range(count):
        piece = found[count - 1]
        for k in range(count - 2, -1, -1):
            piece = jnp.where(me ^ k == j, found[k], piece)
        joined.append(piece)
    return jnp.concatenate(joined)


def add_half(mine, other):
    return mine + swap(other, "expert", 1)


def offset_selector(length):
    place = np.arange(2 * length)
    offsets = np.where(place < 2 * length - ROWS, place, place - 2 * length) - (length - ROWS)
    offsets = np.clip(offsets, -(length - 1), length - 1)
    return (offset_bucket(offsets)[:, None] == np.arange(BUCKETS)[None, :]).astype(np.float32)


def shards(
    tokens,
    cotangent,
    lengths,
    routes,
    gain_attn,
    w_query,
    w_key,
    w_value,
    w_output,
    bucket_head_bias,
    gain_ffn,
    w_router,
    w_inner,
    w_outer,
):
    batches, _, length, width = tokens.shape
    experts = w_router.shape[1]
    local = w_inner.shape[0]
    groups = lax.axis_size("expert")
    planes = lax.axis_size("hidden")
    capacity = (5 * length + 4 * experts - 1) // (4 * experts)
    per = local * capacity
    rows = groups * capacity
    message = padded(per)
    in_groups = (groups, capacity, message)
    selector = jnp.asarray(offset_selector(length))
    vector = lax.dot_general(
        bucket_head_bias, selector, (((0,), (1,)), ((), ())), precision=lax.Precision.HIGHEST
    )[:, None, :]
    gain_a = gain_attn[None, :]
    gain_f = gain_ffn[None, :]
    router_rows = w_router.T
    counts = lengths[:, 0]
    plane = lax.axis_index("hidden")[None]

    def to_groups(values):
        return lax.all_to_all(values, "expert", split_axis=0, concat_axis=0, tiled=True)

    def leaving(values, *after):
        return regroup(False, [to_groups(values)], (2, local // 2 * rows, width), 2, local // 2, *in_groups, after)

    def returning(chain, *after):
        shape = (groups, message, width)
        return regroup(True, chain.scattered(), shape, 2, local // 2, *in_groups, after)

    def arriving(chain, *after):
        return to_groups(returning(chain, *after))

    def attend(b, *after):
        return attention_forward(b, after, counts, tokens, gain_a, w_query, w_key, w_value, vector)

    def routing(b, *after):
        return route(
            b, after, tokens, cotangent, forward[b][1], w_output, gain_f, router_rows, slots[b][0], rcol, groups, per, b > 0
        )

    def place(b, *after):
        return prep(b, after, counts, routes.reshape(batches, length), cotangent, groups, experts, capacity)

    *placed, cot_slots = place(0)
    slots = [placed]
    rcol = routes.reshape(batches, length, 1)
    early_rows = width + experts + 16
    unit = 16 * groups * planes
    first_rows = 2 * early_rows + 3 * width
    first_rows = first_rows + -first_rows % unit
    second_rows = 3 * width + 24
    second_rows = second_rows + -second_rows % unit
    kept, layers, token_grads = [], (), ()
    side = (lax.axis_index("expert") % 2)[None]
    early_part, first_part, second_part = (), (), ()

    def back_tokens(b, after, low, high):
        return combine(
            b,
            b + 1 == batches,
            after,
            layers,
            counts,
            low,
            high,
            slots[b][1],
            rcol,
            *routed[b][:2],
            cotangent,
            gain_f,
            router_rows,
            w_output,
            forward[b][1],
            early_part,
            per,
            2 * early_rows,
        )

    def back_half(b, which, after, mixed_grad, more):
        qkv, _, lse = forward[b]
        last = b + 1 == batches
        return attention_backward(
            b,
            which,
            last,
            after,
            token_grads if which else (),
            side,
            counts,
            qkv,
            lse,
            vector,
            selector,
            mixed_grad,
            tokens,
            gain_a,
            w_query,
            w_key,
            w_value,
            second_part if which else first_part,
            more,
            second_rows if which else first_rows if last else 3 * width,
        )

    def grads_half(h, after, past):
        return expert_grads(h, after, past, local, *([k[h][part] for k in kept] for part in (2, 3, 0, 1)))

    forward = [attend(0, cot_slots)]
    routed = [routing(0)]
    grads = regroup(False, [to_groups(cot_slots)], (local * rows, width), 1, local, *in_groups, (routed[0][2],))
    grad_chain = Chain(planes, grads)
    grad_chain.send()
    inputs = regroup_gated(to_groups(routed[0][2]), local * rows, capacity, (grads,))
    input_chain = Chain(planes, inputs)
    input_chain.send()
    slots.append(place(1, inputs))
    forward.append(attend(1, inputs, grad_chain.up, grad_chain.down))
    grad_chain.send()
    routed.append(routing(1, grad_chain.up, grad_chain.down))
    grad_chain.run()
    input_chain.gate(forward[1][1])
    input_chain.send()
    held = (input_chain.up, input_chain.down, grad_chain.up, grad_chain.down)
    input_chain.run()
    halves = range(2)
    chains = [None, None]
    for b in range(batches):
        last = b + 1 == batches
        before = chains
        messages = [None, None]
        ready = ()
        if not last:
            if b:
                slots.append(place(b + 1))
                forward.append(attend(b + 1))
                routed.append(routing(b + 1))
            messages = [leaving(m, *held) for m in routed[b + 1][2:]]
            held = ()
            ready = tuple(messages)
        chains, worked = [], []
        for h in halves:
            if b == 0:
                done = experts_half(
                    h, ready, plane, None, w_inner, w_outer, input_chain.gathered(), grad_chain.gathered()
                )
            else:
                before[h].mix(*(w[0] for w in worked))
                tied = (before[h].up, before[h].down)
                if h:
                    tied += (before[0].up, before[0].down)
                done = experts_half(h, ready + tied, plane, before[h].gathered(), w_inner, w_outer)
                before[h].send()
            worked.append(done)
            chains.append(Chain(planes, messages[h], done[:planes]))
            chains[h].send()
        kept.append([w[planes:] for w in worked])
        low_chain, high_chain = chains
        if not last:
            for step in range(1, planes):
                for chain in chains:
                    if step > 1:
                        chain.send()
                    if step < planes - 1:
                        chain.mix()
            if b == 0:
                continue
            low, high = (arriving(chain) for chain in before)
            layer, res_grad, mixed_grad, early_part = back_tokens(b - 1, (), low, high)
            *more, first_part = back_half(b - 1, 0, (), mixed_grad, (early_part,) if b > 1 else ())
            token_grad, second_part = back_half(b - 1, 1, (), mixed_grad, (*more, res_grad))
        else:
            low = arriving(before[0], before[1].up, before[1].down)
            high = arriving(before[1])
            low_chain.mix()
            low_chain.send()
            totals = grads_half(0, (low_chain.mixed,), ())
            high_chain.mix(totals[0])
            high_chain.send()
            low_chain.mix(high)
            low_chain.send()
            layer, res_grad, mixed_grad, early_part = back_tokens(b - 1, (low_chain.mixed,), low, high)
            high_chain.mix(mixed_grad)
            high_chain.send()
            *more, first_part = back_half(
                b - 1, 0, (high_chain.mixed,), mixed_grad, (early_part,) if b > 1 else ()
            )
            low = returning(low_chain, first_part)
            token_grad, second_part = back_half(b - 1, 1, (low,), mixed_grad, (*more, res_grad))
            low = to_groups(low)
            high = returning(high_chain, second_part, low)
            totals = grads_half(1, (high,), totals)
            high = to_groups(high)
        layers, token_grads = (layer,), (token_grad,)
        early_part, first_part, second_part = (early_part,), (first_part,), (second_part,)
    layer, res_grad, mixed_grad, early_part = back_tokens(batches - 1, (totals[0],), low, high)
    diagonal, part, *first_part = back_half(batches - 1, 0, (), mixed_grad, (early_part,))
    first_half = add_half(*first_part)
    token_grad, *second_part = back_half(batches - 1, 1, (first_half,), mixed_grad, (diagonal, part, res_grad))
    far = groups // 2
    first = share_sums(first_half, "expert", 2, far)
    second_mine, second_other = second_part
    (second_other,) = gate((second_other,), (first,))
    first = share_sums(first, "hidden", 1, planes)
    second = add_half(second_mine, second_other)
    (first,) = gate((first,), (second,))
    second = share_sums(second, "expert", 2, far)
    first = join_sums(first, "hidden", 1, planes)
    first = join_sums(first, "expert", 2, far)
    second = share_sums(second, "hidden", 1, planes)
    second = join_sums(second, "hidden", 1, planes)
    second = join_sums(second, "expert", 2, far)
    mine, other = first, swap(first, "expert", 1)
    mine_second, other_second = second, swap(second, "expert", 1)
    query_grad, key_grad, value_grad, output_grad, router_grad, gain_f_grad, gain_a_grad, bias_grad = unpack(
        early_rows, experts, side, mine, other, mine_second, other_second
    )
    return (
        layer,
        token_grad,
        gain_a_grad,
        query_grad,
        key_grad,
        value_grad,
        output_grad,
        bias_grad.T,
        gain_f_grad,
        router_grad.T,
        totals[1],
        totals[0],
    )


def solution(mesh):
    token = P(None, ("expert", "hidden"), None, None)
    placed = (
        token,
        token,
        P(None, ("expert", "hidden")),
        token,
        *(P() for _ in range(8)),
        P("expert", None, "hidden"),
        P("expert", "hidden", None),
    )
    return jax.shard_map(
        shards,
        mesh=mesh,
        in_specs=placed,
        out_specs=(
            token,
            token,
            *(P() for _ in range(8)),
            P("expert", None, "hidden"),
            P("expert", "hidden", None),
        ),
        check_vma=False,
    )
```
